32 devices in a mesh: dp: 8 (over y, x, core), fsdp: 4 (over z).
Axes of the slice: x: 2, y: 2, z: 4, core: 2. Of those that a mesh axis runs over, the one named last changes fastest.
Arguments:
- act_short: bfloat16 [1024, 768], P(('dp', 'fsdp')), may hold values from -6 to 6
- act_long: bfloat16 [4096, 768], P(('dp', 'fsdp')), may hold values from -6 to 6
- len_short: int32 [32], P(('dp', 'fsdp')), may hold values from 16 to 32, as said below
- len_long: int32 [32], P(('dp', 'fsdp')), may hold values from 64 to 128, as said below
- w_qkv: bfloat16 [2, 768, 2304], P(None, ('dp', 'fsdp')), may hold values from -0.21875 to 0.21875
- w_out: bfloat16 [2, 768, 768], P(None, ('dp', 'fsdp')), may hold values from -0.21875 to 0.21875
- w_up: bfloat16 [2, 768, 3072], P(None, ('dp', 'fsdp')), may hold values from -0.21875 to 0.21875
- w_down: bfloat16 [2, 3072, 768], P(None, ('dp', 'fsdp')), may hold values from -0.109375 to 0.109375
- gains_d: bfloat16 [2, 3, 768], P(None, None, ('dp', 'fsdp')), may hold values from 0.25 to 1.75
- shifts_d: bfloat16 [2, 7, 768], P(None, None, ('dp', 'fsdp')), may hold values from -1.5 to 1.5
- gains_ff: bfloat16 [2, 3072], P(None, ('dp', 'fsdp')), may hold values from 0.25 to 1.75
- shifts_ff: bfloat16 [2, 2, 3072], P(None, None, ('dp', 'fsdp')), may hold values from -1.5 to 1.5
- cot_short: bfloat16 [1024, 768], P(('dp', 'fsdp')), may hold values from -6 to 6
- cot_long: bfloat16 [4096, 768], P(('dp', 'fsdp')), may hold values from -6 to 6
Outputs:
- out_short: bfloat16 [1024, 768], P(('dp', 'fsdp'))
- out_long: bfloat16 [4096, 768], P(('dp', 'fsdp'))
- grad_short: float32 [1024, 768], P(('dp', 'fsdp'))
- grad_long: float32 [4096, 768], P(('dp', 'fsdp'))
- grad_qkv: float32 [2, 768, 2304], P(None, ('dp', 'fsdp'))
- grad_out: float32 [2, 768, 768], P(None, ('dp', 'fsdp'))
- grad_up: float32 [2, 768, 3072], P(None, ('dp', 'fsdp'))
- grad_down: float32 [2, 3072, 768], P(None, ('dp', 'fsdp'))
- grad_gains_d: float32 [2, 3, 768], P(None, None, ('dp', 'fsdp'))
- grad_shifts_d: float32 [2, 7, 768], P(None, None, ('dp', 'fsdp'))
- grad_gains_ff: float32 [2, 3072], P(None, ('dp', 'fsdp'))
- grad_shifts_ff: float32 [2, 2, 3072], P(None, None, ('dp', 'fsdp'))
The draws below stay inside these ranges and needn't reach their ends.
Inputs may be any that keep to these rules, and one draw needn't show every extreme that they name: `len_short`: each entry is the number of real tokens of one short sequence; at least 16, and exactly 32 for some sequence. `len_long`: each entry is the number of real tokens of one long sequence; at least 64, and exactly 128 for some sequence.
All inputs are finite; a program needn't handle non-finite values.
Results may differ from the reference program's by a relative error of at most 0.015.
Values may be sent and summed in bfloat16 or wider, within the bound.
A program may use at most 320 MiB of HBM per device.

```python
import jax
import jax.numpy as jnp
from jax import lax

HEADS = 12
HEAD_DIM = 64
D = 768
FF = 3072
LAYERS = 2
LEN_SHORT = 32
LEN_LONG = 128
SEQS = 32
ROWS_SHORT = 1024
ROWS_LONG = 4096


def bucket_lengths(key, longest, number):
    key_one, key_two = jax.random.split(key)
    drawn = jax.random.randint(key_one, (number,), longest // 2, longest + 1)
    chosen = jax.random.randint(key_two, (), 0, number)
    return jnp.where(jnp.arange(number) == chosen, longest, drawn).astype(jnp.int32)


def draw_len_short(key, part):
    key = jax.random.fold_in(key, 1)
    return bucket_lengths(key, LEN_SHORT, SEQS)


def draw_len_long(key, part):
    key = jax.random.fold_in(key, 2)
    return bucket_lengths(key, LEN_LONG, SEQS)


def steps_of(stream_key, shape, pieces, smallest, top_value):
    gain = 1.0
    for axis_at, shards_of in pieces:
        draws = jax.random.uniform(jax.random.fold_in(jax.random.fold_in(stream_key, 6), axis_at), (shards_of,), jnp.float32, smallest / len(pieces), top_value / len(pieces))
        gain = gain * jnp.repeat(jnp.exp(draws), shape[axis_at] // shards_of).reshape((-1,) + (1,) * (len(shape) - 1 - axis_at))
    return gain


def noise(key, shape, scale, bound, shards=(), kind=jnp.bfloat16):
    values = jax.random.normal(key, shape, jnp.float32) * scale
    if len(shards) > 0:
        values = steps_of(key, shape, shards, -0.22, 0.18) * values
    return jnp.clip(values, min=-bound, max=bound).astype(kind)


def setup_inputs(seed: int = 0) -> dict:
    arg_keys = jax.random.split(jax.random.key(seed), 15)
    return {
        "act_short": noise(arg_keys[0], (ROWS_SHORT, D), 1.0, 6.0, ((0, 32),)),
        "act_long": noise(arg_keys[1], (ROWS_LONG, D), 1.0, 6.0, ((0, 32),)),
        "len_short": draw_len_short(jax.random.fold_in(arg_keys[14], 71), 0),
        "len_long": draw_len_long(jax.random.fold_in(arg_keys[14], 71), 0),
        "w_qkv": noise(arg_keys[4], (LAYERS, D, 3 * D), D ** -0.5, 0.21875, ((1, 32),)),
        "w_out": noise(arg_keys[5], (LAYERS, D, D), D ** -0.5, 0.21875, ((1, 32),)),
        "w_up": noise(arg_keys[6], (LAYERS, D, FF), D ** -0.5, 0.21875, ((1, 32),)),
        "w_down": noise(arg_keys[7], (LAYERS, FF, D), FF ** -0.5, 0.109375, ((1, 32),)),
        "gains_d": jnp.clip(1.0 + 0.15 * jax.random.normal(arg_keys[8], (LAYERS, 3, D), jnp.float32), 0.25, 1.75).astype(jnp.bfloat16),
        "shifts_d": noise(arg_keys[9], (LAYERS, 7, D), 0.3, 1.5, ((2, 32),)),
        "gains_ff": jnp.clip(1.0 + 0.15 * jax.random.normal(arg_keys[10], (LAYERS, FF), jnp.float32), 0.25, 1.75).astype(jnp.bfloat16),
        "shifts_ff": noise(arg_keys[11], (LAYERS, 2, FF), 0.3, 1.5, ((2, 32),)),
        "cot_short": noise(arg_keys[12], (ROWS_SHORT, D), 1.0, 6.0, ((0, 32),)),
        "cot_long": noise(arg_keys[13], (ROWS_LONG, D), 1.0, 6.0, ((0, 32),)),
    }


epsilon = 1e-05
exact_mode = lax.Precision.HIGHEST
per_group = 8

@jax.custom_vjp
def low(v):
    return lax.optimization_barrier(v.astype(jnp.bfloat16)).astype(jnp.float32)

@jax.custom_vjp
def low_back(v):
    return v

def low_keep(v):
    return (low(v), None)

def low_pass(kept, grad):
    return (grad,)

def back_keep(v):
    return (v, None)

def back_low(kept, grad):
    return (low(grad),)
low.defvjp(low_keep, low_pass)
low_back.defvjp(back_keep, back_low)

def layer_norm(values, gains, shifts):
    centered = values - lax.optimization_barrier(jnp.mean(values, -1, keepdims=True))
    variance = lax.optimization_barrier(jnp.mean(centered * centered, -1, keepdims=True))
    return centered * lax.rsqrt(variance + epsilon) * gains + shifts

def project(block_rows, matrix):
    return jnp.einsum('gld,de->gle', block_rows, matrix, precision=exact_mode)

def attention(qkv_rows, length):
    seq_len = qkv_rows.shape[0]
    split_rows = qkv_rows.reshape(seq_len, 3, HEADS, HEAD_DIM)
    queries = split_rows[:, 0]
    key_rows = split_rows[:, 1]
    value_rows = split_rows[:, 2]
    scores = jnp.einsum('qhd,khd->hqk', queries, key_rows, precision=exact_mode) * HEAD_DIM ** (-0.5)
    scores = low_back(scores)
    valid_keys = jnp.arange(seq_len) < length
    scores = jnp.where(valid_keys[None, None, :], scores, -1000000000.0)
    top_score = lax.optimization_barrier(jnp.max(scores, -1, keepdims=True))
    exp_scores = jnp.exp(scores - top_score)
    probability = low(exp_scores / lax.optimization_barrier(jnp.sum(exp_scores, -1, keepdims=True)))
    context = jnp.einsum('hqk,khd->qhd', probability, value_rows, precision=exact_mode)
    return low_back(context.reshape(seq_len, HEADS * HEAD_DIM))

def one_layer(block_rows, block_len, params):
    w_qkv, w_out, w_up, w_down, gains_d, shifts_d, gains_ff, shifts_ff = params
    normed = low(layer_norm(block_rows, gains_d[0], shifts_d[0]))
    qkv_shift = jnp.concatenate([shifts_d[3], jnp.zeros_like(shifts_d[3]), shifts_d[4]])
    qkv_rows = low(low_back(project(normed, w_qkv) + qkv_shift))
    context = jax.vmap(attention)(qkv_rows, block_len)
    sub_low = low(layer_norm(context, gains_d[1], shifts_d[1]))
    after_attn = block_rows + low_back(project(sub_low, w_out) + shifts_d[5])
    normed_ffn = low(layer_norm(after_attn, gains_d[2], shifts_d[2]))
    hidden = low_back(project(normed_ffn, w_up) + shifts_ff[0])
    sub_ffn = low(layer_norm(jax.nn.gelu(hidden), gains_ff, shifts_ff[1]))
    return after_attn + low_back(project(sub_ffn, w_down) + shifts_d[6])

def run_bucket(params, bucket_rows, lengths):
    seq_len = bucket_rows.shape[1]
    grouped = bucket_rows.reshape(-1, per_group, seq_len, bucket_rows.shape[2])
    grouped_len = lengths.reshape(-1, per_group)

    def run_group(group_pair):
        block_rows, block_len = group_pair
        for layer_idx in range(LAYERS):
            block_rows = one_layer(block_rows, block_len, tuple((member[layer_idx] for member in params)))
        return block_rows
    result = lax.map(jax.checkpoint(run_group), (grouped, grouped_len))
    return result.reshape(bucket_rows.shape)

def reference(act_short, act_long, len_short, len_long, w_qkv, w_out, w_up, w_down, gains_d, shifts_d, gains_ff, shifts_ff, cot_short, cot_long):
    params = tuple((member.astype(jnp.float32) for member in (w_qkv, w_out, w_up, w_down, gains_d, shifts_d, gains_ff, shifts_ff)))
    rows_short = act_short.astype(jnp.float32).reshape(SEQS, LEN_SHORT, D)
    rows_long = act_long.astype(jnp.float32).reshape(SEQS, LEN_LONG, D)

    def whole(params, rows_short, rows_long):
        return (run_bucket(params, rows_short, len_short), run_bucket(params, rows_long, len_long))
    (res_short, res_long), pullback = jax.vjp(whole, params, rows_short, rows_long)
    mask_short = (jnp.arange(LEN_SHORT)[None, :] < len_short[:, None]).astype(jnp.float32)[:, :, None]
    mask_long = (jnp.arange(LEN_LONG)[None, :] < len_long[:, None]).astype(jnp.float32)[:, :, None]
    back_short = cot_short.astype(jnp.float32).reshape(SEQS, LEN_SHORT, D) * mask_short
    back_long = cot_long.astype(jnp.float32).reshape(SEQS, LEN_LONG, D) * mask_long
    grad_params, grad_short, grad_long = pullback((back_short, back_long))
    grad_qkv, grad_out, grad_up, grad_down, grad_gains_d, grad_shifts_d, grad_gains_ff, grad_shifts_ff = grad_params
    return (res_short.reshape(-1, D).astype(jnp.bfloat16), res_long.reshape(-1, D).astype(jnp.bfloat16), grad_short.reshape(-1, D), grad_long.reshape(-1, D), grad_qkv, grad_out, grad_up, grad_down, grad_gains_d, grad_shifts_d, grad_gains_ff, grad_shifts_ff)
```

```python
import functools

import jax
import jax.numpy as jnp
import numpy as np
from jax import lax
from jax.experimental import pallas as pl
from jax.experimental.pallas import tpu as pltpu
from jax.sharding import PartitionSpec as P

HEAD_DIM = 64
LAYERS = 2

epsilon = 1e-05


def layer_norm(values, gains, shifts):
    centered = values - jnp.mean(values, -1, keepdims=True)
    variance = jnp.mean(centered * centered, -1, keepdims=True)
    return centered * lax.rsqrt(variance + epsilon) * gains + shifts


def gelu_norm(hidden, gains, shifts):
    return layer_norm(jax.nn.gelu(hidden), gains, shifts)


def norm_back(values, gains, shifts, incoming):
    outputs, pullback = jax.vjp(layer_norm, values, gains, shifts)
    return pullback(incoming)


def matmul(left, right):
    return jnp.dot(left, right, preferred_element_type=jnp.float32)


def matmul_nt(left, right):
    return lax.dot_general(
        left, right, (((1,), (1,)), ((), ())), preferred_element_type=jnp.float32
    )


def matmul_tn(left, right):
    return lax.dot_general(
        left, right, (((0,), (0,)), ((), ())), preferred_element_type=jnp.float32
    )


def col_sums(values):
    return jnp.sum(values.astype(jnp.float32), 0)


def attention_parts(qkv_low):
    seq_len = qkv_low.shape[0]
    split_rows = qkv_low.reshape(seq_len, 3, -1, HEAD_DIM)
    return (split_rows[:, 0], split_rows[:, 1], split_rows[:, 2])


def raw_scores(queries, key_rows, length):
    scores = jnp.einsum(
        "qhd,khd->hqk", queries, key_rows, preferred_element_type=jnp.float32
    ) * HEAD_DIM ** (-0.5)
    valid_keys = jnp.arange(key_rows.shape[0]) < length
    return jnp.where(valid_keys[None, None, :], scores, -1000000000.0)


def attend_forward(qkv_low, length):
    queries, key_rows, value_rows = attention_parts(qkv_low)
    scores = raw_scores(queries, key_rows, length)
    top_score = jnp.max(scores, -1, keepdims=True)
    exp_scores = jnp.exp(scores - top_score)
    totals = jnp.sum(exp_scores, -1, keepdims=True)
    probability = (exp_scores / totals).astype(jnp.bfloat16)
    context = jnp.einsum(
        "hqk,khd->qhd", probability, value_rows, preferred_element_type=jnp.float32
    )
    return (context.reshape(qkv_low.shape[0], -1), top_score + jnp.log(totals))


def attend_backward(qkv_low, length, log_total, d_context_low):
    queries, key_rows, value_rows = attention_parts(qkv_low)
    seq_len = qkv_low.shape[0]
    probability = jnp.exp(raw_scores(queries, key_rows, length) - log_total)
    prob_low = probability.astype(jnp.bfloat16)
    d_heads = d_context_low.reshape(seq_len, -1, HEAD_DIM)
    d_values = jnp.einsum("hqk,qhd->khd", prob_low, d_heads, preferred_element_type=jnp.float32)
    d_probs = jnp.einsum("qhd,khd->hqk", d_heads, value_rows, preferred_element_type=jnp.float32)
    row_dot = jnp.sum(probability * d_probs, -1, keepdims=True)
    d_scores = (probability * (d_probs - row_dot)).astype(jnp.bfloat16)
    d_queries = jnp.einsum(
        "hqk,khd->qhd", d_scores, key_rows, preferred_element_type=jnp.float32
    ) * HEAD_DIM ** (-0.5)
    d_keys = jnp.einsum(
        "hqk,qhd->khd", d_scores, queries, preferred_element_type=jnp.float32
    ) * HEAD_DIM ** (-0.5)
    return jnp.stack([d_queries, d_keys, d_values], 1).reshape(seq_len, -1)


def by_blocks(left, blocks):
    return jnp.concatenate([matmul(left, block) for block in blocks], 1)


def back_blocks(left, blocks):
    width = blocks[0].shape[1]
    return sum(
        matmul_nt(left[:, at * width : (at + 1) * width], block) for at, block in enumerate(blocks)
    )


def unpack(weights):
    w_qkv, w_out, w_up, w_down, gains_d, shifts_d, gains_ff, shifts_ff = weights
    return (
        w_qkv,
        w_out,
        w_up,
        w_down,
        gains_d.astype(jnp.float32),
        shifts_d.astype(jnp.float32),
        gains_ff.astype(jnp.float32),
        shifts_ff.astype(jnp.float32),
    )


def layer_forward(layer_rows, length, weights):
    w_qkv, w_out, w_up, w_down, gains_d, shifts_d, gains_ff, shifts_ff = unpack(weights)
    normed = layer_norm(layer_rows, gains_d[0], shifts_d[0]).astype(jnp.bfloat16)
    qkv_shift = jnp.concatenate([shifts_d[3], jnp.zeros_like(shifts_d[3]), shifts_d[4]])
    qkv_low = (by_blocks(normed, w_qkv) + qkv_shift).astype(jnp.bfloat16)
    context, log_total = attend_forward(qkv_low, length)
    sub_low = layer_norm(context, gains_d[1], shifts_d[1]).astype(jnp.bfloat16)
    after_attn = layer_rows + (matmul(sub_low, w_out) + shifts_d[5])
    normed_ffn = layer_norm(after_attn, gains_d[2], shifts_d[2]).astype(jnp.bfloat16)
    hidden = by_blocks(normed_ffn, w_up) + shifts_ff[0]
    sub_ffn = gelu_norm(hidden, gains_ff, shifts_ff[1]).astype(jnp.bfloat16)
    result = after_attn + (matmul(sub_ffn, w_down) + shifts_d[6])
    saved_state = (
        layer_rows,
        normed,
        qkv_low,
        context,
        log_total,
        sub_low,
        after_attn,
        normed_ffn,
        hidden,
        sub_ffn,
    )
    return (result, saved_state)


def layer_backward(d_result, length, saved_state, weights):
    w_qkv, w_out, w_up, w_down, gains_d, shifts_d, gains_ff, shifts_ff = unpack(weights)
    (
        layer_rows,
        normed,
        qkv_low,
        context,
        log_total,
        sub_low,
        after_attn,
        normed_ffn,
        hidden,
        sub_ffn,
    ) = saved_state
    model_width = w_out.shape[0]
    d_branch = d_result.astype(jnp.bfloat16)
    grad_down = matmul_tn(sub_ffn, d_branch)
    shift_six = col_sums(d_branch)
    d_sub_ffn = matmul_nt(d_branch, w_down)
    outputs, pullback = jax.vjp(gelu_norm, hidden, gains_ff, shifts_ff[1])
    d_hidden_full, grad_gains_ff, shift_ff_one = pullback(d_sub_ffn)
    d_hidden = d_hidden_full.astype(jnp.bfloat16)
    grad_up = matmul_tn(normed_ffn, d_hidden)
    shift_ff_zero = col_sums(d_hidden)
    d_normed_ffn = back_blocks(d_hidden, w_up)
    d_after_norm, gain_two, shift_two = norm_back(after_attn, gains_d[2], shifts_d[2], d_normed_ffn)
    d_after = d_result + d_after_norm
    d_attn = d_after.astype(jnp.bfloat16)
    grad_out = matmul_tn(sub_low, d_attn)
    shift_five = col_sums(d_attn)
    d_sub_low = matmul_nt(d_attn, w_out)
    d_context, gain_one, shift_one = norm_back(context, gains_d[1], shifts_d[1], d_sub_low)
    d_qkv = attend_backward(qkv_low, length, log_total, d_context.astype(jnp.bfloat16)).astype(
        jnp.bfloat16
    )
    grad_qkv = matmul_tn(normed, d_qkv)
    qkv_sums = col_sums(d_qkv)
    d_normed = back_blocks(d_qkv, w_qkv)
    d_rows_norm, gain_zero, shift_zero = norm_back(layer_rows, gains_d[0], shifts_d[0], d_normed)
    d_rows = d_after + d_rows_norm
    grad_gains = jnp.stack([gain_zero, gain_one, gain_two])
    grad_shifts = jnp.stack(
        [
            shift_zero,
            shift_one,
            shift_two,
            qkv_sums[:model_width],
            qkv_sums[2 * model_width :],
            shift_five,
            shift_six,
        ]
    )
    grad_shifts_ff = jnp.stack([shift_ff_zero, shift_ff_one])
    return (
        d_rows,
        (
            grad_qkv,
            grad_out,
            grad_up,
            grad_down,
            grad_gains,
            grad_shifts,
            grad_gains_ff,
            grad_shifts_ff,
        ),
    )


BF = jnp.bfloat16
F32 = jnp.float32
MESH = pl.DeviceIdType.MESH


def round16(count):
    return (count + 15) // 16 * 16


class Geometry:
    def __init__(self, n_dp, n_z, w_qkv, w_up, w_down, vec_size):
        self.n_dp, self.n_z, self.n_y = n_dp, n_z, n_dp // 4
        self.layers = w_qkv[0]
        self.width = w_qkv[2] // 3
        self.rows_a, self.rows_b = w_qkv[1], w_down[1]
        self.blocks = 4 + w_up[2] // self.width
        self.pairs = self.blocks // 2
        self.halves = 2
        self.kind = {
            "a": (2, round16(2 * self.rows_a), self.rows_a * n_z, self.width),
            "b": (1, round16(self.rows_b), self.rows_b * n_z, self.width // 2),
            "v": (1, round16(-(-vec_size // 128)), round16(-(-vec_size // 128)) * n_z, 128),
        }
        self.real = {"a": self.rows_a, "b": self.rows_b, "v": self.kind["v"][1]}
        self.number = {"a": self.layers * self.pairs, "b": self.layers * self.halves, "v": 1}

    def permuted(self, name):
        k, sent, unit, _ = self.kind[name]
        return k * unit != sent * self.n_z or k > 1

    def permutation(self, name):
        k, sent, unit, _ = self.kind[name]
        real = self.real[name]
        table = np.zeros((k * unit, self.n_z * sent), np.float32)
        for block in range(k):
            for z in range(self.n_z):
                for row in range(real):
                    table[block * unit + z * real + row, z * sent + block * real + row] = 1
        return table

    def whole_shape(self, name):
        _, _, unit, lanes = self.kind[name]
        lead = {"a": self.layers * self.blocks, "b": self.layers, "v": 1}[name]
        lanes = self.width if name == "b" else lanes
        return (lead, self.n_y, 2, 2, unit, lanes)


class Place:
    def __init__(self, geo):
        self.geo = geo
        self.d, self.z = lax.axis_index("dp"), lax.axis_index("fsdp")
        self.core = lax.rem(self.d, 2)
        self.x = lax.rem(self.d // 2, 2)
        self.y = self.d // 4

    def y_off(self, step):
        return lax.rem(self.y + step + self.geo.n_y, self.geo.n_y)

    def z_off(self, step):
        return lax.rem(self.z + step + self.geo.n_z, self.geo.n_z)

    def dev_core(self):
        return (self.d + 1 - 2 * self.core, self.z)

    def dev_x(self):
        return (self.d + 2 - 4 * self.x, self.z)

    def dev_y(self, step):
        return (self.y_off(step) * 4 + self.x * 2 + self.core, self.z)

    def dev_z(self, step):
        return (self.d, self.z_off(step))

    def greet(self):
        barrier = pltpu.get_barrier_semaphore()
        partners = [self.dev_core(), self.dev_x()]
        partners += [self.dev_y(step) for step in range(1, self.geo.n_y)]
        partners += [self.dev_z(step) for step in range(1, self.geo.n_z)]
        for partner in partners:
            pl.semaphore_signal(barrier, inc=1, device_id=partner, device_id_type=MESH)
        pl.semaphore_wait(barrier, len(partners))


def remote(src, dst, send, recv, device):
    return pltpu.make_async_remote_copy(
        src_ref=src, dst_ref=dst, send_sem=send, recv_sem=recv, device_id=device, device_id_type=MESH
    )


def column(whole, name, lead, half, k, lanes):
    def at(*where):
        picked = whole.at[(pl.ds(lead, k),) + where]
        if name == "b":
            picked = whole.at[(pl.ds(lead, k),) + where + (slice(None), pl.ds(half * lanes, lanes))]
        return picked

    return at


def chunk_list(geo, layers):
    found = []
    for layer in layers:
        for pair in range(geo.pairs):
            found.append(("a", layer * geo.pairs + pair, layer * geo.blocks + 2 * pair, 0))
        for half in range(geo.halves):
            found.append(("b", layer * geo.halves + half, layer, half))
    return found


class Gather:
    def __init__(self, place, number, chunk, sources, bufs, units, perms, wholes, sems):
        self.p, self.c = place, number
        name, at, lead, half = chunk
        self.half_a = number % 2 == 0
        k, self.sent, _, lanes = place.geo.kind[name]
        self.source = sources[name].at[at]
        self.buf = bufs[name].at[at]
        self.perm = perms.get(name)
        self.unit_buf = units[name].at[at] if self.perm is not None else None
        self.unit = self.unit_buf if self.perm is not None else bufs[name].at[pl.ds(at, 1)]
        self.to = column(wholes[name], name, lead, half, k, lanes)
        self.sems = sems
        self.pending = []

    def slot(self, z):
        return self.buf.at[pl.ds(pl.multiple_of(z * self.sent, 16), self.sent)]

    def send(self, src, dst, send, recv, device):
        copy = remote(src, dst, send, recv, device)
        copy.start()
        self.pending.append(copy)

    def arrived(self, dst, send, recv, device):
        remote(dst, dst, send, recv, device).wait_recv()

    def start_z(self):
        p, s, c = self.p, self.sems, self.c
        self.local_z = pltpu.make_async_copy(self.source, self.slot(p.z), s["lz"].at[c])
        self.local_z.start()
        for step in range(1, p.geo.n_z):
            self.send(self.source, self.slot(p.z), s["zs"].at[c, step], s["zr"].at[c, step], p.dev_z(step))

    def own(self):
        p, s, c = self.p, self.sems, self.c
        self.local_z.wait()
        for step in range(1, p.geo.n_z):
            self.arrived(self.slot(p.z_off(-step)), s["zs"].at[c, step], s["zr"].at[c, step], p.dev_z(step))
        if self.perm is not None:
            k, unit, lanes = self.unit_buf.shape
            mixed = jnp.dot(self.perm[...], self.buf[...], preferred_element_type=F32)
            self.unit_buf[...] = mixed.astype(BF).reshape(k, unit, lanes)
        here = self.to(p.y, p.x, p.core)
        self.local = pltpu.make_async_copy(self.unit, here, s["lo"].at[c])
        self.send(self.unit, here, s["xs"].at[c], s["xr"].at[c], p.dev_x())
        for step in range(1, p.geo.n_y):
            self.send(self.unit, here, s["ys"].at[c, step], s["yr"].at[c, step], p.dev_y(step))
        self.send(self.unit, here, s["cs"].at[c, 0], s["cr"].at[c, 0], p.dev_core())
        self.local.start()

    def forward(self):
        p, s, c = self.p, self.sems, self.c
        n_y = p.geo.n_y
        from_x = self.to(p.y, 1 - p.x, p.core)
        self.arrived(from_x, s["xs"].at[c], s["xr"].at[c], p.dev_x())
        if self.half_a:
            for step in range(1, n_y):
                self.send(from_x, from_x, s["ds"].at[c, step], s["dr"].at[c, step], p.dev_y(step))
        self.send(from_x, from_x, s["cs"].at[c, 1], s["cr"].at[c, 1], p.dev_core())
        for step in range(1, n_y):
            from_y = self.to(p.y_off(-step), p.x, p.core)
            self.arrived(from_y, s["ys"].at[c, step], s["yr"].at[c, step], p.dev_y(step))
            if not self.half_a:
                self.send(from_y, from_y, s["ds"].at[c, step], s["dr"].at[c, step], p.dev_x())
            self.send(from_y, from_y, s["cs"].at[c, 2 * step], s["cr"].at[c, 2 * step], p.dev_core())

    def corner(self):
        p, s, c = self.p, self.sems, self.c
        for step in range(1, p.geo.n_y):
            far = self.to(p.y_off(-step), 1 - p.x, p.core)
            self.arrived(far, s["ds"].at[c, step], s["dr"].at[c, step], p.dev_x())
            self.send(far, far, s["cs"].at[c, 2 * step + 1], s["cr"].at[c, 2 * step + 1], p.dev_core())

    def finish(self):
        p, s, c = self.p, self.sems, self.c
        for step in range(p.geo.n_y):
            for flip in range(2):
                x = p.x if flip == 0 else 1 - p.x
                got = self.to(p.y_off(-step), x, 1 - p.core)
                at = 2 * step + flip
                self.arrived(got, s["cs"].at[c, at], s["cr"].at[c, at], p.dev_core())
        self.local.wait()
        for copy in self.pending:
            copy.wait_send()


def run_pipeline(stages, count):
    last = max(lag for lag, _ in stages)
    first = min(lag for lag, _ in stages)
    for step in range(first, count + last):
        for lag, act in stages:
            if 0 <= step - lag < count:
                act(step - lag)


def gather_kernel(geo, names_perm, *refs):
    refs = list(refs)
    take = lambda number: [refs.pop(0) for _ in range(number)]
    kinds = ("a", "b", "v")
    sources = dict(zip(kinds, take(3)))
    perms = dict(zip(names_perm, take(len(names_perm))))
    wholes = dict(zip(kinds, take(3)))
    bufs = dict(zip(kinds, take(3)))
    units = dict(zip(names_perm, take(len(names_perm))))
    sems = dict(zip(("lz", "lo", "zs", "zr", "xs", "xr", "ys", "yr", "ds", "dr", "cs", "cr"), take(12)))
    place = Place(geo)
    chunks = [("v", 0, 0, 0)] + chunk_list(geo, range(geo.layers))
    moves = [
        Gather(place, at, chunk, sources, bufs, units, perms, wholes, sems)
        for at, chunk in enumerate(chunks)
    ]
    place.greet()
    run_pipeline(
        [
            (-2, lambda c: moves[c].start_z()),
            (0, lambda c: moves[c].own()),
            (1, lambda c: moves[c].forward()),
            (2, lambda c: moves[c].corner()),
        ],
        len(moves),
    )
    for move in moves:
        move.finish()


def dma(*shape):
    return pltpu.SemaphoreType.DMA(shape)


ANY = pl.BlockSpec(memory_space=pl.ANY)
IN_VMEM = pl.BlockSpec(memory_space=pltpu.VMEM)


def gather_all(geo, source_a, source_b, source_v):
    names_perm = [name for name in ("a", "b", "v") if geo.permuted(name)]
    perms = [jnp.asarray(geo.permutation(name), BF) for name in names_perm]
    total = sum(geo.number.values())
    bufs, units = [], []
    for name in ("a", "b", "v"):
        k, sent, unit, lanes = geo.kind[name]
        bufs.append(pltpu.VMEM((geo.number[name], geo.n_z * sent, lanes), BF))
        if name in names_perm:
            units.append(pltpu.VMEM((geo.number[name], k, unit, lanes), BF))
    n_y, n_z = geo.n_y, geo.n_z
    return pl.pallas_call(
        functools.partial(gather_kernel, geo, names_perm),
        out_shape=[jax.ShapeDtypeStruct(geo.whole_shape(name), BF) for name in ("a", "b", "v")],
        in_specs=[IN_VMEM] * (3 + len(perms)),
        out_specs=[ANY] * 3,
        scratch_shapes=bufs
        + units
        + [
            dma(total),
            dma(total),
            dma(total, n_z),
            dma(total, n_z),
            dma(total),
            dma(total),
            dma(total, n_y),
            dma(total, n_y),
            dma(total, n_y),
            dma(total, n_y),
            dma(total, 2 * n_y),
            dma(total, 2 * n_y),
        ],
        compiler_params=pltpu.CompilerParams(
            collective_id=0, has_side_effects=True, vmem_limit_bytes=40 * 2**20
        ),
    )(source_a, source_b, source_v, *perms)


def wide(values):
    return values.astype(F32)


class Scatter:
    def __init__(self, place, number, chunk, grads, loads, sums, mids, ends, perms, z_send, z_recv, outs, sems):
        self.p, self.c = place, number
        name, at, lead, half = chunk
        self.half_a = number % 2 == 0
        self.k, self.sent, self.rows, self.lanes = place.geo.kind[name]
        self.grad = column(grads[name], name, lead, half, self.k, self.lanes)
        self.load = loads[name].at[number % 2]
        self.sum = sums[name].at[at]
        self.mid = mids[name].at[at]
        self.end = ends[name].at[at]
        self.perm = perms.get(name)
        self.z_send, self.z_recv = z_send[name].at[at], z_recv[name].at[at]
        self.out = outs[name].at[at]
        self.sems = sems
        self.pending = []

    def send(self, src, dst, send, recv, device):
        copy = remote(src, dst, send, recv, device)
        copy.start()
        self.pending.append(copy)

    def arrived(self, dst, send, recv, device):
        remote(dst, dst, send, recv, device).wait_recv()

    def start(self):
        p, s, c = self.p, self.sems, self.c
        every = slice(None)
        self.send(self.grad(every, every, 1 - p.core), self.sum, s["cs"].at[c], s["cr"].at[c], p.dev_core())
        self.local = pltpu.make_async_copy(self.grad(every, every, p.core), self.load, s["lo"].at[c])
        self.local.start()

    def pair(self):
        p, s, c = self.p, self.sems, self.c
        n_y = p.geo.n_y
        self.local.wait()
        self.arrived(self.sum, s["cs"].at[c], s["cr"].at[c], p.dev_core())

        @pl.loop(0, self.k * n_y * 2)
        def _(at):
            where = (at // (2 * n_y), lax.rem(at // 2, n_y), lax.rem(at, 2))
            self.sum[where] = (wide(self.sum[where]) + wide(self.load[where])).astype(BF)

        if self.half_a:
            for step in range(1, n_y):
                self.send(
                    self.sum.at[:, p.y_off(step)], self.mid.at[step - 1, :, pl.ds(0, 2)],
                    s["ms"].at[c, step], s["mr"].at[c, step], p.dev_y(step),
                )
        else:
            self.send(
                self.sum.at[:, :, 1 - p.x], self.mid.at[0, :, pl.ds(0, n_y)],
                s["ms"].at[c, 0], s["mr"].at[c, 0], p.dev_x(),
            )

    def middle(self):
        p, s, c = self.p, self.sems, self.c
        n_y = p.geo.n_y
        if self.half_a:
            for step in range(1, n_y):
                self.arrived(self.mid.at[step - 1, :, pl.ds(0, 2)], s["ms"].at[c, step], s["mr"].at[c, step], p.dev_y(step))

            @pl.loop(0, self.k * 2)
            def _(at):
                where = (at // 2, p.y, lax.rem(at, 2))
                value = wide(self.sum[where])
                for step in range(1, n_y):
                    value = value + wide(self.mid[step - 1, at // 2, lax.rem(at, 2)])
                self.sum[where] = value.astype(BF)

            self.send(
                self.sum.at[:, p.y, 1 - p.x], self.end.at[0], s["es"].at[c, 0], s["er"].at[c, 0], p.dev_x()
            )
        else:
            self.arrived(self.mid.at[0, :, pl.ds(0, n_y)], s["ms"].at[c, 0], s["mr"].at[c, 0], p.dev_x())

            @pl.loop(0, self.k * n_y)
            def _(at):
                where = (at // n_y, lax.rem(at, n_y), p.x)
                value = wide(self.sum[where]) + wide(self.mid[0, at // n_y, lax.rem(at, n_y)])
                self.sum[where] = value.astype(BF)

            for step in range(1, n_y):
                self.send(
                    self.sum.at[:, p.y_off(step), p.x], self.end.at[step - 1],
                    s["es"].at[c, step], s["er"].at[c, step], p.dev_y(step),
                )

    def last(self):
        p, s, c = self.p, self.sems, self.c
        n_y, n_z = p.geo.n_y, p.geo.n_z
        if self.half_a:
            arrivals = [(0, self.end.at[0], p.dev_x())]
        else:
            arrivals = [(step, self.end.at[step - 1], p.dev_y(step)) for step in range(1, n_y)]
        value = wide(self.sum[:, p.y, p.x])
        for at, got, device in arrivals:
            self.arrived(got, s["es"].at[c, at], s["er"].at[c, at], device)
            value = value + wide(got[...])
        value = value.astype(BF).reshape(self.k * self.rows, self.lanes)
        if self.perm is not None:
            value = jnp.dot(self.perm[...], value, preferred_element_type=F32).astype(BF)
        self.z_send[...] = value.reshape(n_z, self.sent, self.lanes)
        for step in range(1, n_z):
            self.send(
                self.z_send.at[p.z_off(step)], self.z_recv.at[step],
                s["zs"].at[c, step], s["zr"].at[c, step], p.dev_z(step),
            )

    def finish(self):
        p, s, c = self.p, self.sems, self.c
        value = wide(self.z_send[p.z])
        for step in range(1, p.geo.n_z):
            self.arrived(self.z_recv.at[step], s["zs"].at[c, step], s["zr"].at[c, step], p.dev_z(step))
            value = value + wide(self.z_recv[step])
        self.out[...] = value

    def drain(self):
        for copy in self.pending:
            copy.wait_send()


def scatter_kernel(geo, names_perm, *refs):
    refs = list(refs)
    take = lambda number: [refs.pop(0) for _ in range(number)]
    kinds = ("a", "b", "v")
    by_kind = lambda: dict(zip(kinds, take(3)))
    grads = by_kind()
    perms = dict(zip(names_perm, take(len(names_perm))))
    outs = by_kind()
    loads, sums, mids, ends, z_send, z_recv = [by_kind() for _ in range(6)]
    sems = dict(zip(("lo", "cs", "cr", "ms", "mr", "es", "er", "zs", "zr"), take(9)))
    place = Place(geo)
    chunks = [("v", 0, 0, 0)] + chunk_list(geo, range(geo.layers))
    moves = [
        Scatter(place, at, chunk, grads, loads, sums, mids, ends, perms, z_send, z_recv, outs, sems)
        for at, chunk in enumerate(chunks)
    ]
    place.greet()
    run_pipeline(
        [
            (-1, lambda c: moves[c].start()),
            (0, lambda c: moves[c].pair()),
            (1, lambda c: moves[c].middle()),
            (2, lambda c: moves[c].last()),
            (4, lambda c: moves[c].finish()),
        ],
        len(moves),
    )
    for move in moves:
        move.drain()


def scatter_all(geo, grad_a, grad_b, grad_v):
    names_perm = [name for name in ("a", "b", "v") if geo.permuted(name)]
    perms = [jnp.asarray(geo.permutation(name).T, BF) for name in names_perm]
    total = sum(geo.number.values())
    n_y, n_z = geo.n_y, geo.n_z
    groups = [[] for _ in range(6)]
    outs = []
    for name in ("a", "b", "v"):
        k, sent, unit, lanes = geo.kind[name]
        number = geo.number[name]
        mid_steps, mid_wide = max(n_y - 1, 1), max(2, n_y)
        groups[0].append(pltpu.VMEM((2, k, n_y, 2, unit, lanes), BF))
        groups[1].append(pltpu.VMEM((number, k, n_y, 2, unit, lanes), BF))
        groups[2].append(pltpu.VMEM((number, mid_steps, k, mid_wide, unit, lanes), BF))
        groups[3].append(pltpu.VMEM((number, mid_steps, k, unit, lanes), BF))
        groups[4].append(pltpu.VMEM((number, n_z, sent, lanes), BF))
        groups[5].append(pltpu.VMEM((number, n_z, sent, lanes), BF))
        outs.append(jax.ShapeDtypeStruct((number, sent, lanes), F32))
    return pl.pallas_call(
        functools.partial(scatter_kernel, geo, names_perm),
        out_shape=outs,
        in_specs=[ANY] * 3 + [IN_VMEM] * len(perms),
        out_specs=[IN_VMEM] * 3,
        scratch_shapes=sum(groups, [])
        + [
            dma(total),
            dma(total),
            dma(total),
            dma(total, n_y),
            dma(total, n_y),
            dma(total, n_y),
            dma(total, n_y),
            dma(total, n_z),
            dma(total, n_z),
        ],
        compiler_params=pltpu.CompilerParams(
            collective_id=1, has_side_effects=True, vmem_limit_bytes=56 * 2**20
        ),
    )(grad_a, grad_b, grad_v, *perms)


def pack_rows(blocks, rows):
    joined = jnp.concatenate(blocks, 0)
    return jnp.pad(joined, ((0, rows - joined.shape[0]), (0, 0)))


VECTOR_DIMS = (1, 1, 0, 1)


def vector_rows(vectors, owners, size):
    rows = []
    for vector in vectors:
        lead = vector.size // vector.shape[-1]
        rows.append(vector.reshape(lead, owners, -1).transpose(1, 0, 2).reshape(owners, -1))
    joined = jnp.concatenate(rows, 1)
    return jnp.pad(joined, ((0, 0), (0, size - joined.shape[1])))


def vector_whole(rows, shapes):
    owners = rows.shape[0]
    found, offset = [], 0
    for shape in shapes:
        size = int(np.prod(shape))
        part = rows[:, offset : offset + size].reshape((owners, -1, shape[-1]))
        offset += size
        part = part.transpose(1, 0, 2).reshape(tuple(shape[:-1]) + (owners * shape[-1],))
        found.append(part)
    return found


def on_device(
    act_short,
    act_long,
    len_short,
    len_long,
    w_qkv,
    w_out,
    w_up,
    w_down,
    gains_d,
    shifts_d,
    gains_ff,
    shifts_ff,
    cot_short,
    cot_long,
):
    vectors = (gains_d, shifts_d, gains_ff, shifts_ff)
    vec_shapes = [vector.shape for vector in vectors]
    vec_size = sum(vector.size for vector in vectors)
    n_dp, n_z = lax.axis_size("dp"), lax.axis_size("fsdp")
    owners = n_dp * n_z
    geo = Geometry(n_dp, n_z, w_qkv.shape, w_up.shape, w_down.shape, vec_size)
    width = geo.width
    cut = lambda array, at: array[:, at * width : (at + 1) * width]
    source_a, source_b = [], []
    for layer in range(geo.layers):
        blocks = [cut(w_qkv[layer], at) for at in range(3)] + [w_out[layer]]
        blocks += [cut(w_up[layer], at) for at in range(geo.blocks - 4)]
        for pair in range(geo.pairs):
            source_a.append(pack_rows(blocks[2 * pair : 2 * pair + 2], geo.kind["a"][1]))
        for half in range(geo.halves):
            lanes = geo.kind["b"][3]
            piece = w_down[layer][:, half * lanes : (half + 1) * lanes]
            source_b.append(pack_rows([piece], geo.kind["b"][1]))
    sent_v = geo.kind["v"][1]
    flat = jnp.concatenate([vector.reshape(-1) for vector in vectors])
    source_v = jnp.pad(flat, (0, sent_v * 128 - vec_size)).reshape(1, sent_v, 128)
    whole_a, whole_b, whole_v = gather_all(geo, jnp.stack(source_a), jnp.stack(source_b), source_v)
    whole_a = whole_a.reshape(geo.layers, geo.blocks, width, width)
    whole_b = whole_b.reshape(geo.layers, -1, width)
    full = vector_whole(whole_v.reshape(owners, -1), vec_shapes)
    gathered = []
    for layer in range(geo.layers):
        blocks = [whole_a[layer, at] for at in range(geo.blocks)]
        gathered.append((blocks[:3], blocks[3], blocks[4:], whole_b[layer]) + tuple(v[layer] for v in full))

    lengths = (len_short[0], len_long[0])
    residuals = [act_short.astype(jnp.float32), act_long.astype(jnp.float32)]
    saved_list = []
    for layer_idx in range(LAYERS):
        saved_here = []
        for bucket in range(2):
            residuals[bucket], saved_state = layer_forward(
                residuals[bucket], lengths[bucket], gathered[layer_idx]
            )
            saved_here.append(saved_state)
        saved_list.append(saved_here)
    out_short = residuals[0].astype(jnp.bfloat16)
    out_long = residuals[1].astype(jnp.bfloat16)
    cotangents = [cot_short, cot_long]
    d_rows = []
    for bucket in range(2):
        slot_count = cotangents[bucket].shape[0]
        valid_rows = (jnp.arange(slot_count) < lengths[bucket]).astype(jnp.float32)
        d_rows.append(cotangents[bucket].astype(jnp.float32) * valid_rows[:, None])
    grad_a = [None] * geo.layers
    grad_b = [None] * geo.layers
    grad_vec = [None] * geo.layers
    for layer_idx in reversed(range(LAYERS)):
        weights = gathered[layer_idx]
        d_rows[0], grad_total = layer_backward(
            d_rows[0], lengths[0], saved_list[layer_idx][0], weights
        )
        d_rows[1], grad_more = layer_backward(
            d_rows[1], lengths[1], saved_list[layer_idx][1], weights
        )
        g_qkv, g_out, g_up, g_down, *g_vec = [
            left_part + right_part for left_part, right_part in zip(grad_total, grad_more)
        ]
        blocks = [cut(g_qkv, at) for at in range(3)] + [g_out]
        blocks += [cut(g_up, at) for at in range(geo.blocks - 4)]
        grad_a[layer_idx] = jnp.stack([block.astype(BF) for block in blocks])
        grad_b[layer_idx] = g_down.astype(BF)
        grad_vec[layer_idx] = g_vec
    stacked = [jnp.stack([grad_vec[layer][at] for layer in range(geo.layers)]) for at in range(4)]
    rows_v = vector_rows(stacked, owners, sent_v * 128).astype(BF)
    own_a, own_b, own_v = scatter_all(
        geo,
        jnp.stack(grad_a).reshape(geo.whole_shape("a")),
        jnp.stack(grad_b).reshape(geo.whole_shape("b")),
        rows_v.reshape(geo.whole_shape("v")),
    )
    rows_a = geo.rows_a
    own_a = own_a[:, : 2 * rows_a].reshape(geo.layers, geo.blocks, rows_a, width)
    own_b = own_b[:, : geo.rows_b].reshape(geo.layers, geo.halves, geo.rows_b, -1)
    join = lambda first, last: jnp.concatenate([own_a[:, at] for at in range(first, last)], 2)
    flat, offset, own_vec = own_v.reshape(-1), 0, []
    for shape in vec_shapes:
        size = int(np.prod(shape))
        own_vec.append(flat[offset : offset + size].reshape(shape))
        offset += size
    return (
        out_short,
        out_long,
        d_rows[0],
        d_rows[1],
        join(0, 3),
        own_a[:, 3],
        join(4, geo.blocks),
        jnp.concatenate([own_b[:, at] for at in range(geo.halves)], 2),
        *own_vec,
    )


def solution(mesh):
    return jax.shard_map(
        on_device,
        mesh=mesh,
        in_specs=(
            P(("dp", "fsdp"), None),
            P(("dp", "fsdp"), None),
            P(("dp", "fsdp")),
            P(("dp", "fsdp")),
            P(None, ("dp", "fsdp"), None),
            P(None, ("dp", "fsdp"), None),
            P(None, ("dp", "fsdp"), None),
            P(None, ("dp", "fsdp"), None),
            P(None, None, ("dp", "fsdp")),
            P(None, None, ("dp", "fsdp")),
            P(None, ("dp", "fsdp")),
            P(None, None, ("dp", "fsdp")),
            P(("dp", "fsdp"), None),
            P(("dp", "fsdp"), None),
        ),
        out_specs=(
            P(("dp", "fsdp"), None),
            P(("dp", "fsdp"), None),
            P(("dp", "fsdp"), None),
            P(("dp", "fsdp"), None),
            P(None, ("dp", "fsdp"), None),
            P(None, ("dp", "fsdp"), None),
            P(None, ("dp", "fsdp"), None),
            P(None, ("dp", "fsdp"), None),
            P(None, None, ("dp", "fsdp")),
            P(None, None, ("dp", "fsdp")),
            P(None, ("dp", "fsdp")),
            P(None, None, ("dp", "fsdp")),
        ),
        check_vma=False,
    )
```

```python
import functools

import jax
import jax.numpy as jnp
import numpy as np
from jax import lax
from jax.experimental import pallas as pl
from jax.experimental.pallas import tpu as pltpu
from jax.sharding import PartitionSpec as P

HEAD_DIM = 64

epsilon = 1e-05


BF = jnp.bfloat16
F32 = jnp.float32
MESH = pl.DeviceIdType.MESH


def round16(count):
    return (count + 15) // 16 * 16


class Geometry:
    def __init__(self, n_dp, n_z, w_qkv, w_up, w_down, vec_size):
        self.n_dp, self.n_z, self.n_y = n_dp, n_z, n_dp // 4
        self.layers = w_qkv[0]
        self.width = w_qkv[2] // 3
        self.rows_a, self.rows_b = w_qkv[1], w_down[1]
        self.blocks = 4 + w_up[2] // self.width
        self.pairs = self.blocks // 2
        self.halves = 2
        self.kind = {
            "a": (2, round16(2 * self.rows_a), self.rows_a * n_z, self.width),
            "b": (1, round16(self.rows_b), self.rows_b * n_z, self.width // 2),
            "v": (1, round16(-(-vec_size // 128)), round16(-(-vec_size // 128)) * n_z, 128),
        }
        self.real = {"a": self.rows_a, "b": self.rows_b, "v": self.kind["v"][1]}
        self.number = {"a": self.layers * self.pairs, "b": self.layers * self.halves, "v": 1}

    def permuted(self, name):
        k, sent, unit, _ = self.kind[name]
        return k * unit != sent * self.n_z or k > 1

    def permutation(self, name):
        k, sent, unit, _ = self.kind[name]
        real = self.real[name]
        table = np.zeros((k * unit, self.n_z * sent), np.float32)
        for block in range(k):
            for z in range(self.n_z):
                for row in range(real):
                    table[block * unit + z * real + row, z * sent + block * real + row] = 1
        return table

    def whole_shape(self, name):
        _, _, unit, lanes = self.kind[name]
        lead = {"a": self.layers * self.blocks, "b": self.layers, "v": 1}[name]
        lanes = self.width if name == "b" else lanes
        return (lead, self.n_y, 2, 2, unit, lanes)


class Place:
    def __init__(self, geo):
        self.geo = geo
        self.d, self.z = lax.axis_index("dp"), lax.axis_index("fsdp")
        self.core = lax.rem(self.d, 2)
        self.x = lax.rem(self.d // 2, 2)
        self.y = self.d // 4

    def y_off(self, step):
        return lax.rem(self.y + step + self.geo.n_y, self.geo.n_y)

    def z_off(self, step):
        return lax.rem(self.z + step + self.geo.n_z, self.geo.n_z)

    def dev_core(self):
        return (self.d + 1 - 2 * self.core, self.z)

    def dev_x(self):
        return (self.d + 2 - 4 * self.x, self.z)

    def dev_y(self, step):
        return (self.y_off(step) * 4 + self.x * 2 + self.core, self.z)

    def dev_z(self, step):
        return (self.d, self.z_off(step))

    def greet(self):
        barrier = pltpu.get_barrier_semaphore()
        partners = [self.dev_core(), self.dev_x()]
        partners += [self.dev_y(step) for step in range(1, self.geo.n_y)]
        partners += [self.dev_z(step) for step in range(1, self.geo.n_z)]
        for partner in partners:
            pl.semaphore_signal(barrier, inc=1, device_id=partner, device_id_type=MESH)
        pl.semaphore_wait(barrier, len(partners))


def remote(src, dst, send, recv, device):
    return pltpu.make_async_remote_copy(
        src_ref=src, dst_ref=dst, send_sem=send, recv_sem=recv, device_id=device, device_id_type=MESH
    )


def column(whole, name, lead, half, k, lanes):
    def at(*where):
        picked = whole.at[(pl.ds(lead, k),) + where]
        if name == "b":
            picked = whole.at[(pl.ds(lead, k),) + where + (slice(None), pl.ds(half * lanes, lanes))]
        return picked

    return at


def chunk_list(geo, layers):
    found = []
    for layer in layers:
        for pair in range(geo.pairs):
            found.append(("a", layer * geo.pairs + pair, layer * geo.blocks + 2 * pair, 0))
        for half in range(geo.halves):
            found.append(("b", layer * geo.halves + half, layer, half))
    return found


class Gather:
    def __init__(self, place, number, chunk, sources, bufs, units, perms, wholes, sems):
        self.p, self.c = place, number
        name, at, lead, half = chunk
        self.half_a = number % 2 == 0
        k, self.sent, _, lanes = place.geo.kind[name]
        self.source = sources[name].at[at]
        self.buf = bufs[name].at[at]
        self.perm = perms.get(name)
        self.unit_buf = units[name].at[at] if self.perm is not None else None
        self.unit = self.unit_buf if self.perm is not None else bufs[name].at[pl.ds(at, 1)]
        self.to = column(wholes[name], name, lead, half, k, lanes)
        self.sems = sems
        self.pending = []

    def slot(self, z):
        return self.buf.at[pl.ds(pl.multiple_of(z * self.sent, 16), self.sent)]

    def send(self, src, dst, send, recv, device):
        copy = remote(src, dst, send, recv, device)
        copy.start()
        self.pending.append(copy)

    def arrived(self, dst, send, recv, device):
        remote(dst, dst, send, recv, device).wait_recv()

    def start_z(self):
        p, s, c = self.p, self.sems, self.c
        self.local_z = pltpu.make_async_copy(self.source, self.slot(p.z), s["lz"].at[c])
        self.local_z.start()
        for step in range(1, p.geo.n_z):
            self.send(self.source, self.slot(p.z), s["zs"].at[c, step], s["zr"].at[c, step], p.dev_z(step))

    def own(self):
        p, s, c = self.p, self.sems, self.c
        self.local_z.wait()
        for step in range(1, p.geo.n_z):
            self.arrived(self.slot(p.z_off(-step)), s["zs"].at[c, step], s["zr"].at[c, step], p.dev_z(step))
        if self.perm is not None:
            k, unit, lanes = self.unit_buf.shape
            mixed = jnp.dot(self.perm[...], self.buf[...], preferred_element_type=F32)
            self.unit_buf[...] = mixed.astype(BF).reshape(k, unit, lanes)
        here = self.to(p.y, p.x, p.core)
        self.local = pltpu.make_async_copy(self.unit, here, s["lo"].at[c])
        self.send(self.unit, here, s["xs"].at[c], s["xr"].at[c], p.dev_x())
        for step in range(1, p.geo.n_y):
            self.send(self.unit, here, s["ys"].at[c, step], s["yr"].at[c, step], p.dev_y(step))
        self.send(self.unit, here, s["cs"].at[c, 0], s["cr"].at[c, 0], p.dev_core())
        self.local.start()

    def forward(self):
        p, s, c = self.p, self.sems, self.c
        n_y = p.geo.n_y
        from_x = self.to(p.y, 1 - p.x, p.core)
        self.arrived(from_x, s["xs"].at[c], s["xr"].at[c], p.dev_x())
        if self.half_a:
            for step in range(1, n_y):
                self.send(from_x, from_x, s["ds"].at[c, step], s["dr"].at[c, step], p.dev_y(step))
        self.send(from_x, from_x, s["cs"].at[c, 1], s["cr"].at[c, 1], p.dev_core())
        for step in range(1, n_y):
            from_y = self.to(p.y_off(-step), p.x, p.core)
            self.arrived(from_y, s["ys"].at[c, step], s["yr"].at[c, step], p.dev_y(step))
            if not self.half_a:
                self.send(from_y, from_y, s["ds"].at[c, step], s["dr"].at[c, step], p.dev_x())
            self.send(from_y, from_y, s["cs"].at[c, 2 * step], s["cr"].at[c, 2 * step], p.dev_core())

    def corner(self):
        p, s, c = self.p, self.sems, self.c
        for step in range(1, p.geo.n_y):
            far = self.to(p.y_off(-step), 1 - p.x, p.core)
            self.arrived(far, s["ds"].at[c, step], s["dr"].at[c, step], p.dev_x())
            self.send(far, far, s["cs"].at[c, 2 * step + 1], s["cr"].at[c, 2 * step + 1], p.dev_core())

    def finish(self):
        p, s, c = self.p, self.sems, self.c
        for step in range(p.geo.n_y):
            for flip in range(2):
                x = p.x if flip == 0 else 1 - p.x
                got = self.to(p.y_off(-step), x, 1 - p.core)
                at = 2 * step + flip
                self.arrived(got, s["cs"].at[c, at], s["cr"].at[c, at], p.dev_core())
        self.local.wait()
        for copy in self.pending:
            copy.wait_send()


def run_pipeline(stages, count):
    last = max(lag for lag, _ in stages)
    first = min(lag for lag, _ in stages)
    for step in range(first, count + last):
        for lag, act in stages:
            if 0 <= step - lag < count:
                act(step - lag)


def gather_kernel(geo, names_perm, *refs):
    refs = list(refs)
    take = lambda number: [refs.pop(0) for _ in range(number)]
    kinds = ("a", "b", "v")
    sources = dict(zip(kinds, take(3)))
    perms = dict(zip(names_perm, take(len(names_perm))))
    wholes = dict(zip(kinds, take(3)))
    bufs = dict(zip(kinds, take(3)))
    units = dict(zip(names_perm, take(len(names_perm))))
    sems = dict(zip(("lz", "lo", "zs", "zr", "xs", "xr", "ys", "yr", "ds", "dr", "cs", "cr"), take(12)))
    place = Place(geo)
    chunks = [("v", 0, 0, 0)] + chunk_list(geo, range(geo.layers))
    moves = [
        Gather(place, at, chunk, sources, bufs, units, perms, wholes, sems)
        for at, chunk in enumerate(chunks)
    ]
    place.greet()
    run_pipeline(
        [
            (-2, lambda c: moves[c].start_z()),
            (0, lambda c: moves[c].own()),
            (1, lambda c: moves[c].forward()),
            (2, lambda c: moves[c].corner()),
        ],
        len(moves),
    )
    for move in moves:
        move.finish()


def dma(*shape):
    return pltpu.SemaphoreType.DMA(shape)


ANY = pl.BlockSpec(memory_space=pl.ANY)
IN_VMEM = pl.BlockSpec(memory_space=pltpu.VMEM)


def gather_all(geo, source_a, source_b, source_v):
    names_perm = [name for name in ("a", "b", "v") if geo.permuted(name)]
    perms = [jnp.asarray(geo.permutation(name), BF) for name in names_perm]
    total = sum(geo.number.values())
    bufs, units = [], []
    for name in ("a", "b", "v"):
        k, sent, unit, lanes = geo.kind[name]
        bufs.append(pltpu.VMEM((geo.number[name], geo.n_z * sent, lanes), BF))
        if name in names_perm:
            units.append(pltpu.VMEM((geo.number[name], k, unit, lanes), BF))
    n_y, n_z = geo.n_y, geo.n_z
    return pl.pallas_call(
        functools.partial(gather_kernel, geo, names_perm),
        out_shape=[jax.ShapeDtypeStruct(geo.whole_shape(name), BF) for name in ("a", "b", "v")],
        in_specs=[IN_VMEM] * (3 + len(perms)),
        out_specs=[ANY] * 3,
        scratch_shapes=bufs
        + units
        + [
            dma(total),
            dma(total),
            dma(total, n_z),
            dma(total, n_z),
            dma(total),
            dma(total),
            dma(total, n_y),
            dma(total, n_y),
            dma(total, n_y),
            dma(total, n_y),
            dma(total, 2 * n_y),
            dma(total, 2 * n_y),
        ],
        compiler_params=pltpu.CompilerParams(
            collective_id=0, has_side_effects=True, vmem_limit_bytes=40 * 2**20
        ),
    )(source_a, source_b, source_v, *perms)


def wide(values):
    return values.astype(F32)


class Scatter:
    def __init__(self, place, number, chunk, grads, loads, sums, mids, ends, perms, z_send, z_recv, outs, sems):
        self.p, self.c = place, number
        name, at, lead, half = chunk
        self.half_a = number % 2 == 0
        self.k, self.sent, self.rows, self.lanes = place.geo.kind[name]
        self.grad = column(grads[name], name, lead, half, self.k, self.lanes)
        self.load = loads[name].at[number % 2]
        self.sum = sums[name].at[at]
        self.mid = mids[name].at[at]
        self.end = ends[name].at[at]
        self.perm = perms.get(name)
        self.z_send, self.z_recv = z_send[name].at[at], z_recv[name].at[at]
        self.out = outs[name].at[at]
        self.sems = sems
        self.pending = []

    def send(self, src, dst, send, recv, device):
        copy = remote(src, dst, send, recv, device)
        copy.start()
        self.pending.append(copy)

    def arrived(self, dst, send, recv, device):
        remote(dst, dst, send, recv, device).wait_recv()

    def start(self):
        p, s, c = self.p, self.sems, self.c
        every = slice(None)
        self.send(self.grad(every, every, 1 - p.core), self.sum, s["cs"].at[c], s["cr"].at[c], p.dev_core())
        self.local = pltpu.make_async_copy(self.grad(every, every, p.core), self.load, s["lo"].at[c])
        self.local.start()

    def pair(self):
        p, s, c = self.p, self.sems, self.c
        n_y = p.geo.n_y
        self.local.wait()
        self.arrived(self.sum, s["cs"].at[c], s["cr"].at[c], p.dev_core())

        @pl.loop(0, self.k * n_y * 2)
        def _(at):
            where = (at // (2 * n_y), lax.rem(at // 2, n_y), lax.rem(at, 2))
            self.sum[where] = (wide(self.sum[where]) + wide(self.load[where])).astype(BF)

        if self.half_a:
            for step in range(1, n_y):
                self.send(
                    self.sum.at[:, p.y_off(step)], self.mid.at[step - 1, :, pl.ds(0, 2)],
                    s["ms"].at[c, step], s["mr"].at[c, step], p.dev_y(step),
                )
        else:
            self.send(
                self.sum.at[:, :, 1 - p.x], self.mid.at[0, :, pl.ds(0, n_y)],
                s["ms"].at[c, 0], s["mr"].at[c, 0], p.dev_x(),
            )

    def middle(self):
        p, s, c = self.p, self.sems, self.c
        n_y = p.geo.n_y
        if self.half_a:
            for step in range(1, n_y):
                self.arrived(self.mid.at[step - 1, :, pl.ds(0, 2)], s["ms"].at[c, step], s["mr"].at[c, step], p.dev_y(step))

            @pl.loop(0, self.k * 2)
            def _(at):
                where = (at // 2, p.y, lax.rem(at, 2))
                value = wide(self.sum[where])
                for step in range(1, n_y):
                    value = value + wide(self.mid[step - 1, at // 2, lax.rem(at, 2)])
                self.sum[where] = value.astype(BF)

            self.send(
                self.sum.at[:, p.y, 1 - p.x], self.end.at[0], s["es"].at[c, 0], s["er"].at[c, 0], p.dev_x()
            )
        else:
            self.arrived(self.mid.at[0, :, pl.ds(0, n_y)], s["ms"].at[c, 0], s["mr"].at[c, 0], p.dev_x())

            @pl.loop(0, self.k * n_y)
            def _(at):
                where = (at // n_y, lax.rem(at, n_y), p.x)
                value = wide(self.sum[where]) + wide(self.mid[0, at // n_y, lax.rem(at, n_y)])
                self.sum[where] = value.astype(BF)

            for step in range(1, n_y):
                self.send(
                    self.sum.at[:, p.y_off(step), p.x], self.end.at[step - 1],
                    s["es"].at[c, step], s["er"].at[c, step], p.dev_y(step),
                )

    def last(self):
        p, s, c = self.p, self.sems, self.c
        n_y, n_z = p.geo.n_y, p.geo.n_z
        if self.half_a:
            arrivals = [(0, self.end.at[0], p.dev_x())]
        else:
            arrivals = [(step, self.end.at[step - 1], p.dev_y(step)) for step in range(1, n_y)]
        value = wide(self.sum[:, p.y, p.x])
        for at, got, device in arrivals:
            self.arrived(got, s["es"].at[c, at], s["er"].at[c, at], device)
            value = value + wide(got[...])
        value = value.astype(BF).reshape(self.k * self.rows, self.lanes)
        if self.perm is not None:
            value = jnp.dot(self.perm[...], value, preferred_element_type=F32).astype(BF)
        self.z_send[...] = value.reshape(n_z, self.sent, self.lanes)
        for step in range(1, n_z):
            self.send(
                self.z_send.at[p.z_off(step)], self.z_recv.at[step],
                s["zs"].at[c, step], s["zr"].at[c, step], p.dev_z(step),
            )

    def finish(self):
        p, s, c = self.p, self.sems, self.c
        value = wide(self.z_send[p.z])
        for step in range(1, p.geo.n_z):
            self.arrived(self.z_recv.at[step], s["zs"].at[c, step], s["zr"].at[c, step], p.dev_z(step))
            value = value + wide(self.z_recv[step])
        self.out[...] = value

    def drain(self):
        for copy in self.pending:
            copy.wait_send()


def scatter_kernel(geo, names_perm, *refs):
    refs = list(refs)
    take = lambda number: [refs.pop(0) for _ in range(number)]
    kinds = ("a", "b", "v")
    by_kind = lambda: dict(zip(kinds, take(3)))
    grads = by_kind()
    perms = dict(zip(names_perm, take(len(names_perm))))
    outs = by_kind()
    loads, sums, mids, ends, z_send, z_recv = [by_kind() for _ in range(6)]
    sems = dict(zip(("lo", "cs", "cr", "ms", "mr", "es", "er", "zs", "zr"), take(9)))
    place = Place(geo)
    chunks = [("v", 0, 0, 0)] + chunk_list(geo, range(geo.layers))
    moves = [
        Scatter(place, at, chunk, grads, loads, sums, mids, ends, perms, z_send, z_recv, outs, sems)
        for at, chunk in enumerate(chunks)
    ]
    place.greet()
    run_pipeline(
        [
            (-1, lambda c: moves[c].start()),
            (0, lambda c: moves[c].pair()),
            (1, lambda c: moves[c].middle()),
            (2, lambda c: moves[c].last()),
            (4, lambda c: moves[c].finish()),
        ],
        len(moves),
    )
    for move in moves:
        move.drain()


def scatter_all(geo, grad_a, grad_b, grad_v):
    names_perm = [name for name in ("a", "b", "v") if geo.permuted(name)]
    perms = [jnp.asarray(geo.permutation(name).T, BF) for name in names_perm]
    total = sum(geo.number.values())
    n_y, n_z = geo.n_y, geo.n_z
    groups = [[] for _ in range(6)]
    outs = []
    for name in ("a", "b", "v"):
        k, sent, unit, lanes = geo.kind[name]
        number = geo.number[name]
        mid_steps, mid_wide = max(n_y - 1, 1), max(2, n_y)
        groups[0].append(pltpu.VMEM((2, k, n_y, 2, unit, lanes), BF))
        groups[1].append(pltpu.VMEM((number, k, n_y, 2, unit, lanes), BF))
        groups[2].append(pltpu.VMEM((number, mid_steps, k, mid_wide, unit, lanes), BF))
        groups[3].append(pltpu.VMEM((number, mid_steps, k, unit, lanes), BF))
        groups[4].append(pltpu.VMEM((number, n_z, sent, lanes), BF))
        groups[5].append(pltpu.VMEM((number, n_z, sent, lanes), BF))
        outs.append(jax.ShapeDtypeStruct((number, sent, lanes), F32))
    return pl.pallas_call(
        functools.partial(scatter_kernel, geo, names_perm),
        out_shape=outs,
        in_specs=[ANY] * 3 + [IN_VMEM] * len(perms),
        out_specs=[IN_VMEM] * 3,
        scratch_shapes=sum(groups, [])
        + [
            dma(total),
            dma(total),
            dma(total),
            dma(total, n_y),
            dma(total, n_y),
            dma(total, n_y),
            dma(total, n_y),
            dma(total, n_z),
            dma(total, n_z),
        ],
        compiler_params=pltpu.CompilerParams(
            collective_id=1, has_side_effects=True, vmem_limit_bytes=56 * 2**20
        ),
    )(grad_a, grad_b, grad_v, *perms)


def mm(left, right):
    return jnp.dot(left, right, preferred_element_type=F32)


def mm_nt(left, right):
    return lax.dot_general(left, right, (((1,), (1,)), ((), ())), preferred_element_type=F32)


def mm_tn(left, right):
    return lax.dot_general(left, right, (((0,), (0,)), ((), ())), preferred_element_type=F32)


def mean_of(values):
    return jnp.sum(values, -1, keepdims=True) * (1.0 / values.shape[-1])


def normal(values):
    centered = values - mean_of(values)
    scale = lax.rsqrt(mean_of(centered * centered) + epsilon)
    return centered * scale, scale


def norm_rows(source, gain, shift, target, block=32):
    @pl.loop(0, source.shape[0] // block)
    def _(at):
        rows = pl.ds(pl.multiple_of(at * block, block), block)
        unit, _ = normal(source[rows, :])
        target[rows, :] = (unit * gain + shift).astype(target.dtype)


def fold(values):
    total = values[0:8]
    for at in range(8, values.shape[0], 8):
        total = total + values[at : at + 8]
    return total


def norm_rows_back(source, gain, incoming, emit, sums, block=32):
    sums[...] = jnp.zeros_like(sums)

    @pl.loop(0, source.shape[0] // block)
    def _(at):
        rows = pl.ds(pl.multiple_of(at * block, block), block)
        unit, scale = normal(source[rows, :])
        back = incoming[rows, :]
        sums[0] += fold(back * unit)
        sums[1] += fold(back)
        inner = back * gain
        emit(rows, scale * (inner - mean_of(inner) - unit * mean_of(inner * unit)))


ROOT = 0.7978845608028654
CUBE = 0.044715


def gelu_parts(values):
    square = values * values
    curve = jnp.tanh(ROOT * (values + CUBE * (values * square)))
    return square, curve


class Layer:
    def __init__(self, refs, weight_a, weight_b, vec_d, vec_f, heads):
        self.__dict__.update(refs)
        self.weight_a, self.weight_b = weight_a, weight_b
        self.gain = [vec_d[at : at + 1, :] for at in range(3)]
        self.shift = [vec_d[at : at + 1, :] for at in range(3, 10)]
        self.vec_f = vec_f
        self.heads = heads

    def lane_half(self, values, side):
        lane = lax.broadcasted_iota(jnp.int32, values.shape, 1)
        return (lane < HEAD_DIM) == (side == 0)

    def forward_qkv(self):
        norm_rows(self.x, self.gain[0], self.shift[0], self.normed)
        shifts = (self.shift[3], None, self.shift[4])
        for part in range(3):
            value = mm(self.normed[...], self.weight_a(part))
            if shifts[part] is not None:
                value = value + shifts[part]
            self.qkv[part] = value.astype(BF)

    def forward_attention(self):
        valid = self.mask[...] > 0.5

        @pl.loop(0, self.heads // 2)
        def _(pair):
            lanes = pl.ds(pl.multiple_of(pair * 128, 128), 128)
            queries, keys, values = [self.qkv[part, :, lanes] for part in range(3)]
            context = None
            for side in range(2):
                half = self.lane_half(queries, side)
                scores = mm_nt(jnp.where(half, queries, jnp.zeros_like(queries)), keys)
                scores = jnp.where(valid, scores * HEAD_DIM**-0.5, -1e9)
                top = jnp.max(scores, -1, keepdims=True)
                grown = jnp.exp(scores - top)
                prob = grown / jnp.sum(grown, -1, keepdims=True)
                self.prob[2 * pair + side] = prob
                product = mm(prob.astype(BF), values)
                context = product if side == 0 else jnp.where(half, product, context)
            self.context[:, lanes] = context

    def forward_out(self):
        norm_rows(self.context, self.gain[1], self.shift[1], self.sub)
        self.after[...] = self.x[...] + (mm(self.sub[...], self.weight_a(3)) + self.shift[5])
        norm_rows(self.after, self.gain[2], self.shift[2], self.normed_ffn)

    def forward_up(self, part):
        width = self.x.shape[1]
        lanes = slice(part * width, (part + 1) * width)
        self.hidden[:, lanes] = mm(self.normed_ffn[...], self.weight_a(4 + part)) + self.vec_f[1:2, lanes]

    def forward_gelu(self):
        @pl.loop(0, self.x.shape[0] // 16)
        def _(at):
            rows = pl.ds(pl.multiple_of(at * 16, 16), 16)
            values = self.hidden[rows, :]
            _, curve = gelu_parts(values)
            unit, _ = normal(0.5 * values * (1.0 + curve))
            self.sub_ffn[rows, :] = (unit * self.vec_f[0:1, :] + self.vec_f[2:3, :]).astype(BF)

    def forward_down(self):
        width = self.x.shape[1]
        for first in range(0, width, 256):
            lanes = slice(first, first + 256)
            value = mm(self.sub_ffn[...], self.weight_b(slice(None), lanes))
            self.x_next[:, lanes] = self.after[:, lanes] + (value + self.shift[6][:, lanes])


    def store_sums(self, target, row, sums):
        target[row : row + 1, :] = jnp.sum(sums, 0, keepdims=True)

    def backward_down(self, put):
        width = self.x.shape[1]
        self.low[...] = self.back[...].astype(BF)
        self.store_sums(self.grad_d, 9, wide(self.low[...]))
        for part in range(self.hidden.shape[1] // width):
            lanes = slice(part * width, (part + 1) * width)
            put("b", part, lambda: mm_tn(self.sub_ffn[:, lanes], self.low[...]))
            self.wide_back[:, lanes] = mm_nt(self.low[...], self.weight_b(lanes, slice(None)))

    def backward_gelu(self):
        self.sums_f[...] = jnp.zeros_like(self.sums_f)

        @pl.loop(0, self.x.shape[0] // 16)
        def _(at):
            rows = pl.ds(pl.multiple_of(at * 16, 16), 16)
            values = self.hidden[rows, :]
            square, curve = gelu_parts(values)
            unit, scale = normal(0.5 * values * (1.0 + curve))
            back = self.wide_back[rows, :]
            self.sums_f[0] += fold(back * unit)
            self.sums_f[1] += fold(back)
            inner = back * self.vec_f[0:1, :]
            d_gelu = scale * (inner - mean_of(inner) - unit * mean_of(inner * unit))
            slope = 0.5 * (1.0 + curve) + 0.5 * values * (1.0 - curve * curve) * (
                ROOT * (1.0 + 3.0 * CUBE * square)
            )
            low = (d_gelu * slope).astype(BF)
            self.d_hidden[rows, :] = low
            self.sums_f[2] += fold(wide(low))

        self.store_sums(self.grad_f, 0, self.sums_f[0])
        self.store_sums(self.grad_f, 2, self.sums_f[1])
        self.store_sums(self.grad_f, 1, self.sums_f[2])

    def backward_up(self, put):
        width = self.x.shape[1]
        total = None
        for part in range(self.hidden.shape[1] // width):
            lanes = slice(part * width, (part + 1) * width)
            put("a", 4 + part, lambda: mm_tn(self.normed_ffn[...], self.d_hidden[:, lanes]))
            value = mm_nt(self.d_hidden[:, lanes], self.weight_a(4 + part))
            if part == 0:
                self.incoming[...] = value
            else:
                self.incoming[...] += value

        def emit(rows, value):
            value = self.back[rows, :] + value
            self.back[rows, :] = value
            self.low[rows, :] = value.astype(BF)

        norm_rows_back(self.after, self.gain[2], self.incoming, emit, self.sums_d)
        self.store_sums(self.grad_d, 2, self.sums_d[0])
        self.store_sums(self.grad_d, 5, self.sums_d[1])

    def backward_out(self, put):
        self.store_sums(self.grad_d, 8, wide(self.low[...]))
        put("a", 3, lambda: mm_tn(self.sub[...], self.low[...]))
        self.incoming[...] = mm_nt(self.low[...], self.weight_a(3))

        def emit(rows, value):
            self.low[rows, :] = value.astype(BF)

        norm_rows_back(self.context, self.gain[1], self.incoming, emit, self.sums_d)
        self.store_sums(self.grad_d, 1, self.sums_d[0])
        self.store_sums(self.grad_d, 4, self.sums_d[1])

    def backward_attention(self):
        @pl.loop(0, self.heads // 2)
        def _(pair):
            lanes = pl.ds(pl.multiple_of(pair * 128, 128), 128)
            queries, keys, values = [self.qkv[part, :, lanes] for part in range(3)]
            d_context = self.low[:, lanes]
            found = [None] * 3
            for side in range(2):
                half = self.lane_half(d_context, side)
                prob = self.prob[2 * pair + side]
                d_prob = mm_nt(jnp.where(half, d_context, jnp.zeros_like(d_context)), values)
                dot = jnp.sum(prob * d_prob, -1, keepdims=True)
                d_scores = (prob * (d_prob - dot)).astype(BF)
                new = (
                    mm(d_scores, keys) * HEAD_DIM**-0.5,
                    mm_tn(d_scores, queries) * HEAD_DIM**-0.5,
                    mm_tn(prob.astype(BF), d_context),
                )
                found = [n if side == 0 else jnp.where(half, n, f) for n, f in zip(new, found)]
            for part in range(3):
                self.d_qkv[part, :, lanes] = found[part].astype(BF)

    def backward_qkv(self, put):
        self.store_sums(self.grad_d, 6, wide(self.d_qkv[0]))
        self.store_sums(self.grad_d, 7, wide(self.d_qkv[2]))
        for part in range(3):
            put("a", part, lambda: mm_tn(self.normed[...], self.d_qkv[part]))
            value = mm_nt(self.d_qkv[part], self.weight_a(part))
            if part == 0:
                self.incoming[...] = value
            else:
                self.incoming[...] += value

        def emit(rows, value):
            self.back[rows, :] = self.back[rows, :] + value

        norm_rows_back(self.x, self.gain[0], self.incoming, emit, self.sums_d)
        self.store_sums(self.grad_d, 0, self.sums_d[0])
        self.store_sums(self.grad_d, 3, self.sums_d[1])


def saved_shapes(rows, width, wide_width, heads):
    return {
        "normed": ((rows, width), BF),
        "qkv": ((3, rows, width), BF),
        "prob": ((heads, rows, rows), F32),
        "context": ((rows, width), F32),
        "sub": ((rows, width), BF),
        "after": ((rows, width), F32),
        "normed_ffn": ((rows, width), BF),
        "hidden": ((rows, wide_width), F32),
        "sub_ffn": ((rows, wide_width), BF),
    }


def work_shapes(rows, width, wide_width):
    return {
        "low": ((rows, width), BF),
        "incoming": ((rows, width), F32),
        "wide_back": ((rows, wide_width), F32),
        "d_hidden": ((rows, wide_width), BF),
        "d_qkv": ((3, rows, width), BF),
        "sums_d": ((2, 8, width), F32),
        "sums_f": ((3, 8, wide_width), F32),
    }


class Putter:
    def __init__(self, stage, sem):
        self.stage, self.sem, self.count, self.copies = stage, sem, 0, [None, None]

    def put(self, target, value):
        slot = self.count % 2
        if self.copies[slot] is not None:
            self.copies[slot].wait()
        rows = self.stage.shape[1]
        self.stage[slot] = value().astype(BF)
        self.copies[slot] = pltpu.make_async_copy(self.stage.at[slot], target, self.sem.at[slot])
        self.copies[slot].start()
        self.count += 1

    def drain(self):
        for copy in self.copies:
            if copy is not None:
                copy.wait()


def model_kernel(layers, blocks, heads, names, *refs):
    refs = list(refs)
    take = lambda number: [refs.pop(0) for _ in range(number)]
    act_ref, cot_ref, mask_ref, vec_d, vec_f, whole_a, whole_b = take(7)
    out_ref, back_ref, grad_a, grad_b, grad_d, grad_f = take(6)
    saved_names, work_names = names
    saved = [dict(zip(saved_names, take(len(saved_names)))) for _ in range(layers)]
    work = dict(zip(work_names, take(len(work_names))))
    xs, weight_a, weight_b, stage, sem_a, sem_b, sem_g = take(7)
    width = act_ref.shape[1]
    halves = whole_b.shape[1] // width
    load_a = [pltpu.make_async_copy(whole_a.at[at], weight_a.at[at], sem_a.at[at]) for at in range(layers * blocks)]
    load_b = [pltpu.make_async_copy(whole_b.at[at], weight_b.at[at], sem_b.at[at]) for at in range(layers)]
    for layer in range(layers):
        for at in range(blocks):
            load_a[layer * blocks + at].start()
        load_b[layer].start()
    xs[0] = wide(act_ref[...])
    net = []
    for layer in range(layers):
        fields = dict(saved[layer], **work)
        fields.update(
            x=xs.at[layer], x_next=xs.at[layer + 1], mask=mask_ref, back=back_ref,
            grad_d=grad_d.at[layer], grad_f=grad_f.at[layer],
        )
        read_a = lambda at, layer=layer: weight_a[layer * blocks + at]
        read_b = lambda rows, lanes, layer=layer: weight_b[layer, rows, lanes]
        net.append(Layer(fields, read_a, read_b, vec_d.at[layer], vec_f.at[layer], heads))
    for layer in range(layers):
        one = net[layer]
        ready = lambda first, last: [load_a[layer * blocks + at].wait() for at in range(first, last)]
        ready(0, 3)
        one.forward_qkv()
        one.forward_attention()
        ready(3, 4)
        one.forward_out()
        for part in range(blocks - 4):
            ready(4 + part, 5 + part)
            one.forward_up(part)
        one.forward_gelu()
        load_b[layer].wait()
        one.forward_down()
    out_ref[...] = xs[layers].astype(BF)
    back_ref[...] = cot_ref[...]
    putter = Putter(stage, sem_g)
    for layer in reversed(range(layers)):
        one = net[layer]

        def put(kind, at, value, layer=layer):
            if kind == "a":
                target = grad_a.at[layer * blocks + at]
            else:
                target = grad_b.at[layer, pl.ds(at * width, width)]
            putter.put(target, value)

        one.backward_down(put)
        one.backward_gelu()
        one.backward_up(put)
        one.backward_out(put)
        one.backward_attention()
        one.backward_qkv(put)
    putter.drain()


def run_model(layers, blocks, act, cot, mask, vec_d, vec_f, whole_a, whole_b):
    rows, width = act.shape
    wide_width = whole_b.shape[1]
    heads = width // HEAD_DIM
    saved, work = saved_shapes(rows, width, wide_width, heads), work_shapes(rows, width, wide_width)
    names = (list(saved), list(work))
    scratch = [pltpu.VMEM(*saved[name]) for _ in range(layers) for name in saved]
    scratch += [pltpu.VMEM(*work[name]) for name in work]
    scratch += [
        pltpu.VMEM((layers + 1, rows, width), F32),
        pltpu.VMEM(whole_a.shape, BF),
        pltpu.VMEM(whole_b.shape, BF),
        pltpu.VMEM((2, width, width), BF),
        dma(layers * blocks),
        dma(layers),
        dma(2),
    ]
    return pl.pallas_call(
        functools.partial(model_kernel, layers, blocks, heads, names),
        out_shape=[
            jax.ShapeDtypeStruct((rows, width), BF),
            jax.ShapeDtypeStruct((rows, width), F32),
            jax.ShapeDtypeStruct(whole_a.shape, BF),
            jax.ShapeDtypeStruct(whole_b.shape, BF),
            jax.ShapeDtypeStruct((layers, 10, width), F32),
            jax.ShapeDtypeStruct((layers, 3, wide_width), F32),
        ],
        in_specs=[IN_VMEM] * 5 + [ANY] * 2,
        out_specs=[IN_VMEM] * 2 + [ANY] * 2 + [IN_VMEM] * 2,
        scratch_shapes=scratch,
        compiler_params=pltpu.CompilerParams(vmem_limit_bytes=60 * 2**20),
    )(act, cot, mask, vec_d, vec_f, whole_a, whole_b)


def pack_rows(blocks, rows):
    joined = jnp.concatenate(blocks, 0)
    return jnp.pad(joined, ((0, rows - joined.shape[0]), (0, 0)))


VECTOR_DIMS = (1, 1, 0, 1)


def vector_rows(vectors, owners, size):
    rows = []
    for vector in vectors:
        lead = vector.size // vector.shape[-1]
        rows.append(vector.reshape(lead, owners, -1).transpose(1, 0, 2).reshape(owners, -1))
    joined = jnp.concatenate(rows, 1)
    return jnp.pad(joined, ((0, 0), (0, size - joined.shape[1])))


def vector_whole(rows, shapes):
    owners = rows.shape[0]
    found, offset = [], 0
    for shape in shapes:
        size = int(np.prod(shape))
        part = rows[:, offset : offset + size].reshape((owners, -1, shape[-1]))
        offset += size
        part = part.transpose(1, 0, 2).reshape(tuple(shape[:-1]) + (owners * shape[-1],))
        found.append(part)
    return found


def on_device(
    act_short,
    act_long,
    len_short,
    len_long,
    w_qkv,
    w_out,
    w_up,
    w_down,
    gains_d,
    shifts_d,
    gains_ff,
    shifts_ff,
    cot_short,
    cot_long,
):
    vectors = (gains_d, shifts_d, gains_ff, shifts_ff)
    vec_shapes = [vector.shape for vector in vectors]
    vec_size = sum(vector.size for vector in vectors)
    n_dp, n_z = lax.axis_size("dp"), lax.axis_size("fsdp")
    owners = n_dp * n_z
    geo = Geometry(n_dp, n_z, w_qkv.shape, w_up.shape, w_down.shape, vec_size)
    width = geo.width
    cut = lambda array, at: array[:, at * width : (at + 1) * width]
    source_a, source_b = [], []
    for layer in range(geo.layers):
        blocks = [cut(w_qkv[layer], at) for at in range(3)] + [w_out[layer]]
        blocks += [cut(w_up[layer], at) for at in range(geo.blocks - 4)]
        for pair in range(geo.pairs):
            source_a.append(pack_rows(blocks[2 * pair : 2 * pair + 2], geo.kind["a"][1]))
        for half in range(geo.halves):
            lanes = geo.kind["b"][3]
            piece = w_down[layer][:, half * lanes : (half + 1) * lanes]
            source_b.append(pack_rows([piece], geo.kind["b"][1]))
    sent_v = geo.kind["v"][1]
    flat = jnp.concatenate([vector.reshape(-1) for vector in vectors])
    source_v = jnp.pad(flat, (0, sent_v * 128 - vec_size)).reshape(1, sent_v, 128)
    whole_a, whole_b, whole_v = gather_all(geo, jnp.stack(source_a), jnp.stack(source_b), source_v)
    whole_b = whole_b.reshape(geo.layers, -1, width)
    full = vector_whole(whole_v.reshape(owners, -1), vec_shapes)
    vec_d = jnp.concatenate([wide(full[0]), wide(full[1])], 1)
    vec_f = jnp.concatenate([wide(full[2])[:, None], wide(full[3])], 1)
    rows_short, rows_long = act_short.shape[0], act_long.shape[0]
    rows = rows_short + rows_long
    at = np.arange(rows)
    bucket = (at >= rows_short).astype(np.int32)
    place = at - rows_short * bucket
    length = jnp.where(bucket == 0, len_short[0], len_long[0])
    valid = place < length
    mask = ((bucket[:, None] == bucket[None, :]) & valid[None, :]).astype(F32)
    cot = jnp.concatenate([cot_short, cot_long]).astype(F32) * valid.astype(F32)[:, None]
    out, back, grad_a, grad_b, grad_d, grad_f = run_model(
        geo.layers,
        geo.blocks,
        jnp.concatenate([act_short, act_long]),
        cot,
        mask,
        vec_d,
        vec_f,
        whole_a.reshape(-1, width, width),
        whole_b,
    )
    grad_vec = [grad_d[:, :3], grad_d[:, 3:], grad_f[:, 0], grad_f[:, 1:]]
    rows_v = vector_rows(grad_vec, owners, sent_v * 128).astype(BF)
    own_a, own_b, own_v = scatter_all(
        geo,
        grad_a.reshape(geo.whole_shape("a")),
        grad_b.reshape(geo.whole_shape("b")),
        rows_v.reshape(geo.whole_shape("v")),
    )
    rows_a = geo.rows_a
    own_a = own_a[:, : 2 * rows_a].reshape(geo.layers, geo.blocks, rows_a, width)
    own_b = own_b[:, : geo.rows_b].reshape(geo.layers, geo.halves, geo.rows_b, -1)
    join = lambda first, last: jnp.concatenate([own_a[:, at] for at in range(first, last)], 2)
    flat, offset, own_vec = own_v.reshape(-1), 0, []
    for shape in vec_shapes:
        size = int(np.prod(shape))
        own_vec.append(flat[offset : offset + size].reshape(shape))
        offset += size
    return (
        out[:rows_short],
        out[rows_short:],
        back[:rows_short],
        back[rows_short:],
        join(0, 3),
        own_a[:, 3],
        join(4, geo.blocks),
        jnp.concatenate([own_b[:, at] for at in range(geo.halves)], 2),
        *own_vec,
    )


def solution(mesh):
    return jax.shard_map(
        on_device,
        mesh=mesh,
        in_specs=(
            P(("dp", "fsdp"), None),
            P(("dp", "fsdp"), None),
            P(("dp", "fsdp")),
            P(("dp", "fsdp")),
            P(None, ("dp", "fsdp"), None),
            P(None, ("dp", "fsdp"), None),
            P(None, ("dp", "fsdp"), None),
            P(None, ("dp", "fsdp"), None),
            P(None, None, ("dp", "fsdp")),
            P(None, None, ("dp", "fsdp")),
            P(None, ("dp", "fsdp")),
            P(None, None, ("dp", "fsdp")),
            P(("dp", "fsdp"), None),
            P(("dp", "fsdp"), None),
        ),
        out_specs=(
            P(("dp", "fsdp"), None),
            P(("dp", "fsdp"), None),
            P(("dp", "fsdp"), None),
            P(("dp", "fsdp"), None),
            P(None, ("dp", "fsdp"), None),
            P(None, ("dp", "fsdp"), None),
            P(None, ("dp", "fsdp"), None),
            P(None, ("dp", "fsdp"), None),
            P(None, None, ("dp", "fsdp")),
            P(None, None, ("dp", "fsdp")),
            P(None, ("dp", "fsdp")),
            P(None, None, ("dp", "fsdp")),
        ),
        check_vma=False,
    )
```

```python
import functools

import jax
import jax.numpy as jnp
import numpy as np
from jax import lax
from jax.experimental import pallas as pl
from jax.experimental.pallas import tpu as pltpu
from jax.sharding import PartitionSpec as P

HEAD_DIM = 64

epsilon = 1e-05


BF = jnp.bfloat16
F32 = jnp.float32
MESH = pl.DeviceIdType.MESH


def round16(count):
    return (count + 15) // 16 * 16


class Geometry:
    def __init__(self, n_dp, n_z, w_qkv, w_up, w_down):
        self.n_dp, self.n_z, self.n_y = n_dp, n_z, n_dp // 4
        self.layers = w_qkv[0]
        self.width = w_qkv[2] // 3
        self.rows_a, self.rows_b = w_qkv[1], w_down[1]
        self.blocks = 4 + w_up[2] // self.width
        self.pairs = self.blocks // 2
        self.halves = 2
        self.owners = n_dp * n_z
        self.wide_width = w_up[2]
        self.slot = 8
        while self.slot < self.rows_a:
            self.slot *= 2
        self.per_row = 128 // self.slot
        self.lines_d = -(-self.layers * 10 // self.per_row)
        lines = round16(self.lines_d + self.layers * 3)
        self.kind = {
            "a": (2, round16(2 * self.rows_a), self.rows_a * n_z, self.width),
            "b": (1, round16(self.rows_b), self.rows_b * n_z, self.width // 2),
            "v": (1, lines, lines * n_z, 128),
        }
        self.real = {"a": self.rows_a, "b": self.rows_b, "v": self.kind["v"][1]}
        self.number = {"a": self.layers * self.pairs, "b": self.layers * self.halves, "v": 1}

    def permuted(self, name):
        k, sent, unit, _ = self.kind[name]
        return k * unit != sent * self.n_z or k > 1

    def permutation(self, name):
        k, sent, unit, _ = self.kind[name]
        real = self.real[name]
        table = np.zeros((k * unit, self.n_z * sent), np.float32)
        for block in range(k):
            for z in range(self.n_z):
                for row in range(real):
                    table[block * unit + z * real + row, z * sent + block * real + row] = 1
        return table

    def whole_shape(self, name):
        _, _, unit, lanes = self.kind[name]
        lead = {"a": self.layers * self.blocks, "b": self.layers, "v": 1}[name]
        lanes = self.width if name == "b" else lanes
        return (lead, self.n_y, 2, 2, unit, lanes)


class Place:
    def __init__(self, geo):
        self.geo = geo
        self.d, self.z = lax.axis_index("dp"), lax.axis_index("fsdp")
        self.core = lax.rem(self.d, 2)
        self.x = lax.rem(self.d // 2, 2)
        self.y = self.d // 4

    def y_off(self, step):
        return lax.rem(self.y + step + self.geo.n_y, self.geo.n_y)

    def z_off(self, step):
        return lax.rem(self.z + step + self.geo.n_z, self.geo.n_z)

    def dev_core(self):
        return (self.d + 1 - 2 * self.core, self.z)

    def dev_x(self):
        return (self.d + 2 - 4 * self.x, self.z)

    def dev_y(self, step):
        return (self.y_off(step) * 4 + self.x * 2 + self.core, self.z)

    def dev_z(self, step):
        return (self.d, self.z_off(step))

    def greet(self):
        barrier = pltpu.get_barrier_semaphore()
        partners = [self.dev_core(), self.dev_x()]
        partners += [self.dev_y(step) for step in range(1, self.geo.n_y)]
        partners += [self.dev_z(step) for step in range(1, self.geo.n_z)]
        for partner in partners:
            pl.semaphore_signal(barrier, inc=1, device_id=partner, device_id_type=MESH)
        pl.semaphore_wait(barrier, len(partners))


def remote(src, dst, send, recv, device):
    return pltpu.make_async_remote_copy(
        src_ref=src, dst_ref=dst, send_sem=send, recv_sem=recv, device_id=device, device_id_type=MESH
    )


def column(whole, name, lead, half, k, lanes):
    def at(*where):
        picked = whole.at[(pl.ds(lead, k),) + where]
        if name == "b":
            picked = whole.at[(pl.ds(lead, k),) + where + (slice(None), pl.ds(half * lanes, lanes))]
        return picked

    return at


def chunk_list(geo, layers):
    found = []
    for layer in layers:
        for pair in range(geo.pairs):
            found.append(("a", layer * geo.pairs + pair, layer * geo.blocks + 2 * pair, 0))
        for half in range(geo.halves):
            found.append(("b", layer * geo.halves + half, layer, half))
    return found


def rows_of(whole, name, lead, half, k, unit, lanes):
    def at(y, x, core):
        rows = pl.ds(pl.multiple_of((y * 4 + x * 2 + core) * unit, 16), unit)
        return whole.at[pl.ds(lead, k), rows, pl.ds(half * lanes, lanes) if name == "b" else slice(None)]

    return at


class Gather:
    def __init__(self, place, number, chunk, sources, bufs, units, perms, wholes, sems):
        self.p, self.c = place, number
        name, at, lead, half = chunk
        self.half_a = number % 2 == 0
        k, self.sent, unit, lanes = place.geo.kind[name]
        self.source = sources[name].at[at]
        self.buf = bufs[name].at[at]
        self.perm = perms.get(name)
        self.unit_buf = units[name].at[at] if self.perm is not None else None
        self.unit = self.unit_buf if self.perm is not None else bufs[name].at[pl.ds(at, 1)]
        self.to = rows_of(wholes[name], name, lead, half, k, unit, lanes)
        self.sems = sems
        self.pending = []

    def slot(self, z):
        return self.buf.at[pl.ds(pl.multiple_of(z * self.sent, 16), self.sent)]

    def send(self, src, dst, send, recv, device):
        copy = remote(src, dst, send, recv, device)
        copy.start()
        self.pending.append(copy)

    def arrived(self, dst, send, recv, device):
        remote(dst, dst, send, recv, device).wait_recv()

    def start_z(self):
        p, s, c = self.p, self.sems, self.c
        self.local_z = pltpu.make_async_copy(self.source, self.slot(p.z), s["lz"].at[c])
        self.local_z.start()
        for step in range(1, p.geo.n_z):
            self.send(self.source, self.slot(p.z), s["zs"].at[c, step], s["zr"].at[c, step], p.dev_z(step))

    def own(self):
        p, s, c = self.p, self.sems, self.c
        self.local_z.wait()
        for step in range(1, p.geo.n_z):
            self.arrived(self.slot(p.z_off(-step)), s["zs"].at[c, step], s["zr"].at[c, step], p.dev_z(step))
        if self.perm is not None:
            k, unit, lanes = self.unit_buf.shape
            mixed = jnp.dot(self.perm[...], self.buf[...], preferred_element_type=F32)
            self.unit_buf[...] = mixed.astype(BF).reshape(k, unit, lanes)
        here = self.to(p.y, p.x, p.core)
        self.local = pltpu.make_async_copy(self.unit, here, s["lo"].at[c])
        self.send(self.unit, here, s["xs"].at[c], s["xr"].at[c], p.dev_x())
        for step in range(1, p.geo.n_y):
            self.send(self.unit, here, s["ys"].at[c, step], s["yr"].at[c, step], p.dev_y(step))
        self.send(self.unit, here, s["cs"].at[c, 0], s["cr"].at[c, 0], p.dev_core())
        self.local.start()

    def forward(self):
        p, s, c = self.p, self.sems, self.c
        n_y = p.geo.n_y
        from_x = self.to(p.y, 1 - p.x, p.core)
        self.arrived(from_x, s["xs"].at[c], s["xr"].at[c], p.dev_x())
        if self.half_a:
            for step in range(1, n_y):
                self.send(from_x, from_x, s["ds"].at[c, step], s["dr"].at[c, step], p.dev_y(step))
        self.send(from_x, from_x, s["cs"].at[c, 1], s["cr"].at[c, 1], p.dev_core())
        for step in range(1, n_y):
            from_y = self.to(p.y_off(-step), p.x, p.core)
            self.arrived(from_y, s["ys"].at[c, step], s["yr"].at[c, step], p.dev_y(step))
            if not self.half_a:
                self.send(from_y, from_y, s["ds"].at[c, step], s["dr"].at[c, step], p.dev_x())
            self.send(from_y, from_y, s["cs"].at[c, 2 * step], s["cr"].at[c, 2 * step], p.dev_core())

    def corner(self):
        p, s, c = self.p, self.sems, self.c
        for step in range(1, p.geo.n_y):
            far = self.to(p.y_off(-step), 1 - p.x, p.core)
            self.arrived(far, s["ds"].at[c, step], s["dr"].at[c, step], p.dev_x())
            self.send(far, far, s["cs"].at[c, 2 * step + 1], s["cr"].at[c, 2 * step + 1], p.dev_core())

    def arrive(self):
        p, s, c = self.p, self.sems, self.c
        for step in range(p.geo.n_y):
            for flip in range(2):
                x = p.x if flip == 0 else 1 - p.x
                got = self.to(p.y_off(-step), x, 1 - p.core)
                at = 2 * step + flip
                self.arrived(got, s["cs"].at[c, at], s["cr"].at[c, at], p.dev_core())
        self.local.wait()

    def drain(self):
        for copy in self.pending:
            copy.wait_send()


def run_pipeline(stages, count):
    last = max(lag for lag, _ in stages)
    first = min(lag for lag, _ in stages)
    for step in range(first, count + last):
        for lag, act in stages:
            if 0 <= step - lag < count:
                act(step - lag)


def dma(*shape):
    return pltpu.SemaphoreType.DMA(shape)


ANY = pl.BlockSpec(memory_space=pl.ANY)
IN_VMEM = pl.BlockSpec(memory_space=pltpu.VMEM)


def wide(values):
    return values.astype(F32)


class Scatter:
    def __init__(self, place, number, chunk, grads, loads, sums, mids, ends, perms, z_send, z_recv, outs, sems):
        self.p, self.c = place, number
        name, at, lead, half = chunk
        self.half_a = number % 2 == 0
        self.k, self.sent, self.rows, self.lanes = place.geo.kind[name]
        self.grad = column(grads[name], name, lead, half, self.k, self.lanes)
        self.load = loads[name].at[number % 2]
        self.sum = sums[name].at[at]
        self.mid = mids[name].at[at]
        self.end = ends[name].at[at]
        self.perm = perms.get(name)
        self.z_send, self.z_recv = z_send[name].at[at], z_recv[name].at[at]
        self.out = outs[name].at[at]
        self.sems = sems
        self.pending = []

    def send(self, src, dst, send, recv, device):
        copy = remote(src, dst, send, recv, device)
        copy.start()
        self.pending.append(copy)

    def arrived(self, dst, send, recv, device):
        remote(dst, dst, send, recv, device).wait_recv()

    def start(self):
        p, s, c = self.p, self.sems, self.c
        every = slice(None)
        self.send(self.grad(every, every, 1 - p.core), self.sum, s["cs"].at[c], s["cr"].at[c], p.dev_core())
        self.local = pltpu.make_async_copy(self.grad(every, every, p.core), self.load, s["lo"].at[c])
        self.local.start()

    def pair(self):
        p, s, c = self.p, self.sems, self.c
        n_y = p.geo.n_y
        self.local.wait()
        self.arrived(self.sum, s["cs"].at[c], s["cr"].at[c], p.dev_core())

        @pl.loop(0, self.k * n_y * 2)
        def _(at):
            where = (at // (2 * n_y), lax.rem(at // 2, n_y), lax.rem(at, 2))
            self.sum[where] = (wide(self.sum[where]) + wide(self.load[where])).astype(BF)

        if self.half_a:
            for step in range(1, n_y):
                self.send(
                    self.sum.at[:, p.y_off(step)], self.mid.at[step - 1, :, pl.ds(0, 2)],
                    s["ms"].at[c, step], s["mr"].at[c, step], p.dev_y(step),
                )
        else:
            self.send(
                self.sum.at[:, :, 1 - p.x], self.mid.at[0, :, pl.ds(0, n_y)],
                s["ms"].at[c, 0], s["mr"].at[c, 0], p.dev_x(),
            )

    def middle(self):
        p, s, c = self.p, self.sems, self.c
        n_y = p.geo.n_y
        if self.half_a:
            for step in range(1, n_y):
                self.arrived(self.mid.at[step - 1, :, pl.ds(0, 2)], s["ms"].at[c, step], s["mr"].at[c, step], p.dev_y(step))

            @pl.loop(0, self.k * 2)
            def _(at):
                where = (at // 2, p.y, lax.rem(at, 2))
                value = wide(self.sum[where])
                for step in range(1, n_y):
                    value = value + wide(self.mid[step - 1, at // 2, lax.rem(at, 2)])
                self.sum[where] = value.astype(BF)

            self.send(
                self.sum.at[:, p.y, 1 - p.x], self.end.at[0], s["es"].at[c, 0], s["er"].at[c, 0], p.dev_x()
            )
        else:
            self.arrived(self.mid.at[0, :, pl.ds(0, n_y)], s["ms"].at[c, 0], s["mr"].at[c, 0], p.dev_x())

            @pl.loop(0, self.k * n_y)
            def _(at):
                where = (at // n_y, lax.rem(at, n_y), p.x)
                value = wide(self.sum[where]) + wide(self.mid[0, at // n_y, lax.rem(at, n_y)])
                self.sum[where] = value.astype(BF)

            for step in range(1, n_y):
                self.send(
                    self.sum.at[:, p.y_off(step), p.x], self.end.at[step - 1],
                    s["es"].at[c, step], s["er"].at[c, step], p.dev_y(step),
                )

    def last(self):
        p, s, c = self.p, self.sems, self.c
        n_y, n_z = p.geo.n_y, p.geo.n_z
        if self.half_a:
            arrivals = [(0, self.end.at[0], p.dev_x())]
        else:
            arrivals = [(step, self.end.at[step - 1], p.dev_y(step)) for step in range(1, n_y)]
        value = wide(self.sum[:, p.y, p.x])
        for at, got, device in arrivals:
            self.arrived(got, s["es"].at[c, at], s["er"].at[c, at], device)
            value = value + wide(got[...])
        value = value.astype(BF).reshape(self.k * self.rows, self.lanes)
        if self.perm is not None:
            value = jnp.dot(self.perm[...], value, preferred_element_type=F32).astype(BF)
        self.z_send[...] = value.reshape(n_z, self.sent, self.lanes)
        for step in range(1, n_z):
            self.send(
                self.z_send.at[p.z_off(step)], self.z_recv.at[step],
                s["zs"].at[c, step], s["zr"].at[c, step], p.dev_z(step),
            )

    def finish(self):
        p, s, c = self.p, self.sems, self.c
        value = wide(self.z_send[p.z])
        for step in range(1, p.geo.n_z):
            self.arrived(self.z_recv.at[step], s["zs"].at[c, step], s["zr"].at[c, step], p.dev_z(step))
            value = value + wide(self.z_recv[step])
        self.out[...] = value

    def drain(self):
        for copy in self.pending:
            copy.wait_send()


def scatter_kernel(geo, names_perm, *refs):
    refs = list(refs)
    take = lambda number: [refs.pop(0) for _ in range(number)]
    kinds = ("a", "b", "v")
    by_kind = lambda: dict(zip(kinds, take(3)))
    grads = by_kind()
    perms = dict(zip(names_perm, take(len(names_perm))))
    outs = by_kind()
    loads, sums, mids, ends, z_send, z_recv = [by_kind() for _ in range(6)]
    sems = dict(zip(("lo", "cs", "cr", "ms", "mr", "es", "er", "zs", "zr"), take(9)))
    place = Place(geo)
    chunks = [("v", 0, 0, 0)] + chunk_list(geo, range(geo.layers))
    moves = [
        Scatter(place, at, chunk, grads, loads, sums, mids, ends, perms, z_send, z_recv, outs, sems)
        for at, chunk in enumerate(chunks)
    ]
    place.greet()
    run_pipeline(
        [
            (-1, lambda c: moves[c].start()),
            (0, lambda c: moves[c].pair()),
            (1, lambda c: moves[c].middle()),
            (2, lambda c: moves[c].last()),
            (4, lambda c: moves[c].finish()),
        ],
        len(moves),
    )
    for move in moves:
        move.drain()


def scatter_all(geo, grad_a, grad_b, grad_v):
    names_perm = [name for name in ("a", "b", "v") if geo.permuted(name)]
    perms = [jnp.asarray(geo.permutation(name).T, BF) for name in names_perm]
    total = sum(geo.number.values())
    n_y, n_z = geo.n_y, geo.n_z
    groups = [[] for _ in range(6)]
    outs = []
    for name in ("a", "b", "v"):
        k, sent, unit, lanes = geo.kind[name]
        number = geo.number[name]
        mid_steps, mid_wide = max(n_y - 1, 1), max(2, n_y)
        groups[0].append(pltpu.VMEM((2, k, n_y, 2, unit, lanes), BF))
        groups[1].append(pltpu.VMEM((number, k, n_y, 2, unit, lanes), BF))
        groups[2].append(pltpu.VMEM((number, mid_steps, k, mid_wide, unit, lanes), BF))
        groups[3].append(pltpu.VMEM((number, mid_steps, k, unit, lanes), BF))
        groups[4].append(pltpu.VMEM((number, n_z, sent, lanes), BF))
        groups[5].append(pltpu.VMEM((number, n_z, sent, lanes), BF))
        outs.append(jax.ShapeDtypeStruct((number, sent, lanes), F32))
    return pl.pallas_call(
        functools.partial(scatter_kernel, geo, names_perm),
        out_shape=outs,
        in_specs=[ANY] * 3 + [IN_VMEM] * len(perms),
        out_specs=[IN_VMEM] * 3,
        scratch_shapes=sum(groups, [])
        + [
            dma(total),
            dma(total),
            dma(total),
            dma(total, n_y),
            dma(total, n_y),
            dma(total, n_y),
            dma(total, n_y),
            dma(total, n_z),
            dma(total, n_z),
        ],
        compiler_params=pltpu.CompilerParams(
            collective_id=1, has_side_effects=True, vmem_limit_bytes=56 * 2**20
        ),
    )(grad_a, grad_b, grad_v, *perms)


def mm(left, right):
    return jnp.dot(left, right, preferred_element_type=F32)


def mm_nt(left, right):
    return lax.dot_general(left, right, (((1,), (1,)), ((), ())), preferred_element_type=F32)


def mm_tn(left, right):
    return lax.dot_general(left, right, (((0,), (0,)), ((), ())), preferred_element_type=F32)


def mean_of(values):
    return jnp.sum(values, -1, keepdims=True) * (1.0 / values.shape[-1])


def normal(values):
    centered = values - mean_of(values)
    scale = lax.rsqrt(mean_of(centered * centered) + epsilon)
    return centered * scale, scale


def norm_rows(source, gain, shift, target, block=32):
    @pl.loop(0, source.shape[0] // block)
    def _(at):
        rows = pl.ds(pl.multiple_of(at * block, block), block)
        unit, _ = normal(source[rows, :])
        target[rows, :] = (unit * gain + shift).astype(target.dtype)


def fold(values):
    total = values[0:8]
    for at in range(8, values.shape[0], 8):
        total = total + values[at : at + 8]
    return total


def norm_rows_back(source, gain, incoming, emit, sums, block=32):
    sums[...] = jnp.zeros_like(sums)

    @pl.loop(0, source.shape[0] // block)
    def _(at):
        rows = pl.ds(pl.multiple_of(at * block, block), block)
        unit, scale = normal(source[rows, :])
        back = incoming[rows, :]
        sums[0] += fold(back * unit)
        sums[1] += fold(back)
        inner = back * gain
        emit(rows, scale * (inner - mean_of(inner) - unit * mean_of(inner * unit)))


ROOT = 0.7978845608028654
CUBE = 0.044715


def gelu_parts(values):
    square = values * values
    curve = jnp.tanh(ROOT * (values + CUBE * (values * square)))
    return square, curve


class Layer:
    def __init__(self, refs, weight_a, weight_b, vec_d, vec_f, layer, heads):
        self.__dict__.update(refs)
        self.weight_a, self.weight_b = weight_a, weight_b
        self.vec_d, self.vec_f = vec_d, vec_f
        self.layer, self.heads = layer, heads

    def gain(self, at):
        return self.vec_d[self.layer * 10 + at : self.layer * 10 + at + 1, :]

    def shift(self, at):
        return self.gain(3 + at)

    def gain_f(self, at):
        return self.vec_f[self.layer * 3 + at : self.layer * 3 + at + 1, :]

    def lane_half(self, values, side):
        lane = lax.broadcasted_iota(jnp.int32, values.shape, 1)
        return (lane < HEAD_DIM) == (side == 0)

    def forward_norm(self):
        norm_rows(self.x, self.gain(0), self.shift(0), self.normed)

    def forward_qkv(self, part):
        value = mm(self.normed[...], self.weight_a(part))
        if part != 1:
            value = value + self.shift(3 if part == 0 else 4)
        self.qkv[part] = value.astype(BF)

    def forward_attention(self):
        valid = self.mask[...] > 0.5

        @pl.loop(0, self.heads // 2)
        def _(pair):
            lanes = pl.ds(pl.multiple_of(pair * 128, 128), 128)
            queries, keys, values = [self.qkv[part, :, lanes] for part in range(3)]
            context = None
            for side in range(2):
                half = self.lane_half(queries, side)
                scores = mm_nt(jnp.where(half, queries, jnp.zeros_like(queries)), keys)
                scores = jnp.where(valid, scores * HEAD_DIM**-0.5, -1e9)
                top = jnp.max(scores, -1, keepdims=True)
                grown = jnp.exp(scores - top)
                prob = grown / jnp.sum(grown, -1, keepdims=True)
                self.prob[2 * pair + side] = prob
                product = mm(prob.astype(BF), values)
                context = product if side == 0 else jnp.where(half, product, context)
            self.context[:, lanes] = context

    def forward_out(self):
        norm_rows(self.context, self.gain(1), self.shift(1), self.sub)
        self.after[...] = self.x[...] + (mm(self.sub[...], self.weight_a(3)) + self.shift(5))
        norm_rows(self.after, self.gain(2), self.shift(2), self.normed_ffn)

    def forward_up(self, part):
        width = self.x.shape[1]
        lanes = slice(part * width, (part + 1) * width)
        self.hidden[:, lanes] = mm(self.normed_ffn[...], self.weight_a(4 + part)) + self.gain_f(1)[:, lanes]

    def forward_gelu(self):
        @pl.loop(0, self.x.shape[0] // 16)
        def _(at):
            rows = pl.ds(pl.multiple_of(at * 16, 16), 16)
            values = self.hidden[rows, :]
            _, curve = gelu_parts(values)
            unit, _ = normal(0.5 * values * (1.0 + curve))
            self.sub_ffn[rows, :] = (unit * self.gain_f(0) + self.gain_f(2)).astype(BF)

    def forward_down(self, half, halves):
        width = self.x.shape[1] // halves
        lanes = slice(half * width, (half + 1) * width)
        value = mm(self.sub_ffn[...], self.weight_b(slice(None), lanes))
        self.x_next[:, lanes] = self.after[:, lanes] + (value + self.shift(6)[:, lanes])


    def store_sums(self, target, row, sums):
        target[row : row + 1, :] = jnp.sum(sums, 0, keepdims=True)

    def backward_start(self):
        self.low[...] = self.back[...].astype(BF)
        self.store_sums(self.grad_d, 9, wide(self.low[...]))

    def backward_down(self, put):
        width = self.x.shape[1]
        for part in range(self.hidden.shape[1] // width):
            lanes = slice(part * width, (part + 1) * width)
            put("b", part, lambda: mm_tn(self.sub_ffn[:, lanes], self.low[...]))
            self.wide_back[:, lanes] = mm_nt(self.low[...], self.weight_b(lanes, slice(None)))

    def backward_gelu(self):
        self.sums_f[...] = jnp.zeros_like(self.sums_f)

        @pl.loop(0, self.x.shape[0] // 16)
        def _(at):
            rows = pl.ds(pl.multiple_of(at * 16, 16), 16)
            values = self.hidden[rows, :]
            square, curve = gelu_parts(values)
            unit, scale = normal(0.5 * values * (1.0 + curve))
            back = self.wide_back[rows, :]
            self.sums_f[0] += fold(back * unit)
            self.sums_f[1] += fold(back)
            inner = back * self.gain_f(0)
            d_gelu = scale * (inner - mean_of(inner) - unit * mean_of(inner * unit))
            slope = 0.5 * (1.0 + curve) + 0.5 * values * (1.0 - curve * curve) * (
                ROOT * (1.0 + 3.0 * CUBE * square)
            )
            low = (d_gelu * slope).astype(BF)
            self.d_hidden[rows, :] = low
            self.sums_f[2] += fold(wide(low))

        self.store_sums(self.grad_f, 0, self.sums_f[0])
        self.store_sums(self.grad_f, 2, self.sums_f[1])
        self.store_sums(self.grad_f, 1, self.sums_f[2])

    def backward_up(self, put):
        width = self.x.shape[1]
        total = None
        for part in range(self.hidden.shape[1] // width):
            lanes = slice(part * width, (part + 1) * width)
            put("a", 4 + part, lambda: mm_tn(self.normed_ffn[...], self.d_hidden[:, lanes]))
            value = mm_nt(self.d_hidden[:, lanes], self.weight_a(4 + part))
            if part == 0:
                self.incoming[...] = value
            else:
                self.incoming[...] += value

        def emit(rows, value):
            value = self.back[rows, :] + value
            self.back[rows, :] = value
            self.low[rows, :] = value.astype(BF)

        norm_rows_back(self.after, self.gain(2), self.incoming, emit, self.sums_d)
        self.store_sums(self.grad_d, 2, self.sums_d[0])
        self.store_sums(self.grad_d, 5, self.sums_d[1])

    def backward_out(self, put):
        self.store_sums(self.grad_d, 8, wide(self.low[...]))
        put("a", 3, lambda: mm_tn(self.sub[...], self.low[...]))
        self.incoming[...] = mm_nt(self.low[...], self.weight_a(3))

        def emit(rows, value):
            self.low[rows, :] = value.astype(BF)

        norm_rows_back(self.context, self.gain(1), self.incoming, emit, self.sums_d)
        self.store_sums(self.grad_d, 1, self.sums_d[0])
        self.store_sums(self.grad_d, 4, self.sums_d[1])

    def backward_attention(self):
        @pl.loop(0, self.heads // 2)
        def _(pair):
            lanes = pl.ds(pl.multiple_of(pair * 128, 128), 128)
            queries, keys, values = [self.qkv[part, :, lanes] for part in range(3)]
            d_context = self.low[:, lanes]
            found = [None] * 3
            for side in range(2):
                half = self.lane_half(d_context, side)
                prob = self.prob[2 * pair + side]
                d_prob = mm_nt(jnp.where(half, d_context, jnp.zeros_like(d_context)), values)
                dot = jnp.sum(prob * d_prob, -1, keepdims=True)
                d_scores = (prob * (d_prob - dot)).astype(BF)
                new = (
                    mm(d_scores, keys) * HEAD_DIM**-0.5,
                    mm_tn(d_scores, queries) * HEAD_DIM**-0.5,
                    mm_tn(prob.astype(BF), d_context),
                )
                found = [n if side == 0 else jnp.where(half, n, f) for n, f in zip(new, found)]
            for part in range(3):
                self.d_qkv[part, :, lanes] = found[part].astype(BF)

    def backward_qkv(self, put):
        self.store_sums(self.grad_d, 6, wide(self.d_qkv[0]))
        self.store_sums(self.grad_d, 7, wide(self.d_qkv[2]))
        for part in range(3):
            put("a", part, lambda: mm_tn(self.normed[...], self.d_qkv[part]))
            value = mm_nt(self.d_qkv[part], self.weight_a(part))
            if part == 0:
                self.incoming[...] = value
            else:
                self.incoming[...] += value

        def emit(rows, value):
            self.back[rows, :] = self.back[rows, :] + value

        norm_rows_back(self.x, self.gain(0), self.incoming, emit, self.sums_d)
        self.store_sums(self.grad_d, 0, self.sums_d[0])
        self.store_sums(self.grad_d, 3, self.sums_d[1])


def saved_shapes(rows, width, wide_width, heads):
    return {
        "normed": ((rows, width), BF),
        "qkv": ((3, rows, width), BF),
        "prob": ((heads, rows, rows), F32),
        "context": ((rows, width), F32),
        "sub": ((rows, width), BF),
        "after": ((rows, width), F32),
        "normed_ffn": ((rows, width), BF),
        "hidden": ((rows, wide_width), F32),
        "sub_ffn": ((rows, wide_width), BF),
    }


def work_shapes(rows, width, wide_width):
    return {
        "low": ((rows, width), BF),
        "incoming": ((rows, width), F32),
        "wide_back": ((rows, wide_width), F32),
        "d_hidden": ((rows, wide_width), BF),
        "d_qkv": ((3, rows, width), BF),
        "sums_d": ((2, 8, width), F32),
        "sums_f": ((3, 8, wide_width), F32),
    }


class Putter:
    def __init__(self, stage, sem):
        self.stage, self.sem, self.count, self.copies = stage, sem, 0, [None, None]

    def put(self, target, value):
        slot = self.count % 2
        if self.copies[slot] is not None:
            self.copies[slot].wait()
        rows = self.stage.shape[1]
        self.stage[slot] = value().astype(BF)
        self.copies[slot] = pltpu.make_async_copy(self.stage.at[slot], target, self.sem.at[slot])
        self.copies[slot].start()
        self.count += 1

    def drain(self):
        for copy in self.copies:
            if copy is not None:
                copy.wait()


def spread_tables(geo):
    tables = []
    for width, real in ((geo.width, geo.rows_a), (geo.wide_width, geo.rows_b)):
        at = np.arange(width)
        owner = (at[None, :] // real == np.arange(geo.owners)[:, None]).astype(np.float32)
        tables += [jnp.asarray(owner, BF), jnp.asarray(at[None, :] % real, jnp.int32)]
    return tables


def unpack_vectors(geo, whole_v, wide_v, tables, vec_d, vec_f):
    owner_d, rest_d, owner_f, rest_f = tables
    lines = geo.kind["v"][1]
    wide_v[...] = wide(whole_v[0])
    line_of = lambda at: wide_v[pl.ds(at, geo.owners, stride=lines), :].astype(BF)
    pick_d = lax.broadcasted_iota(jnp.int32, (geo.slot, geo.width), 0) == rest_d[...]
    for line in range(geo.lines_d):
        spread = mm_tn(line_of(line), owner_d[...])
        for at in range(geo.per_row):
            part = spread[at * geo.slot : (at + 1) * geo.slot]
            row = line * geo.per_row + at
            if row < geo.layers * 10:
                vec_d[row : row + 1, :] = jnp.sum(jnp.where(pick_d, part, 0.0), 0, keepdims=True)
    pick_f = lax.broadcasted_iota(jnp.int32, (128, geo.width), 0)
    for row in range(geo.layers * 3):
        line = line_of(geo.lines_d + row)
        for first in range(0, geo.wide_width, geo.width):
            lanes = slice(first, first + geo.width)
            spread = jnp.where(pick_f == rest_f[:, lanes], mm_tn(line, owner_f[:, lanes]), 0.0)
            vec_f[row : row + 1, lanes] = jnp.sum(spread, 0, keepdims=True)


KINDS = ("a", "b", "v")
GATHER_SEMS = ("lz", "lo", "zs", "zr", "xs", "xr", "ys", "yr", "ds", "dr", "cs", "cr")


def forward_kernel(geo, names_perm, saved_names, *refs):
    refs = list(refs)
    take = lambda number: [refs.pop(0) for _ in range(number)]
    sources = dict(zip(KINDS, take(3)))
    perms = dict(zip(names_perm, take(len(names_perm))))
    act_ref, mask_ref = take(2)
    tables = take(4)
    out_ref, vec_d, vec_f, kept_a, kept_b, kept_x = take(6)
    kept = [dict(zip(saved_names, take(len(saved_names)))) for _ in range(geo.layers)]
    wholes = dict(zip(KINDS, take(3)))
    bufs = dict(zip(KINDS, take(3)))
    units = dict(zip(names_perm, take(len(names_perm))))
    saved = [dict(zip(saved_names, take(len(saved_names)))) for _ in range(geo.layers)]
    xs, wide_v, keep_sem = take(3)
    sems = dict(zip(GATHER_SEMS, take(len(GATHER_SEMS))))
    place = Place(geo)
    chunks = [("v", 0, 0, 0)] + chunk_list(geo, range(geo.layers))
    moves = [
        Gather(place, at, chunk, sources, bufs, units, perms, wholes, sems)
        for at, chunk in enumerate(chunks)
    ]
    keeps = []

    def keep(src, dst):
        copy = pltpu.make_async_copy(src, dst, keep_sem.at[len(keeps)])
        copy.start()
        keeps.append(copy)

    net = []
    for layer in range(geo.layers):
        fields = dict(saved[layer], x=xs.at[layer], x_next=xs.at[layer + 1], mask=mask_ref)
        read_a = lambda at, layer=layer: wholes["a"][layer * geo.blocks + at]
        read_b = lambda rows, lanes, layer=layer: wholes["b"][layer, rows, lanes]
        net.append(Layer(fields, read_a, read_b, vec_d, vec_f, layer, geo.width // HEAD_DIM))

    def compute(number):
        name, at, lead, half = chunks[number]
        moves[number].arrive()
        if name == "v":
            unpack_vectors(geo, wholes["v"], wide_v, tables, vec_d, vec_f)
            return
        k, _, _, lanes = geo.kind[name]
        layer = at // (geo.pairs if name == "a" else geo.halves)
        one = net[layer]
        save = lambda *found: [keep(saved[layer][field], kept[layer][field]) for field in found]
        if name == "a":
            keep(wholes["a"].at[pl.ds(lead, k)], kept_a.at[pl.ds(lead, k)])
            pair = at % geo.pairs
            if pair == 0:
                one.forward_norm()
                one.forward_qkv(0)
                one.forward_qkv(1)
            elif pair == 1:
                one.forward_qkv(2)
                save("normed", "qkv")
                one.forward_attention()
                one.forward_out()
                save("prob", "context", "sub", "after", "normed_ffn")
            else:
                one.forward_up(2 * pair - 4)
                one.forward_up(2 * pair - 3)
                if pair == geo.pairs - 1:
                    one.forward_gelu()
                    save("hidden", "sub_ffn")
        else:
            where = pl.ds(half * lanes, lanes)
            keep(wholes["b"].at[lead, :, where], kept_b.at[lead, :, where])
            one.forward_down(half, geo.halves)
            if half == geo.halves - 1 and layer < geo.layers - 1:
                keep(xs.at[layer + 1], kept_x.at[layer + 1])

    xs[0] = wide(act_ref[...])
    keep(xs.at[0], kept_x.at[0])
    place.greet()
    run_pipeline(
        [
            (-2, lambda c: moves[c].start_z()),
            (0, lambda c: moves[c].own()),
            (1, lambda c: moves[c].forward()),
            (2, lambda c: moves[c].corner()),
            (3, compute),
        ],
        len(moves),
    )
    out_ref[...] = xs[geo.layers].astype(BF)
    for move in moves:
        move.drain()
    for copy in keeps:
        copy.wait()


def run_forward(geo, source_a, source_b, source_v, act, mask):
    names_perm = [name for name in KINDS if geo.permuted(name)]
    perms = [jnp.asarray(geo.permutation(name), BF) for name in names_perm]
    rows, width = act.shape
    total = sum(geo.number.values())
    heads = width // HEAD_DIM
    saved = saved_shapes(rows, width, geo.wide_width, heads)
    bufs, units, wholes = [], [], []
    for name in KINDS:
        k, sent, unit, lanes = geo.kind[name]
        bufs.append(pltpu.VMEM((geo.number[name], geo.n_z * sent, lanes), BF))
        if name in names_perm:
            units.append(pltpu.VMEM((geo.number[name], k, unit, lanes), BF))
        lead, _, _, _, _, whole_lanes = geo.whole_shape(name)
        wholes.append(((lead, geo.n_dp * unit, whole_lanes), BF))
    n_y, n_z = geo.n_y, geo.n_z
    n_keeps = geo.layers * (len(saved) + geo.pairs + geo.halves + 1)
    vec_rows = geo.layers * 10
    outs = [
        jax.ShapeDtypeStruct((rows, width), BF),
        jax.ShapeDtypeStruct((vec_rows, width), F32),
        jax.ShapeDtypeStruct((geo.layers * 3, geo.wide_width), F32),
        jax.ShapeDtypeStruct(*wholes[0]),
        jax.ShapeDtypeStruct(*wholes[1]),
        jax.ShapeDtypeStruct((geo.layers, rows, width), F32),
    ] + [jax.ShapeDtypeStruct(*saved[name]) for _ in range(geo.layers) for name in saved]
    found = pl.pallas_call(
        functools.partial(forward_kernel, geo, names_perm, list(saved)),
        out_shape=outs,
        in_specs=[IN_VMEM] * (3 + len(perms) + 6),
        out_specs=[IN_VMEM] * 3 + [ANY] * (len(outs) - 3),
        scratch_shapes=[pltpu.VMEM(*whole) for whole in wholes]
        + bufs
        + units
        + [pltpu.VMEM(*saved[name]) for _ in range(geo.layers) for name in saved]
        + [
            pltpu.VMEM((geo.layers + 1, rows, width), F32),
            pltpu.VMEM(wholes[2][0][1:], F32),
            dma(n_keeps),
            dma(total),
            dma(total),
            dma(total, n_z),
            dma(total, n_z),
            dma(total),
            dma(total),
            dma(total, n_y),
            dma(total, n_y),
            dma(total, n_y),
            dma(total, n_y),
            dma(total, 2 * n_y),
            dma(total, 2 * n_y),
        ],
        compiler_params=pltpu.CompilerParams(
            collective_id=0, has_side_effects=True, vmem_limit_bytes=60 * 2**20
        ),
    )(source_a, source_b, source_v, *perms, act, mask, *spread_tables(geo))
    names = list(saved)
    kept = [dict(zip(names, found[6 + layer * len(names) :])) for layer in range(geo.layers)]
    return found[:6], kept


def backward_kernel(geo, names, *refs):
    refs = list(refs)
    take = lambda number: [refs.pop(0) for _ in range(number)]
    saved_names, work_names = names
    layers, blocks = geo.layers, geo.blocks
    cot_ref, vec_d, vec_f, whole_a, whole_b, kept_x = take(6)
    kept = [dict(zip(saved_names, take(len(saved_names)))) for _ in range(layers)]
    back_ref, grad_a, grad_b, grad_d, grad_f = take(5)
    saved = [dict(zip(saved_names, take(len(saved_names)))) for _ in range(layers)]
    work = dict(zip(work_names, take(len(work_names))))
    xs, weight_a, weight_b, stage, sem_l, sem_g = take(6)
    width = geo.width
    loads = []

    def load(src, dst):
        copy = pltpu.make_async_copy(src, dst, sem_l.at[len(loads)])
        copy.start()
        loads.append(copy)

    load(kept_x, xs)
    for layer in reversed(range(layers)):
        for name in saved_names:
            load(kept[layer][name], saved[layer][name])
        load(whole_b.at[layer], weight_b.at[layer])
        load(whole_a.at[pl.ds(layer * blocks, blocks)], weight_a.at[pl.ds(layer * blocks, blocks)])
    net = []
    for layer in range(layers):
        fields = dict(saved[layer], **work)
        fields.update(x=xs.at[layer], back=back_ref, grad_d=grad_d.at[layer], grad_f=grad_f.at[layer])
        read_a = lambda at, layer=layer: weight_a[layer * blocks + at]
        read_b = lambda rows, lanes, layer=layer: weight_b[layer, rows, lanes]
        net.append(Layer(fields, read_a, read_b, vec_d, vec_f, layer, width // HEAD_DIM))
    back_ref[...] = cot_ref[...]
    putter = Putter(stage, sem_g)
    for copy in loads:
        copy.wait()
    for layer in reversed(range(layers)):
        one = net[layer]

        def put(kind, at, value, layer=layer):
            if kind == "a":
                target = grad_a.at[layer * blocks + at]
            else:
                target = grad_b.at[layer, pl.ds(at * width, width)]
            putter.put(target, value)

        one.backward_start()
        one.backward_down(put)
        one.backward_gelu()
        one.backward_up(put)
        one.backward_out(put)
        one.backward_attention()
        one.backward_qkv(put)
    putter.drain()


def run_backward(geo, cot, vec_d, vec_f, whole_a, whole_b, kept_x, kept):
    rows, width = cot.shape
    layers = geo.layers
    heads = width // HEAD_DIM
    saved, work = saved_shapes(rows, width, geo.wide_width, heads), work_shapes(rows, width, geo.wide_width)
    names = (list(saved), list(work))
    scratch = [pltpu.VMEM(*saved[name]) for _ in range(layers) for name in saved]
    scratch += [pltpu.VMEM(*work[name]) for name in work]
    scratch += [
        pltpu.VMEM(kept_x.shape, F32),
        pltpu.VMEM(whole_a.shape, BF),
        pltpu.VMEM(whole_b.shape, BF),
        pltpu.VMEM((2, width, width), BF),
        dma(1 + layers * (len(saved) + 2)),
        dma(2),
    ]
    return pl.pallas_call(
        functools.partial(backward_kernel, geo, names),
        out_shape=[
            jax.ShapeDtypeStruct((rows, width), F32),
            jax.ShapeDtypeStruct(whole_a.shape, BF),
            jax.ShapeDtypeStruct(whole_b.shape, BF),
            jax.ShapeDtypeStruct((layers, 10, width), F32),
            jax.ShapeDtypeStruct((layers, 3, geo.wide_width), F32),
        ],
        in_specs=[IN_VMEM] * 3 + [ANY] * (3 + layers * len(saved)),
        out_specs=[IN_VMEM] + [ANY] * 2 + [IN_VMEM] * 2,
        scratch_shapes=scratch,
        compiler_params=pltpu.CompilerParams(vmem_limit_bytes=60 * 2**20),
    )(cot, vec_d, vec_f, whole_a, whole_b, kept_x, *[kept[layer][name] for layer in range(layers) for name in saved])


def pack_rows(blocks, rows):
    joined = jnp.concatenate(blocks, 0)
    return jnp.pad(joined, ((0, rows - joined.shape[0]), (0, 0)))


def pack_vectors(geo, vec_d, vec_f):
    filled = jnp.pad(vec_d, ((0, geo.lines_d * geo.per_row - vec_d.shape[0]), (0, geo.slot - vec_d.shape[1])))
    lines = jnp.concatenate(
        [filled.reshape(geo.lines_d, 128), jnp.pad(vec_f, ((0, 0), (0, 128 - vec_f.shape[1])))]
    )
    return pack_rows([lines], geo.kind["v"][1])


def unpack_lines(geo, lines):
    rows_d = lines[: geo.lines_d].reshape(-1, geo.slot)[: geo.layers * 10, : geo.rows_a]
    rows_f = lines[geo.lines_d : geo.lines_d + geo.layers * 3, : geo.rows_b]
    return rows_d.reshape(geo.layers, 10, -1), rows_f.reshape(geo.layers, 3, -1)


def owner_lines(geo, grad_d, grad_f):
    rows_d = grad_d.reshape(-1, geo.owners, geo.rows_a).transpose(1, 0, 2)
    rows_f = grad_f.reshape(-1, geo.owners, geo.rows_b).transpose(1, 0, 2)
    fill = geo.lines_d * geo.per_row - rows_d.shape[1]
    rows_d = jnp.pad(rows_d, ((0, 0), (0, fill), (0, geo.slot - geo.rows_a)))
    rows_f = jnp.pad(rows_f, ((0, 0), (0, 0), (0, 128 - geo.rows_b)))
    lines = jnp.concatenate([rows_d.reshape(geo.owners, -1, 128), rows_f], 1)
    return jnp.pad(lines, ((0, 0), (0, geo.kind["v"][1] - lines.shape[1]), (0, 0)))


def on_device(
    act_short,
    act_long,
    len_short,
    len_long,
    w_qkv,
    w_out,
    w_up,
    w_down,
    gains_d,
    shifts_d,
    gains_ff,
    shifts_ff,
    cot_short,
    cot_long,
):
    n_dp, n_z = lax.axis_size("dp"), lax.axis_size("fsdp")
    geo = Geometry(n_dp, n_z, w_qkv.shape, w_up.shape, w_down.shape)
    width = geo.width
    cut = lambda array, at: array[:, at * width : (at + 1) * width]
    source_a, source_b = [], []
    for layer in range(geo.layers):
        blocks = [cut(w_qkv[layer], at) for at in range(3)] + [w_out[layer]]
        blocks += [cut(w_up[layer], at) for at in range(geo.blocks - 4)]
        for pair in range(geo.pairs):
            source_a.append(pack_rows(blocks[2 * pair : 2 * pair + 2], geo.kind["a"][1]))
        for half in range(geo.halves):
            lanes = geo.kind["b"][3]
            piece = w_down[layer][:, half * lanes : (half + 1) * lanes]
            source_b.append(pack_rows([piece], geo.kind["b"][1]))
    vec_d = jnp.concatenate([gains_d, shifts_d], 1).reshape(-1, geo.rows_a)
    vec_f = jnp.concatenate([gains_ff[:, None], shifts_ff], 1).reshape(-1, geo.rows_b)
    source_v = pack_vectors(geo, vec_d, vec_f)[None]
    rows_short, rows_long = act_short.shape[0], act_long.shape[0]
    rows = rows_short + rows_long
    at = np.arange(rows)
    bucket = (at >= rows_short).astype(np.int32)
    place = at - rows_short * bucket
    length = jnp.where(bucket == 0, len_short[0], len_long[0])
    valid = place < length
    mask = ((bucket[:, None] == bucket[None, :]) & valid[None, :]).astype(F32)
    cot = jnp.concatenate([cot_short, cot_long]).astype(F32) * valid.astype(F32)[:, None]
    act = jnp.concatenate([act_short, act_long])
    found, kept = run_forward(geo, jnp.stack(source_a), jnp.stack(source_b), source_v, act, mask)
    out, vec_d, vec_f, whole_a, whole_b, kept_x = found
    back, grad_a, grad_b, grad_d, grad_f = run_backward(
        geo, cot, vec_d, vec_f, whole_a, whole_b, kept_x, kept
    )
    rows_v = owner_lines(geo, grad_d, grad_f).astype(BF)
    own_a, own_b, own_v = scatter_all(
        geo,
        grad_a.reshape(geo.whole_shape("a")),
        grad_b.reshape(geo.whole_shape("b")),
        rows_v.reshape(geo.whole_shape("v")),
    )
    rows_a = geo.rows_a
    own_a = own_a[:, : 2 * rows_a].reshape(geo.layers, geo.blocks, rows_a, width)
    own_b = own_b[:, : geo.rows_b].reshape(geo.layers, geo.halves, geo.rows_b, -1)
    join = lambda first, last: jnp.concatenate([own_a[:, at] for at in range(first, last)], 2)
    own_d, own_f = unpack_lines(geo, own_v[0])
    return (
        out[:rows_short],
        out[rows_short:],
        back[:rows_short],
        back[rows_short:],
        join(0, 3),
        own_a[:, 3],
        join(4, geo.blocks),
        jnp.concatenate([own_b[:, at] for at in range(geo.halves)], 2),
        own_d[:, :3],
        own_d[:, 3:],
        own_f[:, 0],
        own_f[:, 1:],
    )


def solution(mesh):
    return jax.shard_map(
        on_device,
        mesh=mesh,
        in_specs=(
            P(("dp", "fsdp"), None),
            P(("dp", "fsdp"), None),
            P(("dp", "fsdp")),
            P(("dp", "fsdp")),
            P(None, ("dp", "fsdp"), None),
            P(None, ("dp", "fsdp"), None),
            P(None, ("dp", "fsdp"), None),
            P(None, ("dp", "fsdp"), None),
            P(None, None, ("dp", "fsdp")),
            P(None, None, ("dp", "fsdp")),
            P(None, ("dp", "fsdp")),
            P(None, None, ("dp", "fsdp")),
            P(("dp", "fsdp"), None),
            P(("dp", "fsdp"), None),
        ),
        out_specs=(
            P(("dp", "fsdp"), None),
            P(("dp", "fsdp"), None),
            P(("dp", "fsdp"), None),
            P(("dp", "fsdp"), None),
            P(None, ("dp", "fsdp"), None),
            P(None, ("dp", "fsdp"), None),
            P(None, ("dp", "fsdp"), None),
            P(None, ("dp", "fsdp"), None),
            P(None, None, ("dp", "fsdp")),
            P(None, None, ("dp", "fsdp")),
            P(None, ("dp", "fsdp")),
            P(None, None, ("dp", "fsdp")),
        ),
        check_vma=False,
    )
```

```python
import functools

import jax
import jax.numpy as jnp
import numpy as np
from jax import lax
from jax.experimental import pallas as pl
from jax.experimental.pallas import tpu as pltpu
from jax.sharding import PartitionSpec as P

HEAD_DIM = 64

epsilon = 1e-05


BF = jnp.bfloat16
F32 = jnp.float32
MESH = pl.DeviceIdType.MESH


def round16(count):
    return (count + 15) // 16 * 16


class Geometry:
    def __init__(self, n_dp, n_z, w_qkv, w_up, w_down):
        self.n_dp, self.n_z, self.n_y = n_dp, n_z, n_dp // 4
        self.layers = w_qkv[0]
        self.width = w_qkv[2] // 3
        self.rows_a, self.rows_b = w_qkv[1], w_down[1]
        self.blocks = 4 + w_up[2] // self.width
        self.pairs = self.blocks // 2
        self.halves = 2
        self.owners = n_dp * n_z
        self.wide_width = w_up[2]
        self.slot = 8
        while self.slot < self.rows_a:
            self.slot *= 2
        self.per_row = 128 // self.slot
        self.lines_d = -(-self.layers * 10 // self.per_row)
        lines = round16(self.lines_d + self.layers * 3)
        self.kind = {
            "a": (2, round16(2 * self.rows_a), self.rows_a * n_z, self.width),
            "b": (1, round16(self.rows_b), self.rows_b * n_z, self.width // 2),
            "v": (1, lines, lines * n_z, 128),
        }
        self.real = {"a": self.rows_a, "b": self.rows_b, "v": self.kind["v"][1]}
        self.number = {"a": self.layers * self.pairs, "b": self.layers * self.halves, "v": 1}

    def permuted(self, name):
        k, sent, unit, _ = self.kind[name]
        return k * unit != sent * self.n_z or k > 1

    def permutation(self, name):
        k, sent, unit, _ = self.kind[name]
        real = self.real[name]
        table = np.zeros((k * unit, self.n_z * sent), np.float32)
        for block in range(k):
            for z in range(self.n_z):
                for row in range(real):
                    table[block * unit + z * real + row, z * sent + block * real + row] = 1
        return table

    def whole_shape(self, name):
        _, _, unit, lanes = self.kind[name]
        lead = {"a": self.layers * self.blocks, "b": self.layers, "v": 1}[name]
        lanes = self.width if name == "b" else lanes
        return (lead, self.n_y, 2, 2, unit, lanes)


class Place:
    def __init__(self, geo):
        self.geo = geo
        self.d, self.z = lax.axis_index("dp"), lax.axis_index("fsdp")
        self.core = lax.rem(self.d, 2)
        self.x = lax.rem(self.d // 2, 2)
        self.y = self.d // 4

    def y_off(self, step):
        return lax.rem(self.y + step + self.geo.n_y, self.geo.n_y)

    def z_off(self, step):
        return lax.rem(self.z + step + self.geo.n_z, self.geo.n_z)

    def dev_core(self):
        return (self.d + 1 - 2 * self.core, self.z)

    def dev_x(self):
        return (self.d + 2 - 4 * self.x, self.z)

    def dev_y(self, step):
        return (self.y_off(step) * 4 + self.x * 2 + self.core, self.z)

    def dev_z(self, step):
        return (self.d, self.z_off(step))

    def greet(self):
        barrier = pltpu.get_barrier_semaphore()
        partners = [self.dev_core(), self.dev_x()]
        partners += [self.dev_y(step) for step in range(1, self.geo.n_y)]
        partners += [self.dev_z(step) for step in range(1, self.geo.n_z)]
        for partner in partners:
            pl.semaphore_signal(barrier, inc=1, device_id=partner, device_id_type=MESH)
        pl.semaphore_wait(barrier, len(partners))


def remote(src, dst, send, recv, device):
    return pltpu.make_async_remote_copy(
        src_ref=src, dst_ref=dst, send_sem=send, recv_sem=recv, device_id=device, device_id_type=MESH
    )


def chunk_list(geo, layers):
    found = []
    for layer in layers:
        for pair in range(geo.pairs):
            found.append(("a", layer * geo.pairs + pair, layer * geo.blocks + 2 * pair, 0))
        for half in range(geo.halves):
            found.append(("b", layer * geo.halves + half, layer, half))
    return found


def rows_of(whole, name, lead, half, k, unit, lanes):
    def at(y, x, core):
        rows = pl.ds(pl.multiple_of((y * 4 + x * 2 + core) * unit, 16), unit)
        return whole.at[pl.ds(lead, k), rows, pl.ds(half * lanes, lanes) if name == "b" else slice(None)]

    return at


class Gather:
    def __init__(self, place, number, chunk, sources, bufs, units, perms, wholes, sems):
        self.p, self.c = place, number
        name, at, lead, half = chunk
        self.half_a = number % 2 == 0
        k, self.sent, unit, lanes = place.geo.kind[name]
        self.source = sources[name].at[at]
        self.buf = bufs[name].at[at]
        self.perm = perms.get(name)
        self.unit_buf = units[name].at[at] if self.perm is not None else None
        self.unit = self.unit_buf if self.perm is not None else bufs[name].at[pl.ds(at, 1)]
        self.to = rows_of(wholes[name], name, lead, half, k, unit, lanes)
        self.sems = sems
        self.pending = []

    def slot(self, z):
        return self.buf.at[pl.ds(pl.multiple_of(z * self.sent, 16), self.sent)]

    def send(self, src, dst, send, recv, device):
        copy = remote(src, dst, send, recv, device)
        copy.start()
        self.pending.append(copy)

    def arrived(self, dst, send, recv, device):
        remote(dst, dst, send, recv, device).wait_recv()

    def start_z(self):
        p, s, c = self.p, self.sems, self.c
        self.local_z = pltpu.make_async_copy(self.source, self.slot(p.z), s["lz"].at[c])
        self.local_z.start()
        for step in range(1, p.geo.n_z):
            self.send(self.source, self.slot(p.z), s["zs"].at[c, step], s["zr"].at[c, step], p.dev_z(step))

    def own(self):
        p, s, c = self.p, self.sems, self.c
        self.local_z.wait()
        for step in range(1, p.geo.n_z):
            self.arrived(self.slot(p.z_off(-step)), s["zs"].at[c, step], s["zr"].at[c, step], p.dev_z(step))
        if self.perm is not None:
            k, unit, lanes = self.unit_buf.shape
            mixed = jnp.dot(self.perm[...], self.buf[...], preferred_element_type=F32)
            self.unit_buf[...] = mixed.astype(BF).reshape(k, unit, lanes)
        here = self.to(p.y, p.x, p.core)
        self.local = pltpu.make_async_copy(self.unit, here, s["lo"].at[c])
        self.send(self.unit, here, s["xs"].at[c], s["xr"].at[c], p.dev_x())
        for step in range(1, p.geo.n_y):
            self.send(self.unit, here, s["ys"].at[c, step], s["yr"].at[c, step], p.dev_y(step))
        self.send(self.unit, here, s["cs"].at[c, 0], s["cr"].at[c, 0], p.dev_core())
        self.local.start()

    def forward(self):
        p, s, c = self.p, self.sems, self.c
        n_y = p.geo.n_y
        from_x = self.to(p.y, 1 - p.x, p.core)
        self.arrived(from_x, s["xs"].at[c], s["xr"].at[c], p.dev_x())
        if self.half_a:
            for step in range(1, n_y):
                self.send(from_x, from_x, s["ds"].at[c, step], s["dr"].at[c, step], p.dev_y(step))
        self.send(from_x, from_x, s["cs"].at[c, 1], s["cr"].at[c, 1], p.dev_core())
        for step in range(1, n_y):
            from_y = self.to(p.y_off(-step), p.x, p.core)
            self.arrived(from_y, s["ys"].at[c, step], s["yr"].at[c, step], p.dev_y(step))
            if not self.half_a:
                self.send(from_y, from_y, s["ds"].at[c, step], s["dr"].at[c, step], p.dev_x())
            self.send(from_y, from_y, s["cs"].at[c, 2 * step], s["cr"].at[c, 2 * step], p.dev_core())

    def corner(self):
        p, s, c = self.p, self.sems, self.c
        for step in range(1, p.geo.n_y):
            far = self.to(p.y_off(-step), 1 - p.x, p.core)
            self.arrived(far, s["ds"].at[c, step], s["dr"].at[c, step], p.dev_x())
            self.send(far, far, s["cs"].at[c, 2 * step + 1], s["cr"].at[c, 2 * step + 1], p.dev_core())

    def arrive(self):
        p, s, c = self.p, self.sems, self.c
        for step in range(p.geo.n_y):
            for flip in range(2):
                x = p.x if flip == 0 else 1 - p.x
                got = self.to(p.y_off(-step), x, 1 - p.core)
                at = 2 * step + flip
                self.arrived(got, s["cs"].at[c, at], s["cr"].at[c, at], p.dev_core())
        self.local.wait()

    def drain(self):
        for copy in self.pending:
            copy.wait_send()


def run_pipeline(stages, count):
    last = max(lag for lag, _ in stages)
    first = min(lag for lag, _ in stages)
    for step in range(first, count + last):
        for lag, act in stages:
            if 0 <= step - lag < count:
                act(step - lag)


def dma(*shape):
    return pltpu.SemaphoreType.DMA(shape)


ANY = pl.BlockSpec(memory_space=pl.ANY)
IN_VMEM = pl.BlockSpec(memory_space=pltpu.VMEM)


def wide(values):
    return values.astype(F32)


class Scatter:
    def __init__(self, place, number, chunk, stage, sums, mids, ends, perms, z_send, z_recv, z_slot, before, put, sems):
        self.p, self.c = place, number
        name, at, lead, half = chunk
        self.half_a = number % 2 == 0
        self.k, self.sent, self.rows, self.lanes = place.geo.kind[name]
        self.stage = stage
        self.sum = sums[name].at[at]
        layer = at // (place.geo.number[name] // place.geo.layers) if name != "v" else None
        self.mid = mids[name].at[at - layer * (place.geo.number[name] // place.geo.layers) if layer is not None else 0]
        self.hands_on = layer is not None and layer > 0
        self.takes_over = layer is not None and layer < place.geo.layers - 1
        self.end = ends[name].at[at]
        self.perm = perms.get(name)
        self.z_send, self.z_recv = z_send[name].at[z_slot], z_recv[name].at[at]
        self.before, self.z_moves = before, []
        self.put = put
        self.sems = sems
        self.pending = []

    def send(self, src, dst, send, recv, device):
        copy = remote(src, dst, send, recv, device)
        copy.start()
        self.pending.append(copy)

    def arrived(self, dst, send, recv, device):
        remote(dst, dst, send, recv, device).wait_recv()

    def start(self):
        p, s, c = self.p, self.sems, self.c
        give = self.stage.at[:, :, :, 1 - p.core]
        self.given = remote(give, self.sum, s["cs"].at[c], s["cr"].at[c], p.dev_core())
        self.given.start()

    def pair(self):
        p, s, c = self.p, self.sems, self.c
        n_y = p.geo.n_y
        self.arrived(self.sum, s["cs"].at[c], s["cr"].at[c], p.dev_core())

        @pl.loop(0, self.k * n_y * 2)
        def _(at):
            where = (at // (2 * n_y), lax.rem(at // 2, n_y), lax.rem(at, 2))
            self.sum[where] = (wide(self.sum[where]) + wide(self.stage[where + (p.core,)])).astype(BF)

        self.given.wait_send()
        if self.takes_over and self.half_a:
            for step in range(1, n_y):
                pl.semaphore_wait(s["fy"].at[step], 1)
        if self.takes_over and not self.half_a:
            pl.semaphore_wait(s["fx"], 1)
        if self.half_a:
            for step in range(1, n_y):
                self.send(
                    self.sum.at[:, p.y_off(step)], self.mid.at[step - 1],
                    s["ms"].at[c, step], s["mr"].at[c, step], p.dev_y(step),
                )
        else:
            for y in range(n_y):
                self.send(
                    self.sum.at[:, y, 1 - p.x], self.mid.at[y // 2, :, y % 2],
                    s["ms"].at[c, y], s["mr"].at[c, y], p.dev_x(),
                )

    def middle(self):
        p, s, c = self.p, self.sems, self.c
        n_y = p.geo.n_y
        if self.half_a:
            for step in range(1, n_y):
                self.arrived(self.mid.at[step - 1], s["ms"].at[c, step], s["mr"].at[c, step], p.dev_y(step))

            @pl.loop(0, self.k * 2)
            def _(at):
                where = (at // 2, p.y, lax.rem(at, 2))
                value = wide(self.sum[where])
                for step in range(1, n_y):
                    value = value + wide(self.mid[step - 1, at // 2, lax.rem(at, 2)])
                self.sum[where] = value.astype(BF)

            if self.hands_on:
                for step in range(1, n_y):
                    pl.semaphore_signal(
                        s["fy"].at[step], inc=1, device_id=p.dev_y(-step), device_id_type=MESH
                    )
            self.send(
                self.sum.at[:, p.y, 1 - p.x], self.end.at[0], s["es"].at[c, 0], s["er"].at[c, 0], p.dev_x()
            )
        else:
            for y in range(n_y):
                self.arrived(self.mid.at[y // 2, :, y % 2], s["ms"].at[c, y], s["mr"].at[c, y], p.dev_x())

            @pl.loop(0, self.k * n_y)
            def _(at):
                y = lax.rem(at, n_y)
                where = (at // n_y, y, p.x)
                value = wide(self.sum[where]) + wide(self.mid[y // 2, at // n_y, lax.rem(y, 2)])
                self.sum[where] = value.astype(BF)

            if self.hands_on:
                pl.semaphore_signal(s["fx"], inc=1, device_id=p.dev_x(), device_id_type=MESH)

            for step in range(1, n_y):
                self.send(
                    self.sum.at[:, p.y_off(step), p.x], self.end.at[step - 1],
                    s["es"].at[c, step], s["er"].at[c, step], p.dev_y(step),
                )

    def last(self):
        p, s, c = self.p, self.sems, self.c
        n_y, n_z = p.geo.n_y, p.geo.n_z
        if self.half_a:
            arrivals = [(0, self.end.at[0], p.dev_x())]
        else:
            arrivals = [(step, self.end.at[step - 1], p.dev_y(step)) for step in range(1, n_y)]
        value = wide(self.sum[:, p.y, p.x])
        for at, got, device in arrivals:
            self.arrived(got, s["es"].at[c, at], s["er"].at[c, at], device)
            value = value + wide(got[...])
        value = value.astype(BF).reshape(self.k * self.rows, self.lanes)
        if self.perm is not None:
            value = jnp.dot(self.perm[...], value, preferred_element_type=F32).astype(BF)
        if self.before is not None:
            self.before.left()
        self.z_send[...] = value.reshape(n_z, self.sent, self.lanes)
        for step in range(1, n_z):
            copy = remote(
                self.z_send.at[p.z_off(step)], self.z_recv.at[step],
                s["zs"].at[c, step], s["zr"].at[c, step], p.dev_z(step),
            )
            copy.start()
            self.z_moves.append(copy)

    def finish(self):
        p, s, c = self.p, self.sems, self.c
        value = wide(self.z_send[p.z])
        for step in range(1, p.geo.n_z):
            self.arrived(self.z_recv.at[step], s["zs"].at[c, step], s["zr"].at[c, step], p.dev_z(step))
            value = value + wide(self.z_recv[step])
        self.put(value)

    def left(self):
        while self.z_moves:
            self.z_moves.pop().wait_send()

    def drain(self):
        self.left()
        for copy in self.pending:
            copy.wait_send()


def mm(left, right):
    return jnp.dot(left, right, preferred_element_type=F32)


def mm_nt(left, right):
    return lax.dot_general(left, right, (((1,), (1,)), ((), ())), preferred_element_type=F32)


def mm_tn(left, right):
    return lax.dot_general(left, right, (((0,), (0,)), ((), ())), preferred_element_type=F32)


def mean_of(values):
    return jnp.sum(values, -1, keepdims=True) * (1.0 / values.shape[-1])


def normal(values):
    centered = values - mean_of(values)
    scale = lax.rsqrt(mean_of(centered * centered) + epsilon)
    return centered * scale, scale


def norm_rows(source, gain, shift, target, block=32):
    @pl.loop(0, source.shape[0] // block)
    def _(at):
        rows = pl.ds(pl.multiple_of(at * block, block), block)
        unit, _ = normal(source[rows, :])
        target[rows, :] = (unit * gain + shift).astype(target.dtype)


def fold(values):
    total = values[0:8]
    for at in range(8, values.shape[0], 8):
        total = total + values[at : at + 8]
    return total


def norm_rows_back(source, gain, incoming, emit, sums, block=32):
    sums[...] = jnp.zeros_like(sums)

    @pl.loop(0, source.shape[0] // block)
    def _(at):
        rows = pl.ds(pl.multiple_of(at * block, block), block)
        unit, scale = normal(source[rows, :])
        back = incoming[rows, :]
        sums[0] += fold(back * unit)
        sums[1] += fold(back)
        inner = back * gain
        emit(rows, scale * (inner - mean_of(inner) - unit * mean_of(inner * unit)))


ROOT = 0.7978845608028654
CUBE = 0.044715


def gelu_parts(values):
    square = values * values
    curve = jnp.tanh(ROOT * (values + CUBE * (values * square)))
    return square, curve


class Layer:
    def __init__(self, refs, weight_a, weight_b, vec_d, vec_f, layer, heads):
        self.__dict__.update(refs)
        self.weight_a, self.weight_b = weight_a, weight_b
        self.vec_d, self.vec_f = vec_d, vec_f
        self.layer, self.heads = layer, heads

    def gain(self, at):
        return self.vec_d[self.layer * 10 + at : self.layer * 10 + at + 1, :]

    def shift(self, at):
        return self.gain(3 + at)

    def gain_f(self, at):
        return self.vec_f[self.layer * 3 + at : self.layer * 3 + at + 1, :]

    def lane_half(self, values, side):
        lane = lax.broadcasted_iota(jnp.int32, values.shape, 1)
        return (lane < HEAD_DIM) == (side == 0)

    def forward_norm(self):
        norm_rows(self.x, self.gain(0), self.shift(0), self.normed)

    def forward_qkv(self, part):
        value = mm(self.normed[...], self.weight_a(part))
        if part != 1:
            value = value + self.shift(3 if part == 0 else 4)
        self.qkv[part] = value.astype(BF)

    def forward_attention(self):
        valid = self.mask[...] > 0.5

        @pl.loop(0, self.heads // 2)
        def _(pair):
            lanes = pl.ds(pl.multiple_of(pair * 128, 128), 128)
            queries, keys, values = [self.qkv[part, :, lanes] for part in range(3)]
            context = None
            for side in range(2):
                half = self.lane_half(queries, side)
                scores = mm_nt(jnp.where(half, queries, jnp.zeros_like(queries)), keys)
                scores = jnp.where(valid, scores * HEAD_DIM**-0.5, -1e9)
                top = jnp.max(scores, -1, keepdims=True)
                grown = jnp.exp(scores - top)
                prob = grown / jnp.sum(grown, -1, keepdims=True)
                self.prob[2 * pair + side] = prob
                product = mm(prob.astype(BF), values)
                context = product if side == 0 else jnp.where(half, product, context)
            self.context[:, lanes] = context

    def forward_out(self):
        norm_rows(self.context, self.gain(1), self.shift(1), self.sub)
        self.after[...] = self.x[...] + (mm(self.sub[...], self.weight_a(3)) + self.shift(5))
        norm_rows(self.after, self.gain(2), self.shift(2), self.normed_ffn)

    def forward_up(self, part):
        width = self.x.shape[1]
        lanes = slice(part * width, (part + 1) * width)
        self.hidden[:, lanes] = mm(self.normed_ffn[...], self.weight_a(4 + part)) + self.gain_f(1)[:, lanes]

    def forward_gelu(self):
        @pl.loop(0, self.x.shape[0] // 16)
        def _(at):
            rows = pl.ds(pl.multiple_of(at * 16, 16), 16)
            values = self.hidden[rows, :]
            _, curve = gelu_parts(values)
            unit, _ = normal(0.5 * values * (1.0 + curve))
            self.sub_ffn[rows, :] = (unit * self.gain_f(0) + self.gain_f(2)).astype(BF)

    def forward_down(self, half, halves):
        width = self.x.shape[1] // halves
        lanes = slice(half * width, (half + 1) * width)
        value = mm(self.sub_ffn[...], self.weight_b(slice(None), lanes))
        self.x_next[:, lanes] = self.after[:, lanes] + (value + self.shift(6)[:, lanes])


    def store_sums_d(self, at, sums):
        row = self.layer * 10 + at
        self.grad_d[row : row + 1, :] = jnp.sum(sums, 0, keepdims=True)

    def store_sums_f(self, at, sums):
        row = self.layer * 3 + at
        self.grad_f[row : row + 1, :] = jnp.sum(sums, 0, keepdims=True)

    def backward_start(self):
        self.low[...] = self.back[...].astype(BF)
        self.store_sums_d(9, wide(self.low[...]))

    def grad_down(self, rows, lanes):
        return mm_tn(self.sub_ffn[:, rows], self.low[:, lanes])

    def grad_up(self, part):
        width = self.x.shape[1]
        return mm_tn(self.normed_ffn[...], self.d_hidden[:, part * width : (part + 1) * width])

    def grad_out(self):
        return mm_tn(self.sub[...], self.low[...])

    def grad_qkv(self, part):
        return mm_tn(self.normed[...], self.d_qkv[part])

    def backward_down(self):
        width = self.x.shape[1]
        for part in range(self.hidden.shape[1] // width):
            lanes = slice(part * width, (part + 1) * width)
            self.wide_back[:, lanes] = mm_nt(self.low[...], self.weight_b(lanes, slice(None)))

    def backward_gelu(self):
        self.sums_f[...] = jnp.zeros_like(self.sums_f)

        @pl.loop(0, self.x.shape[0] // 16)
        def _(at):
            rows = pl.ds(pl.multiple_of(at * 16, 16), 16)
            values = self.hidden[rows, :]
            square, curve = gelu_parts(values)
            unit, scale = normal(0.5 * values * (1.0 + curve))
            back = self.wide_back[rows, :]
            self.sums_f[0] += fold(back * unit)
            self.sums_f[1] += fold(back)
            inner = back * self.gain_f(0)
            d_gelu = scale * (inner - mean_of(inner) - unit * mean_of(inner * unit))
            slope = 0.5 * (1.0 + curve) + 0.5 * values * (1.0 - curve * curve) * (
                ROOT * (1.0 + 3.0 * CUBE * square)
            )
            low = (d_gelu * slope).astype(BF)
            self.d_hidden[rows, :] = low
            self.sums_f[2] += fold(wide(low))

        self.store_sums_f(0, self.sums_f[0])
        self.store_sums_f(2, self.sums_f[1])
        self.store_sums_f(1, self.sums_f[2])

    def backward_up(self):
        width = self.x.shape[1]
        total = None
        for part in range(self.hidden.shape[1] // width):
            lanes = slice(part * width, (part + 1) * width)
            value = mm_nt(self.d_hidden[:, lanes], self.weight_a(4 + part))
            if part == 0:
                self.incoming[...] = value
            else:
                self.incoming[...] += value

        def emit(rows, value):
            value = self.back[rows, :] + value
            self.back[rows, :] = value
            self.low[rows, :] = value.astype(BF)

        norm_rows_back(self.after, self.gain(2), self.incoming, emit, self.sums_d)
        self.store_sums_d(2, self.sums_d[0])
        self.store_sums_d(5, self.sums_d[1])

    def backward_out(self):
        self.store_sums_d(8, wide(self.low[...]))
        self.incoming[...] = mm_nt(self.low[...], self.weight_a(3))

        def emit(rows, value):
            self.low[rows, :] = value.astype(BF)

        norm_rows_back(self.context, self.gain(1), self.incoming, emit, self.sums_d)
        self.store_sums_d(1, self.sums_d[0])
        self.store_sums_d(4, self.sums_d[1])

    def backward_attention(self):
        @pl.loop(0, self.heads // 2)
        def _(pair):
            lanes = pl.ds(pl.multiple_of(pair * 128, 128), 128)
            queries, keys, values = [self.qkv[part, :, lanes] for part in range(3)]
            d_context = self.low[:, lanes]
            found = [None] * 3
            for side in range(2):
                half = self.lane_half(d_context, side)
                prob = self.prob[2 * pair + side]
                d_prob = mm_nt(jnp.where(half, d_context, jnp.zeros_like(d_context)), values)
                dot = jnp.sum(prob * d_prob, -1, keepdims=True)
                d_scores = (prob * (d_prob - dot)).astype(BF)
                new = (
                    mm(d_scores, keys) * HEAD_DIM**-0.5,
                    mm_tn(d_scores, queries) * HEAD_DIM**-0.5,
                    mm_tn(prob.astype(BF), d_context),
                )
                found = [n if side == 0 else jnp.where(half, n, f) for n, f in zip(new, found)]
            for part in range(3):
                self.d_qkv[part, :, lanes] = found[part].astype(BF)

    def backward_qkv(self):
        self.store_sums_d(6, wide(self.d_qkv[0]))
        self.store_sums_d(7, wide(self.d_qkv[2]))
        for part in range(3):
            value = mm_nt(self.d_qkv[part], self.weight_a(part))
            if part == 0:
                self.incoming[...] = value
            else:
                self.incoming[...] += value

        def emit(rows, value):
            self.back[rows, :] = self.back[rows, :] + value

        norm_rows_back(self.x, self.gain(0), self.incoming, emit, self.sums_d)
        self.store_sums_d(0, self.sums_d[0])
        self.store_sums_d(3, self.sums_d[1])


def saved_shapes(rows, width, wide_width, heads):
    return {
        "normed": ((rows, width), BF),
        "qkv": ((3, rows, width), BF),
        "prob": ((heads, rows, rows), F32),
        "context": ((rows, width), F32),
        "sub": ((rows, width), BF),
        "after": ((rows, width), F32),
        "normed_ffn": ((rows, width), BF),
        "hidden": ((rows, wide_width), F32),
        "sub_ffn": ((rows, wide_width), BF),
    }


def work_shapes(rows, width, wide_width):
    return {
        "low": ((rows, width), BF),
        "incoming": ((rows, width), F32),
        "wide_back": ((rows, wide_width), F32),
        "d_qkv": ((3, rows, width), BF),
        "sums_d": ((2, 8, width), F32),
        "sums_f": ((3, 8, wide_width), F32),
    }


def spread_tables(geo):
    tables = []
    for width, real in ((geo.width, geo.rows_a), (geo.wide_width, geo.rows_b)):
        at = np.arange(width)
        owner = (at[None, :] // real == np.arange(geo.owners)[:, None]).astype(np.float32)
        tables += [jnp.asarray(owner, BF), jnp.asarray(at[None, :] % real, jnp.int32)]
    return tables


def unpack_vectors(geo, whole_v, wide_v, tables, vec_d, vec_f):
    owner_d, rest_d, owner_f, rest_f = tables
    lines = geo.kind["v"][1]
    wide_v[...] = wide(whole_v[0])
    line_of = lambda at: wide_v[pl.ds(at, geo.owners, stride=lines), :].astype(BF)
    pick_d = lax.broadcasted_iota(jnp.int32, (geo.slot, geo.width), 0) == rest_d[...]
    for line in range(geo.lines_d):
        spread = mm_tn(line_of(line), owner_d[...])
        for at in range(geo.per_row):
            part = spread[at * geo.slot : (at + 1) * geo.slot]
            row = line * geo.per_row + at
            if row < geo.layers * 10:
                vec_d[row : row + 1, :] = jnp.sum(jnp.where(pick_d, part, 0.0), 0, keepdims=True)
    pick_f = lax.broadcasted_iota(jnp.int32, (128, geo.width), 0)
    for row in range(geo.layers * 3):
        line = line_of(geo.lines_d + row)
        for first in range(0, geo.wide_width, geo.width):
            lanes = slice(first, first + geo.width)
            spread = jnp.where(pick_f == rest_f[:, lanes], mm_tn(line, owner_f[:, lanes]), 0.0)
            vec_f[row : row + 1, lanes] = jnp.sum(spread, 0, keepdims=True)


KINDS = ("a", "b", "v")
GATHER_SEMS = ("lz", "lo", "zs", "zr", "xs", "xr", "ys", "yr", "ds", "dr", "cs", "cr")


def forward_kernel(geo, names_perm, saved_names, *refs):
    refs = list(refs)
    take = lambda number: [refs.pop(0) for _ in range(number)]
    sources = dict(zip(KINDS, take(3)))
    perms = dict(zip(names_perm, take(len(names_perm))))
    act_ref, mask_ref = take(2)
    tables = take(4)
    out_ref, vec_d, vec_f, kept_a, kept_b, kept_x = take(6)
    kept = [dict(zip(saved_names, take(len(saved_names)))) for _ in range(geo.layers)]
    wholes = dict(zip(KINDS, take(3)))
    bufs = dict(zip(KINDS, take(3)))
    units = dict(zip(names_perm, take(len(names_perm))))
    saved = [dict(zip(saved_names, take(len(saved_names)))) for _ in range(geo.layers)]
    xs, wide_v, keep_sem = take(3)
    sems = dict(zip(GATHER_SEMS, take(len(GATHER_SEMS))))
    place = Place(geo)
    chunks = [("v", 0, 0, 0)] + chunk_list(geo, range(geo.layers))
    moves = [
        Gather(place, at, chunk, sources, bufs, units, perms, wholes, sems)
        for at, chunk in enumerate(chunks)
    ]
    keeps = []

    def keep(src, dst):
        copy = pltpu.make_async_copy(src, dst, keep_sem.at[len(keeps)])
        copy.start()
        keeps.append(copy)

    net = []
    for layer in range(geo.layers):
        fields = dict(saved[layer], x=xs.at[layer], x_next=xs.at[layer + 1], mask=mask_ref)
        read_a = lambda at, layer=layer: wholes["a"][layer * geo.blocks + at]
        read_b = lambda rows, lanes, layer=layer: wholes["b"][layer, rows, lanes]
        net.append(Layer(fields, read_a, read_b, vec_d, vec_f, layer, geo.width // HEAD_DIM))

    def compute(number):
        name, at, lead, half = chunks[number]
        moves[number].arrive()
        if name == "v":
            unpack_vectors(geo, wholes["v"], wide_v, tables, vec_d, vec_f)
            return
        k, _, _, lanes = geo.kind[name]
        layer = at // (geo.pairs if name == "a" else geo.halves)
        one = net[layer]
        save = lambda *found: [keep(saved[layer][field], kept[layer][field]) for field in found]
        if name == "a":
            keep(wholes["a"].at[pl.ds(lead, k)], kept_a.at[pl.ds(lead, k)])
            pair = at % geo.pairs
            if pair == 0:
                one.forward_norm()
                one.forward_qkv(0)
                one.forward_qkv(1)
            elif pair == 1:
                one.forward_qkv(2)
                save("normed", "qkv")
                one.forward_attention()
                one.forward_out()
                save("prob", "context", "sub", "after", "normed_ffn")
            else:
                one.forward_up(2 * pair - 4)
                one.forward_up(2 * pair - 3)
                if pair == geo.pairs - 1:
                    one.forward_gelu()
                    save("hidden", "sub_ffn")
        else:
            where = pl.ds(half * lanes, lanes)
            keep(wholes["b"].at[lead, :, where], kept_b.at[lead, :, where])
            one.forward_down(half, geo.halves)
            if half == geo.halves - 1 and layer < geo.layers - 1:
                keep(xs.at[layer + 1], kept_x.at[layer + 1])

    xs[0] = wide(act_ref[...])
    keep(xs.at[0], kept_x.at[0])
    place.greet()
    run_pipeline(
        [
            (-2, lambda c: moves[c].start_z()),
            (0, lambda c: moves[c].own()),
            (1, lambda c: moves[c].forward()),
            (2, lambda c: moves[c].corner()),
            (3, compute),
        ],
        len(moves),
    )
    out_ref[...] = xs[geo.layers].astype(BF)
    for move in moves:
        move.drain()
    for copy in keeps:
        copy.wait()


def run_forward(geo, source_a, source_b, source_v, act, mask):
    names_perm = [name for name in KINDS if geo.permuted(name)]
    perms = [jnp.asarray(geo.permutation(name), BF) for name in names_perm]
    rows, width = act.shape
    total = sum(geo.number.values())
    heads = width // HEAD_DIM
    saved = saved_shapes(rows, width, geo.wide_width, heads)
    bufs, units, wholes = [], [], []
    for name in KINDS:
        k, sent, unit, lanes = geo.kind[name]
        bufs.append(pltpu.VMEM((geo.number[name], geo.n_z * sent, lanes), BF))
        if name in names_perm:
            units.append(pltpu.VMEM((geo.number[name], k, unit, lanes), BF))
        lead, _, _, _, _, whole_lanes = geo.whole_shape(name)
        wholes.append(((lead, geo.n_dp * unit, whole_lanes), BF))
    n_y, n_z = geo.n_y, geo.n_z
    n_keeps = geo.layers * (len(saved) + geo.pairs + geo.halves + 1)
    vec_rows = geo.layers * 10
    outs = [
        jax.ShapeDtypeStruct((rows, width), BF),
        jax.ShapeDtypeStruct((vec_rows, width), F32),
        jax.ShapeDtypeStruct((geo.layers * 3, geo.wide_width), F32),
        jax.ShapeDtypeStruct(*wholes[0]),
        jax.ShapeDtypeStruct(*wholes[1]),
        jax.ShapeDtypeStruct((geo.layers, rows, width), F32),
    ] + [jax.ShapeDtypeStruct(*saved[name]) for _ in range(geo.layers) for name in saved]
    found = pl.pallas_call(
        functools.partial(forward_kernel, geo, names_perm, list(saved)),
        out_shape=outs,
        in_specs=[IN_VMEM] * (3 + len(perms) + 6),
        out_specs=[IN_VMEM] * 3 + [ANY] * (len(outs) - 3),
        scratch_shapes=[pltpu.VMEM(*whole) for whole in wholes]
        + bufs
        + units
        + [pltpu.VMEM(*saved[name]) for _ in range(geo.layers) for name in saved]
        + [
            pltpu.VMEM((geo.layers + 1, rows, width), F32),
            pltpu.VMEM(wholes[2][0][1:], F32),
            dma(n_keeps),
            dma(total),
            dma(total),
            dma(total, n_z),
            dma(total, n_z),
            dma(total),
            dma(total),
            dma(total, n_y),
            dma(total, n_y),
            dma(total, n_y),
            dma(total, n_y),
            dma(total, 2 * n_y),
            dma(total, 2 * n_y),
        ],
        compiler_params=pltpu.CompilerParams(
            collective_id=0, has_side_effects=True, vmem_limit_bytes=60 * 2**20
        ),
    )(source_a, source_b, source_v, *perms, act, mask, *spread_tables(geo))
    names = list(saved)
    kept = [dict(zip(names, found[6 + layer * len(names) :])) for layer in range(geo.layers)]
    return found[:6], kept


def pack_gradients(geo, grad_d, grad_f, tables, wide_v, stage_v):
    owner_d, rest_d, owner_f, rest_f = tables
    lines = geo.kind["v"][1]
    wide_v[...] = jnp.zeros_like(wide_v)
    pick_d = lax.broadcasted_iota(jnp.int32, (geo.slot, geo.width), 0) == rest_d[...]
    for line in range(geo.lines_d):
        parts = []
        for at in range(geo.per_row):
            row = line * geo.per_row + at
            if row < geo.layers * 10:
                parts.append(jnp.where(pick_d, grad_d[row : row + 1, :], 0.0))
            else:
                parts.append(jnp.zeros(pick_d.shape, F32))
        wide_v[pl.ds(line, geo.owners, stride=lines), :] = mm_nt(
            owner_d[...], jnp.concatenate(parts, 0).astype(BF)
        )
    pick_f = lax.broadcasted_iota(jnp.int32, (128, geo.width), 0)
    for row in range(geo.layers * 3):
        total = None
        for first in range(0, geo.wide_width, geo.width):
            lanes = slice(first, first + geo.width)
            part = jnp.where(pick_f == rest_f[:, lanes], grad_f[row : row + 1, lanes], 0.0).astype(BF)
            part = mm_nt(owner_f[:, lanes], part)
            total = part if total is None else total + part
        wide_v[pl.ds(geo.lines_d + row, geo.owners, stride=lines), :] = total
    stage_v[...] = wide_v[...].astype(BF).reshape(stage_v.shape)


class Ring:
    def __init__(self, sources, slots, sems):
        self.slots, self.size, self.used = slots, slots.shape[0], 0
        self.copies = [
            pltpu.make_async_copy(source, slots.at[at % self.size], sems.at[at % self.size])
            for at, source in enumerate(sources)
        ]
        for copy in self.copies[: self.size]:
            copy.start()

    def next(self):
        at = self.used
        self.used += 1
        if 0 < at and at - 1 + self.size < len(self.copies):
            self.copies[at - 1 + self.size].start()
        self.copies[at].wait()
        return self.slots[at % self.size]


SCATTER_SEMS = ("cs", "cr", "ms", "mr", "es", "er", "zs", "zr", "fx", "fy")
Z_SLOTS = 4
SCATTER_LAGS = (0, 1, 3, 5, 7)
RING = 3


def backward_kernel(geo, names_perm, names, *refs):
    refs = list(refs)
    take = lambda number: [refs.pop(0) for _ in range(number)]
    by_kind = lambda: dict(zip(KINDS, take(3)))
    saved_names, work_names = names
    layers, blocks, width = geo.layers, geo.blocks, geo.width
    perms = dict(zip(names_perm, take(len(names_perm))))
    cot_ref, vec_d, vec_f = take(3)
    tables = take(4)
    whole_a, whole_b, kept_x = take(3)
    kept = [dict(zip(saved_names, take(len(saved_names)))) for _ in range(layers)]
    for layer in range(layers):
        kept[layer]["x"] = kept_x.at[layer]
    back_ref, out_qkv, out_out, out_up, out_down, out_d, out_f = take(7)
    fields = dict(zip(saved_names, take(len(saved_names))))
    fields.update(zip(work_names, take(len(work_names))))
    stages, sums, mids, ends, z_send, z_recv = [by_kind() for _ in range(6)]
    x_ref, grad_d, grad_f, wide_v, slots, sem_l, sem_w = take(7)
    sems = dict(zip(SCATTER_SEMS, take(len(SCATTER_SEMS))))
    fields.update(d_hidden=fields["sub_ffn"], x=x_ref, back=back_ref, grad_d=grad_d, grad_f=grad_f)
    place = Place(geo)

    def writer(chunk):
        name, at, lead, half = chunk
        rows_a, rows_b, lines = geo.rows_a, geo.rows_b, geo.lines_d

        def put_a(value):
            layer = at // geo.pairs
            for side in range(2):
                block = 2 * (at % geo.pairs) + side
                piece = value[side * rows_a : (side + 1) * rows_a]
                if block < 3:
                    out_qkv[layer, :, block * width : (block + 1) * width] = piece
                elif block == 3:
                    out_out[layer] = piece
                else:
                    out_up[layer, :, (block - 4) * width : (block - 3) * width] = piece

        def put_b(value):
            lanes = value.shape[1]
            out_down[lead, :, half * lanes : (half + 1) * lanes] = value[:rows_b]

        def put_v(value):
            out_d[...] = value[:lines]
            out_f[...] = value[lines : lines + layers * 3]

        return {"a": put_a, "b": put_b, "v": put_v}[name]

    order, seen = [], {name: [] for name in KINDS}
    for layer in reversed(range(layers)):
        for half in range(geo.halves):
            order.append(("b", layer * geo.halves + half, layer, half))
        for pair in list(range(2, geo.pairs)) + [1, 0]:
            order.append(("a", layer * geo.pairs + pair, layer * blocks + 2 * pair, 0))
    order.append(("v", 0, 0, 0))
    moves, stage_of = [], []
    for number, chunk in enumerate(order):
        name = chunk[0]
        stage = stages[name].at[len(seen[name]) % stages[name].shape[0]]
        slots_z = z_send[name].shape[0]
        z_slot = len(seen[name]) % slots_z
        before = seen[name][-slots_z] if len(seen[name]) >= slots_z else None
        move = Scatter(
            place, number, chunk, stage, sums, mids, ends, perms, z_send, z_recv, z_slot, before,
            writer(chunk), sems,
        )
        seen[name].append(move)
        stage_of.append(stage)
        moves.append(move)
    step = [0]

    def serve():
        acts = (Scatter.start, Scatter.pair, Scatter.middle, Scatter.last, Scatter.finish)
        for lag, act in zip(SCATTER_LAGS, acts):
            if 0 <= step[0] - lag < len(moves):
                act(moves[step[0] - lag])
        step[0] += 1

    def stage_a(side, value):
        stage_of[step[0]][side] = value.astype(BF).reshape(geo.n_y, 2, 2, -1, width)

    loads = {}
    field_names = ["x"] + list(saved_names)

    def fetch(layer, *found):
        for name in found:
            loads[name] = pltpu.make_async_copy(
                kept[layer][name], fields[name], sem_l.at[field_names.index(name)]
            )
            loads[name].start()

    def ready(*found):
        for name in found:
            loads[name].wait()

    fetch(layers - 1, "sub_ffn", "hidden", "normed_ffn", "after", "sub", "context", "prob", "qkv", "normed", "x")
    sources = []
    for layer in reversed(range(layers)):
        parts = geo.wide_width // width
        sources += [whole_b.at[layer, pl.ds(part * width, width)] for part in range(parts)]
        sources += [whole_a.at[layer * blocks + at] for at in list(range(4, blocks)) + [3, 0, 1, 2]]
    ring = Ring(sources, slots, sem_w)
    cot_copy = pltpu.make_async_copy(cot_ref, back_ref, sem_l.at[len(field_names)])
    cot_copy.start()
    place.greet()
    cot_copy.wait()
    for layer in reversed(range(layers)):
        one = Layer(
            fields, lambda at: ring.next(), lambda rows, lanes: ring.next(), vec_d, vec_f, layer,
            width // HEAD_DIM,
        )
        again = (lambda *found: fetch(layer - 1, *found)) if layer > 0 else (lambda *found: None)
        one.backward_start()
        ready("sub_ffn")
        _, _, unit, lanes = geo.kind["b"]
        for half in range(geo.halves):
            for column in range(geo.n_dp // 2):
                rows = slice(column * 2 * unit, (column + 1) * 2 * unit)
                value = one.grad_down(rows, slice(half * lanes, (half + 1) * lanes))
                stage_of[step[0]][0, column // 2, column % 2] = value.astype(BF).reshape(2, unit, lanes)
            serve()
        one.backward_down()
        ready("hidden")
        one.backward_gelu()
        again("hidden")
        ready("normed_ffn")
        for pair in range(2, geo.pairs):
            stage_a(0, one.grad_up(2 * pair - 4))
            stage_a(1, one.grad_up(2 * pair - 3))
            serve()
        again("normed_ffn")
        ready("after")
        one.backward_up()
        again("after", "sub_ffn")
        ready("sub", "context")
        stage_a(1, one.grad_out())
        one.backward_out()
        again("sub", "context")
        ready("prob", "qkv")
        one.backward_attention()
        again("prob", "qkv")
        ready("normed")
        stage_a(0, one.grad_qkv(2))
        serve()
        stage_a(0, one.grad_qkv(0))
        stage_a(1, one.grad_qkv(1))
        serve()
        again("normed")
        ready("x")
        one.backward_qkv()
        again("x")
    pack_gradients(geo, grad_d, grad_f, tables, wide_v, stage_of[step[0]])
    while step[0] < len(moves) + SCATTER_LAGS[-1]:
        serve()
    for move in moves:
        move.drain()


def run_backward(geo, cot, vec_d, vec_f, whole_a, whole_b, kept_x, kept):
    rows, width = cot.shape
    layers, n_y, n_z = geo.layers, geo.n_y, geo.n_z
    heads = width // HEAD_DIM
    saved, work = saved_shapes(rows, width, geo.wide_width, heads), work_shapes(rows, width, geo.wide_width)
    names = (list(saved), list(work))
    names_perm = [name for name in KINDS if geo.permuted(name)]
    perms = [jnp.asarray(geo.permutation(name).T, BF) for name in names_perm]
    total = sum(geo.number.values())
    groups = [[] for _ in range(6)]
    for name in KINDS:
        k, sent, unit, lanes = geo.kind[name]
        number = geo.number[name]
        mid_steps = max(n_y - 1, (n_y + 1) // 2)
        groups[0].append(pltpu.VMEM((min(number, 2), k, n_y, 2, 2, unit, lanes), BF))
        groups[1].append(pltpu.VMEM((number, k, n_y, 2, unit, lanes), BF))
        landing = number if name == "v" else number // layers
        groups[2].append(pltpu.VMEM((landing, mid_steps, k, 2, unit, lanes), BF))
        groups[3].append(pltpu.VMEM((number, mid_steps, k, unit, lanes), BF))
        groups[4].append(pltpu.VMEM((min(number, Z_SLOTS), n_z, sent, lanes), BF))
        groups[5].append(pltpu.VMEM((number, n_z, sent, lanes), BF))
    scratch = [pltpu.VMEM(*saved[name]) for name in saved] + [pltpu.VMEM(*work[name]) for name in work]
    scratch += sum(groups, [])
    scratch += [
        pltpu.VMEM((rows, width), F32),
        pltpu.VMEM((layers * 10, width), F32),
        pltpu.VMEM((layers * 3, geo.wide_width), F32),
        pltpu.VMEM((geo.owners * geo.kind["v"][1], 128), F32),
        pltpu.VMEM((RING, width, width), BF),
        dma(2 + len(saved)),
        dma(RING),
        dma(total),
        dma(total),
        dma(total, n_y),
        dma(total, n_y),
        dma(total, n_y),
        dma(total, n_y),
        dma(total, n_z),
        dma(total, n_z),
        pltpu.SemaphoreType.REGULAR,
        pltpu.SemaphoreType.REGULAR((n_y,)),
    ]
    return pl.pallas_call(
        functools.partial(backward_kernel, geo, names_perm, names),
        out_shape=[
            jax.ShapeDtypeStruct((rows, width), F32),
            jax.ShapeDtypeStruct((layers, geo.rows_a, 3 * width), F32),
            jax.ShapeDtypeStruct((layers, geo.rows_a, width), F32),
            jax.ShapeDtypeStruct((layers, geo.rows_a, geo.wide_width), F32),
            jax.ShapeDtypeStruct((layers, geo.rows_b, width), F32),
            jax.ShapeDtypeStruct((geo.lines_d, 128), F32),
            jax.ShapeDtypeStruct((layers * 3, 128), F32),
        ],
        in_specs=[IN_VMEM] * len(perms) + [ANY] + [IN_VMEM] * 6 + [ANY] * (3 + layers * len(saved)),
        out_specs=[IN_VMEM] * 7,
        scratch_shapes=scratch,
        compiler_params=pltpu.CompilerParams(
            collective_id=1, has_side_effects=True, vmem_limit_bytes=63 * 2**20
        ),
    )(
        *perms, cot, vec_d, vec_f, *spread_tables(geo), whole_a, whole_b, kept_x,
        *[kept[layer][name] for layer in range(layers) for name in saved],
    )


def pack_rows(blocks, rows):
    joined = jnp.concatenate(blocks, 0)
    return jnp.pad(joined, ((0, rows - joined.shape[0]), (0, 0)))


def pack_vectors(geo, vec_d, vec_f):
    filled = jnp.pad(vec_d, ((0, geo.lines_d * geo.per_row - vec_d.shape[0]), (0, geo.slot - vec_d.shape[1])))
    lines = jnp.concatenate(
        [filled.reshape(geo.lines_d, 128), jnp.pad(vec_f, ((0, 0), (0, 128 - vec_f.shape[1])))]
    )
    return pack_rows([lines], geo.kind["v"][1])


def unpack_lines(geo, lines_d, lines_f):
    rows_d = lines_d.reshape(-1, geo.slot)[: geo.layers * 10, : geo.rows_a]
    rows_f = lines_f[:, : geo.rows_b]
    return rows_d.reshape(geo.layers, 10, -1), rows_f.reshape(geo.layers, 3, -1)


def on_device(
    act_short,
    act_long,
    len_short,
    len_long,
    w_qkv,
    w_out,
    w_up,
    w_down,
    gains_d,
    shifts_d,
    gains_ff,
    shifts_ff,
    cot_short,
    cot_long,
):
    n_dp, n_z = lax.axis_size("dp"), lax.axis_size("fsdp")
    geo = Geometry(n_dp, n_z, w_qkv.shape, w_up.shape, w_down.shape)
    width = geo.width
    cut = lambda array, at: array[:, at * width : (at + 1) * width]
    source_a, source_b = [], []
    for layer in range(geo.layers):
        blocks = [cut(w_qkv[layer], at) for at in range(3)] + [w_out[layer]]
        blocks += [cut(w_up[layer], at) for at in range(geo.blocks - 4)]
        for pair in range(geo.pairs):
            source_a.append(pack_rows(blocks[2 * pair : 2 * pair + 2], geo.kind["a"][1]))
        for half in range(geo.halves):
            lanes = geo.kind["b"][3]
            piece = w_down[layer][:, half * lanes : (half + 1) * lanes]
            source_b.append(pack_rows([piece], geo.kind["b"][1]))
    vec_d = jnp.concatenate([gains_d, shifts_d], 1).reshape(-1, geo.rows_a)
    vec_f = jnp.concatenate([gains_ff[:, None], shifts_ff], 1).reshape(-1, geo.rows_b)
    source_v = pack_vectors(geo, vec_d, vec_f)[None]
    rows_short, rows_long = act_short.shape[0], act_long.shape[0]
    rows = rows_short + rows_long
    at = np.arange(rows)
    bucket = (at >= rows_short).astype(np.int32)
    place = at - rows_short * bucket
    length = jnp.where(bucket == 0, len_short[0], len_long[0])
    valid = place < length
    mask = ((bucket[:, None] == bucket[None, :]) & valid[None, :]).astype(F32)
    cot = jnp.concatenate([cot_short, cot_long]).astype(F32) * valid.astype(F32)[:, None]
    act = jnp.concatenate([act_short, act_long])
    found, kept = run_forward(geo, jnp.stack(source_a), jnp.stack(source_b), source_v, act, mask)
    out, vec_d, vec_f, whole_a, whole_b, kept_x = found
    back, grad_qkv, grad_out, grad_up, grad_down, lines_d, lines_f = run_backward(
        geo, cot, vec_d, vec_f, whole_a, whole_b, kept_x, kept
    )
    own_d, own_f = unpack_lines(geo, lines_d, lines_f)
    return (
        out[:rows_short],
        out[rows_short:],
        back[:rows_short],
        back[rows_short:],
        grad_qkv,
        grad_out,
        grad_up,
        grad_down,
        own_d[:, :3],
        own_d[:, 3:],
        own_f[:, 0],
        own_f[:, 1:],
    )


def solution(mesh):
    return jax.shard_map(
        on_device,
        mesh=mesh,
        in_specs=(
            P(("dp", "fsdp"), None),
            P(("dp", "fsdp"), None),
            P(("dp", "fsdp")),
            P(("dp", "fsdp")),
            P(None, ("dp", "fsdp"), None),
            P(None, ("dp", "fsdp"), None),
            P(None, ("dp", "fsdp"), None),
            P(None, ("dp", "fsdp"), None),
            P(None, None, ("dp", "fsdp")),
            P(None, None, ("dp", "fsdp")),
            P(None, ("dp", "fsdp")),
            P(None, None, ("dp", "fsdp")),
            P(("dp", "fsdp"), None),
            P(("dp", "fsdp"), None),
        ),
        out_specs=(
            P(("dp", "fsdp"), None),
            P(("dp", "fsdp"), None),
            P(("dp", "fsdp"), None),
            P(("dp", "fsdp"), None),
            P(None, ("dp", "fsdp"), None),
            P(None, ("dp", "fsdp"), None),
            P(None, ("dp", "fsdp"), None),
            P(None, ("dp", "fsdp"), None),
            P(None, None, ("dp", "fsdp")),
            P(None, None, ("dp", "fsdp")),
            P(None, ("dp", "fsdp")),
            P(None, None, ("dp", "fsdp")),
        ),
        check_vma=False,
    )
```

```python
import functools

import jax
import jax.numpy as jnp
import numpy as np
from jax import lax
from jax.experimental import pallas as pl
from jax.experimental.pallas import tpu as pltpu
from jax.sharding import PartitionSpec as P

HEAD_DIM = 64

epsilon = 1e-05


BF = jnp.bfloat16
F32 = jnp.float32
MESH = pl.DeviceIdType.MESH


def round16(count):
    return (count + 15) // 16 * 16


class Geometry:
    def __init__(self, n_dp, n_z, w_qkv, w_up, w_down):
        self.n_dp, self.n_z, self.n_y = n_dp, n_z, n_dp // 4
        self.layers = w_qkv[0]
        self.width = w_qkv[2] // 3
        self.rows_a, self.rows_b = w_qkv[1], w_down[1]
        self.blocks = 4 + w_up[2] // self.width
        self.pairs = self.blocks // 2
        self.halves = 2
        self.owners = n_dp * n_z
        self.wide_width = w_up[2]
        self.slot = 8
        while self.slot < self.rows_a:
            self.slot *= 2
        self.per_row = 128 // self.slot
        self.lines_d = -(-self.layers * 10 // self.per_row)
        lines = round16(self.lines_d + self.layers * 3)
        self.kind = {
            "a": (2, round16(2 * self.rows_a), self.rows_a * n_z, self.width),
            "b": (1, round16(self.rows_b), self.rows_b * n_z, self.width // 2),
            "v": (1, lines, lines * n_z, 128),
        }
        self.real = {"a": self.rows_a, "b": self.rows_b, "v": self.kind["v"][1]}
        self.number = {"a": self.layers * self.pairs, "b": self.layers * self.halves, "v": 1}

    def permuted(self, name):
        k, sent, unit, _ = self.kind[name]
        return k * unit != sent * self.n_z or k > 1

    def permutation(self, name):
        k, sent, unit, _ = self.kind[name]
        real = self.real[name]
        table = np.zeros((k * unit, self.n_z * sent), np.float32)
        for block in range(k):
            for z in range(self.n_z):
                for row in range(real):
                    table[block * unit + z * real + row, z * sent + block * real + row] = 1
        return table

    def whole_shape(self, name):
        _, _, unit, lanes = self.kind[name]
        lead = {"a": self.layers * self.blocks, "b": self.layers, "v": 1}[name]
        lanes = self.width if name == "b" else lanes
        return (lead, self.n_y, 2, 2, unit, lanes)


class Place:
    def __init__(self, geo):
        self.geo = geo
        self.d, self.z = lax.axis_index("dp"), lax.axis_index("fsdp")
        self.core = lax.rem(self.d, 2)
        self.x = lax.rem(self.d // 2, 2)
        self.y = self.d // 4

    def y_off(self, step):
        return lax.rem(self.y + step + self.geo.n_y, self.geo.n_y)

    def z_off(self, step):
        return lax.rem(self.z + step + self.geo.n_z, self.geo.n_z)

    def dev_core(self):
        return (self.d + 1 - 2 * self.core, self.z)

    def dev_x(self):
        return (self.d + 2 - 4 * self.x, self.z)

    def dev_y(self, step):
        return (self.y_off(step) * 4 + self.x * 2 + self.core, self.z)

    def dev_z(self, step):
        return (self.d, self.z_off(step))

    def greet(self):
        barrier = pltpu.get_barrier_semaphore()
        partners = [self.dev_core(), self.dev_x()]
        partners += [self.dev_y(step) for step in range(1, self.geo.n_y)]
        partners += [self.dev_z(step) for step in range(1, self.geo.n_z)]
        for partner in partners:
            pl.semaphore_signal(barrier, inc=1, device_id=partner, device_id_type=MESH)
        pl.semaphore_wait(barrier, len(partners))


def remote(src, dst, send, recv, device):
    return pltpu.make_async_remote_copy(
        src_ref=src, dst_ref=dst, send_sem=send, recv_sem=recv, device_id=device, device_id_type=MESH
    )


def chunk_list(geo, layers):
    found = []
    for layer in layers:
        for pair in range(geo.pairs):
            found.append(("a", layer * geo.pairs + pair, layer * geo.blocks + 2 * pair, 0))
        for half in range(geo.halves):
            found.append(("b", layer * geo.halves + half, layer, half))
    return found


def rows_of(whole, name, lead, half, k, unit, lanes):
    def at(y, x, core):
        rows = pl.ds(pl.multiple_of((y * 4 + x * 2 + core) * unit, 16), unit)
        return whole.at[pl.ds(lead, k), rows, pl.ds(half * lanes, lanes) if name == "b" else slice(None)]

    return at


class Gather:
    def __init__(self, place, number, chunk, sources, bufs, units, perms, wholes, sems):
        self.p, self.c = place, number
        name, at, lead, half = chunk
        self.half_a = number % 2 == 0
        k, self.sent, unit, lanes = place.geo.kind[name]
        self.source = sources[name].at[at]
        self.buf = bufs[name].at[at]
        self.perm = perms.get(name)
        self.unit_buf = units[name].at[at] if self.perm is not None else None
        self.unit = self.unit_buf if self.perm is not None else bufs[name].at[pl.ds(at, 1)]
        self.to = rows_of(wholes[name], name, lead, half, k, unit, lanes)
        self.sems = sems
        self.pending = []

    def slot(self, z):
        return self.buf.at[pl.ds(pl.multiple_of(z * self.sent, 16), self.sent)]

    def send(self, src, dst, send, recv, device):
        copy = remote(src, dst, send, recv, device)
        copy.start()
        self.pending.append(copy)

    def arrived(self, dst, send, recv, device):
        remote(dst, dst, send, recv, device).wait_recv()

    def start_z(self):
        p, s, c = self.p, self.sems, self.c
        self.local_z = pltpu.make_async_copy(self.source, self.slot(p.z), s["lz"].at[c])
        self.local_z.start()
        for step in range(1, p.geo.n_z):
            self.send(self.source, self.slot(p.z), s["zs"].at[c, step], s["zr"].at[c, step], p.dev_z(step))

    def own(self):
        p, s, c = self.p, self.sems, self.c
        self.local_z.wait()
        for step in range(1, p.geo.n_z):
            self.arrived(self.slot(p.z_off(-step)), s["zs"].at[c, step], s["zr"].at[c, step], p.dev_z(step))
        if self.perm is not None:
            k, unit, lanes = self.unit_buf.shape
            mixed = jnp.dot(self.perm[...], self.buf[...], preferred_element_type=F32)
            self.unit_buf[...] = mixed.astype(BF).reshape(k, unit, lanes)
        here = self.to(p.y, p.x, p.core)
        self.local = pltpu.make_async_copy(self.unit, here, s["lo"].at[c])
        self.send(self.unit, here, s["xs"].at[c], s["xr"].at[c], p.dev_x())
        for step in range(1, p.geo.n_y):
            self.send(self.unit, here, s["ys"].at[c, step], s["yr"].at[c, step], p.dev_y(step))
        self.send(self.unit, here, s["cs"].at[c, 0], s["cr"].at[c, 0], p.dev_core())
        self.local.start()

    def forward(self):
        p, s, c = self.p, self.sems, self.c
        n_y = p.geo.n_y
        from_x = self.to(p.y, 1 - p.x, p.core)
        self.arrived(from_x, s["xs"].at[c], s["xr"].at[c], p.dev_x())
        if self.half_a:
            for step in range(1, n_y):
                self.send(from_x, from_x, s["ds"].at[c, step], s["dr"].at[c, step], p.dev_y(step))
        self.send(from_x, from_x, s["cs"].at[c, 1], s["cr"].at[c, 1], p.dev_core())
        for step in range(1, n_y):
            from_y = self.to(p.y_off(-step), p.x, p.core)
            self.arrived(from_y, s["ys"].at[c, step], s["yr"].at[c, step], p.dev_y(step))
            if not self.half_a:
                self.send(from_y, from_y, s["ds"].at[c, step], s["dr"].at[c, step], p.dev_x())
            self.send(from_y, from_y, s["cs"].at[c, 2 * step], s["cr"].at[c, 2 * step], p.dev_core())

    def corner(self):
        p, s, c = self.p, self.sems, self.c
        for step in range(1, p.geo.n_y):
            far = self.to(p.y_off(-step), 1 - p.x, p.core)
            self.arrived(far, s["ds"].at[c, step], s["dr"].at[c, step], p.dev_x())
            self.send(far, far, s["cs"].at[c, 2 * step + 1], s["cr"].at[c, 2 * step + 1], p.dev_core())

    def arrive(self):
        p, s, c = self.p, self.sems, self.c
        for step in range(p.geo.n_y):
            for flip in range(2):
                x = p.x if flip == 0 else 1 - p.x
                got = self.to(p.y_off(-step), x, 1 - p.core)
                at = 2 * step + flip
                self.arrived(got, s["cs"].at[c, at], s["cr"].at[c, at], p.dev_core())
        self.local.wait()

    def drain(self):
        for copy in self.pending:
            copy.wait_send()


def run_pipeline(stages, count):
    last = max(lag for lag, _ in stages)
    first = min(lag for lag, _ in stages)
    for step in range(first, count + last):
        for lag, act in stages:
            if 0 <= step - lag < count:
                act(step - lag)


def dma(*shape):
    return pltpu.SemaphoreType.DMA(shape)


ANY = pl.BlockSpec(memory_space=pl.ANY)
IN_VMEM = pl.BlockSpec(memory_space=pltpu.VMEM)


def wide(values):
    return values.astype(F32)


class Scatter:
    def __init__(self, place, number, chunk, stage, sums, mids, ends, perms, z_send, z_recv, z_slot, before, put, sems):
        self.p, self.c = place, number
        name, at, lead, half = chunk
        self.half_a = number % 2 == 0
        self.k, self.sent, self.rows, self.lanes = place.geo.kind[name]
        self.stage = stage
        self.sum = sums[name].at[at]
        layer = at // (place.geo.number[name] // place.geo.layers) if name != "v" else None
        self.mid = mids[name].at[at - layer * (place.geo.number[name] // place.geo.layers) if layer is not None else 0]
        self.hands_on = layer is not None and layer > 0
        self.takes_over = layer is not None and layer < place.geo.layers - 1
        self.end = ends[name].at[at]
        self.perm = perms.get(name)
        self.z_send, self.z_recv = z_send[name].at[z_slot], z_recv[name].at[at]
        self.before, self.z_moves = before, []
        self.put = put
        self.sems = sems
        self.pending = []

    def send(self, src, dst, send, recv, device):
        copy = remote(src, dst, send, recv, device)
        copy.start()
        self.pending.append(copy)

    def arrived(self, dst, send, recv, device):
        remote(dst, dst, send, recv, device).wait_recv()

    def start(self):
        p, s, c = self.p, self.sems, self.c
        give = self.stage.at[:, :, :, 1 - p.core]
        self.given = remote(give, self.sum, s["cs"].at[c], s["cr"].at[c], p.dev_core())
        self.given.start()

    def pair(self):
        p, s, c = self.p, self.sems, self.c
        n_y = p.geo.n_y
        self.arrived(self.sum, s["cs"].at[c], s["cr"].at[c], p.dev_core())

        @pl.loop(0, self.k * n_y * 2)
        def _(at):
            where = (at // (2 * n_y), lax.rem(at // 2, n_y), lax.rem(at, 2))
            self.sum[where] = (wide(self.sum[where]) + wide(self.stage[where + (p.core,)])).astype(BF)

        self.given.wait_send()
        if self.takes_over and self.half_a:
            for step in range(1, n_y):
                pl.semaphore_wait(s["fy"].at[step], 1)
        if self.takes_over and not self.half_a:
            pl.semaphore_wait(s["fx"], 1)
        if self.half_a:
            for step in range(1, n_y):
                self.send(
                    self.sum.at[:, p.y_off(step)], self.mid.at[step - 1],
                    s["ms"].at[c, step], s["mr"].at[c, step], p.dev_y(step),
                )
        else:
            for y in range(n_y):
                self.send(
                    self.sum.at[:, y, 1 - p.x], self.mid.at[y // 2, :, y % 2],
                    s["ms"].at[c, y], s["mr"].at[c, y], p.dev_x(),
                )

    def middle(self):
        p, s, c = self.p, self.sems, self.c
        n_y = p.geo.n_y
        if self.half_a:
            for step in range(1, n_y):
                self.arrived(self.mid.at[step - 1], s["ms"].at[c, step], s["mr"].at[c, step], p.dev_y(step))

            @pl.loop(0, self.k * 2)
            def _(at):
                where = (at // 2, p.y, lax.rem(at, 2))
                value = wide(self.sum[where])
                for step in range(1, n_y):
                    value = value + wide(self.mid[step - 1, at // 2, lax.rem(at, 2)])
                self.sum[where] = value.astype(BF)

            if self.hands_on:
                for step in range(1, n_y):
                    pl.semaphore_signal(
                        s["fy"].at[step], inc=1, device_id=p.dev_y(-step), device_id_type=MESH
                    )
            self.send(
                self.sum.at[:, p.y, 1 - p.x], self.end.at[0], s["es"].at[c, 0], s["er"].at[c, 0], p.dev_x()
            )
        else:
            for y in range(n_y):
                self.arrived(self.mid.at[y // 2, :, y % 2], s["ms"].at[c, y], s["mr"].at[c, y], p.dev_x())

            @pl.loop(0, self.k * n_y)
            def _(at):
                y = lax.rem(at, n_y)
                where = (at // n_y, y, p.x)
                value = wide(self.sum[where]) + wide(self.mid[y // 2, at // n_y, lax.rem(y, 2)])
                self.sum[where] = value.astype(BF)

            if self.hands_on:
                pl.semaphore_signal(s["fx"], inc=1, device_id=p.dev_x(), device_id_type=MESH)

            for step in range(1, n_y):
                self.send(
                    self.sum.at[:, p.y_off(step), p.x], self.end.at[step - 1],
                    s["es"].at[c, step], s["er"].at[c, step], p.dev_y(step),
                )

    def last(self):
        p, s, c = self.p, self.sems, self.c
        n_y, n_z = p.geo.n_y, p.geo.n_z
        if self.half_a:
            arrivals = [(0, self.end.at[0], p.dev_x())]
        else:
            arrivals = [(step, self.end.at[step - 1], p.dev_y(step)) for step in range(1, n_y)]
        value = wide(self.sum[:, p.y, p.x])
        for at, got, device in arrivals:
            self.arrived(got, s["es"].at[c, at], s["er"].at[c, at], device)
            value = value + wide(got[...])
        value = value.astype(BF).reshape(self.k * self.rows, self.lanes)
        if self.perm is not None:
            value = jnp.dot(self.perm[...], value, preferred_element_type=F32).astype(BF)
        if self.before is not None:
            self.before.left()
        self.z_send[...] = value.reshape(n_z, self.sent, self.lanes)
        for step in range(1, n_z):
            copy = remote(
                self.z_send.at[p.z_off(step)], self.z_recv.at[step],
                s["zs"].at[c, step], s["zr"].at[c, step], p.dev_z(step),
            )
            copy.start()
            self.z_moves.append(copy)

    def finish(self):
        p, s, c = self.p, self.sems, self.c
        value = wide(self.z_send[p.z])
        for step in range(1, p.geo.n_z):
            self.arrived(self.z_recv.at[step], s["zs"].at[c, step], s["zr"].at[c, step], p.dev_z(step))
            value = value + wide(self.z_recv[step])
        self.put(value)

    def left(self):
        while self.z_moves:
            self.z_moves.pop().wait_send()

    def drain(self):
        self.left()
        for copy in self.pending:
            copy.wait_send()


def mm(left, right):
    return jnp.dot(left, right, preferred_element_type=F32)


def mm_nt(left, right):
    return lax.dot_general(left, right, (((1,), (1,)), ((), ())), preferred_element_type=F32)


def mm_tn(left, right):
    return lax.dot_general(left, right, (((0,), (0,)), ((), ())), preferred_element_type=F32)


def mean_of(values):
    return jnp.sum(values, -1, keepdims=True) * (1.0 / values.shape[-1])


def normal(values):
    centered = values - mean_of(values)
    scale = lax.rsqrt(mean_of(centered * centered) + epsilon)
    return centered * scale, scale


def norm_rows(source, gain, shift, target, block=32):
    @pl.loop(0, source.shape[0] // block)
    def _(at):
        rows = pl.ds(pl.multiple_of(at * block, block), block)
        unit, _ = normal(source[rows, :])
        target[rows, :] = (unit * gain + shift).astype(target.dtype)


def fold(values):
    total = values[0:8]
    for at in range(8, values.shape[0], 8):
        total = total + values[at : at + 8]
    return total


def norm_rows_back(source, gain, incoming, emit, sums, block=32):
    sums[...] = jnp.zeros_like(sums)

    @pl.loop(0, source.shape[0] // block)
    def _(at):
        rows = pl.ds(pl.multiple_of(at * block, block), block)
        unit, scale = normal(source[rows, :])
        back = incoming[rows, :]
        sums[0] += fold(back * unit)
        sums[1] += fold(back)
        inner = back * gain
        emit(rows, scale * (inner - mean_of(inner) - unit * mean_of(inner * unit)))


ROOT = 0.7978845608028654
CUBE = 0.044715


def gelu_parts(values):
    square = values * values
    curve = jnp.tanh(ROOT * (values + CUBE * (values * square)))
    return square, curve


class Layer:
    def __init__(self, refs, weight_a, weight_b, vec_d, vec_f, layer, heads):
        self.__dict__.update(refs)
        self.weight_a, self.weight_b = weight_a, weight_b
        self.vec_d, self.vec_f = vec_d, vec_f
        self.layer, self.heads = layer, heads

    def gain(self, at):
        return self.vec_d[self.layer * 10 + at : self.layer * 10 + at + 1, :]

    def shift(self, at):
        return self.gain(3 + at)

    def gain_f(self, at):
        return self.vec_f[self.layer * 3 + at : self.layer * 3 + at + 1, :]

    def lane_half(self, values, side):
        lane = lax.broadcasted_iota(jnp.int32, values.shape, 1)
        return (lane < HEAD_DIM) == (side == 0)

    def forward_norm(self):
        norm_rows(self.x, self.gain(0), self.shift(0), self.normed)

    def forward_qkv(self, part):
        value = mm(self.normed[...], self.weight_a(part))
        if part != 1:
            value = value + self.shift(3 if part == 0 else 4)
        self.qkv[part] = value.astype(BF)

    def forward_attention(self):
        valid = self.mask[...] > 0.5

        @pl.loop(0, self.heads // 2)
        def _(pair):
            lanes = pl.ds(pl.multiple_of(pair * 128, 128), 128)
            queries, keys, values = [self.qkv[part, :, lanes] for part in range(3)]
            context = None
            for side in range(2):
                half = self.lane_half(queries, side)
                scores = mm_nt(jnp.where(half, queries, jnp.zeros_like(queries)), keys)
                scores = jnp.where(valid, scores * HEAD_DIM**-0.5, -1e9)
                top = jnp.max(scores, -1, keepdims=True)
                grown = jnp.exp(scores - top)
                prob = grown / jnp.sum(grown, -1, keepdims=True)
                self.prob[2 * pair + side] = prob
                product = mm(prob.astype(BF), values)
                context = product if side == 0 else jnp.where(half, product, context)
            self.context[:, lanes] = context

    def forward_out(self):
        norm_rows(self.context, self.gain(1), self.shift(1), self.sub)
        self.after[...] = self.x[...] + (mm(self.sub[...], self.weight_a(3)) + self.shift(5))
        norm_rows(self.after, self.gain(2), self.shift(2), self.normed_ffn)

    def forward_up(self, part):
        width = self.x.shape[1]
        lanes = slice(part * width, (part + 1) * width)
        self.hidden[:, lanes] = mm(self.normed_ffn[...], self.weight_a(4 + part)) + self.gain_f(1)[:, lanes]

    def forward_gelu(self):
        @pl.loop(0, self.x.shape[0] // 16)
        def _(at):
            rows = pl.ds(pl.multiple_of(at * 16, 16), 16)
            values = self.hidden[rows, :]
            _, curve = gelu_parts(values)
            unit, _ = normal(0.5 * values * (1.0 + curve))
            self.sub_ffn[rows, :] = (unit * self.gain_f(0) + self.gain_f(2)).astype(BF)

    def forward_down(self, half, halves):
        width = self.x.shape[1] // halves
        lanes = slice(half * width, (half + 1) * width)
        value = mm(self.sub_ffn[...], self.weight_b(slice(None), lanes))
        self.x_next[:, lanes] = self.after[:, lanes] + (value + self.shift(6)[:, lanes])


    def store_sums_d(self, at, sums):
        row = self.layer * 10 + at
        self.grad_d[row : row + 1, :] = jnp.sum(sums, 0, keepdims=True)

    def store_sums_f(self, at, sums):
        row = self.layer * 3 + at
        self.grad_f[row : row + 1, :] = jnp.sum(sums, 0, keepdims=True)

    def backward_start(self):
        self.low[...] = self.back[...].astype(BF)
        self.store_sums_d(9, wide(self.low[...]))

    def grad_down(self, rows, lanes):
        return mm_tn(self.sub_ffn[:, rows], self.low[:, lanes])

    def grad_up(self, part):
        width = self.x.shape[1]
        return mm_tn(self.normed_ffn[...], self.d_hidden[:, part * width : (part + 1) * width])

    def grad_out(self):
        return mm_tn(self.sub[...], self.low[...])

    def grad_qkv(self, part):
        return mm_tn(self.normed[...], self.d_qkv[part])

    def backward_down(self):
        width = self.x.shape[1]
        for part in range(self.hidden.shape[1] // width):
            lanes = slice(part * width, (part + 1) * width)
            self.wide_back[:, lanes] = mm_nt(self.low[...], self.weight_b(lanes, slice(None)))

    def backward_gelu(self):
        self.sums_f[...] = jnp.zeros_like(self.sums_f)

        @pl.loop(0, self.x.shape[0] // 16)
        def _(at):
            rows = pl.ds(pl.multiple_of(at * 16, 16), 16)
            values = self.hidden[rows, :]
            square, curve = gelu_parts(values)
            unit, scale = normal(0.5 * values * (1.0 + curve))
            back = self.wide_back[rows, :]
            self.sums_f[0] += fold(back * unit)
            self.sums_f[1] += fold(back)
            inner = back * self.gain_f(0)
            d_gelu = scale * (inner - mean_of(inner) - unit * mean_of(inner * unit))
            slope = 0.5 * (1.0 + curve) + 0.5 * values * (1.0 - curve * curve) * (
                ROOT * (1.0 + 3.0 * CUBE * square)
            )
            low = (d_gelu * slope).astype(BF)
            self.d_hidden[rows, :] = low
            self.sums_f[2] += fold(wide(low))

        self.store_sums_f(0, self.sums_f[0])
        self.store_sums_f(2, self.sums_f[1])
        self.store_sums_f(1, self.sums_f[2])

    def backward_up(self):
        width = self.x.shape[1]
        total = None
        for part in range(self.hidden.shape[1] // width):
            lanes = slice(part * width, (part + 1) * width)
            value = mm_nt(self.d_hidden[:, lanes], self.weight_a(4 + part))
            if part == 0:
                self.incoming[...] = value
            else:
                self.incoming[...] += value

        def emit(rows, value):
            value = self.back[rows, :] + value
            self.back[rows, :] = value
            self.low[rows, :] = value.astype(BF)

        norm_rows_back(self.after, self.gain(2), self.incoming, emit, self.sums_d)
        self.store_sums_d(2, self.sums_d[0])
        self.store_sums_d(5, self.sums_d[1])

    def backward_out(self):
        self.store_sums_d(8, wide(self.low[...]))
        self.incoming[...] = mm_nt(self.low[...], self.weight_a(3))

        def emit(rows, value):
            self.low[rows, :] = value.astype(BF)

        norm_rows_back(self.context, self.gain(1), self.incoming, emit, self.sums_d)
        self.store_sums_d(1, self.sums_d[0])
        self.store_sums_d(4, self.sums_d[1])

    def backward_attention(self):
        @pl.loop(0, self.heads // 2)
        def _(pair):
            lanes = pl.ds(pl.multiple_of(pair * 128, 128), 128)
            queries, keys, values = [self.qkv[part, :, lanes] for part in range(3)]
            d_context = self.low[:, lanes]
            found = [None] * 3
            for side in range(2):
                half = self.lane_half(d_context, side)
                prob = self.prob[2 * pair + side]
                d_prob = mm_nt(jnp.where(half, d_context, jnp.zeros_like(d_context)), values)
                dot = jnp.sum(prob * d_prob, -1, keepdims=True)
                d_scores = (prob * (d_prob - dot)).astype(BF)
                new = (
                    mm(d_scores, keys) * HEAD_DIM**-0.5,
                    mm_tn(d_scores, queries) * HEAD_DIM**-0.5,
                    mm_tn(prob.astype(BF), d_context),
                )
                found = [n if side == 0 else jnp.where(half, n, f) for n, f in zip(new, found)]
            for part in range(3):
                self.d_qkv[part, :, lanes] = found[part].astype(BF)

    def backward_qkv(self):
        self.store_sums_d(6, wide(self.d_qkv[0]))
        self.store_sums_d(7, wide(self.d_qkv[2]))
        for part in range(3):
            value = mm_nt(self.d_qkv[part], self.weight_a(part))
            if part == 0:
                self.incoming[...] = value
            else:
                self.incoming[...] += value

        def emit(rows, value):
            self.back[rows, :] = self.back[rows, :] + value

        norm_rows_back(self.x, self.gain(0), self.incoming, emit, self.sums_d)
        self.store_sums_d(0, self.sums_d[0])
        self.store_sums_d(3, self.sums_d[1])


def saved_shapes(rows, width, wide_width, heads):
    return {
        "normed": ((rows, width), BF),
        "qkv": ((3, rows, width), BF),
        "prob": ((heads, rows, rows), F32),
        "context": ((rows, width), F32),
        "sub": ((rows, width), BF),
        "after": ((rows, width), F32),
        "normed_ffn": ((rows, width), BF),
        "hidden": ((rows, wide_width), F32),
        "sub_ffn": ((rows, wide_width), BF),
    }


def work_shapes(rows, width, wide_width):
    return {
        "low": ((rows, width), BF),
        "incoming": ((rows, width), F32),
        "wide_back": ((rows, wide_width), F32),
        "d_qkv": ((3, rows, width), BF),
        "sums_d": ((2, 8, width), F32),
        "sums_f": ((3, 8, wide_width), F32),
    }


def spread_tables(geo):
    tables = []
    for width, real in ((geo.width, geo.rows_a), (geo.wide_width, geo.rows_b)):
        at = np.arange(width)
        owner = (at[None, :] // real == np.arange(geo.owners)[:, None]).astype(np.float32)
        tables += [jnp.asarray(owner, BF), jnp.asarray(at[None, :] % real, jnp.int32)]
    return tables


def unpack_vectors(geo, whole_v, wide_v, tables, vec_d, vec_f):
    owner_d, rest_d, owner_f, rest_f = tables
    lines = geo.kind["v"][1]
    wide_v[...] = wide(whole_v[0])
    line_of = lambda at: wide_v[pl.ds(at, geo.owners, stride=lines), :].astype(BF)
    pick_d = lax.broadcasted_iota(jnp.int32, (geo.slot, geo.width), 0) == rest_d[...]
    for line in range(geo.lines_d):
        spread = mm_tn(line_of(line), owner_d[...])
        for at in range(geo.per_row):
            part = spread[at * geo.slot : (at + 1) * geo.slot]
            row = line * geo.per_row + at
            if row < geo.layers * 10:
                vec_d[row : row + 1, :] = jnp.sum(jnp.where(pick_d, part, 0.0), 0, keepdims=True)
    pick_f = lax.broadcasted_iota(jnp.int32, (128, geo.width), 0)
    for row in range(geo.layers * 3):
        line = line_of(geo.lines_d + row)
        for first in range(0, geo.wide_width, geo.width):
            lanes = slice(first, first + geo.width)
            spread = jnp.where(pick_f == rest_f[:, lanes], mm_tn(line, owner_f[:, lanes]), 0.0)
            vec_f[row : row + 1, lanes] = jnp.sum(spread, 0, keepdims=True)


KINDS = ("a", "b", "v")
GATHER_SEMS = ("lz", "lo", "zs", "zr", "xs", "xr", "ys", "yr", "ds", "dr", "cs", "cr")


def forward_kernel(geo, names_perm, saved_names, *refs):
    refs = list(refs)
    take = lambda number: [refs.pop(0) for _ in range(number)]
    sources = dict(zip(KINDS, take(3)))
    perms = dict(zip(names_perm, take(len(names_perm))))
    act_ref, mask_ref = take(2)
    tables = take(4)
    out_ref, vec_d, vec_f, kept_a, kept_b, kept_x = take(6)
    kept = [dict(zip(saved_names, take(len(saved_names)))) for _ in range(geo.layers)]
    wholes = dict(zip(KINDS, take(3)))
    bufs = dict(zip(KINDS, take(3)))
    units = dict(zip(names_perm, take(len(names_perm))))
    saved = [dict(zip(saved_names, take(len(saved_names)))) for _ in range(geo.layers)]
    xs, wide_v, keep_sem = take(3)
    sems = dict(zip(GATHER_SEMS, take(len(GATHER_SEMS))))
    place = Place(geo)
    chunks = [("v", 0, 0, 0)] + chunk_list(geo, range(geo.layers))
    moves = [
        Gather(place, at, chunk, sources, bufs, units, perms, wholes, sems)
        for at, chunk in enumerate(chunks)
    ]
    keeps = []

    def keep(src, dst):
        copy = pltpu.make_async_copy(src, dst, keep_sem.at[len(keeps)])
        copy.start()
        keeps.append(copy)

    net = []
    for layer in range(geo.layers):
        fields = dict(saved[layer], x=xs.at[layer], x_next=xs.at[layer + 1], mask=mask_ref)
        read_a = lambda at, layer=layer: wholes["a"][layer * geo.blocks + at]
        read_b = lambda rows, lanes, layer=layer: wholes["b"][layer, rows, lanes]
        net.append(Layer(fields, read_a, read_b, vec_d, vec_f, layer, geo.width // HEAD_DIM))

    def compute(number):
        name, at, lead, half = chunks[number]
        moves[number].arrive()
        if name == "v":
            unpack_vectors(geo, wholes["v"], wide_v, tables, vec_d, vec_f)
            return
        k, _, _, lanes = geo.kind[name]
        layer = at // (geo.pairs if name == "a" else geo.halves)
        one = net[layer]
        save = lambda *found: [keep(saved[layer][field], kept[layer][field]) for field in found]
        if name == "a":
            keep(wholes["a"].at[pl.ds(lead, k)], kept_a.at[pl.ds(lead, k)])
            pair = at % geo.pairs
            if pair == 0:
                one.forward_norm()
                one.forward_qkv(0)
                one.forward_qkv(1)
            elif pair == 1:
                one.forward_qkv(2)
                save("normed", "qkv")
                one.forward_attention()
                one.forward_out()
                save("prob", "context", "sub", "after", "normed_ffn")
            else:
                one.forward_up(2 * pair - 4)
                one.forward_up(2 * pair - 3)
                if pair == geo.pairs - 1:
                    one.forward_gelu()
                    save("hidden", "sub_ffn")
        else:
            where = pl.ds(half * lanes, lanes)
            keep(wholes["b"].at[lead, :, where], kept_b.at[lead, :, where])
            one.forward_down(half, geo.halves)
            if half == geo.halves - 1 and layer < geo.layers - 1:
                keep(xs.at[layer + 1], kept_x.at[layer + 1])

    xs[0] = wide(act_ref[...])
    keep(xs.at[0], kept_x.at[0])
    place.greet()
    run_pipeline(
        [
            (-2, lambda c: moves[c].start_z()),
            (0, lambda c: moves[c].own()),
            (1, lambda c: moves[c].forward()),
            (2, lambda c: moves[c].corner()),
            (3, compute),
        ],
        len(moves),
    )
    out_ref[...] = xs[geo.layers].astype(BF)
    for move in moves:
        move.drain()
    for copy in keeps:
        copy.wait()


def run_forward(geo, source_a, source_b, source_v, act, mask):
    names_perm = [name for name in KINDS if geo.permuted(name)]
    perms = [jnp.asarray(geo.permutation(name), BF) for name in names_perm]
    rows, width = act.shape
    total = sum(geo.number.values())
    heads = width // HEAD_DIM
    saved = saved_shapes(rows, width, geo.wide_width, heads)
    bufs, units, wholes = [], [], []
    for name in KINDS:
        k, sent, unit, lanes = geo.kind[name]
        bufs.append(pltpu.VMEM((geo.number[name], geo.n_z * sent, lanes), BF))
        if name in names_perm:
            units.append(pltpu.VMEM((geo.number[name], k, unit, lanes), BF))
        lead, _, _, _, _, whole_lanes = geo.whole_shape(name)
        wholes.append(((lead, geo.n_dp * unit, whole_lanes), BF))
    n_y, n_z = geo.n_y, geo.n_z
    n_keeps = geo.layers * (len(saved) + geo.pairs + geo.halves + 1)
    vec_rows = geo.layers * 10
    outs = [
        jax.ShapeDtypeStruct((rows, width), BF),
        jax.ShapeDtypeStruct((vec_rows, width), F32),
        jax.ShapeDtypeStruct((geo.layers * 3, geo.wide_width), F32),
        jax.ShapeDtypeStruct(*wholes[0]),
        jax.ShapeDtypeStruct(*wholes[1]),
        jax.ShapeDtypeStruct((geo.layers, rows, width), F32),
    ] + [jax.ShapeDtypeStruct(*saved[name]) for _ in range(geo.layers) for name in saved]
    found = pl.pallas_call(
        functools.partial(forward_kernel, geo, names_perm, list(saved)),
        out_shape=outs,
        in_specs=[IN_VMEM] * (3 + len(perms) + 6),
        out_specs=[IN_VMEM] * 3 + [ANY] * (len(outs) - 3),
        scratch_shapes=[pltpu.VMEM(*whole) for whole in wholes]
        + bufs
        + units
        + [pltpu.VMEM(*saved[name]) for _ in range(geo.layers) for name in saved]
        + [
            pltpu.VMEM((geo.layers + 1, rows, width), F32),
            pltpu.VMEM(wholes[2][0][1:], F32),
            dma(n_keeps),
            dma(total),
            dma(total),
            dma(total, n_z),
            dma(total, n_z),
            dma(total),
            dma(total),
            dma(total, n_y),
            dma(total, n_y),
            dma(total, n_y),
            dma(total, n_y),
            dma(total, 2 * n_y),
            dma(total, 2 * n_y),
        ],
        compiler_params=pltpu.CompilerParams(
            collective_id=0, has_side_effects=True, vmem_limit_bytes=60 * 2**20
        ),
    )(source_a, source_b, source_v, *perms, act, mask, *spread_tables(geo))
    names = list(saved)
    kept = [dict(zip(names, found[6 + layer * len(names) :])) for layer in range(geo.layers)]
    return found[:6], kept


def pack_gradients(geo, grad_d, grad_f, tables, wide_v, stage_v):
    owner_d, rest_d, owner_f, rest_f = tables
    lines = geo.kind["v"][1]
    wide_v[...] = jnp.zeros_like(wide_v)
    pick_d = lax.broadcasted_iota(jnp.int32, (geo.slot, geo.width), 0) == rest_d[...]
    for line in range(geo.lines_d):
        parts = []
        for at in range(geo.per_row):
            row = line * geo.per_row + at
            if row < geo.layers * 10:
                parts.append(jnp.where(pick_d, grad_d[row : row + 1, :], 0.0))
            else:
                parts.append(jnp.zeros(pick_d.shape, F32))
        wide_v[pl.ds(line, geo.owners, stride=lines), :] = mm_nt(
            owner_d[...], jnp.concatenate(parts, 0).astype(BF)
        )
    pick_f = lax.broadcasted_iota(jnp.int32, (128, geo.width), 0)
    for row in range(geo.layers * 3):
        total = None
        for first in range(0, geo.wide_width, geo.width):
            lanes = slice(first, first + geo.width)
            part = jnp.where(pick_f == rest_f[:, lanes], grad_f[row : row + 1, lanes], 0.0).astype(BF)
            part = mm_nt(owner_f[:, lanes], part)
            total = part if total is None else total + part
        wide_v[pl.ds(geo.lines_d + row, geo.owners, stride=lines), :] = total
    stage_v[...] = wide_v[...].astype(BF).reshape(stage_v.shape)


class Ring:
    def __init__(self, sources, slots, sems):
        self.slots, self.size, self.used = slots, slots.shape[0], 0
        self.copies = [
            pltpu.make_async_copy(source, slots.at[at % self.size], sems.at[at % self.size])
            for at, source in enumerate(sources)
        ]
        for copy in self.copies[: self.size]:
            copy.start()

    def next(self):
        at = self.used
        self.used += 1
        if 0 < at and at - 1 + self.size < len(self.copies):
            self.copies[at - 1 + self.size].start()
        self.copies[at].wait()
        return self.slots[at % self.size]


SCATTER_SEMS = ("cs", "cr", "ms", "mr", "es", "er", "zs", "zr", "fx", "fy")
Z_SLOTS = 4
SCATTER_LAGS = (0, 1, 3, 5, 7)
RING = 3


def backward_kernel(geo, names_perm, names, *refs):
    refs = list(refs)
    take = lambda number: [refs.pop(0) for _ in range(number)]
    by_kind = lambda: dict(zip(KINDS, take(3)))
    saved_names, work_names = names
    layers, blocks, width = geo.layers, geo.blocks, geo.width
    perms = dict(zip(names_perm, take(len(names_perm))))
    cot_ref, vec_d, vec_f = take(3)
    tables = take(4)
    whole_a, whole_b, kept_x = take(3)
    kept = [dict(zip(saved_names, take(len(saved_names)))) for _ in range(layers)]
    for layer in range(layers):
        kept[layer]["x"] = kept_x.at[layer]
    back_ref, out_qkv, out_out, out_up, out_down, out_d, out_f = take(7)
    fields = dict(zip(saved_names, take(len(saved_names))))
    fields.update(zip(work_names, take(len(work_names))))
    stages, sums, mids, ends, z_send, z_recv = [by_kind() for _ in range(6)]
    x_ref, grad_d, grad_f, wide_v, slots, sem_l, sem_w = take(7)
    sems = dict(zip(SCATTER_SEMS, take(len(SCATTER_SEMS))))
    fields.update(d_hidden=fields["sub_ffn"], x=x_ref, back=back_ref, grad_d=grad_d, grad_f=grad_f)
    place = Place(geo)

    def writer(chunk):
        name, at, lead, half = chunk
        rows_a, rows_b, lines = geo.rows_a, geo.rows_b, geo.lines_d

        def put_a(value):
            layer = at // geo.pairs
            for side in range(2):
                block = 2 * (at % geo.pairs) + side
                piece = value[side * rows_a : (side + 1) * rows_a]
                if block < 3:
                    out_qkv[layer, :, block * width : (block + 1) * width] = piece
                elif block == 3:
                    out_out[layer] = piece
                else:
                    out_up[layer, :, (block - 4) * width : (block - 3) * width] = piece

        def put_b(value):
            lanes = value.shape[1]
            out_down[lead, :, half * lanes : (half + 1) * lanes] = value[:rows_b]

        def put_v(value):
            out_d[...] = value[:lines]
            out_f[...] = value[lines : lines + layers * 3]

        return {"a": put_a, "b": put_b, "v": put_v}[name]

    order, seen = [], {name: [] for name in KINDS}
    for layer in reversed(range(layers)):
        for half in range(geo.halves):
            order.append(("b", layer * geo.halves + half, layer, half))
        for pair in list(range(2, geo.pairs)) + [1, 0]:
            order.append(("a", layer * geo.pairs + pair, layer * blocks + 2 * pair, 0))
    order.append(("v", 0, 0, 0))
    moves, stage_of = [], []
    for number, chunk in enumerate(order):
        name = chunk[0]
        stage = stages[name].at[len(seen[name]) % stages[name].shape[0]]
        slots_z = z_send[name].shape[0]
        z_slot = len(seen[name]) % slots_z
        before = seen[name][-slots_z] if len(seen[name]) >= slots_z else None
        move = Scatter(
            place, number, chunk, stage, sums, mids, ends, perms, z_send, z_recv, z_slot, before,
            writer(chunk), sems,
        )
        seen[name].append(move)
        stage_of.append(stage)
        moves.append(move)
    step = [0]

    def serve():
        acts = (Scatter.start, Scatter.pair, Scatter.middle, Scatter.last, Scatter.finish)
        for lag, act in zip(SCATTER_LAGS, acts):
            if 0 <= step[0] - lag < len(moves):
                act(moves[step[0] - lag])
        step[0] += 1

    def stage_a(side, value):
        stage_of[step[0]][side] = value.astype(BF).reshape(geo.n_y, 2, 2, -1, width)

    loads = {}
    field_names = ["x"] + list(saved_names)

    def fetch(layer, *found):
        for name in found:
            loads[name] = pltpu.make_async_copy(
                kept[layer][name], fields[name], sem_l.at[field_names.index(name)]
            )
            loads[name].start()

    def ready(*found):
        for name in found:
            loads[name].wait()

    fetch(layers - 1, "sub_ffn", "hidden", "normed_ffn", "after", "sub", "context", "prob", "qkv", "normed", "x")
    sources = []
    for layer in reversed(range(layers)):
        parts = geo.wide_width // width
        sources += [whole_b.at[layer, pl.ds(part * width, width)] for part in range(parts)]
        sources += [whole_a.at[layer * blocks + at] for at in list(range(4, blocks)) + [3, 0, 1, 2]]
    ring = Ring(sources, slots, sem_w)
    cot_copy = pltpu.make_async_copy(cot_ref, back_ref, sem_l.at[len(field_names)])
    cot_copy.start()
    place.greet()
    cot_copy.wait()
    for layer in reversed(range(layers)):
        one = Layer(
            fields, lambda at: ring.next(), lambda rows, lanes: ring.next(), vec_d, vec_f, layer,
            width // HEAD_DIM,
        )
        again = (lambda *found: fetch(layer - 1, *found)) if layer > 0 else (lambda *found: None)
        one.backward_start()
        ready("sub_ffn")
        _, _, unit, lanes = geo.kind["b"]
        for half in range(geo.halves):
            for column in range(geo.n_dp // 2):
                rows = slice(column * 2 * unit, (column + 1) * 2 * unit)
                value = one.grad_down(rows, slice(half * lanes, (half + 1) * lanes))
                stage_of[step[0]][0, column // 2, column % 2] = value.astype(BF).reshape(2, unit, lanes)
            serve()
        one.backward_down()
        ready("hidden")
        one.backward_gelu()
        again("hidden")
        ready("normed_ffn")
        for pair in range(2, geo.pairs):
            stage_a(0, one.grad_up(2 * pair - 4))
            stage_a(1, one.grad_up(2 * pair - 3))
            serve()
        again("normed_ffn")
        ready("after")
        one.backward_up()
        again("after", "sub_ffn")
        ready("sub", "context")
        stage_a(1, one.grad_out())
        one.backward_out()
        again("sub", "context")
        ready("prob", "qkv")
        one.backward_attention()
        again("prob", "qkv")
        ready("normed")
        stage_a(0, one.grad_qkv(2))
        serve()
        stage_a(0, one.grad_qkv(0))
        stage_a(1, one.grad_qkv(1))
        serve()
        again("normed")
        ready("x")
        one.backward_qkv()
        again("x")
    pack_gradients(geo, grad_d, grad_f, tables, wide_v, stage_of[step[0]])
    while step[0] < len(moves) + SCATTER_LAGS[-1]:
        serve()
    for move in moves:
        move.drain()


def run_backward(geo, cot, vec_d, vec_f, whole_a, whole_b, kept_x, kept):
    rows, width = cot.shape
    layers, n_y, n_z = geo.layers, geo.n_y, geo.n_z
    heads = width // HEAD_DIM
    saved, work = saved_shapes(rows, width, geo.wide_width, heads), work_shapes(rows, width, geo.wide_width)
    names = (list(saved), list(work))
    names_perm = [name for name in KINDS if geo.permuted(name)]
    perms = [jnp.asarray(geo.permutation(name).T, BF) for name in names_perm]
    total = sum(geo.number.values())
    groups = [[] for _ in range(6)]
    for name in KINDS:
        k, sent, unit, lanes = geo.kind[name]
        number = geo.number[name]
        mid_steps = max(n_y - 1, (n_y + 1) // 2)
        groups[0].append(pltpu.VMEM((min(number, 2), k, n_y, 2, 2, unit, lanes), BF))
        groups[1].append(pltpu.VMEM((number, k, n_y, 2, unit, lanes), BF))
        landing = number if name == "v" else number // layers
        groups[2].append(pltpu.VMEM((landing, mid_steps, k, 2, unit, lanes), BF))
        groups[3].append(pltpu.VMEM((number, mid_steps, k, unit, lanes), BF))
        groups[4].append(pltpu.VMEM((min(number, Z_SLOTS), n_z, sent, lanes), BF))
        groups[5].append(pltpu.VMEM((number, n_z, sent, lanes), BF))
    scratch = [pltpu.VMEM(*saved[name]) for name in saved] + [pltpu.VMEM(*work[name]) for name in work]
    scratch += sum(groups, [])
    scratch += [
        pltpu.VMEM((rows, width), F32),
        pltpu.VMEM((layers * 10, width), F32),
        pltpu.VMEM((layers * 3, geo.wide_width), F32),
        pltpu.VMEM((geo.owners * geo.kind["v"][1], 128), F32),
        pltpu.VMEM((RING, width, width), BF),
        dma(2 + len(saved)),
        dma(RING),
        dma(total),
        dma(total),
        dma(total, n_y),
        dma(total, n_y),
        dma(total, n_y),
        dma(total, n_y),
        dma(total, n_z),
        dma(total, n_z),
        pltpu.SemaphoreType.REGULAR,
        pltpu.SemaphoreType.REGULAR((n_y,)),
    ]
    return pl.pallas_call(
        functools.partial(backward_kernel, geo, names_perm, names),
        out_shape=[
            jax.ShapeDtypeStruct((rows, width), F32),
            jax.ShapeDtypeStruct((layers, geo.rows_a, 3 * width), F32),
            jax.ShapeDtypeStruct((layers, geo.rows_a, width), F32),
            jax.ShapeDtypeStruct((layers, geo.rows_a, geo.wide_width), F32),
            jax.ShapeDtypeStruct((layers, geo.rows_b, width), F32),
            jax.ShapeDtypeStruct((geo.lines_d, 128), F32),
            jax.ShapeDtypeStruct((layers * 3, 128), F32),
        ],
        in_specs=[IN_VMEM] * len(perms) + [ANY] + [IN_VMEM] * 6 + [ANY] * (3 + layers * len(saved)),
        out_specs=[IN_VMEM] * 7,
        scratch_shapes=scratch,
        compiler_params=pltpu.CompilerParams(
            collective_id=1, has_side_effects=True, vmem_limit_bytes=63 * 2**20
        ),
    )(
        *perms, cot, vec_d, vec_f, *spread_tables(geo), whole_a, whole_b, kept_x,
        *[kept[layer][name] for layer in range(layers) for name in saved],
    )


def pack_kernel(geo, *refs):
    act_short, act_long, len_short, len_long, w_qkv, w_out, w_up, w_down = refs[:8]
    gains_d, shifts_d, gains_ff, shifts_ff, cot_short, cot_long = refs[8:14]
    source_a, source_b, source_v, act, mask, cot, lines = refs[14:]
    width, rows_a, rows_b = geo.width, geo.rows_a, geo.rows_b

    def block(layer, at):
        if at == 3:
            return wide(w_out[layer])
        first = at if at < 3 else at - 4
        return wide((w_qkv if at < 3 else w_up)[layer, :, first * width : (first + 1) * width])

    def filled(pieces, rows):
        have = sum(piece.shape[0] for piece in pieces)
        if have < rows:
            pieces = pieces + [jnp.zeros((rows - have, pieces[0].shape[1]), F32)]
        return (jnp.concatenate(pieces, 0) if len(pieces) > 1 else pieces[0]).astype(BF)

    for layer in range(geo.layers):
        for pair in range(geo.pairs):
            pieces = [block(layer, 2 * pair), block(layer, 2 * pair + 1)]
            source_a[layer * geo.pairs + pair] = filled(pieces, geo.kind["a"][1])
        for half in range(geo.halves):
            lanes = geo.kind["b"][3]
            piece = w_down[layer, :, half * lanes : (half + 1) * lanes]
            if rows_b == geo.kind["b"][1]:
                source_b[layer * geo.halves + half] = piece
            else:
                source_b[layer * geo.halves + half] = filled([wide(piece)], geo.kind["b"][1])
    lines[...] = jnp.zeros_like(lines)
    gains_wide = wide(gains_ff[...])
    for layer in range(geo.layers):
        gains, shifts, shifts_wide = wide(gains_d[layer]), wide(shifts_d[layer]), wide(shifts_ff[layer])
        for at in range(10):
            line, lane = divmod(layer * 10 + at, geo.per_row)
            value = gains[at : at + 1] if at < 3 else shifts[at - 3 : at - 2]
            lines[line : line + 1, lane * geo.slot : lane * geo.slot + rows_a] = value
        for at in range(3):
            line = geo.lines_d + layer * 3 + at
            lines[line : line + 1, :rows_b] = gains_wide[layer : layer + 1] if at == 0 else shifts_wide[at - 1 : at]
    source_v[0] = lines[...].astype(BF)
    short = act_short.shape[0]
    act[:short] = act_short[...]
    act[short:] = act_long[...]
    rows = act.shape[0]

    def valid(shape, dim):
        at = lax.broadcasted_iota(jnp.int32, shape, dim)
        return jnp.where(jnp.where(at < short, at - len_short[0], at - short - len_long[0]) < 0, 1.0, 0.0)

    def bucket(dim):
        return jnp.where(lax.broadcasted_iota(jnp.int32, (rows, rows), dim) < short, 0, 1)

    mask[...] = jnp.where(bucket(0) == bucket(1), valid((rows, rows), 1), 0.0)
    keep = valid((rows, width), 0)
    cot[:short] = wide(cot_short[...]) * keep[:short]
    cot[short:] = wide(cot_long[...]) * keep[short:]


def run_pack(geo, args):
    rows = args[0].shape[0] + args[1].shape[0]
    shapes = []
    for name in KINDS:
        _, sent, _, lanes = geo.kind[name]
        shapes.append(jax.ShapeDtypeStruct((geo.number[name], sent, lanes), BF))
    shapes += [
        jax.ShapeDtypeStruct((rows, geo.width), BF),
        jax.ShapeDtypeStruct((rows, rows), F32),
        jax.ShapeDtypeStruct((rows, geo.width), F32),
    ]
    in_smem = pl.BlockSpec(memory_space=pltpu.SMEM)
    return pl.pallas_call(
        functools.partial(pack_kernel, geo),
        out_shape=shapes,
        in_specs=[IN_VMEM] * 2 + [in_smem] * 2 + [IN_VMEM] * 10,
        out_specs=[IN_VMEM] * len(shapes),
        scratch_shapes=[pltpu.VMEM((geo.kind["v"][1], 128), F32)],
        compiler_params=pltpu.CompilerParams(vmem_limit_bytes=63 * 2**20),
    )(*args)


def unpack_kernel(geo, *refs):
    out, back, g_qkv, g_out, g_up, g_down, lines_d, lines_f = refs[:8]
    out_short, out_long, back_short, back_long, t_qkv, t_out, t_up, t_down = refs[8:16]
    t_gains_d, t_shifts_d, t_gains_ff, t_shifts_ff = refs[16:]
    short = out_short.shape[0]
    out_short[...] = out[:short]
    out_long[...] = out[short:]
    back_short[...] = back[:short]
    back_long[...] = back[short:]
    for source, target in ((g_qkv, t_qkv), (g_out, t_out), (g_up, t_up), (g_down, t_down)):
        target[...] = source[...]
    for layer in range(geo.layers):
        for at in range(10):
            line, lane = divmod(layer * 10 + at, geo.per_row)
            value = lines_d[line : line + 1, lane * geo.slot : lane * geo.slot + geo.rows_a]
            if at < 3:
                t_gains_d[layer, at : at + 1, :] = value
            else:
                t_shifts_d[layer, at - 3 : at - 2, :] = value
        for at in range(3):
            value = lines_f[layer * 3 + at : layer * 3 + at + 1, : geo.rows_b]
            if at == 0:
                t_gains_ff[layer : layer + 1, :] = value
            else:
                t_shifts_ff[layer, at - 1 : at, :] = value


def run_unpack(geo, found, args):
    like = lambda index, dtype: jax.ShapeDtypeStruct(args[index].shape, dtype)
    shapes = [like(0, BF), like(1, BF), like(0, F32), like(1, F32)]
    shapes += [like(index, F32) for index in range(4, 12)]
    return pl.pallas_call(
        functools.partial(unpack_kernel, geo),
        out_shape=shapes,
        in_specs=[IN_VMEM] * len(found),
        out_specs=[IN_VMEM] * len(shapes),
        compiler_params=pltpu.CompilerParams(vmem_limit_bytes=63 * 2**20),
    )(*found)


def on_device(*args):
    n_dp, n_z = lax.axis_size("dp"), lax.axis_size("fsdp")
    geo = Geometry(n_dp, n_z, args[4].shape, args[6].shape, args[7].shape)
    source_a, source_b, source_v, act, mask, cot = run_pack(geo, args)
    found, kept = run_forward(geo, source_a, source_b, source_v, act, mask)
    out, vec_d, vec_f, whole_a, whole_b, kept_x = found
    grads = run_backward(geo, cot, vec_d, vec_f, whole_a, whole_b, kept_x, kept)
    return tuple(run_unpack(geo, (out,) + tuple(grads), args))


def solution(mesh):
    return jax.shard_map(
        on_device,
        mesh=mesh,
        in_specs=(
            P(("dp", "fsdp"), None),
            P(("dp", "fsdp"), None),
            P(("dp", "fsdp")),
            P(("dp", "fsdp")),
            P(None, ("dp", "fsdp"), None),
            P(None, ("dp", "fsdp"), None),
            P(None, ("dp", "fsdp"), None),
            P(None, ("dp", "fsdp"), None),
            P(None, None, ("dp", "fsdp")),
            P(None, None, ("dp", "fsdp")),
            P(None, ("dp", "fsdp")),
            P(None, None, ("dp", "fsdp")),
            P(("dp", "fsdp"), None),
            P(("dp", "fsdp"), None),
        ),
        out_specs=(
            P(("dp", "fsdp"), None),
            P(("dp", "fsdp"), None),
            P(("dp", "fsdp"), None),
            P(("dp", "fsdp"), None),
            P(None, ("dp", "fsdp"), None),
            P(None, ("dp", "fsdp"), None),
            P(None, ("dp", "fsdp"), None),
            P(None, ("dp", "fsdp"), None),
            P(None, None, ("dp", "fsdp")),
            P(None, None, ("dp", "fsdp")),
            P(None, ("dp", "fsdp")),
            P(None, None, ("dp", "fsdp")),
        ),
        check_vma=False,
    )
```

```python
import functools

import jax
import jax.numpy as jnp
import numpy as np
from jax import lax
from jax.experimental import pallas as pl
from jax.experimental.pallas import tpu as pltpu
from jax.sharding import PartitionSpec as P

HEAD_DIM = 64

epsilon = 1e-05


BF = jnp.bfloat16
F32 = jnp.float32
MESH = pl.DeviceIdType.MESH


def round16(count):
    return (count + 15) // 16 * 16


class Geometry:
    def __init__(self, n_dp, n_z, w_qkv, w_up, w_down):
        self.n_dp, self.n_z, self.n_y = n_dp, n_z, n_dp // 4
        self.layers = w_qkv[0]
        self.width = w_qkv[2] // 3
        self.rows_a, self.rows_b = w_qkv[1], w_down[1]
        self.blocks = 4 + w_up[2] // self.width
        self.pairs = self.blocks // 2
        half = self.width // 2
        self.lined = self.rows_b % 16 == 0
        self.roomy = self.n_y <= 2
        self.first_down = "l" if self.lined else "b"
        self.lanes_of = {self.first_down: (0, half), "c": (half, half - 128), "d": (2 * half - 128, 128)}
        self.down = tuple(self.lanes_of)
        self.kinds = ("a", "v") + self.down
        self.plain = tuple(name for name in self.kinds if name != "l")
        self.owners = n_dp * n_z
        self.wide_width = w_up[2]
        self.slot = 8
        while self.slot < self.rows_a:
            self.slot *= 2
        self.per_row = 128 // self.slot
        self.lines_d = -(-self.layers * 10 // self.per_row)
        lines = round16(self.lines_d + self.layers * 3)
        self.kind = {
            "a": (2, round16(2 * self.rows_a), self.rows_a * n_z, self.width),
            "v": (1, lines, lines * n_z, 128),
        }
        self.real = {"a": self.rows_a, "v": self.kind["v"][1]}
        self.number = {"a": self.layers * self.pairs, "v": 1}
        for name, (_, lanes) in self.lanes_of.items():
            self.kind[name] = (1, round16(self.rows_b), self.rows_b * n_z, lanes)
            self.real[name] = self.rows_b
            self.number[name] = self.layers

    def permuted(self, name):
        k, sent, unit, _ = self.kind[name]
        return k * unit != sent * self.n_z or k > 1

    def permutation(self, name):
        k, sent, unit, _ = self.kind[name]
        real = self.real[name]
        table = np.zeros((k * unit, self.n_z * sent), np.float32)
        for block in range(k):
            for z in range(self.n_z):
                for row in range(real):
                    table[block * unit + z * real + row, z * sent + block * real + row] = 1
        return table

    def whole_shape(self, name):
        _, _, unit, lanes = self.kind[name]
        lead = {"a": self.layers * self.blocks, "v": 1}.get(name, self.layers)
        return (lead, self.n_dp * unit, lanes if name == "v" else self.width)


class Place:
    def __init__(self, geo):
        self.geo = geo
        self.d, self.z = lax.axis_index("dp"), lax.axis_index("fsdp")
        self.core = lax.rem(self.d, 2)
        self.x = lax.rem(self.d // 2, 2)
        self.y = self.d // 4

    def y_off(self, step):
        return lax.rem(self.y + step + self.geo.n_y, self.geo.n_y)

    def z_off(self, step):
        return lax.rem(self.z + step + self.geo.n_z, self.geo.n_z)

    def dev_core(self):
        return (self.d + 1 - 2 * self.core, self.z)

    def dev_x(self):
        return (self.d + 2 - 4 * self.x, self.z)

    def dev_y(self, step):
        return (self.y_off(step) * 4 + self.x * 2 + self.core, self.z)

    def dev_z(self, step):
        return (self.d, self.z_off(step))

    def greet(self):
        barrier = pltpu.get_barrier_semaphore()
        partners = [self.dev_core(), self.dev_x()]
        partners += [self.dev_y(step) for step in range(1, self.geo.n_y)]
        partners += [self.dev_z(step) for step in range(1, self.geo.n_z)]
        for partner in partners:
            pl.semaphore_signal(barrier, inc=1, device_id=partner, device_id_type=MESH)
        pl.semaphore_wait(barrier, len(partners))


def remote(src, dst, send, recv, device):
    return pltpu.make_async_remote_copy(
        src_ref=src, dst_ref=dst, send_sem=send, recv_sem=recv, device_id=device, device_id_type=MESH
    )


def chunk_a(geo, layer, pair):
    return ("a", layer * geo.pairs + pair, layer * geo.blocks + 2 * pair, 0)


def chunk_down(geo, layer, name):
    return (name, layer, layer, geo.lanes_of[name][0])


def rows_of(whole, name, lead, first, k, unit, lanes):
    def at(y, x, core):
        rows = pl.ds(pl.multiple_of((y * 4 + x * 2 + core) * unit, 16), unit)
        return whole.at[pl.ds(lead, k), rows, slice(None) if name in ("a", "v") else pl.ds(first, lanes)]

    return at


class Gather:
    def __init__(self, place, number, chunk, sources, bufs, units, perms, wholes, sems):
        self.p, self.c = place, number
        name, at, lead, first = chunk
        self.half_a = number % 2 == 0
        k, self.sent, unit, lanes = place.geo.kind[name]
        self.source = sources[name].at[at]
        self.buf = bufs[name].at[at]
        self.perm = perms.get(name)
        self.unit_buf = units[name].at[at] if self.perm is not None else None
        self.unit = self.unit_buf if self.perm is not None else bufs[name].at[pl.ds(at, 1)]
        self.to = rows_of(wholes[name], name, lead, first, k, unit, lanes)
        self.sems = sems
        self.pending = []

    def slot(self, z):
        return self.buf.at[pl.ds(pl.multiple_of(z * self.sent, 16), self.sent)]

    def send(self, src, dst, send, recv, device):
        copy = remote(src, dst, send, recv, device)
        copy.start()
        self.pending.append(copy)

    def arrived(self, dst, send, recv, device):
        remote(dst, dst, send, recv, device).wait_recv()

    def start_z(self):
        p, s, c = self.p, self.sems, self.c
        self.local_z = pltpu.make_async_copy(self.source, self.slot(p.z), s["lz"].at[c])
        self.local_z.start()
        for step in range(1, p.geo.n_z):
            self.send(self.source, self.slot(p.z), s["zs"].at[c, step], s["zr"].at[c, step], p.dev_z(step))

    def own(self):
        p, s, c = self.p, self.sems, self.c
        self.local_z.wait()
        for step in range(1, p.geo.n_z):
            self.arrived(self.slot(p.z_off(-step)), s["zs"].at[c, step], s["zr"].at[c, step], p.dev_z(step))
        if self.perm is not None:
            k, unit, lanes = self.unit_buf.shape
            mixed = jnp.dot(self.perm[...], self.buf[...], preferred_element_type=F32)
            self.unit_buf[...] = mixed.astype(BF).reshape(k, unit, lanes)
        here = self.to(p.y, p.x, p.core)
        self.local = pltpu.make_async_copy(self.unit, here, s["lo"].at[c])
        self.send(self.unit, here, s["xs"].at[c], s["xr"].at[c], p.dev_x())
        for step in range(1, p.geo.n_y):
            self.send(self.unit, here, s["ys"].at[c, step], s["yr"].at[c, step], p.dev_y(step))
        self.send(self.unit, here, s["cs"].at[c, 0], s["cr"].at[c, 0], p.dev_core())
        self.local.start()

    def forward(self):
        p, s, c = self.p, self.sems, self.c
        n_y = p.geo.n_y
        from_x = self.to(p.y, 1 - p.x, p.core)
        self.arrived(from_x, s["xs"].at[c], s["xr"].at[c], p.dev_x())
        if self.half_a:
            for step in range(1, n_y):
                self.send(from_x, from_x, s["ds"].at[c, step], s["dr"].at[c, step], p.dev_y(step))
        self.send(from_x, from_x, s["cs"].at[c, 1], s["cr"].at[c, 1], p.dev_core())
        for step in range(1, n_y):
            from_y = self.to(p.y_off(-step), p.x, p.core)
            self.arrived(from_y, s["ys"].at[c, step], s["yr"].at[c, step], p.dev_y(step))
            if not self.half_a:
                self.send(from_y, from_y, s["ds"].at[c, step], s["dr"].at[c, step], p.dev_x())
            self.send(from_y, from_y, s["cs"].at[c, 2 * step], s["cr"].at[c, 2 * step], p.dev_core())

    def corner(self):
        p, s, c = self.p, self.sems, self.c
        for step in range(1, p.geo.n_y):
            far = self.to(p.y_off(-step), 1 - p.x, p.core)
            self.arrived(far, s["ds"].at[c, step], s["dr"].at[c, step], p.dev_x())
            self.send(far, far, s["cs"].at[c, 2 * step + 1], s["cr"].at[c, 2 * step + 1], p.dev_core())

    def arrive(self):
        p, s, c = self.p, self.sems, self.c
        for step in range(p.geo.n_y):
            for flip in range(2):
                x = p.x if flip == 0 else 1 - p.x
                got = self.to(p.y_off(-step), x, 1 - p.core)
                at = 2 * step + flip
                self.arrived(got, s["cs"].at[c, at], s["cr"].at[c, at], p.dev_core())
        self.local.wait()

    def drain(self):
        for copy in self.pending:
            copy.wait_send()


def when(condition, act):
    pl.when(condition)(act)


def on_line(place, way, step):
    at = place.z - step if way == 0 else place.z + step
    return (at >= 0) & (at < place.geo.n_z), at


class GatherLine:
    def __init__(self, place, number, chunk, sources, wholes, sems):
        self.p, self.c = place, number
        _, at, lead, first = chunk
        _, sent, _, lanes = place.geo.kind["l"]
        self.source = sources["l"].at[at]
        self.half_a = number % 2 == 0
        whole = wholes["l"]

        def piece(y, x, core, z):
            device = (y * 4 + x * 2 + core) * place.geo.n_z + z
            rows = pl.ds(pl.multiple_of(device * sent, 16), sent)
            return whole.at[lead, rows, pl.ds(first, lanes)]

        self.piece = piece
        self.sems = sems
        self.pending, self.line_pending = [], []

    def send(self, src, dst, send, recv, device):
        copy = remote(src, dst, send, recv, device)
        copy.start()
        self.pending.append(copy)

    def arrived(self, dst, send, recv, device):
        remote(dst, dst, send, recv, device).wait_recv()

    def from_column(self, at, z, core):
        p = self.p
        return self.piece(p.y_off(-(at // 2)), p.x if at % 2 == 0 else 1 - p.x, core, z)

    def line_send(self, column, hop):
        p, s, c = self.p, self.sems, self.c
        for way in range(2):
            valid, z = on_line(p, way, hop - 1)
            further, target = on_line(p, 1 - way, 1)

            def copy(z=z, target=target, way=way):
                rows = self.from_column(column, z, p.core)
                at = (c, way, hop, column)
                return remote(rows, rows, s["gs"].at[at], s["gr"].at[at], (p.d, target))

            when(valid & further, lambda copy=copy: copy().start())
            self.line_pending.append((valid & further, copy))

    def to_core(self, column, z, at):
        s = self.sems
        rows = self.from_column(column, z, self.p.core)
        return remote(rows, rows, s["hs"].at[at], s["hr"].at[at], self.p.dev_core())

    def start(self):
        p, s, c = self.p, self.sems, self.c
        here = self.piece(p.y, p.x, p.core, p.z)
        self.local = pltpu.make_async_copy(self.source, here, s["gl"].at[c])
        self.send(self.source, here, s["gx"].at[c, 0], s["gx"].at[c, 1], p.dev_x())
        for step in range(1, p.geo.n_y):
            self.send(self.source, here, s["gy"].at[c, 0, step], s["gy"].at[c, 1, step], p.dev_y(step))
        self.local.start()
        at = (c, 0, 0, 0)
        self.send(self.source, here, s["hs"].at[at], s["hr"].at[at], p.dev_core())

    def forward(self):
        p, s, c = self.p, self.sems, self.c
        n_y = p.geo.n_y
        self.local.wait()
        rows = self.from_column(1, p.z, p.core)
        self.arrived(rows, s["gx"].at[c, 0], s["gx"].at[c, 1], p.dev_x())
        if self.half_a:
            for step in range(1, n_y):
                self.send(rows, rows, s["gd"].at[c, 0, step], s["gd"].at[c, 1, step], p.dev_y(step))
        self.keep_core(1)
        for step in range(1, n_y):
            rows = self.from_column(2 * step, p.z, p.core)
            self.arrived(rows, s["gy"].at[c, 0, step], s["gy"].at[c, 1, step], p.dev_y(step))
            if not self.half_a:
                self.send(rows, rows, s["gd"].at[c, 0, step], s["gd"].at[c, 1, step], p.dev_x())
            self.keep_core(2 * step)

    def keep_core(self, column):
        copy = self.to_core(column, self.p.z, (self.c, 0, 0, column))
        copy.start()
        self.pending.append(copy)

    def corner(self):
        p, s, c = self.p, self.sems, self.c
        for step in range(1, p.geo.n_y):
            rows = self.from_column(2 * step + 1, p.z, p.core)
            self.arrived(rows, s["gd"].at[c, 0, step], s["gd"].at[c, 1, step], p.dev_x())
            self.keep_core(2 * step + 1)

    def relay(self, hop, half):
        p, s, c = self.p, self.sems, self.c
        n_y = p.geo.n_y
        for column in range(half * n_y, (half + 1) * n_y):
            for way in range(2) if hop > 0 else ():
                valid, z = on_line(p, way, hop)
                at = (c, way, hop, column)

                def act(z=z, at=at):
                    rows = self.from_column(column, z, p.core)
                    remote(rows, rows, s["gs"].at[at], s["gr"].at[at], p.dev_x()).wait_recv()
                    self.to_core(column, z, at).start()

                when(valid, act)
                self.line_pending.append(
                    (valid, lambda column=column, z=z, at=at: self.to_core(column, z, at))
                )
            if hop < p.geo.n_z - 1:
                self.line_send(column, hop + 1)

    def arrive(self):
        p, s, c = self.p, self.sems, self.c
        for column in range(2 * p.geo.n_y):
            rows = self.from_column(column, p.z, 1 - p.core)
            at = (c, 0, 0, column)
            self.arrived(rows, s["hs"].at[at], s["hr"].at[at], p.dev_core())
            for hop in range(1, p.geo.n_z):
                for way in range(2):
                    valid, z = on_line(p, way, hop)
                    at = (c, way, hop, column)

                    def act(z=z, at=at):
                        rows = self.from_column(column, z, 1 - p.core)
                        self.arrived(rows, s["hs"].at[at], s["hr"].at[at], p.dev_core())

                    when(valid, act)

    def drain(self):
        for copy in self.pending:
            copy.wait_send()
        for valid, copy in self.line_pending:
            when(valid, lambda copy=copy: copy().wait_send())


def run_pipeline(stages, count, extra):
    last = max(lag for lag, _ in stages)
    first = min(lag for lag, _ in stages)
    for step in range(first, count + last):
        ahead = [stage for stage in stages if stage[0] < 0]
        for lag, act in ahead + [(None, act) for act in extra.get(step, ())] + stages[len(ahead) :]:
            if lag is None:
                act()
            elif 0 <= step - lag < count:
                act(step - lag)


def dma(*shape):
    return pltpu.SemaphoreType.DMA(shape)


ANY = pl.BlockSpec(memory_space=pl.ANY)
IN_VMEM = pl.BlockSpec(memory_space=pltpu.VMEM)


def wide(values):
    return values.astype(F32)


class Scatter:
    def __init__(self, place, number, chunk, stage, sums, mids, ends, perms, z_send, z_recv, z_slot, before, put, sems):
        self.p, self.c = place, number
        name, at, _, _ = chunk
        self.half_a = number % 2 == 0
        self.k, self.sent, self.rows, self.lanes = place.geo.kind[name]
        self.part = slice(None)
        self.stage = stage
        self.sum = sums[name].at[at]
        shared, per_layer = name == "a", place.geo.pairs
        self.mid = mids[name].at[at % per_layer if shared else at]
        self.hands_on = shared and at >= per_layer
        self.takes_over = shared and at < place.geo.number[name] - per_layer
        self.heir = None
        self.end = ends[name].at[at]
        self.perm = perms.get(name)
        if name in z_send:
            self.z_send, self.z_recv = z_send[name].at[z_slot], z_recv[name].at[at]
        self.before, self.z_moves = before, []
        self.put = put
        self.sems = sems
        self.pending = []

    def send(self, src, dst, send, recv, device):
        copy = remote(src, dst, send, recv, device)
        copy.start()
        self.pending.append(copy)

    def arrived(self, dst, send, recv, device):
        remote(dst, dst, send, recv, device).wait_recv()

    def start(self):
        p, s, c = self.p, self.sems, self.c
        give = self.stage.at[:, :, :, 1 - p.core]
        self.given = remote(give, self.sum, s["cs"].at[c], s["cr"].at[c], p.dev_core())
        self.given.start()

    def pair(self):
        p, s, c = self.p, self.sems, self.c
        n_y = p.geo.n_y
        self.arrived(self.sum, s["cs"].at[c], s["cr"].at[c], p.dev_core())

        @pl.loop(0, self.k * n_y * 2)
        def _(at):
            where = (at // (2 * n_y), lax.rem(at // 2, n_y), lax.rem(at, 2))
            self.sum[where] = (wide(self.sum[where]) + wide(self.stage[where + (p.core,)])).astype(BF)

        self.given.wait_send()
        self.send_middle()

    def hand_on(self):
        p, s = self.p, self.sems
        if not self.hands_on:
            return
        if self.heir.half_a:
            for step in range(1, p.geo.n_y):
                pl.semaphore_signal(
                    s["fy"].at[self.heir.c, step], inc=1, device_id=p.dev_y(-step), device_id_type=MESH
                )
        else:
            pl.semaphore_signal(s["fx"].at[self.heir.c], inc=1, device_id=p.dev_x(), device_id_type=MESH)

    def send_middle(self):
        p, s, c = self.p, self.sems, self.c
        n_y = p.geo.n_y
        if self.takes_over and self.half_a:
            for step in range(1, n_y):
                pl.semaphore_wait(s["fy"].at[c, step], 1)
        if self.takes_over and not self.half_a:
            pl.semaphore_wait(s["fx"].at[c], 1)
        if self.half_a:
            for step in range(1, n_y):
                self.send(
                    self.sum.at[:, p.y_off(step), :, self.part], self.mid.at[step - 1],
                    s["ms"].at[c, step], s["mr"].at[c, step], p.dev_y(step),
                )
        else:
            for y in range(n_y):
                self.send(
                    self.sum.at[:, y, 1 - p.x, self.part], self.mid.at[y // 2, :, y % 2],
                    s["ms"].at[c, y], s["mr"].at[c, y], p.dev_x(),
                )

    def middle(self):
        p, s, c = self.p, self.sems, self.c
        n_y = p.geo.n_y
        if self.half_a:
            for step in range(1, n_y):
                self.arrived(self.mid.at[step - 1], s["ms"].at[c, step], s["mr"].at[c, step], p.dev_y(step))

            @pl.loop(0, self.k * 2)
            def _(at):
                where = (at // 2, p.y, lax.rem(at, 2), self.part)
                value = wide(self.sum[where])
                for step in range(1, n_y):
                    value = value + wide(self.mid[step - 1, at // 2, lax.rem(at, 2)])
                self.sum[where] = value.astype(BF)

            self.hand_on()
            self.send(
                self.sum.at[:, p.y, 1 - p.x, self.part], self.end.at[0], s["es"].at[c, 0], s["er"].at[c, 0], p.dev_x()
            )
        else:
            for y in range(n_y):
                self.arrived(self.mid.at[y // 2, :, y % 2], s["ms"].at[c, y], s["mr"].at[c, y], p.dev_x())

            @pl.loop(0, self.k * n_y)
            def _(at):
                y = lax.rem(at, n_y)
                where = (at // n_y, y, p.x, self.part)
                value = wide(self.sum[where]) + wide(self.mid[y // 2, at // n_y, lax.rem(y, 2)])
                self.sum[where] = value.astype(BF)

            self.hand_on()
            for step in range(1, n_y):
                self.send(
                    self.sum.at[:, p.y_off(step), p.x, self.part], self.end.at[step - 1],
                    s["es"].at[c, step], s["er"].at[c, step], p.dev_y(step),
                )

    def column_sum(self):
        p, s, c = self.p, self.sems, self.c
        n_y = p.geo.n_y
        if self.half_a:
            arrivals = [(0, self.end.at[0], p.dev_x())]
        else:
            arrivals = [(step, self.end.at[step - 1], p.dev_y(step)) for step in range(1, n_y)]
        value = wide(self.sum[:, p.y, p.x, self.part])
        for at, got, device in arrivals:
            self.arrived(got, s["es"].at[c, at], s["er"].at[c, at], device)
            value = value + wide(got[...])
        return value

    def last(self):
        p, s, c = self.p, self.sems, self.c
        n_z = p.geo.n_z
        value = self.column_sum().astype(BF).reshape(self.k * self.rows, self.lanes)
        if self.perm is not None:
            value = jnp.dot(self.perm[...], value, preferred_element_type=F32).astype(BF)
        if self.before is not None:
            self.before.left()
        self.z_send[...] = value.reshape(n_z, self.sent, self.lanes)
        for step in range(1, n_z):
            copy = remote(
                self.z_send.at[p.z_off(step)], self.z_recv.at[step],
                s["zs"].at[c, step], s["zr"].at[c, step], p.dev_z(step),
            )
            copy.start()
            self.z_moves.append(copy)

    def finish(self):
        p, s, c = self.p, self.sems, self.c
        value = wide(self.z_send[p.z])
        for step in range(1, p.geo.n_z):
            self.arrived(self.z_recv.at[step], s["zs"].at[c, step], s["zr"].at[c, step], p.dev_z(step))
            value = value + wide(self.z_recv[step])
        self.put(value)

    def left(self):
        while self.z_moves:
            self.z_moves.pop().wait_send()

    def drain(self):
        self.left()
        for copy in self.pending:
            copy.wait_send()


class ScatterLine(Scatter):
    def land(self, line):
        self.line = line
        p = self.p
        self.unit = self.rows // p.geo.n_z
        self.part = pl.ds(pl.multiple_of(p.z * self.unit, 16), self.unit)
        self.line_pending = []
        return self

    def slice_of(self, target):
        return pl.ds(target * self.unit, self.unit)

    def line_copy(self, src, way, target, further):
        s = self.sems
        at = (self.c_line, way, target)
        return remote(src, self.line.at[way, target], s["ls"].at[at], s["lr"].at[at], (self.p.d, further))

    def send_middle(self):
        p, last = self.p, self.p.geo.n_z - 1
        for way in range(2):
            ours = p.z == (0 if way == 0 else last)
            targets = range(last, 0, -1) if way == 0 else range(last)
            further = p.z + 1 if way == 0 else p.z - 1
            for target in targets:

                def copy(way=way, target=target, further=further):
                    return self.line_copy(self.sum.at[0, :, :, self.slice_of(target)], way, target, further)

                when(ours, lambda copy=copy: copy().start())
                self.line_pending.append((ours, copy))

    def relay(self, hop):
        p, s, last = self.p, self.sems, self.p.geo.n_z - 1
        for way in range(2):
            here = hop if way == 0 else last - hop
            targets = range(last, here, -1) if way == 0 else range(here)
            further = p.z + 1 if way == 0 else p.z - 1
            for target in targets:

                def copy(way=way, target=target, further=further):
                    return self.line_copy(self.line.at[way, target], way, target, further)

                def act(way=way, target=target, copy=copy):
                    self.add_line(way, target)
                    copy().start()

                when(p.z == here, act)
                self.line_pending.append((p.z == here, copy))

    def add_line(self, way, target):
        s, n_y = self.sems, self.p.geo.n_y
        at = (self.c_line, way, target)
        got = self.line.at[way, target]
        remote(got, got, s["ls"].at[at], s["lr"].at[at], self.p.dev_x()).wait_recv()

        @pl.loop(0, 2 * n_y)
        def _(index):
            where = (index // 2, lax.rem(index, 2))
            mine = wide(self.sum[(0,) + where + (self.slice_of(target),)])
            got[where] = (wide(got[where]) + mine).astype(BF)

    def collect(self):
        p, s, n_y, last = self.p, self.sems, self.p.geo.n_y, self.p.geo.n_z - 1
        for way in range(2):

            def act(way=way):
                at = (self.c_line, way, p.z)
                got = self.line.at[way, p.z]
                remote(got, got, s["ls"].at[at], s["lr"].at[at], p.dev_x()).wait_recv()

                @pl.loop(0, 2 * n_y)
                def _(index):
                    where = (index // 2, lax.rem(index, 2))
                    place = (0,) + where + (self.part,)
                    self.sum[place] = (wide(self.sum[place]) + wide(got[where])).astype(BF)

            when(p.z > 0 if way == 0 else p.z < last, act)
        Scatter.send_middle(self)

    def last(self):
        self.put(self.column_sum().reshape(self.unit, self.lanes))

    def finish(self):
        pass

    def drain(self):
        for valid, copy in self.line_pending:
            when(valid, lambda copy=copy: copy().wait_send())
        Scatter.drain(self)


def mm(left, right):
    return jnp.dot(left, right, preferred_element_type=F32)


def mm_nt(left, right):
    return lax.dot_general(left, right, (((1,), (1,)), ((), ())), preferred_element_type=F32)


def mm_tn(left, right):
    return lax.dot_general(left, right, (((0,), (0,)), ((), ())), preferred_element_type=F32)


def mean_of(values):
    return jnp.sum(values, -1, keepdims=True) * (1.0 / values.shape[-1])


def normal(values):
    centered = values - mean_of(values)
    scale = lax.rsqrt(mean_of(centered * centered) + epsilon)
    return centered * scale, scale


def norm_rows(source, gain, shift, target, block=32):
    @pl.loop(0, source.shape[0] // block)
    def _(at):
        rows = pl.ds(pl.multiple_of(at * block, block), block)
        unit, _ = normal(source[rows, :])
        target[rows, :] = (unit * gain + shift).astype(target.dtype)


def fold(values):
    total = values[0:8]
    for at in range(8, values.shape[0], 8):
        total = total + values[at : at + 8]
    return total


def norm_rows_back(source, gain, incoming, emit, sums, block=32):
    sums[...] = jnp.zeros_like(sums)

    @pl.loop(0, source.shape[0] // block)
    def _(at):
        rows = pl.ds(pl.multiple_of(at * block, block), block)
        unit, scale = normal(source[rows, :])
        back = incoming[rows, :]
        sums[0] += fold(back * unit)
        sums[1] += fold(back)
        inner = back * gain
        emit(rows, scale * (inner - mean_of(inner) - unit * mean_of(inner * unit)))


ROOT = 0.7978845608028654
CUBE = 0.044715


def gelu_parts(values):
    square = values * values
    curve = jnp.tanh(ROOT * (values + CUBE * (values * square)))
    return square, curve


class Layer:
    def __init__(self, refs, weight_a, weight_b, vec_d, vec_f, layer, heads):
        self.__dict__.update(refs)
        self.weight_a, self.weight_b = weight_a, weight_b
        self.vec_d, self.vec_f = vec_d, vec_f
        self.layer, self.heads = layer, heads

    def gain(self, at):
        return self.vec_d[self.layer * 10 + at : self.layer * 10 + at + 1, :]

    def shift(self, at):
        return self.gain(3 + at)

    def gain_f(self, at):
        return self.vec_f[self.layer * 3 + at : self.layer * 3 + at + 1, :]

    def lane_half(self, values, side):
        lane = lax.broadcasted_iota(jnp.int32, values.shape, 1)
        return (lane < HEAD_DIM) == (side == 0)

    def forward_norm(self):
        norm_rows(self.x, self.gain(0), self.shift(0), self.normed)

    def forward_qkv(self, part):
        value = mm(self.normed[...], self.weight_a(part))
        if part != 1:
            value = value + self.shift(3 if part == 0 else 4)
        self.qkv[part] = value.astype(BF)

    def forward_attention(self):
        valid = self.mask[...] > 0.5

        @pl.loop(0, self.heads // 2)
        def _(pair):
            lanes = pl.ds(pl.multiple_of(pair * 128, 128), 128)
            queries, keys, values = [self.qkv[part, :, lanes] for part in range(3)]
            context = None
            for side in range(2):
                half = self.lane_half(queries, side)
                scores = mm_nt(jnp.where(half, queries, jnp.zeros_like(queries)), keys)
                scores = jnp.where(valid, scores * HEAD_DIM**-0.5, -1e9)
                top = jnp.max(scores, -1, keepdims=True)
                grown = jnp.exp(scores - top)
                prob = grown / jnp.sum(grown, -1, keepdims=True)
                self.prob[2 * pair + side] = prob
                product = mm(prob.astype(BF), values)
                context = product if side == 0 else jnp.where(half, product, context)
            self.context[:, lanes] = context

    def forward_out(self):
        norm_rows(self.context, self.gain(1), self.shift(1), self.sub)
        self.after[...] = self.x[...] + (mm(self.sub[...], self.weight_a(3)) + self.shift(5))
        norm_rows(self.after, self.gain(2), self.shift(2), self.normed_ffn)

    def forward_up(self, part):
        width = self.x.shape[1]
        lanes = slice(part * width, (part + 1) * width)
        self.hidden[:, lanes] = mm(self.normed_ffn[...], self.weight_a(4 + part)) + self.gain_f(1)[:, lanes]

    def forward_gelu(self):
        @pl.loop(0, self.x.shape[0] // 16)
        def _(at):
            rows = pl.ds(pl.multiple_of(at * 16, 16), 16)
            values = self.hidden[rows, :]
            _, curve = gelu_parts(values)
            unit, _ = normal(0.5 * values * (1.0 + curve))
            self.sub_ffn[rows, :] = (unit * self.gain_f(0) + self.gain_f(2)).astype(BF)

    def forward_down(self, lanes):
        value = mm(self.sub_ffn[...], self.weight_b(slice(None), lanes))
        self.x_next[:, lanes] = self.after[:, lanes] + (value + self.shift(6)[:, lanes])


    def store_sums_d(self, at, sums):
        row = self.layer * 10 + at
        self.grad_d[row : row + 1, :] = jnp.sum(sums, 0, keepdims=True)

    def store_sums_f(self, at, sums):
        row = self.layer * 3 + at
        self.grad_f[row : row + 1, :] = jnp.sum(sums, 0, keepdims=True)

    def backward_start(self):
        self.low[...] = self.back[...].astype(BF)
        self.store_sums_d(9, wide(self.low[...]))

    def grad_up(self, part):
        width = self.x.shape[1]
        return mm_tn(self.normed_ffn[...], self.d_hidden[:, part * width : (part + 1) * width])

    def grad_out(self):
        return mm_tn(self.sub[...], self.low[...])

    def grad_qkv(self, part):
        return mm_tn(self.normed[...], self.d_qkv[part])

    def backward_down(self):
        width = self.x.shape[1]
        for part in range(self.hidden.shape[1] // width):
            lanes = slice(part * width, (part + 1) * width)
            self.wide_back[:, lanes] = mm_nt(self.low[...], self.weight_b(lanes, slice(None)))

    def backward_gelu(self):
        self.sums_f[...] = jnp.zeros_like(self.sums_f)

        @pl.loop(0, self.x.shape[0] // 16)
        def _(at):
            rows = pl.ds(pl.multiple_of(at * 16, 16), 16)
            values = self.hidden[rows, :]
            square, curve = gelu_parts(values)
            unit, scale = normal(0.5 * values * (1.0 + curve))
            back = self.wide_back[rows, :]
            self.sums_f[0] += fold(back * unit)
            self.sums_f[1] += fold(back)
            inner = back * self.gain_f(0)
            d_gelu = scale * (inner - mean_of(inner) - unit * mean_of(inner * unit))
            slope = 0.5 * (1.0 + curve) + 0.5 * values * (1.0 - curve * curve) * (
                ROOT * (1.0 + 3.0 * CUBE * square)
            )
            low = (d_gelu * slope).astype(BF)
            self.d_hidden[rows, :] = low
            self.sums_f[2] += fold(wide(low))

        self.store_sums_f(0, self.sums_f[0])
        self.store_sums_f(2, self.sums_f[1])
        self.store_sums_f(1, self.sums_f[2])

    def backward_up(self):
        width = self.x.shape[1]
        total = None
        for part in range(self.hidden.shape[1] // width):
            lanes = slice(part * width, (part + 1) * width)
            value = mm_nt(self.d_hidden[:, lanes], self.weight_a(4 + part))
            if part == 0:
                self.incoming[...] = value
            else:
                self.incoming[...] += value

        def emit(rows, value):
            value = self.back[rows, :] + value
            self.back[rows, :] = value
            self.low[rows, :] = value.astype(BF)

        norm_rows_back(self.after, self.gain(2), self.incoming, emit, self.sums_d)
        self.store_sums_d(2, self.sums_d[0])
        self.store_sums_d(5, self.sums_d[1])

    def backward_out(self):
        self.store_sums_d(8, wide(self.low[...]))
        self.incoming[...] = mm_nt(self.low[...], self.weight_a(3))

        def emit(rows, value):
            self.low[rows, :] = value.astype(BF)

        norm_rows_back(self.context, self.gain(1), self.incoming, emit, self.sums_d)
        self.store_sums_d(1, self.sums_d[0])
        self.store_sums_d(4, self.sums_d[1])

    def backward_attention(self):
        @pl.loop(0, self.heads // 2)
        def _(pair):
            lanes = pl.ds(pl.multiple_of(pair * 128, 128), 128)
            queries, keys, values = [self.qkv[part, :, lanes] for part in range(3)]
            d_context = self.low[:, lanes]
            found = [None] * 3
            for side in range(2):
                half = self.lane_half(d_context, side)
                prob = self.prob[2 * pair + side]
                d_prob = mm_nt(jnp.where(half, d_context, jnp.zeros_like(d_context)), values)
                dot = jnp.sum(prob * d_prob, -1, keepdims=True)
                d_scores = (prob * (d_prob - dot)).astype(BF)
                new = (
                    mm(d_scores, keys) * HEAD_DIM**-0.5,
                    mm_tn(d_scores, queries) * HEAD_DIM**-0.5,
                    mm_tn(prob.astype(BF), d_context),
                )
                found = [n if side == 0 else jnp.where(half, n, f) for n, f in zip(new, found)]
            for part in range(3):
                self.d_qkv[part, :, lanes] = found[part].astype(BF)

    def backward_qkv(self):
        self.store_sums_d(6, wide(self.d_qkv[0]))
        self.store_sums_d(7, wide(self.d_qkv[2]))
        for part in range(3):
            value = mm_nt(self.d_qkv[part], self.weight_a(part))
            if part == 0:
                self.incoming[...] = value
            else:
                self.incoming[...] += value

        def emit(rows, value):
            self.back[rows, :] = self.back[rows, :] + value

        norm_rows_back(self.x, self.gain(0), self.incoming, emit, self.sums_d)
        self.store_sums_d(0, self.sums_d[0])
        self.store_sums_d(3, self.sums_d[1])


def saved_shapes(rows, width, wide_width, heads):
    return {
        "normed": ((rows, width), BF),
        "qkv": ((3, rows, width), BF),
        "prob": ((heads, rows, rows), F32),
        "context": ((rows, width), F32),
        "sub": ((rows, width), BF),
        "after": ((rows, width), F32),
        "normed_ffn": ((rows, width), BF),
        "hidden": ((rows, wide_width), F32),
        "sub_ffn": ((rows, wide_width), BF),
    }


def work_shapes(rows, width, wide_width):
    return {
        "low": ((rows, width), BF),
        "incoming": ((rows, width), F32),
        "wide_back": ((rows, wide_width), F32),
        "d_qkv": ((3, rows, width), BF),
        "sums_d": ((2, 8, width), F32),
        "sums_f": ((3, 8, wide_width), F32),
    }


def spread_tables(geo):
    tables = []
    for width, real in ((geo.width, geo.rows_a), (geo.wide_width, geo.rows_b)):
        at = np.arange(width)
        owner = (at[None, :] // real == np.arange(geo.owners)[:, None]).astype(np.float32)
        tables += [jnp.asarray(owner, BF), jnp.asarray(at[None, :] % real, jnp.int32)]
    return tables


def unpack_vectors(geo, whole_v, wide_v, tables, vec_d, vec_f):
    owner_d, rest_d, owner_f, rest_f = tables
    lines = geo.kind["v"][1]
    wide_v[...] = wide(whole_v[0])
    line_of = lambda at: wide_v[pl.ds(at, geo.owners, stride=lines), :].astype(BF)
    pick_d = lax.broadcasted_iota(jnp.int32, (geo.slot, geo.width), 0) == rest_d[...]
    for line in range(geo.lines_d):
        spread = mm_tn(line_of(line), owner_d[...])
        for at in range(geo.per_row):
            part = spread[at * geo.slot : (at + 1) * geo.slot]
            row = line * geo.per_row + at
            if row < geo.layers * 10:
                vec_d[row : row + 1, :] = jnp.sum(jnp.where(pick_d, part, 0.0), 0, keepdims=True)
    pick_f = lax.broadcasted_iota(jnp.int32, (128, geo.width), 0)
    for row in range(geo.layers * 3):
        line = line_of(geo.lines_d + row)
        for first in range(0, geo.wide_width, geo.width):
            lanes = slice(first, first + geo.width)
            spread = jnp.where(pick_f == rest_f[:, lanes], mm_tn(line, owner_f[:, lanes]), 0.0)
            vec_f[row : row + 1, lanes] = jnp.sum(spread, 0, keepdims=True)


GATHER_SEMS = (
    "lz", "lo", "zs", "zr", "xs", "xr", "ys", "yr", "ds", "dr", "cs", "cr",
    "gl", "gx", "gy", "gd", "gs", "gr", "hs", "hr",
)
LINE_FIRST = (1, 6)


def forward_kernel(geo, names_perm, saved_names, *refs):
    refs = list(refs)
    take = lambda number: [refs.pop(0) for _ in range(number)]
    sources = dict(zip(geo.kinds, take(len(geo.kinds))))
    perms = dict(zip(names_perm, take(len(names_perm))))
    act_ref, mask_ref = take(2)
    tables = take(4)
    out_ref, vec_d, vec_f, kept_a, kept_b, kept_x = take(6)
    kept = [dict(zip(saved_names, take(len(saved_names)))) for _ in range(geo.layers)]
    wholes = dict(zip(("a", "v", "b"), take(3)))
    wholes.update({name: wholes["b"] for name in geo.down})
    bufs = dict(zip(geo.plain, take(len(geo.plain))))
    units = dict(zip(names_perm, take(len(names_perm))))
    saved = [dict(zip(saved_names, take(len(saved_names)))) for _ in range(geo.layers)]
    xs, wide_v, keep_sem = take(3)
    sems = dict(zip(GATHER_SEMS, take(len(GATHER_SEMS))))
    place = Place(geo)
    chunks, line_chunks = [("v", 0, 0, 0)], []
    for layer in range(geo.layers):
        chunks += [chunk_a(geo, layer, pair) for pair in range(geo.pairs)]
        for name in geo.down:
            (line_chunks if name == "l" else chunks).append(chunk_down(geo, layer, name))
    moves = [
        Gather(place, at, chunk, sources, bufs, units, perms, wholes, sems)
        for at, chunk in enumerate(chunks)
    ]
    lines = [
        GatherLine(place, at, chunk, sources, wholes, sems) for at, chunk in enumerate(line_chunks)
    ]
    keeps = []

    def keep(src, dst):
        copy = pltpu.make_async_copy(src, dst, keep_sem.at[len(keeps)])
        copy.start()
        keeps.append(copy)

    net = []
    for layer in range(geo.layers):
        fields = dict(saved[layer], x=xs.at[layer], x_next=xs.at[layer + 1], mask=mask_ref)
        read_a = lambda at, layer=layer: wholes["a"][layer * geo.blocks + at]
        read_b = lambda rows, lanes, layer=layer: wholes["b"][layer, rows, lanes]
        net.append(Layer(fields, read_a, read_b, vec_d, vec_f, layer, geo.width // HEAD_DIM))

    def compute(number):
        name, at, lead, first = chunks[number]
        if geo.lined and name == "c":
            lines[lead].arrive()
            down(lead, *geo.lanes_of["l"])
        moves[number].arrive()
        if name == "v":
            unpack_vectors(geo, wholes["v"], wide_v, tables, vec_d, vec_f)
            return
        k, _, _, lanes = geo.kind[name]
        layer = at // geo.pairs if name == "a" else at
        one = net[layer]
        save = lambda *found: [keep(saved[layer][field], kept[layer][field]) for field in found]
        if name == "a":
            keep(wholes["a"].at[pl.ds(lead, k)], kept_a.at[pl.ds(lead, k)])
            pair = at % geo.pairs
            if pair == 0:
                one.forward_norm()
                one.forward_qkv(0)
                one.forward_qkv(1)
            elif pair == 1:
                one.forward_qkv(2)
                save("normed", "qkv")
                one.forward_attention()
                one.forward_out()
                save("prob", "context", "sub", "after", "normed_ffn")
            else:
                one.forward_up(2 * pair - 4)
                one.forward_up(2 * pair - 3)
                if pair == geo.pairs - 1:
                    one.forward_gelu()
                    save("hidden", "sub_ffn")
        else:
            down(layer, first, lanes)
            if name == geo.down[-1] and layer < geo.layers - 1:
                keep(xs.at[layer + 1], kept_x.at[layer + 1])

    def down(layer, first, lanes):
        where = pl.ds(first, lanes)
        keep(wholes["b"].at[layer, :, where], kept_b.at[layer, :, where])
        net[layer].forward_down(slice(first, first + lanes))

    extra = {}
    for layer, line in enumerate(lines):
        plan = [line.start, line.forward, line.corner]
        plan += [
            lambda line=line, hop=hop, half=half: line.relay(hop, half)
            for hop in range(geo.n_z)
            for half in range(2)
        ]
        needed = chunks.index(chunk_down(geo, layer, "c")) + 3
        for at, act in enumerate(plan):
            step = at - 2 if at < 3 else LINE_FIRST[min(layer, 1)] + at - 3
            extra.setdefault(min(step, needed), []).append(act)

    xs[0] = wide(act_ref[...])
    keep(xs.at[0], kept_x.at[0])
    place.greet()
    run_pipeline(
        [
            (-2, lambda c: moves[c].start_z()),
            (0, lambda c: moves[c].own()),
            (1, lambda c: moves[c].forward()),
            (2, lambda c: moves[c].corner()),
            (3, compute),
        ],
        len(moves),
        extra,
    )
    out_ref[...] = xs[geo.layers].astype(BF)
    for move in moves + lines:
        move.drain()
    for copy in keeps:
        copy.wait()


def run_forward(geo, sources, act, mask):
    names_perm = [name for name in geo.plain if geo.permuted(name)]
    perms = [jnp.asarray(geo.permutation(name), BF) for name in names_perm]
    rows, width = act.shape
    total = sum(geo.number.values())
    heads = width // HEAD_DIM
    saved = saved_shapes(rows, width, geo.wide_width, heads)
    bufs, units, wholes = [], [], []
    for name in geo.plain:
        k, sent, unit, lanes = geo.kind[name]
        bufs.append(pltpu.VMEM((geo.number[name], geo.n_z * sent, lanes), BF))
        if name in names_perm:
            units.append(pltpu.VMEM((geo.number[name], k, unit, lanes), BF))
    wholes = [(geo.whole_shape(name), BF) for name in ("a", "v", "c")]
    n_y, n_z = geo.n_y, geo.n_z
    n_keeps = geo.layers * (len(saved) + geo.pairs + len(geo.down) + 1)
    vec_rows = geo.layers * 10
    outs = [
        jax.ShapeDtypeStruct((rows, width), BF),
        jax.ShapeDtypeStruct((vec_rows, width), F32),
        jax.ShapeDtypeStruct((geo.layers * 3, geo.wide_width), F32),
        jax.ShapeDtypeStruct(*wholes[0]),
        jax.ShapeDtypeStruct(*wholes[2]),
        jax.ShapeDtypeStruct((geo.layers, rows, width), F32),
    ] + [jax.ShapeDtypeStruct(*saved[name]) for _ in range(geo.layers) for name in saved]
    found = pl.pallas_call(
        functools.partial(forward_kernel, geo, names_perm, list(saved)),
        out_shape=outs,
        in_specs=[IN_VMEM] * (len(sources) + len(perms) + 6),
        out_specs=[IN_VMEM] * 3 + [ANY] * (len(outs) - 3),
        scratch_shapes=[pltpu.VMEM(*whole) for whole in wholes]
        + bufs
        + units
        + [pltpu.VMEM(*saved[name]) for _ in range(geo.layers) for name in saved]
        + [
            pltpu.VMEM((geo.layers + 1, rows, width), F32),
            pltpu.VMEM(wholes[1][0][1:], F32),
            dma(n_keeps),
            dma(total),
            dma(total),
            dma(total, n_z),
            dma(total, n_z),
            dma(total),
            dma(total),
            dma(total, n_y),
            dma(total, n_y),
            dma(total, n_y),
            dma(total, n_y),
            dma(total, 2 * n_y),
            dma(total, 2 * n_y),
            dma(geo.layers),
            dma(geo.layers, 2),
            dma(geo.layers, 2, n_y),
            dma(geo.layers, 2, n_y),
        ]
        + [dma(geo.layers, 2, n_z, 2 * n_y)] * 4,
        compiler_params=pltpu.CompilerParams(
            collective_id=0, has_side_effects=True, vmem_limit_bytes=60 * 2**20
        ),
    )(*sources, *perms, act, mask, *spread_tables(geo))
    names = list(saved)
    kept = [dict(zip(names, found[6 + layer * len(names) :])) for layer in range(geo.layers)]
    return found[:6], kept


def pack_gradients(geo, grad_d, grad_f, tables, wide_v, stage_v):
    owner_d, rest_d, owner_f, rest_f = tables
    lines = geo.kind["v"][1]
    wide_v[...] = jnp.zeros_like(wide_v)
    pick_d = lax.broadcasted_iota(jnp.int32, (geo.slot, geo.width), 0) == rest_d[...]
    for line in range(geo.lines_d):
        parts = []
        for at in range(geo.per_row):
            row = line * geo.per_row + at
            if row < geo.layers * 10:
                parts.append(jnp.where(pick_d, grad_d[row : row + 1, :], 0.0))
            else:
                parts.append(jnp.zeros(pick_d.shape, F32))
        wide_v[pl.ds(line, geo.owners, stride=lines), :] = mm_nt(
            owner_d[...], jnp.concatenate(parts, 0).astype(BF)
        )
    pick_f = lax.broadcasted_iota(jnp.int32, (128, geo.width), 0)
    for row in range(geo.layers * 3):
        total = None
        for first in range(0, geo.wide_width, geo.width):
            lanes = slice(first, first + geo.width)
            part = jnp.where(pick_f == rest_f[:, lanes], grad_f[row : row + 1, lanes], 0.0).astype(BF)
            part = mm_nt(owner_f[:, lanes], part)
            total = part if total is None else total + part
        wide_v[pl.ds(geo.lines_d + row, geo.owners, stride=lines), :] = total
    stage_v[...] = wide_v[...].astype(BF).reshape(stage_v.shape)


class Ring:
    def __init__(self, sources, slots, sems):
        self.slots, self.size, self.used = slots, slots.shape[0], 0
        self.copies = [
            pltpu.make_async_copy(source, slots.at[at % self.size], sems.at[at % self.size])
            for at, source in enumerate(sources)
        ]
        for copy in self.copies[: self.size]:
            copy.start()

    def next(self):
        at = self.used
        self.used += 1
        if 0 < at and at - 1 + self.size < len(self.copies):
            self.copies[at - 1 + self.size].start()
        self.copies[at].wait()
        return self.slots[at % self.size]


SCATTER_SEMS = ("cs", "cr", "ms", "mr", "es", "er", "zs", "zr", "ls", "lr", "fx", "fy")
Z_SLOTS = 3
LINE_LAGS = (4, 3)
SCATTER_LAGS = (0, 1, 3, 5, 7)


def ring_slots(geo):
    return 3 if geo.roomy else 2


def backward_kernel(geo, names_perm, names, *refs):
    refs = list(refs)
    take = lambda number: [refs.pop(0) for _ in range(number)]
    by_kind = lambda kinds=geo.kinds: dict(zip(kinds, take(len(kinds))))
    saved_names, work_names = names
    layers, blocks, width = geo.layers, geo.blocks, geo.width
    perms = dict(zip(names_perm, take(len(names_perm))))
    cot_ref, vec_d, vec_f = take(3)
    tables = take(4)
    whole_a, whole_b, kept_x = take(3)
    kept = [dict(zip(saved_names, take(len(saved_names)))) for _ in range(layers)]
    for layer in range(layers):
        kept[layer]["x"] = kept_x.at[layer]
    back_ref, out_qkv, out_out, out_up, out_down, out_d, out_f = take(7)
    fields = dict(zip(saved_names, take(len(saved_names))))
    fields.update(zip(work_names, take(len(work_names))))
    stages, sums, mids, ends = [by_kind() for _ in range(4)]
    z_send, z_recv = [by_kind(geo.plain) for _ in range(2)]
    line_refs = take(1) if geo.lined else []
    x_ref, grad_d, grad_f, wide_v, slots = take(5)
    last_low, last_ffn = take(2) if geo.roomy else (None, None)
    sem_l, sem_w = take(2)
    sems = dict(zip(SCATTER_SEMS, take(len(SCATTER_SEMS))))
    fields.update(d_hidden=fields["sub_ffn"], x=x_ref, back=back_ref, grad_d=grad_d, grad_f=grad_f)
    place = Place(geo)

    def writer(chunk):
        name, at, lead, first = chunk
        rows_a, rows_b, lines = geo.rows_a, geo.rows_b, geo.lines_d

        def put_a(value):
            layer = at // geo.pairs
            for side in range(2):
                block = 2 * (at % geo.pairs) + side
                piece = value[side * rows_a : (side + 1) * rows_a]
                if block < 3:
                    out_qkv[layer, :, block * width : (block + 1) * width] = piece
                elif block == 3:
                    out_out[layer] = piece
                else:
                    out_up[layer, :, (block - 4) * width : (block - 3) * width] = piece

        def put_down(value):
            out_down[lead, :, first : first + value.shape[1]] = value[:rows_b]

        def put_v(value):
            out_d[...] = value[:lines]
            out_f[...] = value[lines : lines + layers * 3]

        return {"a": put_a, "v": put_v}.get(name, put_down)

    order, seen = [], {name: [] for name in geo.kinds}
    early = {layer: geo.down for layer in range(layers)}
    late = ("c", "d") if geo.roomy else ()
    early[0] = tuple(name for name in geo.down if name not in late)
    for layer in reversed(range(layers)):
        early[layer] = early[layer][::-1]
        order += [chunk_down(geo, layer, name) for name in early[layer]]
        order += [chunk_a(geo, layer, pair) for pair in list(range(2, geo.pairs)) + [1, 0]]
    order.append(("v", 0, 0, 0))
    order += [chunk_down(geo, 0, name) for name in late]
    moves, stage_of = [], []
    for number, chunk in enumerate(order):
        name = chunk[0]
        stage = stages[name].at[len(seen[name]) % stages[name].shape[0]]
        slots_z = z_send[name].shape[0] if name in z_send else 1
        z_slot = len(seen[name]) % slots_z
        before = seen[name][-slots_z] if len(seen[name]) >= slots_z else None
        move = (ScatterLine if name == "l" else Scatter)(
            place, number, chunk, stage, sums, mids, ends, perms, z_send, z_recv, z_slot, before,
            writer(chunk), sems,
        )
        if name == "l":
            move.c_line = len(seen[name])
            move.land(line_refs[0].at[move.c_line])
        seen[name].append(move)
        stage_of.append(stage)
        moves.append(move)
    for number, chunk in enumerate(order):
        if chunk[0] == "a" and chunk[1] >= geo.pairs:
            moves[number].heir = moves[[later[:2] for later in order].index(("a", chunk[1] - geo.pairs))]
    step, plan = [0], {}
    for number, chunk in enumerate(order):
        move = moves[number]
        acts = [move.start, move.pair, move.middle, move.last, move.finish]
        lags = list(SCATTER_LAGS)
        if chunk[0] == "l":
            hops = [lambda move=move, hop=hop: move.relay(hop) for hop in range(1, geo.n_z - 1)]
            acts[2:2] = hops + [move.collect]
            first, each = LINE_LAGS
            lags[2:] = [first + each * at for at in range(len(hops) + 1)]
            lags += [lags[-1] + 1, lags[-1] + 2, lags[-1] + 2]
        for lag, act in zip(lags, acts):
            plan.setdefault(number + lag, []).append((lag, act))

    def serve():
        for _, act in sorted(plan.get(step[0], []), key=lambda pair: pair[0]):
            act()
        step[0] += 1

    def stage_down(name, rows_ref, low_ref):
        unit = geo.kind[name][2]
        first, lanes = geo.lanes_of[name]
        for column in range(geo.n_dp // 2):
            rows = slice(column * 2 * unit, (column + 1) * 2 * unit)
            value = mm_tn(rows_ref[:, rows], low_ref[:, first : first + lanes])
            stage_of[step[0]][0, column // 2, column % 2] = value.astype(BF).reshape(2, unit, lanes)

    def stage_a(side, value):
        stage_of[step[0]][side] = value.astype(BF).reshape(geo.n_y, 2, 2, -1, width)

    loads = {}
    field_names = ["x"] + list(saved_names)

    def fetch(layer, *found):
        for name in found:
            loads[name] = pltpu.make_async_copy(
                kept[layer][name], fields[name], sem_l.at[field_names.index(name)]
            )
            loads[name].start()

    def ready(*found):
        for name in found:
            loads[name].wait()

    fetch(layers - 1, "sub_ffn", "hidden", "normed_ffn", "after", "sub", "context", "prob", "qkv", "normed", "x")
    sources = []
    for layer in reversed(range(layers)):
        parts = geo.wide_width // width
        sources += [whole_b.at[layer, pl.ds(part * width, width)] for part in range(parts)]
        sources += [whole_a.at[layer * blocks + at] for at in list(range(4, blocks)) + [3, 0, 1, 2]]
    ring = Ring(sources, slots, sem_w)
    cot_copy = pltpu.make_async_copy(cot_ref, back_ref, sem_l.at[len(field_names)])
    cot_copy.start()
    place.greet()
    cot_copy.wait()
    for layer in reversed(range(layers)):
        one = Layer(
            fields, lambda at: ring.next(), lambda rows, lanes: ring.next(), vec_d, vec_f, layer,
            width // HEAD_DIM,
        )
        again = (lambda *found: fetch(layer - 1, *found)) if layer > 0 else (lambda *found: None)
        one.backward_start()
        ready("sub_ffn")
        for name in early[layer]:
            stage_down(name, one.sub_ffn, one.low)
            serve()
        if layer == 0 and late:
            last_low[...] = one.low[...]
            last_ffn[...] = one.sub_ffn[...]
        one.backward_down()
        ready("hidden")
        one.backward_gelu()
        again("hidden")
        ready("normed_ffn")
        for pair in range(2, geo.pairs):
            stage_a(0, one.grad_up(2 * pair - 4))
            stage_a(1, one.grad_up(2 * pair - 3))
            serve()
        again("normed_ffn")
        ready("after")
        one.backward_up()
        again("after", "sub_ffn")
        ready("sub", "context")
        stage_a(1, one.grad_out())
        one.backward_out()
        again("sub", "context")
        ready("prob", "qkv")
        one.backward_attention()
        again("prob", "qkv")
        ready("normed")
        stage_a(0, one.grad_qkv(2))
        serve()
        stage_a(0, one.grad_qkv(0))
        stage_a(1, one.grad_qkv(1))
        serve()
        again("normed")
        ready("x")
        one.backward_qkv()
        again("x")
    pack_gradients(geo, grad_d, grad_f, tables, wide_v, stage_of[step[0]])
    serve()
    for name in late:
        stage_down(name, last_ffn, last_low)
        serve()
    while step[0] <= max(plan):
        serve()
    for move in moves:
        move.drain()


def run_backward(geo, cot, vec_d, vec_f, whole_a, whole_b, kept_x, kept):
    rows, width = cot.shape
    layers, n_y, n_z = geo.layers, geo.n_y, geo.n_z
    heads = width // HEAD_DIM
    saved, work = saved_shapes(rows, width, geo.wide_width, heads), work_shapes(rows, width, geo.wide_width)
    names = (list(saved), list(work))
    names_perm = [name for name in geo.plain if geo.permuted(name)]
    perms = [jnp.asarray(geo.permutation(name).T, BF) for name in names_perm]
    total = sum(geo.number.values())
    groups = [[] for _ in range(6)]
    for name in geo.kinds:
        k, sent, unit, lanes = geo.kind[name]
        number = geo.number[name]
        mid_steps = max(n_y - 1, (n_y + 1) // 2)
        groups[0].append(pltpu.VMEM((2 if name == "a" else 1, k, n_y, 2, 2, unit, lanes), BF))
        groups[1].append(pltpu.VMEM((number, k, n_y, 2, unit, lanes), BF))
        landing = geo.pairs if name == "a" else number
        unit = sent if name == "l" else unit
        groups[2].append(pltpu.VMEM((landing, mid_steps, k, 2, unit, lanes), BF))
        groups[3].append(pltpu.VMEM((number, mid_steps, k, unit, lanes), BF))
        if name == "l":
            continue
        groups[4].append(pltpu.VMEM((min(number, Z_SLOTS), n_z, sent, lanes), BF))
        groups[5].append(pltpu.VMEM((number, n_z, sent, lanes), BF))
    scratch = [pltpu.VMEM(*saved[name]) for name in saved] + [pltpu.VMEM(*work[name]) for name in work]
    scratch += sum(groups, [])
    if geo.lined:
        _, sent, _, lanes = geo.kind["l"]
        scratch.append(pltpu.VMEM((layers, 2, n_z, n_y, 2, sent, lanes), BF))
    scratch += [
        pltpu.VMEM((rows, width), F32),
        pltpu.VMEM((layers * 10, width), F32),
        pltpu.VMEM((layers * 3, geo.wide_width), F32),
        pltpu.VMEM((geo.owners * geo.kind["v"][1], 128), F32),
        pltpu.VMEM((ring_slots(geo), width, width), BF),
    ]
    if geo.roomy:
        scratch += [pltpu.VMEM((rows, width), BF), pltpu.VMEM((rows, geo.wide_width), BF)]
    scratch += [
        dma(2 + len(saved)),
        dma(ring_slots(geo)),
        dma(total),
        dma(total),
        dma(total, n_y),
        dma(total, n_y),
        dma(total, n_y),
        dma(total, n_y),
        dma(total, n_z),
        dma(total, n_z),
        dma(layers, 2, n_z),
        dma(layers, 2, n_z),
        pltpu.SemaphoreType.REGULAR((total,)),
        pltpu.SemaphoreType.REGULAR((total, n_y)),
    ]
    return pl.pallas_call(
        functools.partial(backward_kernel, geo, names_perm, names),
        out_shape=[
            jax.ShapeDtypeStruct((rows, width), F32),
            jax.ShapeDtypeStruct((layers, geo.rows_a, 3 * width), F32),
            jax.ShapeDtypeStruct((layers, geo.rows_a, width), F32),
            jax.ShapeDtypeStruct((layers, geo.rows_a, geo.wide_width), F32),
            jax.ShapeDtypeStruct((layers, geo.rows_b, width), F32),
            jax.ShapeDtypeStruct((geo.lines_d, 128), F32),
            jax.ShapeDtypeStruct((layers * 3, 128), F32),
        ],
        in_specs=[IN_VMEM] * len(perms) + [ANY] + [IN_VMEM] * 6 + [ANY] * (3 + layers * len(saved)),
        out_specs=[IN_VMEM] * 7,
        scratch_shapes=scratch,
        compiler_params=pltpu.CompilerParams(
            collective_id=1, has_side_effects=True, vmem_limit_bytes=63 * 2**20
        ),
    )(
        *perms, cot, vec_d, vec_f, *spread_tables(geo), whole_a, whole_b, kept_x,
        *[kept[layer][name] for layer in range(layers) for name in saved],
    )


def pack_kernel(geo, *refs):
    act_short, act_long, len_short, len_long, w_qkv, w_out, w_up, w_down = refs[:8]
    gains_d, shifts_d, gains_ff, shifts_ff, cot_short, cot_long = refs[8:14]
    sources = dict(zip(geo.kinds, refs[14:]))
    act, mask, cot, lines = refs[14 + len(geo.kinds) :]
    width, rows_a, rows_b = geo.width, geo.rows_a, geo.rows_b

    def block(layer, at):
        if at == 3:
            return wide(w_out[layer])
        first = at if at < 3 else at - 4
        return wide((w_qkv if at < 3 else w_up)[layer, :, first * width : (first + 1) * width])

    def filled(pieces, rows):
        have = sum(piece.shape[0] for piece in pieces)
        if have < rows:
            pieces = pieces + [jnp.zeros((rows - have, pieces[0].shape[1]), F32)]
        return (jnp.concatenate(pieces, 0) if len(pieces) > 1 else pieces[0]).astype(BF)

    for layer in range(geo.layers):
        for pair in range(geo.pairs):
            pieces = [block(layer, 2 * pair), block(layer, 2 * pair + 1)]
            sources["a"][layer * geo.pairs + pair] = filled(pieces, geo.kind["a"][1])
        for name in geo.down:
            first, lanes = geo.lanes_of[name]
            piece = w_down[layer, :, first : first + lanes]
            if rows_b != geo.kind[name][1]:
                piece = filled([wide(piece)], geo.kind[name][1])
            sources[name][layer] = piece
    lines[...] = jnp.zeros_like(lines)
    gains_wide = wide(gains_ff[...])
    for layer in range(geo.layers):
        gains, shifts, shifts_wide = wide(gains_d[layer]), wide(shifts_d[layer]), wide(shifts_ff[layer])
        for at in range(10):
            line, lane = divmod(layer * 10 + at, geo.per_row)
            value = gains[at : at + 1] if at < 3 else shifts[at - 3 : at - 2]
            lines[line : line + 1, lane * geo.slot : lane * geo.slot + rows_a] = value
        for at in range(3):
            line = geo.lines_d + layer * 3 + at
            lines[line : line + 1, :rows_b] = gains_wide[layer : layer + 1] if at == 0 else shifts_wide[at - 1 : at]
    sources["v"][0] = lines[...].astype(BF)
    short = act_short.shape[0]
    act[:short] = act_short[...]
    act[short:] = act_long[...]
    rows = act.shape[0]

    def valid(shape, dim):
        at = lax.broadcasted_iota(jnp.int32, shape, dim)
        return jnp.where(jnp.where(at < short, at - len_short[0], at - short - len_long[0]) < 0, 1.0, 0.0)

    def bucket(dim):
        return jnp.where(lax.broadcasted_iota(jnp.int32, (rows, rows), dim) < short, 0, 1)

    mask[...] = jnp.where(bucket(0) == bucket(1), valid((rows, rows), 1), 0.0)
    keep = valid((rows, width), 0)
    cot[:short] = wide(cot_short[...]) * keep[:short]
    cot[short:] = wide(cot_long[...]) * keep[short:]


def run_pack(geo, args):
    rows = args[0].shape[0] + args[1].shape[0]
    shapes = []
    for name in geo.kinds:
        _, sent, _, lanes = geo.kind[name]
        shapes.append(jax.ShapeDtypeStruct((geo.number[name], sent, lanes), BF))
    shapes += [
        jax.ShapeDtypeStruct((rows, geo.width), BF),
        jax.ShapeDtypeStruct((rows, rows), F32),
        jax.ShapeDtypeStruct((rows, geo.width), F32),
    ]
    in_smem = pl.BlockSpec(memory_space=pltpu.SMEM)
    return pl.pallas_call(
        functools.partial(pack_kernel, geo),
        out_shape=shapes,
        in_specs=[IN_VMEM] * 2 + [in_smem] * 2 + [IN_VMEM] * 10,
        out_specs=[IN_VMEM] * len(shapes),
        scratch_shapes=[pltpu.VMEM((geo.kind["v"][1], 128), F32)],
        compiler_params=pltpu.CompilerParams(vmem_limit_bytes=63 * 2**20),
    )(*args)


def unpack_kernel(geo, *refs):
    out, back, g_qkv, g_out, g_up, g_down, lines_d, lines_f = refs[:8]
    out_short, out_long, back_short, back_long, t_qkv, t_out, t_up, t_down = refs[8:16]
    t_gains_d, t_shifts_d, t_gains_ff, t_shifts_ff = refs[16:]
    short = out_short.shape[0]
    out_short[...] = out[:short]
    out_long[...] = out[short:]
    back_short[...] = back[:short]
    back_long[...] = back[short:]
    for source, target in ((g_qkv, t_qkv), (g_out, t_out), (g_up, t_up), (g_down, t_down)):
        target[...] = source[...]
    for layer in range(geo.layers):
        for at in range(10):
            line, lane = divmod(layer * 10 + at, geo.per_row)
            value = lines_d[line : line + 1, lane * geo.slot : lane * geo.slot + geo.rows_a]
            if at < 3:
                t_gains_d[layer, at : at + 1, :] = value
            else:
                t_shifts_d[layer, at - 3 : at - 2, :] = value
        for at in range(3):
            value = lines_f[layer * 3 + at : layer * 3 + at + 1, : geo.rows_b]
            if at == 0:
                t_gains_ff[layer : layer + 1, :] = value
            else:
                t_shifts_ff[layer, at - 1 : at, :] = value


def run_unpack(geo, found, args):
    like = lambda index, dtype: jax.ShapeDtypeStruct(args[index].shape, dtype)
    shapes = [like(0, BF), like(1, BF), like(0, F32), like(1, F32)]
    shapes += [like(index, F32) for index in range(4, 12)]
    return pl.pallas_call(
        functools.partial(unpack_kernel, geo),
        out_shape=shapes,
        in_specs=[IN_VMEM] * len(found),
        out_specs=[IN_VMEM] * len(shapes),
        compiler_params=pltpu.CompilerParams(vmem_limit_bytes=63 * 2**20),
    )(*found)


def on_device(*args):
    n_dp, n_z = lax.axis_size("dp"), lax.axis_size("fsdp")
    geo = Geometry(n_dp, n_z, args[4].shape, args[6].shape, args[7].shape)
    *sources, act, mask, cot = run_pack(geo, args)
    found, kept = run_forward(geo, sources, act, mask)
    out, vec_d, vec_f, whole_a, whole_b, kept_x = found
    grads = run_backward(geo, cot, vec_d, vec_f, whole_a, whole_b, kept_x, kept)
    return tuple(run_unpack(geo, (out,) + tuple(grads), args))


def solution(mesh):
    return jax.shard_map(
        on_device,
        mesh=mesh,
        in_specs=(
            P(("dp", "fsdp"), None),
            P(("dp", "fsdp"), None),
            P(("dp", "fsdp")),
            P(("dp", "fsdp")),
            P(None, ("dp", "fsdp"), None),
            P(None, ("dp", "fsdp"), None),
            P(None, ("dp", "fsdp"), None),
            P(None, ("dp", "fsdp"), None),
            P(None, None, ("dp", "fsdp")),
            P(None, None, ("dp", "fsdp")),
            P(None, ("dp", "fsdp")),
            P(None, None, ("dp", "fsdp")),
            P(("dp", "fsdp"), None),
            P(("dp", "fsdp"), None),
        ),
        out_specs=(
            P(("dp", "fsdp"), None),
            P(("dp", "fsdp"), None),
            P(("dp", "fsdp"), None),
            P(("dp", "fsdp"), None),
            P(None, ("dp", "fsdp"), None),
            P(None, ("dp", "fsdp"), None),
            P(None, ("dp", "fsdp"), None),
            P(None, ("dp", "fsdp"), None),
            P(None, None, ("dp", "fsdp")),
            P(None, None, ("dp", "fsdp")),
            P(None, ("dp", "fsdp")),
            P(None, None, ("dp", "fsdp")),
        ),
        check_vma=False,
    )
```

```python
import functools

import jax
import jax.numpy as jnp
import numpy as np
from jax import lax
from jax.experimental import pallas as pl
from jax.experimental.pallas import tpu as pltpu
from jax.sharding import PartitionSpec as P

HEAD_DIM = 64

epsilon = 1e-05


BF = jnp.bfloat16
F32 = jnp.float32
MESH = pl.DeviceIdType.MESH


def round16(count):
    return (count + 15) // 16 * 16


class Geometry:
    def __init__(self, n_dp, n_z, w_qkv, w_up, w_down):
        self.n_dp, self.n_z, self.n_y = n_dp, n_z, n_dp // 4
        self.layers = w_qkv[0]
        self.width = w_qkv[2] // 3
        self.rows_a, self.rows_b = w_qkv[1], w_down[1]
        self.blocks = 4 + w_up[2] // self.width
        self.pairs = self.blocks // 2
        half = self.width // 2
        self.lined = self.rows_b % 16 == 0
        self.roomy = self.n_y <= 2
        self.first_down = "l" if self.lined else "b"
        self.lanes_of = {self.first_down: (0, half), "c": (half, half - 128), "d": (2 * half - 128, 128)}
        self.down = tuple(self.lanes_of)
        self.kinds = ("a", "v") + self.down
        self.plain = tuple(name for name in self.kinds if name != "l")
        self.owners = n_dp * n_z
        self.wide_width = w_up[2]
        self.slot = 8
        while self.slot < self.rows_a:
            self.slot *= 2
        self.per_row = 128 // self.slot
        self.lines_d = -(-self.layers * 10 // self.per_row)
        lines = round16(self.lines_d + self.layers * 3)
        self.kind = {
            "a": (2, round16(2 * self.rows_a), self.rows_a * n_z, self.width),
            "v": (1, lines, lines * n_z, 128),
        }
        self.real = {"a": self.rows_a, "v": self.kind["v"][1]}
        self.number = {"a": self.layers * self.pairs, "v": 1}
        for name, (_, lanes) in self.lanes_of.items():
            self.kind[name] = (1, round16(self.rows_b), self.rows_b * n_z, lanes)
            self.real[name] = self.rows_b
            self.number[name] = self.layers

    def permuted(self, name):
        k, sent, unit, _ = self.kind[name]
        return k * unit != sent * self.n_z or k > 1

    def permutation(self, name):
        k, sent, unit, _ = self.kind[name]
        real = self.real[name]
        table = np.zeros((k * unit, self.n_z * sent), np.float32)
        for block in range(k):
            for z in range(self.n_z):
                for row in range(real):
                    table[block * unit + z * real + row, z * sent + block * real + row] = 1
        return table

    def whole_shape(self, name):
        _, _, unit, lanes = self.kind[name]
        lead = {"a": self.layers * self.blocks, "v": 1}.get(name, self.layers)
        return (lead, self.n_dp * unit, lanes if name == "v" else self.width)


class Place:
    def __init__(self, geo):
        self.geo = geo
        self.d, self.z = lax.axis_index("dp"), lax.axis_index("fsdp")
        self.core = lax.rem(self.d, 2)
        self.x = lax.rem(self.d // 2, 2)
        self.y = self.d // 4

    def y_off(self, step):
        return lax.rem(self.y + step + self.geo.n_y, self.geo.n_y)

    def z_off(self, step):
        return lax.rem(self.z + step + self.geo.n_z, self.geo.n_z)

    def dev_core(self):
        return (self.d + 1 - 2 * self.core, self.z)

    def dev_x(self):
        return (self.d + 2 - 4 * self.x, self.z)

    def dev_y(self, step):
        return (self.y_off(step) * 4 + self.x * 2 + self.core, self.z)

    def dev_z(self, step):
        return (self.d, self.z_off(step))

    def greet(self):
        barrier = pltpu.get_barrier_semaphore()
        partners = [self.dev_core(), self.dev_x()]
        partners += [self.dev_y(step) for step in range(1, self.geo.n_y)]
        partners += [self.dev_z(step) for step in range(1, self.geo.n_z)]
        for partner in partners:
            pl.semaphore_signal(barrier, inc=1, device_id=partner, device_id_type=MESH)
        pl.semaphore_wait(barrier, len(partners))


def remote(src, dst, send, recv, device):
    return pltpu.make_async_remote_copy(
        src_ref=src, dst_ref=dst, send_sem=send, recv_sem=recv, device_id=device, device_id_type=MESH
    )


def chunk_a(geo, layer, pair):
    return ("a", layer * geo.pairs + pair, layer * geo.blocks + 2 * pair, 0)


def chunk_down(geo, layer, name):
    return (name, layer, layer, geo.lanes_of[name][0])


def rows_of(whole, name, lead, first, k, unit, lanes):
    def at(y, x, core):
        rows = pl.ds(pl.multiple_of((y * 4 + x * 2 + core) * unit, 16), unit)
        return whole.at[pl.ds(lead, k), rows, slice(None) if name in ("a", "v") else pl.ds(first, lanes)]

    return at


def ways_of(number, k):
    if k == 1:
        return [(slice(0, 1), number % 2 == 0)]
    return [(slice(0, 1), True), (slice(1, k), False)]


class Gather:
    def __init__(self, place, number, chunk, sources, bufs, units, perms, wholes, sems):
        self.p, self.c = place, number
        name, at, lead, first = chunk
        self.ways = ways_of(number, place.geo.kind[name][0])
        k, self.sent, unit, lanes = place.geo.kind[name]
        self.source = sources[name].at[at]
        self.buf = bufs[name].at[at]
        self.perm = perms.get(name)
        self.unit_buf = units[name].at[at] if self.perm is not None else None
        self.unit = self.unit_buf if self.perm is not None else bufs[name].at[pl.ds(at, 1)]
        self.to = rows_of(wholes[name], name, lead, first, k, unit, lanes)
        self.sems = sems
        self.pending = []

    def slot(self, z):
        return self.buf.at[pl.ds(pl.multiple_of(z * self.sent, 16), self.sent)]

    def send(self, src, dst, send, recv, device):
        copy = remote(src, dst, send, recv, device)
        copy.start()
        self.pending.append(copy)

    def arrived(self, dst, send, recv, device):
        remote(dst, dst, send, recv, device).wait_recv()

    def start_z(self):
        p, s, c = self.p, self.sems, self.c
        self.local_z = pltpu.make_async_copy(self.source, self.slot(p.z), s["lz"].at[c])
        self.local_z.start()
        for step in range(1, p.geo.n_z):
            self.send(self.source, self.slot(p.z), s["zs"].at[c, step], s["zr"].at[c, step], p.dev_z(step))

    def own(self):
        p, s, c = self.p, self.sems, self.c
        self.local_z.wait()
        for step in range(1, p.geo.n_z):
            self.arrived(self.slot(p.z_off(-step)), s["zs"].at[c, step], s["zr"].at[c, step], p.dev_z(step))
        if self.perm is not None:
            k, unit, lanes = self.unit_buf.shape
            mixed = jnp.dot(self.perm[...], self.buf[...], preferred_element_type=F32)
            self.unit_buf[...] = mixed.astype(BF).reshape(k, unit, lanes)
        here = self.to(p.y, p.x, p.core)
        self.local = pltpu.make_async_copy(self.unit, here, s["lo"].at[c])
        self.send(self.unit, here, s["xs"].at[c], s["xr"].at[c], p.dev_x())
        for step in range(1, p.geo.n_y):
            self.send(self.unit, here, s["ys"].at[c, step], s["yr"].at[c, step], p.dev_y(step))
        self.send(self.unit, here, s["cs"].at[c, 0], s["cr"].at[c, 0], p.dev_core())
        self.local.start()

    def forward(self):
        p, s, c = self.p, self.sems, self.c
        n_y = p.geo.n_y
        from_x = self.to(p.y, 1 - p.x, p.core)
        self.arrived(from_x, s["xs"].at[c], s["xr"].at[c], p.dev_x())
        for way, (blocks, by_x) in enumerate(self.ways):
            for step in range(1, n_y) if by_x else ():
                at = (c, way, step)
                rows = from_x.at[blocks]
                self.send(rows, rows, s["ds"].at[at], s["dr"].at[at], p.dev_y(step))
        self.send(from_x, from_x, s["cs"].at[c, 1], s["cr"].at[c, 1], p.dev_core())
        for step in range(1, n_y):
            from_y = self.to(p.y_off(-step), p.x, p.core)
            self.arrived(from_y, s["ys"].at[c, step], s["yr"].at[c, step], p.dev_y(step))
            for way, (blocks, by_x) in enumerate(self.ways):
                if not by_x:
                    at = (c, way, step)
                    rows = from_y.at[blocks]
                    self.send(rows, rows, s["ds"].at[at], s["dr"].at[at], p.dev_x())
            self.send(from_y, from_y, s["cs"].at[c, 2 * step], s["cr"].at[c, 2 * step], p.dev_core())

    def corner(self):
        p, s, c = self.p, self.sems, self.c
        for step in range(1, p.geo.n_y):
            far = self.to(p.y_off(-step), 1 - p.x, p.core)
            for way, (blocks, _) in enumerate(self.ways):
                at = (c, way, step)
                self.arrived(far.at[blocks], s["ds"].at[at], s["dr"].at[at], p.dev_x())
            self.send(far, far, s["cs"].at[c, 2 * step + 1], s["cr"].at[c, 2 * step + 1], p.dev_core())

    def arrive(self):
        p, s, c = self.p, self.sems, self.c
        for step in range(p.geo.n_y):
            for flip in range(2):
                x = p.x if flip == 0 else 1 - p.x
                got = self.to(p.y_off(-step), x, 1 - p.core)
                at = 2 * step + flip
                self.arrived(got, s["cs"].at[c, at], s["cr"].at[c, at], p.dev_core())
        self.local.wait()

    def drain(self):
        for copy in self.pending:
            copy.wait_send()


def when(condition, act):
    pl.when(condition)(act)


def on_line(place, way, step):
    at = place.z - step if way == 0 else place.z + step
    return (at >= 0) & (at < place.geo.n_z), at


class GatherLine:
    def __init__(self, place, number, chunk, sources, wholes, sems):
        self.p, self.c = place, number
        _, at, lead, first = chunk
        _, sent, _, lanes = place.geo.kind["l"]
        self.source = sources["l"].at[at]
        self.half_a = number % 2 == 0
        whole = wholes["l"]

        def piece(y, x, core, z):
            device = (y * 4 + x * 2 + core) * place.geo.n_z + z
            rows = pl.ds(pl.multiple_of(device * sent, 16), sent)
            return whole.at[lead, rows, pl.ds(first, lanes)]

        self.piece = piece
        self.sems = sems
        self.pending, self.line_pending = [], []

    def send(self, src, dst, send, recv, device):
        copy = remote(src, dst, send, recv, device)
        copy.start()
        self.pending.append(copy)

    def arrived(self, dst, send, recv, device):
        remote(dst, dst, send, recv, device).wait_recv()

    def from_column(self, at, z, core):
        p = self.p
        return self.piece(p.y_off(-(at // 2)), p.x if at % 2 == 0 else 1 - p.x, core, z)

    def line_send(self, column, hop):
        p, s, c = self.p, self.sems, self.c
        for way in range(2):
            valid, z = on_line(p, way, hop - 1)
            further, target = on_line(p, 1 - way, 1)

            def copy(z=z, target=target, way=way):
                rows = self.from_column(column, z, p.core)
                at = (c, way, hop, column)
                return remote(rows, rows, s["gs"].at[at], s["gr"].at[at], (p.d, target))

            when(valid & further, lambda copy=copy: copy().start())
            self.line_pending.append((valid & further, copy))

    def to_core(self, column, z, at):
        s = self.sems
        rows = self.from_column(column, z, self.p.core)
        return remote(rows, rows, s["hs"].at[at], s["hr"].at[at], self.p.dev_core())

    def start(self):
        p, s, c = self.p, self.sems, self.c
        here = self.piece(p.y, p.x, p.core, p.z)
        self.local = pltpu.make_async_copy(self.source, here, s["gl"].at[c])
        self.send(self.source, here, s["gx"].at[c, 0], s["gx"].at[c, 1], p.dev_x())
        for step in range(1, p.geo.n_y):
            self.send(self.source, here, s["gy"].at[c, 0, step], s["gy"].at[c, 1, step], p.dev_y(step))
        self.local.start()
        at = (c, 0, 0, 0)
        self.send(self.source, here, s["hs"].at[at], s["hr"].at[at], p.dev_core())

    def forward(self):
        p, s, c = self.p, self.sems, self.c
        n_y = p.geo.n_y
        self.local.wait()
        rows = self.from_column(1, p.z, p.core)
        self.arrived(rows, s["gx"].at[c, 0], s["gx"].at[c, 1], p.dev_x())
        if self.half_a:
            for step in range(1, n_y):
                self.send(rows, rows, s["gd"].at[c, 0, step], s["gd"].at[c, 1, step], p.dev_y(step))
        self.keep_core(1)
        for step in range(1, n_y):
            rows = self.from_column(2 * step, p.z, p.core)
            self.arrived(rows, s["gy"].at[c, 0, step], s["gy"].at[c, 1, step], p.dev_y(step))
            if not self.half_a:
                self.send(rows, rows, s["gd"].at[c, 0, step], s["gd"].at[c, 1, step], p.dev_x())
            self.keep_core(2 * step)

    def keep_core(self, column):
        copy = self.to_core(column, self.p.z, (self.c, 0, 0, column))
        copy.start()
        self.pending.append(copy)

    def corner(self):
        p, s, c = self.p, self.sems, self.c
        for step in range(1, p.geo.n_y):
            rows = self.from_column(2 * step + 1, p.z, p.core)
            self.arrived(rows, s["gd"].at[c, 0, step], s["gd"].at[c, 1, step], p.dev_x())
            self.keep_core(2 * step + 1)

    def relay(self, hop, half):
        p, s, c = self.p, self.sems, self.c
        n_y = p.geo.n_y
        for column in range(half * n_y, (half + 1) * n_y):
            for way in range(2) if hop > 0 else ():
                valid, z = on_line(p, way, hop)
                at = (c, way, hop, column)

                def act(z=z, at=at):
                    rows = self.from_column(column, z, p.core)
                    remote(rows, rows, s["gs"].at[at], s["gr"].at[at], p.dev_x()).wait_recv()
                    self.to_core(column, z, at).start()

                when(valid, act)
                self.line_pending.append(
                    (valid, lambda column=column, z=z, at=at: self.to_core(column, z, at))
                )
            if hop < p.geo.n_z - 1:
                self.line_send(column, hop + 1)

    def arrive(self):
        p, s, c = self.p, self.sems, self.c
        for column in range(2 * p.geo.n_y):
            rows = self.from_column(column, p.z, 1 - p.core)
            at = (c, 0, 0, column)
            self.arrived(rows, s["hs"].at[at], s["hr"].at[at], p.dev_core())
            for hop in range(1, p.geo.n_z):
                for way in range(2):
                    valid, z = on_line(p, way, hop)
                    at = (c, way, hop, column)

                    def act(z=z, at=at):
                        rows = self.from_column(column, z, 1 - p.core)
                        self.arrived(rows, s["hs"].at[at], s["hr"].at[at], p.dev_core())

                    when(valid, act)

    def drain(self):
        for copy in self.pending:
            copy.wait_send()
        for valid, copy in self.line_pending:
            when(valid, lambda copy=copy: copy().wait_send())


def run_pipeline(stages, count, extra):
    last = max(lag for lag, _ in stages)
    first = min(lag for lag, _ in stages)
    for step in range(first, count + last):
        ahead = [stage for stage in stages if stage[0] < 0]
        ahead += stages[1:3]
        for lag, act in ahead + [(None, act) for act in extra.get(step, ())] + stages[len(ahead) :]:
            if lag is None:
                act()
            elif 0 <= step - lag < count:
                act(step - lag)


def dma(*shape):
    return pltpu.SemaphoreType.DMA(shape)


ANY = pl.BlockSpec(memory_space=pl.ANY)
IN_VMEM = pl.BlockSpec(memory_space=pltpu.VMEM)


def wide(values):
    return values.astype(F32)


class Scatter:
    def __init__(self, place, number, chunk, stage, sums, mids, ends, perms, z_send, z_recv, z_slot, before, put, sems):
        self.p, self.c = place, number
        name, at, _, _ = chunk
        self.k, self.sent, self.rows, self.lanes = place.geo.kind[name]
        self.ways = ways_of(number, self.k)
        self.part = slice(None)
        self.stage = stage
        self.sum = sums[name].at[at]
        shared, per_layer = name == "a", place.geo.pairs
        self.mid = mids[name].at[at % per_layer if shared else at]
        self.hands_on = shared and at >= per_layer
        self.takes_over = shared and at < place.geo.number[name] - per_layer
        self.heir = None
        self.end = ends[name].at[at]
        self.perm = perms.get(name)
        if name in z_send:
            self.z_send, self.z_recv = z_send[name].at[z_slot], z_recv[name].at[at]
        self.before, self.z_moves = before, []
        self.put = put
        self.sems = sems
        self.pending = []

    def send(self, src, dst, send, recv, device):
        copy = remote(src, dst, send, recv, device)
        copy.start()
        self.pending.append(copy)

    def arrived(self, dst, send, recv, device):
        remote(dst, dst, send, recv, device).wait_recv()

    def start(self):
        p, s, c = self.p, self.sems, self.c
        give = self.stage.at[:, :, :, 1 - p.core]
        self.given = remote(give, self.sum, s["cs"].at[c], s["cr"].at[c], p.dev_core())
        self.given.start()

    def pair(self):
        p, s, c = self.p, self.sems, self.c
        n_y = p.geo.n_y
        self.arrived(self.sum, s["cs"].at[c], s["cr"].at[c], p.dev_core())

        @pl.loop(0, self.k * n_y * 2)
        def _(at):
            where = (at // (2 * n_y), lax.rem(at // 2, n_y), lax.rem(at, 2))
            self.sum[where] = (wide(self.sum[where]) + wide(self.stage[where + (p.core,)])).astype(BF)

        self.given.wait_send()
        self.send_middle()

    def send_middle(self):
        p, s, c = self.p, self.sems, self.c
        n_y = p.geo.n_y
        for way, (blocks, by_x) in enumerate(self.ways):
            if self.takes_over:
                for step in range(1, n_y) if by_x else ():
                    pl.semaphore_wait(s["fy"].at[c, step], 1)
                if not by_x:
                    pl.semaphore_wait(s["fx"].at[c], 1)
            if by_x:
                for step in range(1, n_y):
                    at = (c, way, step)
                    self.send(
                        self.sum.at[blocks, p.y_off(step), :, self.part], self.mid.at[step - 1, blocks],
                        s["ms"].at[at], s["mr"].at[at], p.dev_y(step),
                    )
            else:
                for y in range(n_y):
                    at = (c, way, y)
                    self.send(
                        self.sum.at[blocks, y, 1 - p.x, self.part], self.mid.at[y // 2, blocks, y % 2],
                        s["ms"].at[at], s["mr"].at[at], p.dev_x(),
                    )

    def middle(self):
        for way, (blocks, by_x) in enumerate(self.ways):
            (self.middle_x if by_x else self.middle_y)(way, blocks)

    def middle_x(self, way, blocks):
        p, s, c = self.p, self.sems, self.c
        n_y, first = p.geo.n_y, blocks.start
        for step in range(1, n_y):
            at = (c, way, step)
            self.arrived(self.mid.at[step - 1, blocks], s["ms"].at[at], s["mr"].at[at], p.dev_y(step))

        @pl.loop(0, (blocks.stop - first) * 2)
        def _(at):
            where = (first + at // 2, p.y, lax.rem(at, 2), self.part)
            value = wide(self.sum[where])
            for step in range(1, n_y):
                value = value + wide(self.mid[step - 1, first + at // 2, lax.rem(at, 2)])
            self.sum[where] = value.astype(BF)

        if self.hands_on:
            for step in range(1, n_y):
                pl.semaphore_signal(
                    s["fy"].at[self.heir.c, step], inc=1, device_id=p.dev_y(-step), device_id_type=MESH
                )
        at = (c, way, 0)
        self.send(
            self.sum.at[blocks, p.y, 1 - p.x, self.part], self.end.at[0, blocks],
            s["es"].at[at], s["er"].at[at], p.dev_x(),
        )

    def middle_y(self, way, blocks):
        p, s, c = self.p, self.sems, self.c
        n_y, first = p.geo.n_y, blocks.start
        for y in range(n_y):
            at = (c, way, y)
            self.arrived(self.mid.at[y // 2, blocks, y % 2], s["ms"].at[at], s["mr"].at[at], p.dev_x())

        @pl.loop(0, (blocks.stop - first) * n_y)
        def _(at):
            y = lax.rem(at, n_y)
            where = (first + at // n_y, y, p.x, self.part)
            value = wide(self.sum[where]) + wide(self.mid[y // 2, first + at // n_y, lax.rem(y, 2)])
            self.sum[where] = value.astype(BF)

        if self.hands_on:
            pl.semaphore_signal(s["fx"].at[self.heir.c], inc=1, device_id=p.dev_x(), device_id_type=MESH)
        for step in range(1, n_y):
            at = (c, way, step)
            self.send(
                self.sum.at[blocks, p.y_off(step), p.x, self.part], self.end.at[step - 1, blocks],
                s["es"].at[at], s["er"].at[at], p.dev_y(step),
            )

    def column_sum(self):
        p, s, c = self.p, self.sems, self.c
        n_y = p.geo.n_y
        found = []
        for way, (blocks, by_x) in enumerate(self.ways):
            value = wide(self.sum[blocks, p.y, p.x, self.part])
            for step in (0,) if by_x else range(1, n_y):
                at = (c, way, step)
                got = self.end.at[0 if by_x else step - 1, blocks]
                self.arrived(got, s["es"].at[at], s["er"].at[at], p.dev_x())
                value = value + wide(got[...])
            found.append(value)
        return found[0] if len(found) == 1 else jnp.concatenate(found, 0)

    def last(self):
        p, s, c = self.p, self.sems, self.c
        n_z = p.geo.n_z
        value = self.column_sum().astype(BF).reshape(self.k * self.rows, self.lanes)
        if self.perm is not None:
            value = jnp.dot(self.perm[...], value, preferred_element_type=F32).astype(BF)
        if self.before is not None:
            self.before.left()
        self.z_send[...] = value.reshape(n_z, self.sent, self.lanes)
        for step in range(1, n_z):
            copy = remote(
                self.z_send.at[p.z_off(step)], self.z_recv.at[step],
                s["zs"].at[c, step], s["zr"].at[c, step], p.dev_z(step),
            )
            copy.start()
            self.z_moves.append(copy)

    def finish(self):
        p, s, c = self.p, self.sems, self.c
        value = wide(self.z_send[p.z])
        for step in range(1, p.geo.n_z):
            self.arrived(self.z_recv.at[step], s["zs"].at[c, step], s["zr"].at[c, step], p.dev_z(step))
            value = value + wide(self.z_recv[step])
        self.put(value)

    def left(self):
        while self.z_moves:
            self.z_moves.pop().wait_send()

    def drain(self):
        self.left()
        for copy in self.pending:
            copy.wait_send()


class ScatterLine(Scatter):
    def land(self, line):
        self.line = line
        p = self.p
        self.unit = self.rows // p.geo.n_z
        self.part = pl.ds(pl.multiple_of(p.z * self.unit, 16), self.unit)
        self.line_pending = []
        return self

    def slice_of(self, target):
        return pl.ds(target * self.unit, self.unit)

    def line_copy(self, src, way, target, further):
        s = self.sems
        at = (self.c_line, way, target)
        return remote(src, self.line.at[way, target], s["ls"].at[at], s["lr"].at[at], (self.p.d, further))

    def send_middle(self):
        p, last = self.p, self.p.geo.n_z - 1
        for way in range(2):
            ours = p.z == (0 if way == 0 else last)
            targets = range(last, 0, -1) if way == 0 else range(last)
            further = p.z + 1 if way == 0 else p.z - 1
            for target in targets:

                def copy(way=way, target=target, further=further):
                    return self.line_copy(self.sum.at[0, :, :, self.slice_of(target)], way, target, further)

                when(ours, lambda copy=copy: copy().start())
                self.line_pending.append((ours, copy))

    def relay(self, hop):
        p, s, last = self.p, self.sems, self.p.geo.n_z - 1
        for way in range(2):
            here = hop if way == 0 else last - hop
            targets = range(last, here, -1) if way == 0 else range(here)
            further = p.z + 1 if way == 0 else p.z - 1
            for target in targets:

                def copy(way=way, target=target, further=further):
                    return self.line_copy(self.line.at[way, target], way, target, further)

                def act(way=way, target=target, copy=copy):
                    self.add_line(way, target)
                    copy().start()

                when(p.z == here, act)
                self.line_pending.append((p.z == here, copy))

    def add_line(self, way, target):
        s, n_y = self.sems, self.p.geo.n_y
        at = (self.c_line, way, target)
        got = self.line.at[way, target]
        remote(got, got, s["ls"].at[at], s["lr"].at[at], self.p.dev_x()).wait_recv()

        @pl.loop(0, 2 * n_y)
        def _(index):
            where = (index // 2, lax.rem(index, 2))
            mine = wide(self.sum[(0,) + where + (self.slice_of(target),)])
            got[where] = (wide(got[where]) + mine).astype(BF)

    def collect(self):
        p, s, n_y, last = self.p, self.sems, self.p.geo.n_y, self.p.geo.n_z - 1
        for way in range(2):

            def act(way=way):
                at = (self.c_line, way, p.z)
                got = self.line.at[way, p.z]
                remote(got, got, s["ls"].at[at], s["lr"].at[at], p.dev_x()).wait_recv()

                @pl.loop(0, 2 * n_y)
                def _(index):
                    where = (index // 2, lax.rem(index, 2))
                    place = (0,) + where + (self.part,)
                    self.sum[place] = (wide(self.sum[place]) + wide(got[where])).astype(BF)

            when(p.z > 0 if way == 0 else p.z < last, act)
        Scatter.send_middle(self)

    def last(self):
        self.put(self.column_sum().reshape(self.unit, self.lanes))

    def finish(self):
        pass

    def drain(self):
        for valid, copy in self.line_pending:
            when(valid, lambda copy=copy: copy().wait_send())
        Scatter.drain(self)


def mm(left, right):
    return jnp.dot(left, right, preferred_element_type=F32)


def mm_nt(left, right):
    return lax.dot_general(left, right, (((1,), (1,)), ((), ())), preferred_element_type=F32)


def mm_tn(left, right):
    return lax.dot_general(left, right, (((0,), (0,)), ((), ())), preferred_element_type=F32)


def mean_of(values):
    return jnp.sum(values, -1, keepdims=True) * (1.0 / values.shape[-1])


def normal(values):
    centered = values - mean_of(values)
    scale = lax.rsqrt(mean_of(centered * centered) + epsilon)
    return centered * scale, scale


def norm_rows(source, gain, shift, target, block=32):
    @pl.loop(0, source.shape[0] // block)
    def _(at):
        rows = pl.ds(pl.multiple_of(at * block, block), block)
        unit, _ = normal(source[rows, :])
        target[rows, :] = (unit * gain + shift).astype(target.dtype)


def fold(values):
    total = values[0:8]
    for at in range(8, values.shape[0], 8):
        total = total + values[at : at + 8]
    return total


def norm_rows_back(source, gain, incoming, emit, sums, block=32):
    sums[...] = jnp.zeros_like(sums)

    @pl.loop(0, source.shape[0] // block)
    def _(at):
        rows = pl.ds(pl.multiple_of(at * block, block), block)
        unit, scale = normal(source[rows, :])
        back = incoming[rows, :]
        sums[0] += fold(back * unit)
        sums[1] += fold(back)
        inner = back * gain
        emit(rows, scale * (inner - mean_of(inner) - unit * mean_of(inner * unit)))


ROOT = 0.7978845608028654
CUBE = 0.044715


def gelu_parts(values):
    square = values * values
    curve = jnp.tanh(ROOT * (values + CUBE * (values * square)))
    return square, curve


class Layer:
    def __init__(self, refs, weight_a, weight_b, vec_d, vec_f, layer, heads):
        self.__dict__.update(refs)
        self.weight_a, self.weight_b = weight_a, weight_b
        self.vec_d, self.vec_f = vec_d, vec_f
        self.layer, self.heads = layer, heads

    def gain(self, at):
        return self.vec_d[self.layer * 10 + at : self.layer * 10 + at + 1, :]

    def shift(self, at):
        return self.gain(3 + at)

    def gain_f(self, at):
        return self.vec_f[self.layer * 3 + at : self.layer * 3 + at + 1, :]

    def lane_half(self, values, side):
        lane = lax.broadcasted_iota(jnp.int32, values.shape, 1)
        return (lane < HEAD_DIM) == (side == 0)

    def forward_norm(self):
        norm_rows(self.x, self.gain(0), self.shift(0), self.normed)

    def forward_qkv(self, part):
        value = mm(self.normed[...], self.weight_a(part))
        if part != 1:
            value = value + self.shift(3 if part == 0 else 4)
        self.qkv[part] = value.astype(BF)

    def forward_attention(self):
        valid = self.mask[...] > 0.5

        @pl.loop(0, self.heads // 2)
        def _(pair):
            lanes = pl.ds(pl.multiple_of(pair * 128, 128), 128)
            queries, keys, values = [self.qkv[part, :, lanes] for part in range(3)]
            context = None
            for side in range(2):
                half = self.lane_half(queries, side)
                scores = mm_nt(jnp.where(half, queries, jnp.zeros_like(queries)), keys)
                scores = jnp.where(valid, scores * HEAD_DIM**-0.5, -1e9)
                top = jnp.max(scores, -1, keepdims=True)
                grown = jnp.exp(scores - top)
                prob = grown / jnp.sum(grown, -1, keepdims=True)
                self.prob[2 * pair + side] = prob
                product = mm(prob.astype(BF), values)
                context = product if side == 0 else jnp.where(half, product, context)
            self.context[:, lanes] = context

    def forward_out(self):
        norm_rows(self.context, self.gain(1), self.shift(1), self.sub)
        self.after[...] = self.x[...] + (mm(self.sub[...], self.weight_a(3)) + self.shift(5))
        norm_rows(self.after, self.gain(2), self.shift(2), self.normed_ffn)

    def forward_up(self, part):
        width = self.x.shape[1]
        lanes = slice(part * width, (part + 1) * width)
        self.hidden[:, lanes] = mm(self.normed_ffn[...], self.weight_a(4 + part)) + self.gain_f(1)[:, lanes]

    def forward_gelu(self):
        @pl.loop(0, self.x.shape[0] // 16)
        def _(at):
            rows = pl.ds(pl.multiple_of(at * 16, 16), 16)
            values = self.hidden[rows, :]
            _, curve = gelu_parts(values)
            unit, _ = normal(0.5 * values * (1.0 + curve))
            self.sub_ffn[rows, :] = (unit * self.gain_f(0) + self.gain_f(2)).astype(BF)

    def forward_down(self, lanes):
        value = mm(self.sub_ffn[...], self.weight_b(slice(None), lanes))
        self.x_next[:, lanes] = self.after[:, lanes] + (value + self.shift(6)[:, lanes])


    def store_sums_d(self, at, sums):
        row = self.layer * 10 + at
        self.grad_d[row : row + 1, :] = jnp.sum(sums, 0, keepdims=True)

    def store_sums_f(self, at, sums):
        row = self.layer * 3 + at
        self.grad_f[row : row + 1, :] = jnp.sum(sums, 0, keepdims=True)

    def backward_start(self):
        self.low[...] = self.back[...].astype(BF)
        self.store_sums_d(9, wide(self.low[...]))

    def grad_up(self, part):
        width = self.x.shape[1]
        return mm_tn(self.normed_ffn[...], self.d_hidden[:, part * width : (part + 1) * width])

    def grad_out(self):
        return mm_tn(self.sub[...], self.low[...])

    def grad_qkv(self, part):
        return mm_tn(self.normed[...], self.d_qkv[part])

    def backward_down(self):
        width = self.x.shape[1]
        for part in range(self.hidden.shape[1] // width):
            lanes = slice(part * width, (part + 1) * width)
            self.wide_back[:, lanes] = mm_nt(self.low[...], self.weight_b(lanes, slice(None)))

    def backward_gelu(self):
        self.sums_f[...] = jnp.zeros_like(self.sums_f)

        @pl.loop(0, self.x.shape[0] // 16)
        def _(at):
            rows = pl.ds(pl.multiple_of(at * 16, 16), 16)
            values = self.hidden[rows, :]
            square, curve = gelu_parts(values)
            unit, scale = normal(0.5 * values * (1.0 + curve))
            back = self.wide_back[rows, :]
            self.sums_f[0] += fold(back * unit)
            self.sums_f[1] += fold(back)
            inner = back * self.gain_f(0)
            d_gelu = scale * (inner - mean_of(inner) - unit * mean_of(inner * unit))
            slope = 0.5 * (1.0 + curve) + 0.5 * values * (1.0 - curve * curve) * (
                ROOT * (1.0 + 3.0 * CUBE * square)
            )
            low = (d_gelu * slope).astype(BF)
            self.d_hidden[rows, :] = low
            self.sums_f[2] += fold(wide(low))

        self.store_sums_f(0, self.sums_f[0])
        self.store_sums_f(2, self.sums_f[1])
        self.store_sums_f(1, self.sums_f[2])

    def backward_up(self):
        width = self.x.shape[1]
        total = None
        for part in range(self.hidden.shape[1] // width):
            lanes = slice(part * width, (part + 1) * width)
            value = mm_nt(self.d_hidden[:, lanes], self.weight_a(4 + part))
            if part == 0:
                self.incoming[...] = value
            else:
                self.incoming[...] += value

        def emit(rows, value):
            value = self.back[rows, :] + value
            self.back[rows, :] = value
            self.low[rows, :] = value.astype(BF)

        norm_rows_back(self.after, self.gain(2), self.incoming, emit, self.sums_d)
        self.store_sums_d(2, self.sums_d[0])
        self.store_sums_d(5, self.sums_d[1])

    def backward_out(self):
        self.store_sums_d(8, wide(self.low[...]))
        self.incoming[...] = mm_nt(self.low[...], self.weight_a(3))

        def emit(rows, value):
            self.low[rows, :] = value.astype(BF)

        norm_rows_back(self.context, self.gain(1), self.incoming, emit, self.sums_d)
        self.store_sums_d(1, self.sums_d[0])
        self.store_sums_d(4, self.sums_d[1])

    def backward_attention(self):
        @pl.loop(0, self.heads // 2)
        def _(pair):
            lanes = pl.ds(pl.multiple_of(pair * 128, 128), 128)
            queries, keys, values = [self.qkv[part, :, lanes] for part in range(3)]
            d_context = self.low[:, lanes]
            found = [None] * 3
            for side in range(2):
                half = self.lane_half(d_context, side)
                prob = self.prob[2 * pair + side]
                d_prob = mm_nt(jnp.where(half, d_context, jnp.zeros_like(d_context)), values)
                dot = jnp.sum(prob * d_prob, -1, keepdims=True)
                d_scores = (prob * (d_prob - dot)).astype(BF)
                new = (
                    mm(d_scores, keys) * HEAD_DIM**-0.5,
                    mm_tn(d_scores, queries) * HEAD_DIM**-0.5,
                    mm_tn(prob.astype(BF), d_context),
                )
                found = [n if side == 0 else jnp.where(half, n, f) for n, f in zip(new, found)]
            for part in range(3):
                self.d_qkv[part, :, lanes] = found[part].astype(BF)

    def backward_qkv(self):
        self.store_sums_d(6, wide(self.d_qkv[0]))
        self.store_sums_d(7, wide(self.d_qkv[2]))
        for part in range(3):
            value = mm_nt(self.d_qkv[part], self.weight_a(part))
            if part == 0:
                self.incoming[...] = value
            else:
                self.incoming[...] += value

        def emit(rows, value):
            self.back[rows, :] = self.back[rows, :] + value

        norm_rows_back(self.x, self.gain(0), self.incoming, emit, self.sums_d)
        self.store_sums_d(0, self.sums_d[0])
        self.store_sums_d(3, self.sums_d[1])


def saved_shapes(rows, width, wide_width, heads):
    return {
        "normed": ((rows, width), BF),
        "qkv": ((3, rows, width), BF),
        "prob": ((heads, rows, rows), F32),
        "context": ((rows, width), F32),
        "sub": ((rows, width), BF),
        "after": ((rows, width), F32),
        "normed_ffn": ((rows, width), BF),
        "hidden": ((rows, wide_width), F32),
        "sub_ffn": ((rows, wide_width), BF),
    }


def work_shapes(rows, width, wide_width):
    return {
        "low": ((rows, width), BF),
        "incoming": ((rows, width), F32),
        "wide_back": ((rows, wide_width), F32),
        "d_qkv": ((3, rows, width), BF),
        "sums_d": ((2, 8, width), F32),
        "sums_f": ((3, 8, wide_width), F32),
    }


def spread_tables(geo):
    tables = []
    for width, real in ((geo.width, geo.rows_a), (geo.wide_width, geo.rows_b)):
        at = np.arange(width)
        owner = (at[None, :] // real == np.arange(geo.owners)[:, None]).astype(np.float32)
        tables += [jnp.asarray(owner, BF), jnp.asarray(at[None, :] % real, jnp.int32)]
    return tables


def unpack_vectors(geo, whole_v, wide_v, tables, vec_d, vec_f):
    owner_d, rest_d, owner_f, rest_f = tables
    lines = geo.kind["v"][1]
    wide_v[...] = wide(whole_v[0])
    line_of = lambda at: wide_v[pl.ds(at, geo.owners, stride=lines), :].astype(BF)
    pick_d = lax.broadcasted_iota(jnp.int32, (geo.slot, geo.width), 0) == rest_d[...]
    for line in range(geo.lines_d):
        spread = mm_tn(line_of(line), owner_d[...])
        for at in range(geo.per_row):
            part = spread[at * geo.slot : (at + 1) * geo.slot]
            row = line * geo.per_row + at
            if row < geo.layers * 10:
                vec_d[row : row + 1, :] = jnp.sum(jnp.where(pick_d, part, 0.0), 0, keepdims=True)
    pick_f = lax.broadcasted_iota(jnp.int32, (128, geo.width), 0)
    for row in range(geo.layers * 3):
        line = line_of(geo.lines_d + row)
        for first in range(0, geo.wide_width, geo.width):
            lanes = slice(first, first + geo.width)
            spread = jnp.where(pick_f == rest_f[:, lanes], mm_tn(line, owner_f[:, lanes]), 0.0)
            vec_f[row : row + 1, lanes] = jnp.sum(spread, 0, keepdims=True)


GATHER_SEMS = (
    "lz", "lo", "zs", "zr", "xs", "xr", "ys", "yr", "ds", "dr", "cs", "cr",
    "gl", "gx", "gy", "gd", "gs", "gr", "hs", "hr",
)
LINE_FIRST = (1, 6)


def forward_kernel(geo, names_perm, saved_names, *refs):
    refs = list(refs)
    take = lambda number: [refs.pop(0) for _ in range(number)]
    sources = dict(zip(geo.kinds, take(len(geo.kinds))))
    perms = dict(zip(names_perm, take(len(names_perm))))
    act_ref, mask_ref = take(2)
    tables = take(4)
    out_ref, vec_d, vec_f, kept_a, kept_b, kept_x = take(6)
    kept = [dict(zip(saved_names, take(len(saved_names)))) for _ in range(geo.layers)]
    wholes = dict(zip(("a", "v", "b"), take(3)))
    wholes.update({name: wholes["b"] for name in geo.down})
    bufs = dict(zip(geo.plain, take(len(geo.plain))))
    units = dict(zip(names_perm, take(len(names_perm))))
    saved = [dict(zip(saved_names, take(len(saved_names)))) for _ in range(geo.layers)]
    xs, wide_v, keep_sem = take(3)
    sems = dict(zip(GATHER_SEMS, take(len(GATHER_SEMS))))
    place = Place(geo)
    chunks, line_chunks = [("v", 0, 0, 0)], []
    for layer in range(geo.layers):
        chunks += [chunk_a(geo, layer, pair) for pair in range(geo.pairs)]
        for name in geo.down:
            (line_chunks if name == "l" else chunks).append(chunk_down(geo, layer, name))
    moves = [
        Gather(place, at, chunk, sources, bufs, units, perms, wholes, sems)
        for at, chunk in enumerate(chunks)
    ]
    lines = [
        GatherLine(place, at, chunk, sources, wholes, sems) for at, chunk in enumerate(line_chunks)
    ]
    keeps = []

    def keep(src, dst):
        copy = pltpu.make_async_copy(src, dst, keep_sem.at[len(keeps)])
        copy.start()
        keeps.append(copy)

    net = []
    for layer in range(geo.layers):
        fields = dict(saved[layer], x=xs.at[layer], x_next=xs.at[layer + 1], mask=mask_ref)
        read_a = lambda at, layer=layer: wholes["a"][layer * geo.blocks + at]
        read_b = lambda rows, lanes, layer=layer: wholes["b"][layer, rows, lanes]
        net.append(Layer(fields, read_a, read_b, vec_d, vec_f, layer, geo.width // HEAD_DIM))

    def compute(number):
        name, at, lead, first = chunks[number]
        if geo.lined and name == "c":
            lines[lead].arrive()
            down(lead, *geo.lanes_of["l"])
        moves[number].arrive()
        if name == "v":
            unpack_vectors(geo, wholes["v"], wide_v, tables, vec_d, vec_f)
            return
        k, _, _, lanes = geo.kind[name]
        layer = at // geo.pairs if name == "a" else at
        one = net[layer]
        save = lambda *found: [keep(saved[layer][field], kept[layer][field]) for field in found]
        if name == "a":
            keep(wholes["a"].at[pl.ds(lead, k)], kept_a.at[pl.ds(lead, k)])
            pair = at % geo.pairs
            if pair == 0:
                one.forward_norm()
                one.forward_qkv(0)
                one.forward_qkv(1)
            elif pair == 1:
                one.forward_qkv(2)
                save("normed", "qkv")
                one.forward_attention()
                one.forward_out()
                save("prob", "context", "sub", "after", "normed_ffn")
            else:
                one.forward_up(2 * pair - 4)
                one.forward_up(2 * pair - 3)
                if pair == geo.pairs - 1:
                    one.forward_gelu()
                    save("hidden", "sub_ffn")
        else:
            down(layer, first, lanes)
            if name == geo.down[-1] and layer < geo.layers - 1:
                keep(xs.at[layer + 1], kept_x.at[layer + 1])

    def down(layer, first, lanes):
        where = pl.ds(first, lanes)
        keep(wholes["b"].at[layer, :, where], kept_b.at[layer, :, where])
        net[layer].forward_down(slice(first, first + lanes))

    extra = {}
    for layer, line in enumerate(lines):
        plan = [line.start, line.forward, line.corner]
        plan += [
            lambda line=line, hop=hop, half=half: line.relay(hop, half)
            for hop in range(geo.n_z)
            for half in range(2)
        ]
        needed = chunks.index(chunk_down(geo, layer, "c")) + 2
        for at, act in enumerate(plan):
            step = at - 2 if at < 3 else LINE_FIRST[min(layer, 1)] + at - 3
            extra.setdefault(min(step, needed), []).append(act)

    xs[0] = wide(act_ref[...])
    keep(xs.at[0], kept_x.at[0])
    place.greet()
    run_pipeline(
        [
            (-2, lambda c: moves[c].start_z()),
            (0, lambda c: moves[c].own()),
            (3, compute),
            (1, lambda c: moves[c].forward()),
            (2, lambda c: moves[c].corner()),
        ],
        len(moves),
        extra,
    )
    out_ref[...] = xs[geo.layers].astype(BF)
    for move in moves + lines:
        move.drain()
    for copy in keeps:
        copy.wait()


def run_forward(geo, sources, act, mask):
    names_perm = [name for name in geo.plain if geo.permuted(name)]
    perms = [jnp.asarray(geo.permutation(name), BF) for name in names_perm]
    rows, width = act.shape
    total = sum(geo.number.values())
    heads = width // HEAD_DIM
    saved = saved_shapes(rows, width, geo.wide_width, heads)
    bufs, units, wholes = [], [], []
    for name in geo.plain:
        k, sent, unit, lanes = geo.kind[name]
        bufs.append(pltpu.VMEM((geo.number[name], geo.n_z * sent, lanes), BF))
        if name in names_perm:
            units.append(pltpu.VMEM((geo.number[name], k, unit, lanes), BF))
    wholes = [(geo.whole_shape(name), BF) for name in ("a", "v", "c")]
    n_y, n_z = geo.n_y, geo.n_z
    n_keeps = geo.layers * (len(saved) + geo.pairs + len(geo.down) + 1)
    vec_rows = geo.layers * 10
    outs = [
        jax.ShapeDtypeStruct((rows, width), BF),
        jax.ShapeDtypeStruct((vec_rows, width), F32),
        jax.ShapeDtypeStruct((geo.layers * 3, geo.wide_width), F32),
        jax.ShapeDtypeStruct(*wholes[0]),
        jax.ShapeDtypeStruct(*wholes[2]),
        jax.ShapeDtypeStruct((geo.layers, rows, width), F32),
    ] + [jax.ShapeDtypeStruct(*saved[name]) for _ in range(geo.layers) for name in saved]
    found = pl.pallas_call(
        functools.partial(forward_kernel, geo, names_perm, list(saved)),
        out_shape=outs,
        in_specs=[IN_VMEM] * (len(sources) + len(perms) + 6),
        out_specs=[IN_VMEM] * 3 + [ANY] * (len(outs) - 3),
        scratch_shapes=[pltpu.VMEM(*whole) for whole in wholes]
        + bufs
        + units
        + [pltpu.VMEM(*saved[name]) for _ in range(geo.layers) for name in saved]
        + [
            pltpu.VMEM((geo.layers + 1, rows, width), F32),
            pltpu.VMEM(wholes[1][0][1:], F32),
            dma(n_keeps),
            dma(total),
            dma(total),
            dma(total, n_z),
            dma(total, n_z),
            dma(total),
            dma(total),
            dma(total, n_y),
            dma(total, n_y),
            dma(total, 2, n_y),
            dma(total, 2, n_y),
            dma(total, 2 * n_y),
            dma(total, 2 * n_y),
            dma(geo.layers),
            dma(geo.layers, 2),
            dma(geo.layers, 2, n_y),
            dma(geo.layers, 2, n_y),
        ]
        + [dma(geo.layers, 2, n_z, 2 * n_y)] * 4,
        compiler_params=pltpu.CompilerParams(
            collective_id=0, has_side_effects=True, vmem_limit_bytes=60 * 2**20
        ),
    )(*sources, *perms, act, mask, *spread_tables(geo))
    names = list(saved)
    kept = [dict(zip(names, found[6 + layer * len(names) :])) for layer in range(geo.layers)]
    return found[:6], kept


def pack_gradients(geo, grad_d, grad_f, tables, wide_v, stage_v):
    owner_d, rest_d, owner_f, rest_f = tables
    lines = geo.kind["v"][1]
    wide_v[...] = jnp.zeros_like(wide_v)
    pick_d = lax.broadcasted_iota(jnp.int32, (geo.slot, geo.width), 0) == rest_d[...]
    for line in range(geo.lines_d):
        parts = []
        for at in range(geo.per_row):
            row = line * geo.per_row + at
            if row < geo.layers * 10:
                parts.append(jnp.where(pick_d, grad_d[row : row + 1, :], 0.0))
            else:
                parts.append(jnp.zeros(pick_d.shape, F32))
        wide_v[pl.ds(line, geo.owners, stride=lines), :] = mm_nt(
            owner_d[...], jnp.concatenate(parts, 0).astype(BF)
        )
    pick_f = lax.broadcasted_iota(jnp.int32, (128, geo.width), 0)
    for row in range(geo.layers * 3):
        total = None
        for first in range(0, geo.wide_width, geo.width):
            lanes = slice(first, first + geo.width)
            part = jnp.where(pick_f == rest_f[:, lanes], grad_f[row : row + 1, lanes], 0.0).astype(BF)
            part = mm_nt(owner_f[:, lanes], part)
            total = part if total is None else total + part
        wide_v[pl.ds(geo.lines_d + row, geo.owners, stride=lines), :] = total
    stage_v[...] = wide_v[...].astype(BF).reshape(stage_v.shape)


class Ring:
    def __init__(self, sources, slots, sems):
        self.slots, self.size, self.used = slots, slots.shape[0], 0
        self.copies = [
            pltpu.make_async_copy(source, slots.at[at % self.size], sems.at[at % self.size])
            for at, source in enumerate(sources)
        ]
        for copy in self.copies[: self.size]:
            copy.start()

    def next(self):
        at = self.used
        self.used += 1
        if 0 < at and at - 1 + self.size < len(self.copies):
            self.copies[at - 1 + self.size].start()
        self.copies[at].wait()
        return self.slots[at % self.size]


SCATTER_SEMS = ("cs", "cr", "ms", "mr", "es", "er", "zs", "zr", "ls", "lr", "fx", "fy")
Z_SLOTS = 3
LINE_LAGS = (4, 3)
SCATTER_LAGS = (0, 1, 3, 5, 7)


def ring_slots(geo):
    return 3 if geo.roomy else 2


def backward_kernel(geo, names_perm, names, *refs):
    refs = list(refs)
    take = lambda number: [refs.pop(0) for _ in range(number)]
    by_kind = lambda kinds=geo.kinds: dict(zip(kinds, take(len(kinds))))
    saved_names, work_names = names
    layers, blocks, width = geo.layers, geo.blocks, geo.width
    perms = dict(zip(names_perm, take(len(names_perm))))
    cot_ref, vec_d, vec_f = take(3)
    tables = take(4)
    whole_a, whole_b, kept_x = take(3)
    kept = [dict(zip(saved_names, take(len(saved_names)))) for _ in range(layers)]
    for layer in range(layers):
        kept[layer]["x"] = kept_x.at[layer]
    back_ref, out_qkv, out_out, out_up, out_down, out_d, out_f = take(7)
    fields = dict(zip(saved_names, take(len(saved_names))))
    fields.update(zip(work_names, take(len(work_names))))
    stages, sums, mids, ends = [by_kind() for _ in range(4)]
    z_send, z_recv = [by_kind(geo.plain) for _ in range(2)]
    line_refs = take(1) if geo.lined else []
    x_ref, grad_d, grad_f, wide_v, slots = take(5)
    last_low, last_ffn = take(2) if geo.roomy else (None, None)
    sem_l, sem_w = take(2)
    sems = dict(zip(SCATTER_SEMS, take(len(SCATTER_SEMS))))
    fields.update(d_hidden=fields["sub_ffn"], x=x_ref, back=back_ref, grad_d=grad_d, grad_f=grad_f)
    place = Place(geo)

    def writer(chunk):
        name, at, lead, first = chunk
        rows_a, rows_b, lines = geo.rows_a, geo.rows_b, geo.lines_d

        def put_a(value):
            layer = at // geo.pairs
            for side in range(2):
                block = 2 * (at % geo.pairs) + side
                piece = value[side * rows_a : (side + 1) * rows_a]
                if block < 3:
                    out_qkv[layer, :, block * width : (block + 1) * width] = piece
                elif block == 3:
                    out_out[layer] = piece
                else:
                    out_up[layer, :, (block - 4) * width : (block - 3) * width] = piece

        def put_down(value):
            out_down[lead, :, first : first + value.shape[1]] = value[:rows_b]

        def put_v(value):
            out_d[...] = value[:lines]
            out_f[...] = value[lines : lines + layers * 3]

        return {"a": put_a, "v": put_v}.get(name, put_down)

    order, seen = [], {name: [] for name in geo.kinds}
    early = {layer: geo.down for layer in range(layers)}
    late = ("c", "d") if geo.roomy else ()
    early[0] = tuple(name for name in geo.down if name not in late)
    for layer in reversed(range(layers)):
        early[layer] = early[layer][::-1]
        order += [chunk_down(geo, layer, name) for name in early[layer]]
        order += [chunk_a(geo, layer, pair) for pair in list(range(2, geo.pairs)) + [1, 0]]
    order.append(("v", 0, 0, 0))
    order += [chunk_down(geo, 0, name) for name in late]
    moves, stage_of = [], []
    for number, chunk in enumerate(order):
        name = chunk[0]
        stage = stages[name].at[len(seen[name]) % stages[name].shape[0]]
        slots_z = z_send[name].shape[0] if name in z_send else 1
        z_slot = len(seen[name]) % slots_z
        before = seen[name][-slots_z] if len(seen[name]) >= slots_z else None
        move = (ScatterLine if name == "l" else Scatter)(
            place, number, chunk, stage, sums, mids, ends, perms, z_send, z_recv, z_slot, before,
            writer(chunk), sems,
        )
        if name == "l":
            move.c_line = len(seen[name])
            move.land(line_refs[0].at[move.c_line])
        seen[name].append(move)
        stage_of.append(stage)
        moves.append(move)
    for number, chunk in enumerate(order):
        if chunk[0] == "a" and chunk[1] >= geo.pairs:
            moves[number].heir = moves[[later[:2] for later in order].index(("a", chunk[1] - geo.pairs))]
    step, plan = [0], {}
    for number, chunk in enumerate(order):
        move = moves[number]
        acts = [move.start, move.pair, move.middle, move.last, move.finish]
        lags = list(SCATTER_LAGS)
        if chunk[0] == "l":
            hops = [lambda move=move, hop=hop: move.relay(hop) for hop in range(1, geo.n_z - 1)]
            acts[2:2] = hops + [move.collect]
            first, each = LINE_LAGS
            lags[2:] = [first + each * at for at in range(len(hops) + 1)]
            lags += [lags[-1] + 1, lags[-1] + 2, lags[-1] + 2]
        for lag, act in zip(lags, acts):
            plan.setdefault(number + lag, []).append((lag, act))

    def serve():
        for _, act in sorted(plan.get(step[0], []), key=lambda pair: pair[0]):
            act()
        step[0] += 1

    def stage_down(name, rows_ref, low_ref):
        unit = geo.kind[name][2]
        first, lanes = geo.lanes_of[name]
        for column in range(geo.n_dp // 2):
            rows = slice(column * 2 * unit, (column + 1) * 2 * unit)
            value = mm_tn(rows_ref[:, rows], low_ref[:, first : first + lanes])
            stage_of[step[0]][0, column // 2, column % 2] = value.astype(BF).reshape(2, unit, lanes)

    def stage_a(side, value):
        stage_of[step[0]][side] = value.astype(BF).reshape(geo.n_y, 2, 2, -1, width)

    loads = {}
    field_names = ["x"] + list(saved_names)

    def fetch(layer, *found):
        for name in found:
            loads[name] = pltpu.make_async_copy(
                kept[layer][name], fields[name], sem_l.at[field_names.index(name)]
            )
            loads[name].start()

    def ready(*found):
        for name in found:
            loads[name].wait()

    fetch(layers - 1, "sub_ffn", "hidden", "normed_ffn", "after", "sub", "context", "prob", "qkv", "normed", "x")
    sources = []
    for layer in reversed(range(layers)):
        parts = geo.wide_width // width
        sources += [whole_b.at[layer, pl.ds(part * width, width)] for part in range(parts)]
        sources += [whole_a.at[layer * blocks + at] for at in list(range(4, blocks)) + [3, 0, 1, 2]]
    ring = Ring(sources, slots, sem_w)
    cot_copy = pltpu.make_async_copy(cot_ref, back_ref, sem_l.at[len(field_names)])
    cot_copy.start()
    place.greet()
    cot_copy.wait()
    for layer in reversed(range(layers)):
        one = Layer(
            fields, lambda at: ring.next(), lambda rows, lanes: ring.next(), vec_d, vec_f, layer,
            width // HEAD_DIM,
        )
        again = (lambda *found: fetch(layer - 1, *found)) if layer > 0 else (lambda *found: None)
        one.backward_start()
        ready("sub_ffn")
        for name in early[layer]:
            stage_down(name, one.sub_ffn, one.low)
            serve()
        if layer == 0 and late:
            last_low[...] = one.low[...]
            last_ffn[...] = one.sub_ffn[...]
        one.backward_down()
        ready("hidden")
        one.backward_gelu()
        again("hidden")
        ready("normed_ffn")
        for pair in range(2, geo.pairs):
            stage_a(0, one.grad_up(2 * pair - 4))
            stage_a(1, one.grad_up(2 * pair - 3))
            serve()
        again("normed_ffn")
        ready("after")
        one.backward_up()
        again("after", "sub_ffn")
        ready("sub", "context")
        stage_a(1, one.grad_out())
        one.backward_out()
        again("sub", "context")
        ready("prob", "qkv")
        one.backward_attention()
        again("prob", "qkv")
        ready("normed")
        stage_a(0, one.grad_qkv(2))
        serve()
        stage_a(0, one.grad_qkv(0))
        stage_a(1, one.grad_qkv(1))
        serve()
        again("normed")
        ready("x")
        one.backward_qkv()
        again("x")
    pack_gradients(geo, grad_d, grad_f, tables, wide_v, stage_of[step[0]])
    serve()
    for name in late:
        stage_down(name, last_ffn, last_low)
        serve()
    while step[0] <= max(plan):
        serve()
    for move in moves:
        move.drain()


def run_backward(geo, cot, vec_d, vec_f, whole_a, whole_b, kept_x, kept):
    rows, width = cot.shape
    layers, n_y, n_z = geo.layers, geo.n_y, geo.n_z
    heads = width // HEAD_DIM
    saved, work = saved_shapes(rows, width, geo.wide_width, heads), work_shapes(rows, width, geo.wide_width)
    names = (list(saved), list(work))
    names_perm = [name for name in geo.plain if geo.permuted(name)]
    perms = [jnp.asarray(geo.permutation(name).T, BF) for name in names_perm]
    total = sum(geo.number.values())
    groups = [[] for _ in range(6)]
    for name in geo.kinds:
        k, sent, unit, lanes = geo.kind[name]
        number = geo.number[name]
        mid_steps = max(n_y - 1, (n_y + 1) // 2)
        groups[0].append(pltpu.VMEM((2 if name == "a" else 1, k, n_y, 2, 2, unit, lanes), BF))
        groups[1].append(pltpu.VMEM((number, k, n_y, 2, unit, lanes), BF))
        landing = geo.pairs if name == "a" else number
        unit = sent if name == "l" else unit
        groups[2].append(pltpu.VMEM((landing, mid_steps, k, 2, unit, lanes), BF))
        groups[3].append(pltpu.VMEM((number, mid_steps, k, unit, lanes), BF))
        if name == "l":
            continue
        groups[4].append(pltpu.VMEM((min(number, Z_SLOTS), n_z, sent, lanes), BF))
        groups[5].append(pltpu.VMEM((number, n_z, sent, lanes), BF))
    scratch = [pltpu.VMEM(*saved[name]) for name in saved] + [pltpu.VMEM(*work[name]) for name in work]
    scratch += sum(groups, [])
    if geo.lined:
        _, sent, _, lanes = geo.kind["l"]
        scratch.append(pltpu.VMEM((layers, 2, n_z, n_y, 2, sent, lanes), BF))
    scratch += [
        pltpu.VMEM((rows, width), F32),
        pltpu.VMEM((layers * 10, width), F32),
        pltpu.VMEM((layers * 3, geo.wide_width), F32),
        pltpu.VMEM((geo.owners * geo.kind["v"][1], 128), F32),
        pltpu.VMEM((ring_slots(geo), width, width), BF),
    ]
    if geo.roomy:
        scratch += [pltpu.VMEM((rows, width), BF), pltpu.VMEM((rows, geo.wide_width), BF)]
    scratch += [
        dma(2 + len(saved)),
        dma(ring_slots(geo)),
        dma(total),
        dma(total),
        dma(total, 2, n_y),
        dma(total, 2, n_y),
        dma(total, 2, n_y),
        dma(total, 2, n_y),
        dma(total, n_z),
        dma(total, n_z),
        dma(layers, 2, n_z),
        dma(layers, 2, n_z),
        pltpu.SemaphoreType.REGULAR((total,)),
        pltpu.SemaphoreType.REGULAR((total, n_y)),
    ]
    return pl.pallas_call(
        functools.partial(backward_kernel, geo, names_perm, names),
        out_shape=[
            jax.ShapeDtypeStruct((rows, width), F32),
            jax.ShapeDtypeStruct((layers, geo.rows_a, 3 * width), F32),
            jax.ShapeDtypeStruct((layers, geo.rows_a, width), F32),
            jax.ShapeDtypeStruct((layers, geo.rows_a, geo.wide_width), F32),
            jax.ShapeDtypeStruct((layers, geo.rows_b, width), F32),
            jax.ShapeDtypeStruct((geo.lines_d, 128), F32),
            jax.ShapeDtypeStruct((layers * 3, 128), F32),
        ],
        in_specs=[IN_VMEM] * len(perms) + [ANY] + [IN_VMEM] * 6 + [ANY] * (3 + layers * len(saved)),
        out_specs=[IN_VMEM] * 7,
        scratch_shapes=scratch,
        compiler_params=pltpu.CompilerParams(
            collective_id=1, has_side_effects=True, vmem_limit_bytes=63 * 2**20
        ),
    )(
        *perms, cot, vec_d, vec_f, *spread_tables(geo), whole_a, whole_b, kept_x,
        *[kept[layer][name] for layer in range(layers) for name in saved],
    )


def pack_kernel(geo, *refs):
    act_short, act_long, len_short, len_long, w_qkv, w_out, w_up, w_down = refs[:8]
    gains_d, shifts_d, gains_ff, shifts_ff, cot_short, cot_long = refs[8:14]
    sources = dict(zip(geo.kinds, refs[14:]))
    act, mask, cot, lines = refs[14 + len(geo.kinds) :]
    width, rows_a, rows_b = geo.width, geo.rows_a, geo.rows_b

    def block(layer, at):
        if at == 3:
            return wide(w_out[layer])
        first = at if at < 3 else at - 4
        return wide((w_qkv if at < 3 else w_up)[layer, :, first * width : (first + 1) * width])

    def filled(pieces, rows):
        have = sum(piece.shape[0] for piece in pieces)
        if have < rows:
            pieces = pieces + [jnp.zeros((rows - have, pieces[0].shape[1]), F32)]
        return (jnp.concatenate(pieces, 0) if len(pieces) > 1 else pieces[0]).astype(BF)

    for layer in range(geo.layers):
        for pair in range(geo.pairs):
            pieces = [block(layer, 2 * pair), block(layer, 2 * pair + 1)]
            sources["a"][layer * geo.pairs + pair] = filled(pieces, geo.kind["a"][1])
        for name in geo.down:
            first, lanes = geo.lanes_of[name]
            piece = w_down[layer, :, first : first + lanes]
            if rows_b != geo.kind[name][1]:
                piece = filled([wide(piece)], geo.kind[name][1])
            sources[name][layer] = piece
    lines[...] = jnp.zeros_like(lines)
    gains_wide = wide(gains_ff[...])
    for layer in range(geo.layers):
        gains, shifts, shifts_wide = wide(gains_d[layer]), wide(shifts_d[layer]), wide(shifts_ff[layer])
        for at in range(10):
            line, lane = divmod(layer * 10 + at, geo.per_row)
            value = gains[at : at + 1] if at < 3 else shifts[at - 3 : at - 2]
            lines[line : line + 1, lane * geo.slot : lane * geo.slot + rows_a] = value
        for at in range(3):
            line = geo.lines_d + layer * 3 + at
            lines[line : line + 1, :rows_b] = gains_wide[layer : layer + 1] if at == 0 else shifts_wide[at - 1 : at]
    sources["v"][0] = lines[...].astype(BF)
    short = act_short.shape[0]
    act[:short] = act_short[...]
    act[short:] = act_long[...]
    rows = act.shape[0]

    def valid(shape, dim):
        at = lax.broadcasted_iota(jnp.int32, shape, dim)
        return jnp.where(jnp.where(at < short, at - len_short[0], at - short - len_long[0]) < 0, 1.0, 0.0)

    def bucket(dim):
        return jnp.where(lax.broadcasted_iota(jnp.int32, (rows, rows), dim) < short, 0, 1)

    mask[...] = jnp.where(bucket(0) == bucket(1), valid((rows, rows), 1), 0.0)
    keep = valid((rows, width), 0)
    cot[:short] = wide(cot_short[...]) * keep[:short]
    cot[short:] = wide(cot_long[...]) * keep[short:]


def run_pack(geo, args):
    rows = args[0].shape[0] + args[1].shape[0]
    shapes = []
    for name in geo.kinds:
        _, sent, _, lanes = geo.kind[name]
        shapes.append(jax.ShapeDtypeStruct((geo.number[name], sent, lanes), BF))
    shapes += [
        jax.ShapeDtypeStruct((rows, geo.width), BF),
        jax.ShapeDtypeStruct((rows, rows), F32),
        jax.ShapeDtypeStruct((rows, geo.width), F32),
    ]
    in_smem = pl.BlockSpec(memory_space=pltpu.SMEM)
    return pl.pallas_call(
        functools.partial(pack_kernel, geo),
        out_shape=shapes,
        in_specs=[IN_VMEM] * 2 + [in_smem] * 2 + [IN_VMEM] * 10,
        out_specs=[IN_VMEM] * len(shapes),
        scratch_shapes=[pltpu.VMEM((geo.kind["v"][1], 128), F32)],
        compiler_params=pltpu.CompilerParams(vmem_limit_bytes=63 * 2**20),
    )(*args)


def unpack_kernel(geo, *refs):
    out, back, g_qkv, g_out, g_up, g_down, lines_d, lines_f = refs[:8]
    out_short, out_long, back_short, back_long, t_qkv, t_out, t_up, t_down = refs[8:16]
    t_gains_d, t_shifts_d, t_gains_ff, t_shifts_ff = refs[16:]
    short = out_short.shape[0]
    out_short[...] = out[:short]
    out_long[...] = out[short:]
    back_short[...] = back[:short]
    back_long[...] = back[short:]
    for source, target in ((g_qkv, t_qkv), (g_out, t_out), (g_up, t_up), (g_down, t_down)):
        target[...] = source[...]
    for layer in range(geo.layers):
        for at in range(10):
            line, lane = divmod(layer * 10 + at, geo.per_row)
            value = lines_d[line : line + 1, lane * geo.slot : lane * geo.slot + geo.rows_a]
            if at < 3:
                t_gains_d[layer, at : at + 1, :] = value
            else:
                t_shifts_d[layer, at - 3 : at - 2, :] = value
        for at in range(3):
            value = lines_f[layer * 3 + at : layer * 3 + at + 1, : geo.rows_b]
            if at == 0:
                t_gains_ff[layer : layer + 1, :] = value
            else:
                t_shifts_ff[layer, at - 1 : at, :] = value


def run_unpack(geo, found, args):
    like = lambda index, dtype: jax.ShapeDtypeStruct(args[index].shape, dtype)
    shapes = [like(0, BF), like(1, BF), like(0, F32), like(1, F32)]
    shapes += [like(index, F32) for index in range(4, 12)]
    return pl.pallas_call(
        functools.partial(unpack_kernel, geo),
        out_shape=shapes,
        in_specs=[IN_VMEM] * len(found),
        out_specs=[IN_VMEM] * len(shapes),
        compiler_params=pltpu.CompilerParams(vmem_limit_bytes=63 * 2**20),
    )(*found)


def on_device(*args):
    n_dp, n_z = lax.axis_size("dp"), lax.axis_size("fsdp")
    geo = Geometry(n_dp, n_z, args[4].shape, args[6].shape, args[7].shape)
    *sources, act, mask, cot = run_pack(geo, args)
    found, kept = run_forward(geo, sources, act, mask)
    out, vec_d, vec_f, whole_a, whole_b, kept_x = found
    grads = run_backward(geo, cot, vec_d, vec_f, whole_a, whole_b, kept_x, kept)
    return tuple(run_unpack(geo, (out,) + tuple(grads), args))


def solution(mesh):
    return jax.shard_map(
        on_device,
        mesh=mesh,
        in_specs=(
            P(("dp", "fsdp"), None),
            P(("dp", "fsdp"), None),
            P(("dp", "fsdp")),
            P(("dp", "fsdp")),
            P(None, ("dp", "fsdp"), None),
            P(None, ("dp", "fsdp"), None),
            P(None, ("dp", "fsdp"), None),
            P(None, ("dp", "fsdp"), None),
            P(None, None, ("dp", "fsdp")),
            P(None, None, ("dp", "fsdp")),
            P(None, ("dp", "fsdp")),
            P(None, None, ("dp", "fsdp")),
            P(("dp", "fsdp"), None),
            P(("dp", "fsdp"), None),
        ),
        out_specs=(
            P(("dp", "fsdp"), None),
            P(("dp", "fsdp"), None),
            P(("dp", "fsdp"), None),
            P(("dp", "fsdp"), None),
            P(None, ("dp", "fsdp"), None),
            P(None, ("dp", "fsdp"), None),
            P(None, ("dp", "fsdp"), None),
            P(None, ("dp", "fsdp"), None),
            P(None, None, ("dp", "fsdp")),
            P(None, None, ("dp", "fsdp")),
            P(None, ("dp", "fsdp")),
            P(None, None, ("dp", "fsdp")),
        ),
        check_vma=False,
    )
```

```python
import functools

import jax
import jax.numpy as jnp
import numpy as np
from jax import lax
from jax.experimental import pallas as pl
from jax.experimental.pallas import tpu as pltpu
from jax.sharding import PartitionSpec as P

HEAD_DIM = 64

epsilon = 1e-05


BF = jnp.bfloat16
F32 = jnp.float32
MESH = pl.DeviceIdType.MESH


def round16(count):
    return (count + 15) // 16 * 16


class Geometry:
    def __init__(self, n_dp, n_z, w_qkv, w_up, w_down):
        self.n_dp, self.n_z, self.n_y = n_dp, n_z, n_dp // 4
        self.layers = w_qkv[0]
        self.width = w_qkv[2] // 3
        self.rows_a, self.rows_b = w_qkv[1], w_down[1]
        self.blocks = 4 + w_up[2] // self.width
        self.pairs = self.blocks // 2
        half = self.width // 2
        self.lined = self.rows_b % 16 == 0
        self.roomy = self.n_y <= 2
        self.first_down = "l" if self.lined else "b"
        self.lanes_of = {self.first_down: (0, half), "c": (half, half - 128), "d": (2 * half - 128, 128)}
        self.down = tuple(self.lanes_of)
        self.kinds = ("a", "v") + self.down
        self.plain = tuple(name for name in self.kinds if name != "l")
        self.owners = n_dp * n_z
        self.wide_width = w_up[2]
        self.slot = 8
        while self.slot < self.rows_a:
            self.slot *= 2
        self.per_row = 128 // self.slot
        self.lines_d = -(-self.layers * 10 // self.per_row)
        lines = round16(self.lines_d + self.layers * 3)
        self.kind = {
            "a": (2, round16(2 * self.rows_a), self.rows_a * n_z, self.width),
            "v": (1, lines, lines * n_z, 128),
        }
        self.real = {"a": self.rows_a, "v": self.kind["v"][1]}
        self.number = {"a": self.layers * self.pairs, "v": 1}
        for name, (_, lanes) in self.lanes_of.items():
            self.kind[name] = (1, round16(self.rows_b), self.rows_b * n_z, lanes)
            self.real[name] = self.rows_b
            self.number[name] = self.layers

    def permuted(self, name):
        k, sent, unit, _ = self.kind[name]
        return k * unit != sent * self.n_z or k > 1

    def permutation(self, name):
        k, sent, unit, _ = self.kind[name]
        real = self.real[name]
        table = np.zeros((k * unit, self.n_z * sent), np.float32)
        for block in range(k):
            for z in range(self.n_z):
                for row in range(real):
                    table[block * unit + z * real + row, z * sent + block * real + row] = 1
        return table

    def whole_shape(self, name):
        _, _, unit, lanes = self.kind[name]
        lead = {"a": self.layers * self.blocks, "v": 1}.get(name, self.layers)
        return (lead, self.n_dp * unit, lanes if name == "v" else self.width)


class Place:
    def __init__(self, geo):
        self.geo = geo
        self.d, self.z = lax.axis_index("dp"), lax.axis_index("fsdp")
        self.core = lax.rem(self.d, 2)
        self.x = lax.rem(self.d // 2, 2)
        self.y = self.d // 4

    def y_off(self, step):
        return lax.rem(self.y + step + self.geo.n_y, self.geo.n_y)

    def z_off(self, step):
        return lax.rem(self.z + step + self.geo.n_z, self.geo.n_z)

    def dev_core(self):
        return (self.d + 1 - 2 * self.core, self.z)

    def dev_x(self):
        return (self.d + 2 - 4 * self.x, self.z)

    def dev_y(self, step):
        return (self.y_off(step) * 4 + self.x * 2 + self.core, self.z)

    def dev_z(self, step):
        return (self.d, self.z_off(step))

    def greet(self):
        barrier = pltpu.get_barrier_semaphore()
        partners = [self.dev_core(), self.dev_x()]
        partners += [self.dev_y(step) for step in range(1, self.geo.n_y)]
        partners += [self.dev_z(step) for step in range(1, self.geo.n_z)]
        for partner in partners:
            pl.semaphore_signal(barrier, inc=1, device_id=partner, device_id_type=MESH)
        pl.semaphore_wait(barrier, len(partners))


def remote(src, dst, send, recv, device):
    return pltpu.make_async_remote_copy(
        src_ref=src, dst_ref=dst, send_sem=send, recv_sem=recv, device_id=device, device_id_type=MESH
    )


def chunk_a(geo, layer, pair):
    return ("a", layer * geo.pairs + pair, layer * geo.blocks + 2 * pair, 0)


def chunk_down(geo, layer, name):
    return (name, layer, layer, geo.lanes_of[name][0])


def rows_of(whole, name, lead, first, k, unit, lanes):
    def at(y, x, core):
        rows = pl.ds(pl.multiple_of((y * 4 + x * 2 + core) * unit, 16), unit)
        return whole.at[pl.ds(lead, k), rows, slice(None) if name in ("a", "v") else pl.ds(first, lanes)]

    return at


def ways_of(number, k):
    if k == 1:
        return [(slice(0, 1), number % 2 == 0)]
    return [(slice(0, 1), True), (slice(1, k), False)]


class Gather:
    def __init__(self, place, number, chunk, sources, bufs, units, perms, wholes, sems):
        self.p, self.c = place, number
        name, at, lead, first = chunk
        self.ways = ways_of(number, place.geo.kind[name][0])
        k, self.sent, unit, lanes = place.geo.kind[name]
        self.source = sources[name].at[at]
        self.buf = bufs[name].at[at]
        self.perm = perms.get(name)
        self.unit_buf = units[name].at[at] if self.perm is not None else None
        self.unit = self.unit_buf if self.perm is not None else bufs[name].at[pl.ds(at, 1)]
        self.to = rows_of(wholes[name], name, lead, first, k, unit, lanes)
        self.sems = sems
        self.pending = []

    def slot(self, z):
        return self.buf.at[pl.ds(pl.multiple_of(z * self.sent, 16), self.sent)]

    def send(self, src, dst, send, recv, device):
        copy = remote(src, dst, send, recv, device)
        copy.start()
        self.pending.append(copy)

    def arrived(self, dst, send, recv, device):
        remote(dst, dst, send, recv, device).wait_recv()

    def start_z(self):
        p, s, c = self.p, self.sems, self.c
        self.local_z = pltpu.make_async_copy(self.source, self.slot(p.z), s["lz"].at[c])
        self.local_z.start()
        for step in range(1, p.geo.n_z):
            self.send(self.source, self.slot(p.z), s["zs"].at[c, step], s["zr"].at[c, step], p.dev_z(step))

    def own(self):
        p, s, c = self.p, self.sems, self.c
        self.local_z.wait()
        for step in range(1, p.geo.n_z):
            self.arrived(self.slot(p.z_off(-step)), s["zs"].at[c, step], s["zr"].at[c, step], p.dev_z(step))
        if self.perm is not None:
            k, unit, lanes = self.unit_buf.shape
            mixed = jnp.dot(self.perm[...], self.buf[...], preferred_element_type=F32)
            self.unit_buf[...] = mixed.astype(BF).reshape(k, unit, lanes)
        here = self.to(p.y, p.x, p.core)
        self.local = pltpu.make_async_copy(self.unit, here, s["lo"].at[c])
        self.send(self.unit, here, s["xs"].at[c], s["xr"].at[c], p.dev_x())
        for step in range(1, p.geo.n_y):
            self.send(self.unit, here, s["ys"].at[c, step], s["yr"].at[c, step], p.dev_y(step))
        self.send(self.unit, here, s["cs"].at[c, 0], s["cr"].at[c, 0], p.dev_core())
        self.local.start()

    def forward(self):
        p, s, c = self.p, self.sems, self.c
        n_y = p.geo.n_y
        from_x = self.to(p.y, 1 - p.x, p.core)
        self.arrived(from_x, s["xs"].at[c], s["xr"].at[c], p.dev_x())
        for way, (blocks, by_x) in enumerate(self.ways):
            for step in range(1, n_y) if by_x else ():
                at = (c, way, step)
                rows = from_x.at[blocks]
                self.send(rows, rows, s["ds"].at[at], s["dr"].at[at], p.dev_y(step))
        self.send(from_x, from_x, s["cs"].at[c, 1], s["cr"].at[c, 1], p.dev_core())
        for step in range(1, n_y):
            from_y = self.to(p.y_off(-step), p.x, p.core)
            self.arrived(from_y, s["ys"].at[c, step], s["yr"].at[c, step], p.dev_y(step))
            for way, (blocks, by_x) in enumerate(self.ways):
                if not by_x:
                    at = (c, way, step)
                    rows = from_y.at[blocks]
                    self.send(rows, rows, s["ds"].at[at], s["dr"].at[at], p.dev_x())
            self.send(from_y, from_y, s["cs"].at[c, 2 * step], s["cr"].at[c, 2 * step], p.dev_core())

    def corner(self):
        p, s, c = self.p, self.sems, self.c
        for step in range(1, p.geo.n_y):
            far = self.to(p.y_off(-step), 1 - p.x, p.core)
            for way, (blocks, _) in enumerate(self.ways):
                at = (c, way, step)
                self.arrived(far.at[blocks], s["ds"].at[at], s["dr"].at[at], p.dev_x())
            self.send(far, far, s["cs"].at[c, 2 * step + 1], s["cr"].at[c, 2 * step + 1], p.dev_core())

    def arrive(self):
        p, s, c = self.p, self.sems, self.c
        for step in range(p.geo.n_y):
            for flip in range(2):
                x = p.x if flip == 0 else 1 - p.x
                got = self.to(p.y_off(-step), x, 1 - p.core)
                at = 2 * step + flip
                self.arrived(got, s["cs"].at[c, at], s["cr"].at[c, at], p.dev_core())
        self.local.wait()

    def drain(self):
        for copy in self.pending:
            copy.wait_send()


def when(condition, act):
    pl.when(condition)(act)


def on_line(place, way, step):
    at = place.z - step if way == 0 else place.z + step
    return (at >= 0) & (at < place.geo.n_z), at


class GatherLine:
    def __init__(self, place, number, chunk, sources, wholes, sems):
        self.p, self.c = place, number
        _, at, lead, first = chunk
        _, sent, _, lanes = place.geo.kind["l"]
        self.source = sources["l"].at[at]
        self.half_a = number % 2 == 0
        whole = wholes["l"]

        def piece(y, x, core, z):
            device = (y * 4 + x * 2 + core) * place.geo.n_z + z
            rows = pl.ds(pl.multiple_of(device * sent, 16), sent)
            return whole.at[lead, rows, pl.ds(first, lanes)]

        self.piece = piece
        self.sems = sems
        self.pending, self.line_pending = [], []

    def send(self, src, dst, send, recv, device):
        copy = remote(src, dst, send, recv, device)
        copy.start()
        self.pending.append(copy)

    def arrived(self, dst, send, recv, device):
        remote(dst, dst, send, recv, device).wait_recv()

    def from_column(self, at, z, core):
        p = self.p
        return self.piece(p.y_off(-(at // 2)), p.x if at % 2 == 0 else 1 - p.x, core, z)

    def line_send(self, column, hop):
        p, s, c = self.p, self.sems, self.c
        for way in range(2):
            valid, z = on_line(p, way, hop - 1)
            further, target = on_line(p, 1 - way, 1)

            def copy(z=z, target=target, way=way):
                rows = self.from_column(column, z, p.core)
                at = (c, way, hop, column)
                return remote(rows, rows, s["gs"].at[at], s["gr"].at[at], (p.d, target))

            when(valid & further, lambda copy=copy: copy().start())
            self.line_pending.append((valid & further, copy))

    def to_core(self, column, z, at):
        s = self.sems
        rows = self.from_column(column, z, self.p.core)
        return remote(rows, rows, s["hs"].at[at], s["hr"].at[at], self.p.dev_core())

    def start(self):
        p, s, c = self.p, self.sems, self.c
        here = self.piece(p.y, p.x, p.core, p.z)
        self.local = pltpu.make_async_copy(self.source, here, s["gl"].at[c])
        self.send(self.source, here, s["gx"].at[c, 0], s["gx"].at[c, 1], p.dev_x())
        for step in range(1, p.geo.n_y):
            self.send(self.source, here, s["gy"].at[c, 0, step], s["gy"].at[c, 1, step], p.dev_y(step))
        self.local.start()
        at = (c, 0, 0, 0)
        self.send(self.source, here, s["hs"].at[at], s["hr"].at[at], p.dev_core())

    def forward(self):
        p, s, c = self.p, self.sems, self.c
        n_y = p.geo.n_y
        self.local.wait()
        rows = self.from_column(1, p.z, p.core)
        self.arrived(rows, s["gx"].at[c, 0], s["gx"].at[c, 1], p.dev_x())
        if self.half_a:
            for step in range(1, n_y):
                self.send(rows, rows, s["gd"].at[c, 0, step], s["gd"].at[c, 1, step], p.dev_y(step))
        self.keep_core(1)
        for step in range(1, n_y):
            rows = self.from_column(2 * step, p.z, p.core)
            self.arrived(rows, s["gy"].at[c, 0, step], s["gy"].at[c, 1, step], p.dev_y(step))
            if not self.half_a:
                self.send(rows, rows, s["gd"].at[c, 0, step], s["gd"].at[c, 1, step], p.dev_x())
            self.keep_core(2 * step)

    def keep_core(self, column):
        copy = self.to_core(column, self.p.z, (self.c, 0, 0, column))
        copy.start()
        self.pending.append(copy)

    def corner(self):
        p, s, c = self.p, self.sems, self.c
        for step in range(1, p.geo.n_y):
            rows = self.from_column(2 * step + 1, p.z, p.core)
            self.arrived(rows, s["gd"].at[c, 0, step], s["gd"].at[c, 1, step], p.dev_x())
            self.keep_core(2 * step + 1)

    def relay(self, hop, half):
        p, s, c = self.p, self.sems, self.c
        n_y = p.geo.n_y
        for column in range(half * n_y, (half + 1) * n_y):
            for way in range(2) if hop > 0 else ():
                valid, z = on_line(p, way, hop)
                at = (c, way, hop, column)

                def act(z=z, at=at):
                    rows = self.from_column(column, z, p.core)
                    remote(rows, rows, s["gs"].at[at], s["gr"].at[at], p.dev_x()).wait_recv()
                    self.to_core(column, z, at).start()

                when(valid, act)
                self.line_pending.append(
                    (valid, lambda column=column, z=z, at=at: self.to_core(column, z, at))
                )
            if hop < p.geo.n_z - 1:
                self.line_send(column, hop + 1)

    def arrive(self):
        p, s, c = self.p, self.sems, self.c
        for column in range(2 * p.geo.n_y):
            rows = self.from_column(column, p.z, 1 - p.core)
            at = (c, 0, 0, column)
            self.arrived(rows, s["hs"].at[at], s["hr"].at[at], p.dev_core())
            for hop in range(1, p.geo.n_z):
                for way in range(2):
                    valid, z = on_line(p, way, hop)
                    at = (c, way, hop, column)

                    def act(z=z, at=at):
                        rows = self.from_column(column, z, 1 - p.core)
                        self.arrived(rows, s["hs"].at[at], s["hr"].at[at], p.dev_core())

                    when(valid, act)

    def drain(self):
        for copy in self.pending:
            copy.wait_send()
        for valid, copy in self.line_pending:
            when(valid, lambda copy=copy: copy().wait_send())


def run_pipeline(stages, count, extra):
    last = max(lag for lag, _ in stages)
    first = min(lag for lag, _ in stages)
    for step in range(first, count + last):
        ahead = [stage for stage in stages if stage[0] < 0]
        ahead += stages[1:3]
        for lag, act in ahead + [(None, act) for act in extra.get(step, ())] + stages[len(ahead) :]:
            if lag is None:
                act()
            elif 0 <= step - lag < count:
                act(step - lag)


def dma(*shape):
    return pltpu.SemaphoreType.DMA(shape)


ANY = pl.BlockSpec(memory_space=pl.ANY)
IN_VMEM = pl.BlockSpec(memory_space=pltpu.VMEM)


def wide(values):
    return values.astype(F32)


class Scatter:
    def __init__(self, place, number, chunk, stage, sums, mids, ends, perms, z_send, z_recv, z_slot, before, put, sems):
        self.p, self.c = place, number
        name, at, _, _ = chunk
        self.k, self.sent, self.rows, self.lanes = place.geo.kind[name]
        self.ways = ways_of(number, self.k)
        self.part = slice(None)
        self.stage = stage
        self.sum = sums[name].at[at]
        shared, per_layer = name == "a", place.geo.pairs
        self.mid = mids[name].at[at % per_layer if shared else at]
        self.hands_on = shared and at >= per_layer
        self.takes_over = shared and at < place.geo.number[name] - per_layer
        self.heir = None
        self.end = ends[name].at[at]
        self.perm = perms.get(name)
        if name in z_send:
            self.z_send, self.z_recv = z_send[name].at[z_slot], z_recv[name].at[at]
        self.before, self.z_moves = before, []
        self.put = put
        self.sems = sems
        self.pending = []

    def send(self, src, dst, send, recv, device):
        copy = remote(src, dst, send, recv, device)
        copy.start()
        self.pending.append(copy)

    def arrived(self, dst, send, recv, device):
        remote(dst, dst, send, recv, device).wait_recv()

    def start(self):
        p, s, c = self.p, self.sems, self.c
        give = self.stage.at[:, :, :, 1 - p.core]
        self.given = remote(give, self.sum, s["cs"].at[c], s["cr"].at[c], p.dev_core())
        self.given.start()

    def pair(self):
        p, s, c = self.p, self.sems, self.c
        n_y = p.geo.n_y
        self.arrived(self.sum, s["cs"].at[c], s["cr"].at[c], p.dev_core())

        @pl.loop(0, self.k * n_y * 2)
        def _(at):
            where = (at // (2 * n_y), lax.rem(at // 2, n_y), lax.rem(at, 2))
            self.sum[where] = (wide(self.sum[where]) + wide(self.stage[where + (p.core,)])).astype(BF)

        self.given.wait_send()
        self.send_middle()

    def send_middle(self):
        p, s, c = self.p, self.sems, self.c
        n_y = p.geo.n_y
        for way, (blocks, by_x) in enumerate(self.ways):
            if self.takes_over:
                for step in range(1, n_y) if by_x else ():
                    pl.semaphore_wait(s["fy"].at[c, step], 1)
                if not by_x:
                    pl.semaphore_wait(s["fx"].at[c], 1)
            if by_x:
                for step in range(1, n_y):
                    at = (c, way, step)
                    self.send(
                        self.sum.at[blocks, p.y_off(step), :, self.part], self.mid.at[step - 1, blocks],
                        s["ms"].at[at], s["mr"].at[at], p.dev_y(step),
                    )
            else:
                for y in range(n_y):
                    at = (c, way, y)
                    self.send(
                        self.sum.at[blocks, y, 1 - p.x, self.part], self.mid.at[y // 2, blocks, y % 2],
                        s["ms"].at[at], s["mr"].at[at], p.dev_x(),
                    )

    def middle(self):
        for way, (blocks, by_x) in enumerate(self.ways):
            (self.middle_x if by_x else self.middle_y)(way, blocks)

    def middle_x(self, way, blocks):
        p, s, c = self.p, self.sems, self.c
        n_y, first = p.geo.n_y, blocks.start
        for step in range(1, n_y):
            at = (c, way, step)
            self.arrived(self.mid.at[step - 1, blocks], s["ms"].at[at], s["mr"].at[at], p.dev_y(step))

        @pl.loop(0, (blocks.stop - first) * 2)
        def _(at):
            where = (first + at // 2, p.y, lax.rem(at, 2), self.part)
            value = wide(self.sum[where])
            for step in range(1, n_y):
                value = value + wide(self.mid[step - 1, first + at // 2, lax.rem(at, 2)])
            self.sum[where] = value.astype(BF)

        if self.hands_on:
            for step in range(1, n_y):
                pl.semaphore_signal(
                    s["fy"].at[self.heir.c, step], inc=1, device_id=p.dev_y(-step), device_id_type=MESH
                )
        at = (c, way, 0)
        self.send(
            self.sum.at[blocks, p.y, 1 - p.x, self.part], self.end.at[0, blocks],
            s["es"].at[at], s["er"].at[at], p.dev_x(),
        )

    def middle_y(self, way, blocks):
        p, s, c = self.p, self.sems, self.c
        n_y, first = p.geo.n_y, blocks.start
        for y in range(n_y):
            at = (c, way, y)
            self.arrived(self.mid.at[y // 2, blocks, y % 2], s["ms"].at[at], s["mr"].at[at], p.dev_x())

        @pl.loop(0, (blocks.stop - first) * n_y)
        def _(at):
            y = lax.rem(at, n_y)
            where = (first + at // n_y, y, p.x, self.part)
            value = wide(self.sum[where]) + wide(self.mid[y // 2, first + at // n_y, lax.rem(y, 2)])
            self.sum[where] = value.astype(BF)

        if self.hands_on:
            pl.semaphore_signal(s["fx"].at[self.heir.c], inc=1, device_id=p.dev_x(), device_id_type=MESH)
        for step in range(1, n_y):
            at = (c, way, step)
            self.send(
                self.sum.at[blocks, p.y_off(step), p.x, self.part], self.end.at[step - 1, blocks],
                s["es"].at[at], s["er"].at[at], p.dev_y(step),
            )

    def column_sum(self):
        p, s, c = self.p, self.sems, self.c
        n_y = p.geo.n_y
        found = []
        for way, (blocks, by_x) in enumerate(self.ways):
            value = wide(self.sum[blocks, p.y, p.x, self.part])
            for step in (0,) if by_x else range(1, n_y):
                at = (c, way, step)
                got = self.end.at[0 if by_x else step - 1, blocks]
                self.arrived(got, s["es"].at[at], s["er"].at[at], p.dev_x())
                value = value + wide(got[...])
            found.append(value)
        return found[0] if len(found) == 1 else jnp.concatenate(found, 0)

    def last(self):
        p, s, c = self.p, self.sems, self.c
        n_z = p.geo.n_z
        value = self.column_sum().astype(BF).reshape(self.k * self.rows, self.lanes)
        if self.perm is not None:
            value = jnp.dot(self.perm[...], value, preferred_element_type=F32).astype(BF)
        if self.before is not None:
            self.before.left()
        self.z_send[...] = value.reshape(n_z, self.sent, self.lanes)
        for step in range(1, n_z):
            copy = remote(
                self.z_send.at[p.z_off(step)], self.z_recv.at[step],
                s["zs"].at[c, step], s["zr"].at[c, step], p.dev_z(step),
            )
            copy.start()
            self.z_moves.append(copy)

    def finish(self):
        p, s, c = self.p, self.sems, self.c
        value = wide(self.z_send[p.z])
        for step in range(1, p.geo.n_z):
            self.arrived(self.z_recv.at[step], s["zs"].at[c, step], s["zr"].at[c, step], p.dev_z(step))
            value = value + wide(self.z_recv[step])
        self.put(value)

    def left(self):
        while self.z_moves:
            self.z_moves.pop().wait_send()

    def drain(self):
        self.left()
        for copy in self.pending:
            copy.wait_send()


class ScatterLine(Scatter):
    def land(self, line):
        self.line = line
        p = self.p
        self.unit = self.rows // p.geo.n_z
        self.part = pl.ds(pl.multiple_of(p.z * self.unit, 16), self.unit)
        self.line_pending = []
        return self

    def slice_of(self, target):
        return pl.ds(target * self.unit, self.unit)

    def line_copy(self, src, way, target, further):
        s = self.sems
        at = (self.c_line, way, target)
        return remote(src, self.line.at[way, target], s["ls"].at[at], s["lr"].at[at], (self.p.d, further))

    def send_middle(self):
        p, last = self.p, self.p.geo.n_z - 1
        for way in range(2):
            ours = p.z == (0 if way == 0 else last)
            targets = range(last, 0, -1) if way == 0 else range(last)
            further = p.z + 1 if way == 0 else p.z - 1
            for target in targets:

                def copy(way=way, target=target, further=further):
                    return self.line_copy(self.sum.at[0, :, :, self.slice_of(target)], way, target, further)

                when(ours, lambda copy=copy: copy().start())
                self.line_pending.append((ours, copy))

    def relay(self, hop):
        p, s, last = self.p, self.sems, self.p.geo.n_z - 1
        for way in range(2):
            here = hop if way == 0 else last - hop
            targets = range(last, here, -1) if way == 0 else range(here)
            further = p.z + 1 if way == 0 else p.z - 1
            for target in targets:

                def copy(way=way, target=target, further=further):
                    return self.line_copy(self.line.at[way, target], way, target, further)

                def act(way=way, target=target, copy=copy):
                    self.add_line(way, target)
                    copy().start()

                when(p.z == here, act)
                self.line_pending.append((p.z == here, copy))

    def add_line(self, way, target):
        s, n_y = self.sems, self.p.geo.n_y
        at = (self.c_line, way, target)
        got = self.line.at[way, target]
        remote(got, got, s["ls"].at[at], s["lr"].at[at], self.p.dev_x()).wait_recv()

        @pl.loop(0, 2 * n_y)
        def _(index):
            where = (index // 2, lax.rem(index, 2))
            mine = wide(self.sum[(0,) + where + (self.slice_of(target),)])
            got[where] = (wide(got[where]) + mine).astype(BF)

    def collect(self):
        p, s, n_y, last = self.p, self.sems, self.p.geo.n_y, self.p.geo.n_z - 1
        for way in range(2):

            def act(way=way):
                at = (self.c_line, way, p.z)
                got = self.line.at[way, p.z]
                remote(got, got, s["ls"].at[at], s["lr"].at[at], p.dev_x()).wait_recv()

                @pl.loop(0, 2 * n_y)
                def _(index):
                    where = (index // 2, lax.rem(index, 2))
                    place = (0,) + where + (self.part,)
                    self.sum[place] = (wide(self.sum[place]) + wide(got[where])).astype(BF)

            when(p.z > 0 if way == 0 else p.z < last, act)
        Scatter.send_middle(self)

    def last(self):
        self.put(self.column_sum().reshape(self.unit, self.lanes))

    def finish(self):
        pass

    def drain(self):
        for valid, copy in self.line_pending:
            when(valid, lambda copy=copy: copy().wait_send())
        Scatter.drain(self)


def mm(left, right):
    return jnp.dot(left, right, preferred_element_type=F32)


def mm_nt(left, right):
    return lax.dot_general(left, right, (((1,), (1,)), ((), ())), preferred_element_type=F32)


def mm_tn(left, right):
    return lax.dot_general(left, right, (((0,), (0,)), ((), ())), preferred_element_type=F32)


def mean_of(values):
    return jnp.sum(values, -1, keepdims=True) * (1.0 / values.shape[-1])


def normal(values):
    centered = values - mean_of(values)
    scale = lax.rsqrt(mean_of(centered * centered) + epsilon)
    return centered * scale, scale


def norm_rows(source, gain, shift, target, block=32):
    @pl.loop(0, source.shape[0] // block)
    def _(at):
        rows = pl.ds(pl.multiple_of(at * block, block), block)
        unit, _ = normal(source[rows, :])
        target[rows, :] = (unit * gain + shift).astype(target.dtype)


def fold(values):
    total = values[0:8]
    for at in range(8, values.shape[0], 8):
        total = total + values[at : at + 8]
    return total


def norm_rows_back(source, gain, incoming, emit, sums, block=32):
    sums[...] = jnp.zeros_like(sums)

    @pl.loop(0, source.shape[0] // block)
    def _(at):
        rows = pl.ds(pl.multiple_of(at * block, block), block)
        unit, scale = normal(source[rows, :])
        back = incoming[rows, :]
        sums[0] += fold(back * unit)
        sums[1] += fold(back)
        inner = back * gain
        emit(rows, scale * (inner - mean_of(inner) - unit * mean_of(inner * unit)))


ROOT = 0.7978845608028654
CUBE = 0.044715


def gelu_parts(values):
    square = values * values
    curve = jnp.tanh(ROOT * (values + CUBE * (values * square)))
    return square, curve


class Layer:
    def __init__(self, refs, weight_a, weight_b, vec_d, vec_f, layer, heads):
        self.__dict__.update(refs)
        self.weight_a, self.weight_b = weight_a, weight_b
        self.vec_d, self.vec_f = vec_d, vec_f
        self.layer, self.heads = layer, heads

    def gain(self, at):
        return self.vec_d[self.layer * 10 + at : self.layer * 10 + at + 1, :]

    def shift(self, at):
        return self.gain(3 + at)

    def gain_f(self, at):
        return self.vec_f[self.layer * 3 + at : self.layer * 3 + at + 1, :]

    def lane_half(self, values, side):
        lane = lax.broadcasted_iota(jnp.int32, values.shape, 1)
        return (lane < HEAD_DIM) == (side == 0)

    def forward_norm(self):
        norm_rows(self.x, self.gain(0), self.shift(0), self.normed)

    def forward_qkv(self, part):
        value = mm(self.normed[...], self.weight_a(part))
        if part != 1:
            value = value + self.shift(3 if part == 0 else 4)
        self.qkv[part] = value.astype(BF)

    def forward_attention(self):
        valid = self.mask[...] > 0.5

        @pl.loop(0, self.heads // 2)
        def _(pair):
            lanes = pl.ds(pl.multiple_of(pair * 128, 128), 128)
            queries, keys, values = [self.qkv[part, :, lanes] for part in range(3)]
            context = None
            for side in range(2):
                half = self.lane_half(queries, side)
                scores = mm_nt(jnp.where(half, queries, jnp.zeros_like(queries)), keys)
                scores = jnp.where(valid, scores * HEAD_DIM**-0.5, -1e9)
                top = jnp.max(scores, -1, keepdims=True)
                grown = jnp.exp(scores - top)
                prob = grown / jnp.sum(grown, -1, keepdims=True)
                self.prob[2 * pair + side] = prob
                product = mm(prob.astype(BF), values)
                context = product if side == 0 else jnp.where(half, product, context)
            self.context[:, lanes] = context

    def forward_out(self):
        norm_rows(self.context, self.gain(1), self.shift(1), self.sub)
        self.after[...] = self.x[...] + (mm(self.sub[...], self.weight_a(3)) + self.shift(5))
        norm_rows(self.after, self.gain(2), self.shift(2), self.normed_ffn)

    def forward_up(self, part):
        width = self.x.shape[1]
        lanes = slice(part * width, (part + 1) * width)
        self.hidden[:, lanes] = mm(self.normed_ffn[...], self.weight_a(4 + part)) + self.gain_f(1)[:, lanes]

    def forward_gelu(self):
        @pl.loop(0, self.x.shape[0] // 16)
        def _(at):
            rows = pl.ds(pl.multiple_of(at * 16, 16), 16)
            values = self.hidden[rows, :]
            _, curve = gelu_parts(values)
            unit, _ = normal(0.5 * values * (1.0 + curve))
            self.sub_ffn[rows, :] = (unit * self.gain_f(0) + self.gain_f(2)).astype(BF)

    def forward_down(self, lanes):
        value = mm(self.sub_ffn[...], self.weight_b(slice(None), lanes))
        self.x_next[:, lanes] = self.after[:, lanes] + (value + self.shift(6)[:, lanes])


    def store_sums_d(self, at, sums):
        row = self.layer * 10 + at
        self.grad_d[row : row + 1, :] = jnp.sum(sums, 0, keepdims=True)

    def store_sums_f(self, at, sums):
        row = self.layer * 3 + at
        self.grad_f[row : row + 1, :] = jnp.sum(sums, 0, keepdims=True)

    def backward_start(self):
        self.low[...] = self.back[...].astype(BF)
        self.store_sums_d(9, wide(self.low[...]))

    def grad_up(self, part):
        width = self.x.shape[1]
        return mm_tn(self.normed_ffn[...], self.d_hidden[:, part * width : (part + 1) * width])

    def grad_out(self):
        return mm_tn(self.sub[...], self.low[...])

    def grad_qkv(self, part):
        return mm_tn(self.normed[...], self.d_qkv[part])

    def backward_down(self):
        width = self.x.shape[1]
        for part in range(self.hidden.shape[1] // width):
            lanes = slice(part * width, (part + 1) * width)
            self.wide_back[:, lanes] = mm_nt(self.low[...], self.weight_b(lanes, slice(None)))

    def backward_gelu(self):
        self.sums_f[...] = jnp.zeros_like(self.sums_f)

        @pl.loop(0, self.x.shape[0] // 16)
        def _(at):
            rows = pl.ds(pl.multiple_of(at * 16, 16), 16)
            values = self.hidden[rows, :]
            square, curve = gelu_parts(values)
            unit, scale = normal(0.5 * values * (1.0 + curve))
            back = self.wide_back[rows, :]
            self.sums_f[0] += fold(back * unit)
            self.sums_f[1] += fold(back)
            inner = back * self.gain_f(0)
            d_gelu = scale * (inner - mean_of(inner) - unit * mean_of(inner * unit))
            slope = 0.5 * (1.0 + curve) + 0.5 * values * (1.0 - curve * curve) * (
                ROOT * (1.0 + 3.0 * CUBE * square)
            )
            low = (d_gelu * slope).astype(BF)
            self.d_hidden[rows, :] = low
            self.sums_f[2] += fold(wide(low))

        self.store_sums_f(0, self.sums_f[0])
        self.store_sums_f(2, self.sums_f[1])
        self.store_sums_f(1, self.sums_f[2])

    def backward_up(self):
        width = self.x.shape[1]
        total = None
        for part in range(self.hidden.shape[1] // width):
            lanes = slice(part * width, (part + 1) * width)
            value = mm_nt(self.d_hidden[:, lanes], self.weight_a(4 + part))
            if part == 0:
                self.incoming[...] = value
            else:
                self.incoming[...] += value

        def emit(rows, value):
            value = self.back[rows, :] + value
            self.back[rows, :] = value
            self.low[rows, :] = value.astype(BF)

        norm_rows_back(self.after, self.gain(2), self.incoming, emit, self.sums_d)
        self.store_sums_d(2, self.sums_d[0])
        self.store_sums_d(5, self.sums_d[1])

    def backward_out(self):
        self.store_sums_d(8, wide(self.low[...]))
        self.incoming[...] = mm_nt(self.low[...], self.weight_a(3))

        def emit(rows, value):
            self.low[rows, :] = value.astype(BF)

        norm_rows_back(self.context, self.gain(1), self.incoming, emit, self.sums_d)
        self.store_sums_d(1, self.sums_d[0])
        self.store_sums_d(4, self.sums_d[1])

    def backward_attention(self):
        @pl.loop(0, self.heads // 2)
        def _(pair):
            lanes = pl.ds(pl.multiple_of(pair * 128, 128), 128)
            queries, keys, values = [self.qkv[part, :, lanes] for part in range(3)]
            d_context = self.low[:, lanes]
            found = [None] * 3
            for side in range(2):
                half = self.lane_half(d_context, side)
                prob = self.prob[2 * pair + side]
                d_prob = mm_nt(jnp.where(half, d_context, jnp.zeros_like(d_context)), values)
                dot = jnp.sum(prob * d_prob, -1, keepdims=True)
                d_scores = (prob * (d_prob - dot)).astype(BF)
                new = (
                    mm(d_scores, keys) * HEAD_DIM**-0.5,
                    mm_tn(d_scores, queries) * HEAD_DIM**-0.5,
                    mm_tn(prob.astype(BF), d_context),
                )
                found = [n if side == 0 else jnp.where(half, n, f) for n, f in zip(new, found)]
            for part in range(3):
                self.d_qkv[part, :, lanes] = found[part].astype(BF)

    def backward_qkv(self):
        self.store_sums_d(6, wide(self.d_qkv[0]))
        self.store_sums_d(7, wide(self.d_qkv[2]))
        for part in range(3):
            value = mm_nt(self.d_qkv[part], self.weight_a(part))
            if part == 0:
                self.incoming[...] = value
            else:
                self.incoming[...] += value

        def emit(rows, value):
            self.back[rows, :] = self.back[rows, :] + value

        norm_rows_back(self.x, self.gain(0), self.incoming, emit, self.sums_d)
        self.store_sums_d(0, self.sums_d[0])
        self.store_sums_d(3, self.sums_d[1])


def saved_shapes(rows, width, wide_width, heads):
    return {
        "normed": ((rows, width), BF),
        "qkv": ((3, rows, width), BF),
        "prob": ((heads, rows, rows), F32),
        "context": ((rows, width), F32),
        "sub": ((rows, width), BF),
        "after": ((rows, width), F32),
        "normed_ffn": ((rows, width), BF),
        "hidden": ((rows, wide_width), F32),
        "sub_ffn": ((rows, wide_width), BF),
    }


def work_shapes(rows, width, wide_width):
    return {
        "low": ((rows, width), BF),
        "incoming": ((rows, width), F32),
        "wide_back": ((rows, wide_width), F32),
        "d_qkv": ((3, rows, width), BF),
        "sums_d": ((2, 8, width), F32),
        "sums_f": ((3, 8, wide_width), F32),
    }


def spread_tables(geo):
    tables = []
    for width, real in ((geo.width, geo.rows_a), (geo.wide_width, geo.rows_b)):
        at = np.arange(width)
        owner = (at[None, :] // real == np.arange(geo.owners)[:, None]).astype(np.float32)
        tables += [jnp.asarray(owner, BF), jnp.asarray(at[None, :] % real, jnp.int32)]
    return tables


def unpack_vectors(geo, whole_v, wide_v, tables, vec_d, vec_f):
    owner_d, rest_d, owner_f, rest_f = tables
    lines = geo.kind["v"][1]
    wide_v[...] = wide(whole_v[0])
    line_of = lambda at: wide_v[pl.ds(at, geo.owners, stride=lines), :].astype(BF)
    pick_d = lax.broadcasted_iota(jnp.int32, (geo.slot, geo.width), 0) == rest_d[...]
    for line in range(geo.lines_d):
        spread = mm_tn(line_of(line), owner_d[...])
        for at in range(geo.per_row):
            part = spread[at * geo.slot : (at + 1) * geo.slot]
            row = line * geo.per_row + at
            if row < geo.layers * 10:
                vec_d[row : row + 1, :] = jnp.sum(jnp.where(pick_d, part, 0.0), 0, keepdims=True)
    pick_f = lax.broadcasted_iota(jnp.int32, (128, geo.width), 0)
    for row in range(geo.layers * 3):
        line = line_of(geo.lines_d + row)
        for first in range(0, geo.wide_width, geo.width):
            lanes = slice(first, first + geo.width)
            spread = jnp.where(pick_f == rest_f[:, lanes], mm_tn(line, owner_f[:, lanes]), 0.0)
            vec_f[row : row + 1, lanes] = jnp.sum(spread, 0, keepdims=True)


GATHER_SEMS = (
    "lz", "lo", "zs", "zr", "xs", "xr", "ys", "yr", "ds", "dr", "cs", "cr",
    "gl", "gx", "gy", "gd", "gs", "gr", "hs", "hr",
)
LINE_FIRST = (1, 6)


def forward_kernel(geo, names_perm, saved_names, *refs):
    refs = list(refs)
    take = lambda number: [refs.pop(0) for _ in range(number)]
    sources = dict(zip(geo.kinds, take(len(geo.kinds))))
    perms = dict(zip(names_perm, take(len(names_perm))))
    act_ref, mask_ref = take(2)
    tables = take(4)
    out_ref, vec_d, vec_f, kept_a, kept_b, kept_x = take(6)
    kept = [dict(zip(saved_names, take(len(saved_names)))) for _ in range(geo.layers)]
    wholes = dict(zip(("a", "v", "b"), take(3)))
    wholes.update({name: wholes["b"] for name in geo.down})
    bufs = dict(zip(geo.plain, take(len(geo.plain))))
    units = dict(zip(names_perm, take(len(names_perm))))
    saved = [dict(zip(saved_names, take(len(saved_names)))) for _ in range(geo.layers)]
    xs, wide_v, keep_sem = take(3)
    sems = dict(zip(GATHER_SEMS, take(len(GATHER_SEMS))))
    place = Place(geo)
    chunks, line_chunks = [("v", 0, 0, 0)], []
    for layer in range(geo.layers):
        chunks += [chunk_a(geo, layer, pair) for pair in range(geo.pairs)]
        for name in geo.down:
            (line_chunks if name == "l" else chunks).append(chunk_down(geo, layer, name))
    moves = [
        Gather(place, at, chunk, sources, bufs, units, perms, wholes, sems)
        for at, chunk in enumerate(chunks)
    ]
    lines = [
        GatherLine(place, at, chunk, sources, wholes, sems) for at, chunk in enumerate(line_chunks)
    ]
    keeps = []

    def keep(src, dst):
        copy = pltpu.make_async_copy(src, dst, keep_sem.at[len(keeps)])
        copy.start()
        keeps.append(copy)

    net = []
    for layer in range(geo.layers):
        fields = dict(saved[layer], x=xs.at[layer], x_next=xs.at[layer + 1], mask=mask_ref)
        read_a = lambda at, layer=layer: wholes["a"][layer * geo.blocks + at]
        read_b = lambda rows, lanes, layer=layer: wholes["b"][layer, rows, lanes]
        net.append(Layer(fields, read_a, read_b, vec_d, vec_f, layer, geo.width // HEAD_DIM))

    def compute(number):
        name, at, lead, first = chunks[number]
        if geo.lined and name == "c":
            lines[lead].arrive()
            down(lead, *geo.lanes_of["l"])
        moves[number].arrive()
        if name == "v":
            unpack_vectors(geo, wholes["v"], wide_v, tables, vec_d, vec_f)
            return
        k, _, _, lanes = geo.kind[name]
        layer = at // geo.pairs if name == "a" else at
        one = net[layer]
        save = lambda *found: [keep(saved[layer][field], kept[layer][field]) for field in found]
        if name == "a":
            keep(wholes["a"].at[pl.ds(lead, k)], kept_a.at[pl.ds(lead, k)])
            pair = at % geo.pairs
            if pair == 0:
                one.forward_norm()
                one.forward_qkv(0)
                one.forward_qkv(1)
            elif pair == 1:
                one.forward_qkv(2)
                save("normed", "qkv")
                one.forward_attention()
                one.forward_out()
                save("prob", "context", "sub", "after", "normed_ffn")
            else:
                one.forward_up(2 * pair - 4)
                one.forward_up(2 * pair - 3)
                if pair == geo.pairs - 1:
                    one.forward_gelu()
                    save("hidden", "sub_ffn")
        else:
            down(layer, first, lanes)
            if name == geo.down[-1] and layer < geo.layers - 1:
                keep(xs.at[layer + 1], kept_x.at[layer + 1])

    def down(layer, first, lanes):
        where = pl.ds(first, lanes)
        keep(wholes["b"].at[layer, :, where], kept_b.at[layer, :, where])
        net[layer].forward_down(slice(first, first + lanes))

    extra = {}
    for layer, line in enumerate(lines):
        plan = [line.start, line.forward, line.corner]
        plan += [
            lambda line=line, hop=hop, half=half: line.relay(hop, half)
            for hop in range(geo.n_z)
            for half in range(2)
        ]
        needed = chunks.index(chunk_down(geo, layer, "c")) + 2
        for at, act in enumerate(plan):
            step = at - 2 if at < 3 else LINE_FIRST[min(layer, 1)] + at - 3
            extra.setdefault(min(step, needed), []).append(act)

    xs[0] = wide(act_ref[...])
    keep(xs.at[0], kept_x.at[0])
    place.greet()
    run_pipeline(
        [
            (-2, lambda c: moves[c].start_z()),
            (0, lambda c: moves[c].own()),
            (3, compute),
            (1, lambda c: moves[c].forward()),
            (2, lambda c: moves[c].corner()),
        ],
        len(moves),
        extra,
    )
    out_ref[...] = xs[geo.layers].astype(BF)
    for move in moves + lines:
        move.drain()
    for copy in keeps:
        copy.wait()


def run_forward(geo, sources, act, mask):
    names_perm = [name for name in geo.plain if geo.permuted(name)]
    perms = [jnp.asarray(geo.permutation(name), BF) for name in names_perm]
    rows, width = act.shape
    total = sum(geo.number.values())
    heads = width // HEAD_DIM
    saved = saved_shapes(rows, width, geo.wide_width, heads)
    bufs, units, wholes = [], [], []
    for name in geo.plain:
        k, sent, unit, lanes = geo.kind[name]
        bufs.append(pltpu.VMEM((geo.number[name], geo.n_z * sent, lanes), BF))
        if name in names_perm:
            units.append(pltpu.VMEM((geo.number[name], k, unit, lanes), BF))
    wholes = [(geo.whole_shape(name), BF) for name in ("a", "v", "c")]
    n_y, n_z = geo.n_y, geo.n_z
    n_keeps = geo.layers * (len(saved) + geo.pairs + len(geo.down) + 1)
    vec_rows = geo.layers * 10
    outs = [
        jax.ShapeDtypeStruct((rows, width), BF),
        jax.ShapeDtypeStruct((vec_rows, width), F32),
        jax.ShapeDtypeStruct((geo.layers * 3, geo.wide_width), F32),
        jax.ShapeDtypeStruct(*wholes[0]),
        jax.ShapeDtypeStruct(*wholes[2]),
        jax.ShapeDtypeStruct((geo.layers, rows, width), F32),
    ] + [jax.ShapeDtypeStruct(*saved[name]) for _ in range(geo.layers) for name in saved]
    found = pl.pallas_call(
        functools.partial(forward_kernel, geo, names_perm, list(saved)),
        out_shape=outs,
        in_specs=[IN_VMEM] * (len(sources) + len(perms) + 6),
        out_specs=[IN_VMEM] * 3 + [ANY] * (len(outs) - 3),
        scratch_shapes=[pltpu.VMEM(*whole) for whole in wholes]
        + bufs
        + units
        + [pltpu.VMEM(*saved[name]) for _ in range(geo.layers) for name in saved]
        + [
            pltpu.VMEM((geo.layers + 1, rows, width), F32),
            pltpu.VMEM(wholes[1][0][1:], F32),
            dma(n_keeps),
            dma(total),
            dma(total),
            dma(total, n_z),
            dma(total, n_z),
            dma(total),
            dma(total),
            dma(total, n_y),
            dma(total, n_y),
            dma(total, 2, n_y),
            dma(total, 2, n_y),
            dma(total, 2 * n_y),
            dma(total, 2 * n_y),
            dma(geo.layers),
            dma(geo.layers, 2),
            dma(geo.layers, 2, n_y),
            dma(geo.layers, 2, n_y),
        ]
        + [dma(geo.layers, 2, n_z, 2 * n_y)] * 4,
        compiler_params=pltpu.CompilerParams(
            collective_id=0, has_side_effects=True, vmem_limit_bytes=60 * 2**20
        ),
    )(*sources, *perms, act, mask, *spread_tables(geo))
    names = list(saved)
    kept = [dict(zip(names, found[6 + layer * len(names) :])) for layer in range(geo.layers)]
    return found[:6], kept


def pack_gradients(geo, grad_d, grad_f, tables, wide_v, stage_v):
    owner_d, rest_d, owner_f, rest_f = tables
    lines = geo.kind["v"][1]
    wide_v[...] = jnp.zeros_like(wide_v)
    pick_d = lax.broadcasted_iota(jnp.int32, (geo.slot, geo.width), 0) == rest_d[...]
    for line in range(geo.lines_d):
        parts = []
        for at in range(geo.per_row):
            row = line * geo.per_row + at
            if row < geo.layers * 10:
                parts.append(jnp.where(pick_d, grad_d[row : row + 1, :], 0.0))
            else:
                parts.append(jnp.zeros(pick_d.shape, F32))
        wide_v[pl.ds(line, geo.owners, stride=lines), :] = mm_nt(
            owner_d[...], jnp.concatenate(parts, 0).astype(BF)
        )
    pick_f = lax.broadcasted_iota(jnp.int32, (128, geo.width), 0)
    for row in range(geo.layers * 3):
        total = None
        for first in range(0, geo.wide_width, geo.width):
            lanes = slice(first, first + geo.width)
            part = jnp.where(pick_f == rest_f[:, lanes], grad_f[row : row + 1, lanes], 0.0).astype(BF)
            part = mm_nt(owner_f[:, lanes], part)
            total = part if total is None else total + part
        wide_v[pl.ds(geo.lines_d + row, geo.owners, stride=lines), :] = total
    stage_v[...] = wide_v[...].astype(BF).reshape(stage_v.shape)


class Ring:
    def __init__(self, sources, slots, sems):
        self.slots, self.size, self.used = slots, slots.shape[0], 0
        self.copies = [
            pltpu.make_async_copy(source, slots.at[at % self.size], sems.at[at % self.size])
            for at, source in enumerate(sources)
        ]
        for copy in self.copies[: self.size]:
            copy.start()

    def next(self):
        at = self.used
        self.used += 1
        if 0 < at and at - 1 + self.size < len(self.copies):
            self.copies[at - 1 + self.size].start()
        self.copies[at].wait()
        return self.slots[at % self.size]


SCATTER_SEMS = ("cs", "cr", "ms", "mr", "es", "er", "zs", "zr", "ls", "lr", "fx", "fy")
Z_SLOTS = 3
LINE_LAGS = (4, 3)
SCATTER_LAGS = (0, 1, 3, 5, 7)


def ring_slots(geo):
    return 3 if geo.roomy else 2


def backward_kernel(geo, names_perm, names, *refs):
    refs = list(refs)
    take = lambda number: [refs.pop(0) for _ in range(number)]
    by_kind = lambda kinds=geo.kinds: dict(zip(kinds, take(len(kinds))))
    saved_names, work_names = names
    layers, blocks, width = geo.layers, geo.blocks, geo.width
    perms = dict(zip(names_perm, take(len(names_perm))))
    cot_ref, vec_d, vec_f = take(3)
    tables = take(4)
    whole_a, whole_b, kept_x = take(3)
    kept = [dict(zip(saved_names, take(len(saved_names)))) for _ in range(layers)]
    for layer in range(layers):
        kept[layer]["x"] = kept_x.at[layer]
    back_ref, out_qkv, out_out, out_up, out_down, out_d, out_f = take(7)
    fields = dict(zip(saved_names, take(len(saved_names))))
    fields.update(zip(work_names, take(len(work_names))))
    stages, sums, mids, ends = [by_kind() for _ in range(4)]
    z_send, z_recv = [by_kind(geo.plain) for _ in range(2)]
    line_refs = take(1) if geo.lined else []
    x_ref, grad_d, grad_f, wide_v, slots = take(5)
    last_low, last_ffn = take(2) if geo.roomy else (None, None)
    sem_l, sem_w = take(2)
    sems = dict(zip(SCATTER_SEMS, take(len(SCATTER_SEMS))))
    fields.update(d_hidden=fields["sub_ffn"], x=x_ref, back=back_ref, grad_d=grad_d, grad_f=grad_f)
    place = Place(geo)

    def writer(chunk):
        name, at, lead, first = chunk
        rows_a, rows_b, lines = geo.rows_a, geo.rows_b, geo.lines_d

        def put_a(value):
            layer = at // geo.pairs
            for side in range(2):
                block = 2 * (at % geo.pairs) + side
                piece = value[side * rows_a : (side + 1) * rows_a]
                if block < 3:
                    out_qkv[layer, :, block * width : (block + 1) * width] = piece
                elif block == 3:
                    out_out[layer] = piece
                else:
                    out_up[layer, :, (block - 4) * width : (block - 3) * width] = piece

        def put_down(value):
            out_down[lead, :, first : first + value.shape[1]] = value[:rows_b]

        def put_v(value):
            out_d[...] = value[:lines]
            out_f[...] = value[lines : lines + layers * 3]

        return {"a": put_a, "v": put_v}.get(name, put_down)

    order, seen = [], {name: [] for name in geo.kinds}
    early = {layer: geo.down for layer in range(layers)}
    late = ("c", "d") if geo.roomy else ()
    early[0] = tuple(name for name in geo.down if name not in late)
    for layer in reversed(range(layers)):
        early[layer] = early[layer][::-1]
        order += [chunk_down(geo, layer, name) for name in early[layer]]
        order += [chunk_a(geo, layer, pair) for pair in list(range(2, geo.pairs)) + [1, 0]]
    order.append(("v", 0, 0, 0))
    order += [chunk_down(geo, 0, name) for name in late]
    moves, stage_of = [], []
    for number, chunk in enumerate(order):
        name = chunk[0]
        stage = stages[name].at[len(seen[name]) % stages[name].shape[0]]
        slots_z = z_send[name].shape[0] if name in z_send else 1
        z_slot = len(seen[name]) % slots_z
        before = seen[name][-slots_z] if len(seen[name]) >= slots_z else None
        move = (ScatterLine if name == "l" else Scatter)(
            place, number, chunk, stage, sums, mids, ends, perms, z_send, z_recv, z_slot, before,
            writer(chunk), sems,
        )
        if name == "l":
            move.c_line = len(seen[name])
            move.land(line_refs[0].at[move.c_line])
        seen[name].append(move)
        stage_of.append(stage)
        moves.append(move)
    for number, chunk in enumerate(order):
        if chunk[0] == "a" and chunk[1] >= geo.pairs:
            moves[number].heir = moves[[later[:2] for later in order].index(("a", chunk[1] - geo.pairs))]
    step, plan = [0], {}
    for number, chunk in enumerate(order):
        move = moves[number]
        acts = [move.start, move.pair, move.middle, move.last, move.finish]
        lags = list(SCATTER_LAGS)
        if chunk[0] == "l":
            hops = [lambda move=move, hop=hop: move.relay(hop) for hop in range(1, geo.n_z - 1)]
            acts[2:2] = hops + [move.collect]
            first, each = LINE_LAGS
            lags[2:] = [first + each * at for at in range(len(hops) + 1)]
            lags += [lags[-1] + 1, lags[-1] + 2, lags[-1] + 2]
        for lag, act in zip(lags, acts):
            plan.setdefault(number + lag, []).append((lag, act))

    def serve():
        for _, act in sorted(plan.get(step[0], []), key=lambda pair: pair[0]):
            act()
        step[0] += 1

    def stage_down(name, rows_ref, low_ref):
        unit = geo.kind[name][2]
        first, lanes = geo.lanes_of[name]
        for column in range(geo.n_dp // 2):
            rows = slice(column * 2 * unit, (column + 1) * 2 * unit)
            value = mm_tn(rows_ref[:, rows], low_ref[:, first : first + lanes])
            stage_of[step[0]][0, column // 2, column % 2] = value.astype(BF).reshape(2, unit, lanes)

    def stage_a(side, value):
        stage_of[step[0]][side] = value.astype(BF).reshape(geo.n_y, 2, 2, -1, width)

    loads = {}
    field_names = ["x"] + list(saved_names)

    def fetch(layer, *found):
        for name in found:
            loads[name] = pltpu.make_async_copy(
                kept[layer][name], fields[name], sem_l.at[field_names.index(name)]
            )
            loads[name].start()

    def ready(*found):
        for name in found:
            loads[name].wait()

    fetch(layers - 1, "sub_ffn")
    sources = []
    for layer in reversed(range(layers)):
        parts = geo.wide_width // width
        sources += [whole_b.at[layer, pl.ds(part * width, width)] for part in range(parts)]
        sources += [whole_a.at[layer * blocks + at] for at in list(range(4, blocks)) + [3, 0, 1, 2]]
    cot_copy = pltpu.make_async_copy(cot_ref, back_ref, sem_l.at[len(field_names)])
    cot_copy.start()
    place.greet()
    cot_copy.wait()
    loads["sub_ffn"].wait()
    ring = Ring(sources, slots, sem_w)
    fetch(
        layers - 1, "hidden", "normed_ffn", "after", "sub", "context", "prob", "qkv", "normed", "x"
    )
    for layer in reversed(range(layers)):
        one = Layer(
            fields, lambda at: ring.next(), lambda rows, lanes: ring.next(), vec_d, vec_f, layer,
            width // HEAD_DIM,
        )
        again = (lambda *found: fetch(layer - 1, *found)) if layer > 0 else (lambda *found: None)
        one.backward_start()
        if layer < layers - 1:
            ready("sub_ffn")
        for name in early[layer]:
            stage_down(name, one.sub_ffn, one.low)
            serve()
        if layer == 0 and late:
            last_low[...] = one.low[...]
            last_ffn[...] = one.sub_ffn[...]
        one.backward_down()
        ready("hidden")
        one.backward_gelu()
        again("hidden")
        ready("normed_ffn")
        for pair in range(2, geo.pairs):
            stage_a(0, one.grad_up(2 * pair - 4))
            stage_a(1, one.grad_up(2 * pair - 3))
            serve()
        again("normed_ffn")
        ready("after")
        one.backward_up()
        again("after", "sub_ffn")
        ready("sub", "context")
        stage_a(1, one.grad_out())
        one.backward_out()
        again("sub", "context")
        ready("prob", "qkv")
        one.backward_attention()
        again("prob", "qkv")
        ready("normed")
        stage_a(0, one.grad_qkv(2))
        serve()
        stage_a(0, one.grad_qkv(0))
        stage_a(1, one.grad_qkv(1))
        serve()
        again("normed")
        ready("x")
        one.backward_qkv()
        again("x")
    pack_gradients(geo, grad_d, grad_f, tables, wide_v, stage_of[step[0]])
    serve()
    for name in late:
        stage_down(name, last_ffn, last_low)
        serve()
    while step[0] <= max(plan):
        serve()
    for move in moves:
        move.drain()


def run_backward(geo, cot, vec_d, vec_f, whole_a, whole_b, kept_x, kept):
    rows, width = cot.shape
    layers, n_y, n_z = geo.layers, geo.n_y, geo.n_z
    heads = width // HEAD_DIM
    saved, work = saved_shapes(rows, width, geo.wide_width, heads), work_shapes(rows, width, geo.wide_width)
    names = (list(saved), list(work))
    names_perm = [name for name in geo.plain if geo.permuted(name)]
    perms = [jnp.asarray(geo.permutation(name).T, BF) for name in names_perm]
    total = sum(geo.number.values())
    groups = [[] for _ in range(6)]
    for name in geo.kinds:
        k, sent, unit, lanes = geo.kind[name]
        number = geo.number[name]
        mid_steps = max(n_y - 1, (n_y + 1) // 2)
        groups[0].append(pltpu.VMEM((2 if name == "a" else 1, k, n_y, 2, 2, unit, lanes), BF))
        groups[1].append(pltpu.VMEM((number, k, n_y, 2, unit, lanes), BF))
        landing = geo.pairs if name == "a" else number
        unit = sent if name == "l" else unit
        groups[2].append(pltpu.VMEM((landing, mid_steps, k, 2, unit, lanes), BF))
        groups[3].append(pltpu.VMEM((number, mid_steps, k, unit, lanes), BF))
        if name == "l":
            continue
        groups[4].append(pltpu.VMEM((min(number, Z_SLOTS), n_z, sent, lanes), BF))
        groups[5].append(pltpu.VMEM((number, n_z, sent, lanes), BF))
    scratch = [pltpu.VMEM(*saved[name]) for name in saved] + [pltpu.VMEM(*work[name]) for name in work]
    scratch += sum(groups, [])
    if geo.lined:
        _, sent, _, lanes = geo.kind["l"]
        scratch.append(pltpu.VMEM((layers, 2, n_z, n_y, 2, sent, lanes), BF))
    scratch += [
        pltpu.VMEM((rows, width), F32),
        pltpu.VMEM((layers * 10, width), F32),
        pltpu.VMEM((layers * 3, geo.wide_width), F32),
        pltpu.VMEM((geo.owners * geo.kind["v"][1], 128), F32),
        pltpu.VMEM((ring_slots(geo), width, width), BF),
    ]
    if geo.roomy:
        scratch += [pltpu.VMEM((rows, width), BF), pltpu.VMEM((rows, geo.wide_width), BF)]
    scratch += [
        dma(2 + len(saved)),
        dma(ring_slots(geo)),
        dma(total),
        dma(total),
        dma(total, 2, n_y),
        dma(total, 2, n_y),
        dma(total, 2, n_y),
        dma(total, 2, n_y),
        dma(total, n_z),
        dma(total, n_z),
        dma(layers, 2, n_z),
        dma(layers, 2, n_z),
        pltpu.SemaphoreType.REGULAR((total,)),
        pltpu.SemaphoreType.REGULAR((total, n_y)),
    ]
    return pl.pallas_call(
        functools.partial(backward_kernel, geo, names_perm, names),
        out_shape=[
            jax.ShapeDtypeStruct((rows, width), F32),
            jax.ShapeDtypeStruct((layers, geo.rows_a, 3 * width), F32),
            jax.ShapeDtypeStruct((layers, geo.rows_a, width), F32),
            jax.ShapeDtypeStruct((layers, geo.rows_a, geo.wide_width), F32),
            jax.ShapeDtypeStruct((layers, geo.rows_b, width), F32),
            jax.ShapeDtypeStruct((geo.lines_d, 128), F32),
            jax.ShapeDtypeStruct((layers * 3, 128), F32),
        ],
        in_specs=[IN_VMEM] * len(perms) + [ANY] + [IN_VMEM] * 6 + [ANY] * (3 + layers * len(saved)),
        out_specs=[IN_VMEM] * 7,
        scratch_shapes=scratch,
        compiler_params=pltpu.CompilerParams(
            collective_id=1, has_side_effects=True, vmem_limit_bytes=63 * 2**20
        ),
    )(
        *perms, cot, vec_d, vec_f, *spread_tables(geo), whole_a, whole_b, kept_x,
        *[kept[layer][name] for layer in range(layers) for name in saved],
    )


def pack_kernel(geo, *refs):
    act_short, act_long, len_short, len_long, w_qkv, w_out, w_up, w_down = refs[:8]
    norms_d, gains_ff, shifts_ff, cot_short, cot_long = refs[8:13]
    sources = dict(zip(geo.kinds, refs[13:]))
    act, mask, cot, lines = refs[13 + len(geo.kinds) :]
    width, rows_a, rows_b = geo.width, geo.rows_a, geo.rows_b

    def block(layer, at):
        if at == 3:
            return wide(w_out[layer])
        first = at if at < 3 else at - 4
        return wide((w_qkv if at < 3 else w_up)[layer, :, first * width : (first + 1) * width])

    def filled(pieces, rows):
        have = sum(piece.shape[0] for piece in pieces)
        if have < rows:
            pieces = pieces + [jnp.zeros((rows - have, pieces[0].shape[1]), F32)]
        return (jnp.concatenate(pieces, 0) if len(pieces) > 1 else pieces[0]).astype(BF)

    for layer in range(geo.layers):
        for pair in range(geo.pairs):
            pieces = [block(layer, 2 * pair), block(layer, 2 * pair + 1)]
            sources["a"][layer * geo.pairs + pair] = filled(pieces, geo.kind["a"][1])
        for name in geo.down:
            first, lanes = geo.lanes_of[name]
            piece = w_down[layer, :, first : first + lanes]
            if rows_b != geo.kind[name][1]:
                piece = filled([wide(piece)], geo.kind[name][1])
            sources[name][layer] = piece
    lines[...] = jnp.zeros_like(lines)
    gains_wide = wide(gains_ff[...])
    for layer in range(geo.layers):
        norms, shifts_wide = wide(norms_d[layer]), wide(shifts_ff[layer])
        for at in range(10):
            line, lane = divmod(layer * 10 + at, geo.per_row)
            lines[line : line + 1, lane * geo.slot : lane * geo.slot + rows_a] = norms[at : at + 1]
        for at in range(3):
            line = geo.lines_d + layer * 3 + at
            lines[line : line + 1, :rows_b] = gains_wide[layer : layer + 1] if at == 0 else shifts_wide[at - 1 : at]
    sources["v"][0] = lines[...].astype(BF)
    short = act_short.shape[0]
    act[:short] = act_short[...]
    act[short:] = act_long[...]
    rows = act.shape[0]

    def valid(shape, dim):
        at = lax.broadcasted_iota(jnp.int32, shape, dim)
        return jnp.where(jnp.where(at < short, at - len_short[0], at - short - len_long[0]) < 0, 1.0, 0.0)

    def bucket(dim):
        return jnp.where(lax.broadcasted_iota(jnp.int32, (rows, rows), dim) < short, 0, 1)

    mask[...] = jnp.where(bucket(0) == bucket(1), valid((rows, rows), 1), 0.0)
    keep = valid((rows, width), 0)
    cot[:short] = wide(cot_short[...]) * keep[:short]
    cot[short:] = wide(cot_long[...]) * keep[short:]


def run_pack(geo, args):
    rows = args[0].shape[0] + args[1].shape[0]
    shapes = []
    for name in geo.kinds:
        _, sent, _, lanes = geo.kind[name]
        shapes.append(jax.ShapeDtypeStruct((geo.number[name], sent, lanes), BF))
    shapes += [
        jax.ShapeDtypeStruct((rows, geo.width), BF),
        jax.ShapeDtypeStruct((rows, rows), F32),
        jax.ShapeDtypeStruct((rows, geo.width), F32),
    ]
    in_smem = pl.BlockSpec(memory_space=pltpu.SMEM)
    return pl.pallas_call(
        functools.partial(pack_kernel, geo),
        out_shape=shapes,
        in_specs=[IN_VMEM] * 2 + [in_smem] * 2 + [IN_VMEM] * 9,
        out_specs=[IN_VMEM] * len(shapes),
        scratch_shapes=[pltpu.VMEM((geo.kind["v"][1], 128), F32)],
        compiler_params=pltpu.CompilerParams(vmem_limit_bytes=63 * 2**20),
    )(*args[:8], jnp.concatenate(args[8:10], 1), *args[10:])


def unpack_kernel(geo, *refs):
    out, back, g_qkv, g_out, g_up, g_down, lines_d, lines_f = refs[:8]
    out_short, out_long, back_short, back_long, t_qkv, t_out, t_up, t_down = refs[8:16]
    t_gains_d, t_shifts_d, t_gains_ff, t_shifts_ff = refs[16:]
    short = out_short.shape[0]
    out_short[...] = out[:short]
    out_long[...] = out[short:]
    back_short[...] = back[:short]
    back_long[...] = back[short:]
    for source, target in ((g_qkv, t_qkv), (g_out, t_out), (g_up, t_up), (g_down, t_down)):
        target[...] = source[...]
    for layer in range(geo.layers):
        for at in range(10):
            line, lane = divmod(layer * 10 + at, geo.per_row)
            value = lines_d[line : line + 1, lane * geo.slot : lane * geo.slot + geo.rows_a]
            if at < 3:
                t_gains_d[layer, at : at + 1, :] = value
            else:
                t_shifts_d[layer, at - 3 : at - 2, :] = value
        for at in range(3):
            value = lines_f[layer * 3 + at : layer * 3 + at + 1, : geo.rows_b]
            if at == 0:
                t_gains_ff[layer : layer + 1, :] = value
            else:
                t_shifts_ff[layer, at - 1 : at, :] = value


def run_unpack(geo, found, args):
    like = lambda index, dtype: jax.ShapeDtypeStruct(args[index].shape, dtype)
    shapes = [like(0, BF), like(1, BF), like(0, F32), like(1, F32)]
    shapes += [like(index, F32) for index in range(4, 12)]
    return pl.pallas_call(
        functools.partial(unpack_kernel, geo),
        out_shape=shapes,
        in_specs=[IN_VMEM] * len(found),
        out_specs=[IN_VMEM] * len(shapes),
        compiler_params=pltpu.CompilerParams(vmem_limit_bytes=63 * 2**20),
    )(*found)


def on_device(*args):
    n_dp, n_z = lax.axis_size("dp"), lax.axis_size("fsdp")
    geo = Geometry(n_dp, n_z, args[4].shape, args[6].shape, args[7].shape)
    *sources, act, mask, cot = run_pack(geo, args)
    found, kept = run_forward(geo, sources, act, mask)
    out, vec_d, vec_f, whole_a, whole_b, kept_x = found
    grads = run_backward(geo, cot, vec_d, vec_f, whole_a, whole_b, kept_x, kept)
    return tuple(run_unpack(geo, (out,) + tuple(grads), args))


def solution(mesh):
    return jax.shard_map(
        on_device,
        mesh=mesh,
        in_specs=(
            P(("dp", "fsdp"), None),
            P(("dp", "fsdp"), None),
            P(("dp", "fsdp")),
            P(("dp", "fsdp")),
            P(None, ("dp", "fsdp"), None),
            P(None, ("dp", "fsdp"), None),
            P(None, ("dp", "fsdp"), None),
            P(None, ("dp", "fsdp"), None),
            P(None, None, ("dp", "fsdp")),
            P(None, None, ("dp", "fsdp")),
            P(None, ("dp", "fsdp")),
            P(None, None, ("dp", "fsdp")),
            P(("dp", "fsdp"), None),
            P(("dp", "fsdp"), None),
        ),
        out_specs=(
            P(("dp", "fsdp"), None),
            P(("dp", "fsdp"), None),
            P(("dp", "fsdp"), None),
            P(("dp", "fsdp"), None),
            P(None, ("dp", "fsdp"), None),
            P(None, ("dp", "fsdp"), None),
            P(None, ("dp", "fsdp"), None),
            P(None, ("dp", "fsdp"), None),
            P(None, None, ("dp", "fsdp")),
            P(None, None, ("dp", "fsdp")),
            P(None, ("dp", "fsdp")),
            P(None, None, ("dp", "fsdp")),
        ),
        check_vma=False,
    )
```

```python
import functools

import jax
import jax.numpy as jnp
import numpy as np
from jax import lax
from jax.experimental import pallas as pl
from jax.experimental.pallas import tpu as pltpu
from jax.sharding import PartitionSpec as P

HEAD_DIM = 64

epsilon = 1e-05


BF = jnp.bfloat16
F32 = jnp.float32
MESH = pl.DeviceIdType.MESH


def round16(count):
    return (count + 15) // 16 * 16


class Geometry:
    def __init__(self, n_dp, n_z, w_qkv, w_up, w_down):
        self.n_dp, self.n_z, self.n_y = n_dp, n_z, n_dp // 4
        self.layers = w_qkv[0]
        self.width = w_qkv[2] // 3
        self.rows_a, self.rows_b = w_qkv[1], w_down[1]
        self.blocks = 4 + w_up[2] // self.width
        self.pairs = self.blocks // 2
        half = self.width // 2
        self.lined = self.rows_b % 16 == 0
        self.roomy = self.n_y <= 2
        self.first_down = "l" if self.lined else "b"
        self.lanes_of = {self.first_down: (0, half), "c": (half, half - 128), "d": (2 * half - 128, 128)}
        self.down = tuple(self.lanes_of)
        self.kinds = ("a", "v") + self.down
        self.plain = tuple(name for name in self.kinds if name != "l")
        self.owners = n_dp * n_z
        self.wide_width = w_up[2]
        self.slot = 8
        while self.slot < self.rows_a:
            self.slot *= 2
        self.per_row = 128 // self.slot
        self.lines_d = -(-self.layers * 10 // self.per_row)
        lines = round16(self.lines_d + self.layers * 3)
        self.kind = {
            "a": (2, round16(2 * self.rows_a), self.rows_a * n_z, self.width),
            "v": (1, lines, lines * n_z, 128),
        }
        self.real = {"a": self.rows_a, "v": self.kind["v"][1]}
        self.number = {"a": self.layers * self.pairs, "v": 1}
        for name, (_, lanes) in self.lanes_of.items():
            self.kind[name] = (1, round16(self.rows_b), self.rows_b * n_z, lanes)
            self.real[name] = self.rows_b
            self.number[name] = self.layers

    def permuted(self, name):
        k, sent, unit, _ = self.kind[name]
        return k * unit != sent * self.n_z or k > 1

    def permutation(self, name):
        k, sent, unit, _ = self.kind[name]
        real = self.real[name]
        table = np.zeros((k * unit, self.n_z * sent), np.float32)
        for block in range(k):
            for z in range(self.n_z):
                for row in range(real):
                    table[block * unit + z * real + row, z * sent + block * real + row] = 1
        return table

    def whole_shape(self, name):
        _, _, unit, lanes = self.kind[name]
        lead = {"a": self.layers * self.blocks, "v": 1}.get(name, self.layers)
        return (lead, self.n_dp * unit, lanes if name == "v" else self.width)


class Place:
    def __init__(self, geo):
        self.geo = geo
        self.d, self.z = lax.axis_index("dp"), lax.axis_index("fsdp")
        self.core = lax.rem(self.d, 2)
        self.x = lax.rem(self.d // 2, 2)
        self.y = self.d // 4

    def y_off(self, step):
        return lax.rem(self.y + step + self.geo.n_y, self.geo.n_y)

    def z_off(self, step):
        return lax.rem(self.z + step + self.geo.n_z, self.geo.n_z)

    def dev_core(self):
        return (self.d + 1 - 2 * self.core, self.z)

    def dev_x(self):
        return (self.d + 2 - 4 * self.x, self.z)

    def dev_y(self, step):
        return (self.y_off(step) * 4 + self.x * 2 + self.core, self.z)

    def dev_z(self, step):
        return (self.d, self.z_off(step))

    def greet(self):
        barrier = pltpu.get_barrier_semaphore()
        partners = [self.dev_core(), self.dev_x()]
        partners += [self.dev_y(step) for step in range(1, self.geo.n_y)]
        partners += [self.dev_z(step) for step in range(1, self.geo.n_z)]
        for partner in partners:
            pl.semaphore_signal(barrier, inc=1, device_id=partner, device_id_type=MESH)
        self.awaited = len(partners)

    def meet(self):
        pl.semaphore_wait(pltpu.get_barrier_semaphore(), self.awaited)


def remote(src, dst, send, recv, device):
    return pltpu.make_async_remote_copy(
        src_ref=src, dst_ref=dst, send_sem=send, recv_sem=recv, device_id=device, device_id_type=MESH
    )


def chunk_a(geo, layer, pair):
    return ("a", layer * geo.pairs + pair, layer * geo.blocks + 2 * pair, 0)


def chunk_down(geo, layer, name):
    return (name, layer, layer, geo.lanes_of[name][0])


def rows_of(whole, name, lead, first, k, unit, lanes):
    def at(y, x, core):
        rows = pl.ds(pl.multiple_of((y * 4 + x * 2 + core) * unit, 16), unit)
        return whole.at[pl.ds(lead, k), rows, slice(None) if name in ("a", "v") else pl.ds(first, lanes)]

    return at


def ways_of(number, k):
    if k == 1:
        return [(slice(0, 1), number % 2 == 0)]
    return [(slice(0, 1), True), (slice(1, k), False)]


class Gather:
    def __init__(self, place, number, chunk, sources, bufs, units, perms, wholes, sems):
        self.p, self.c = place, number
        name, at, lead, first = chunk
        self.ways = ways_of(number, place.geo.kind[name][0])
        k, self.sent, unit, lanes = place.geo.kind[name]
        self.source = sources[name].at[at]
        self.buf = bufs[name].at[at]
        self.perm = perms.get(name)
        self.unit_buf = units[name].at[at] if self.perm is not None else None
        self.unit = self.unit_buf if self.perm is not None else bufs[name].at[pl.ds(at, 1)]
        self.to = rows_of(wholes[name], name, lead, first, k, unit, lanes)
        self.sems = sems
        self.pending = []

    def slot(self, z):
        return self.buf.at[pl.ds(pl.multiple_of(z * self.sent, 16), self.sent)]

    def send(self, src, dst, send, recv, device):
        copy = remote(src, dst, send, recv, device)
        copy.start()
        self.pending.append(copy)

    def arrived(self, dst, send, recv, device):
        remote(dst, dst, send, recv, device).wait_recv()

    def start_z(self):
        p, s, c = self.p, self.sems, self.c
        self.local_z = pltpu.make_async_copy(self.source, self.slot(p.z), s["lz"].at[c])
        self.local_z.start()
        for step in range(1, p.geo.n_z):
            self.send(self.source, self.slot(p.z), s["zs"].at[c, step], s["zr"].at[c, step], p.dev_z(step))

    def own(self):
        p, s, c = self.p, self.sems, self.c
        self.local_z.wait()
        for step in range(1, p.geo.n_z):
            self.arrived(self.slot(p.z_off(-step)), s["zs"].at[c, step], s["zr"].at[c, step], p.dev_z(step))
        if self.perm is not None:
            k, unit, lanes = self.unit_buf.shape
            mixed = jnp.dot(self.perm[...], self.buf[...], preferred_element_type=F32)
            self.unit_buf[...] = mixed.astype(BF).reshape(k, unit, lanes)
        here = self.to(p.y, p.x, p.core)
        self.local = pltpu.make_async_copy(self.unit, here, s["lo"].at[c])
        self.send(self.unit, here, s["xs"].at[c], s["xr"].at[c], p.dev_x())
        for step in range(1, p.geo.n_y):
            self.send(self.unit, here, s["ys"].at[c, step], s["yr"].at[c, step], p.dev_y(step))
        self.send(self.unit, here, s["cs"].at[c, 0], s["cr"].at[c, 0], p.dev_core())
        self.local.start()

    def forward(self):
        p, s, c = self.p, self.sems, self.c
        n_y = p.geo.n_y
        from_x = self.to(p.y, 1 - p.x, p.core)
        self.arrived(from_x, s["xs"].at[c], s["xr"].at[c], p.dev_x())
        for way, (blocks, by_x) in enumerate(self.ways):
            for step in range(1, n_y) if by_x else ():
                at = (c, way, step)
                rows = from_x.at[blocks]
                self.send(rows, rows, s["ds"].at[at], s["dr"].at[at], p.dev_y(step))
        self.send(from_x, from_x, s["cs"].at[c, 1], s["cr"].at[c, 1], p.dev_core())
        for step in range(1, n_y):
            from_y = self.to(p.y_off(-step), p.x, p.core)
            self.arrived(from_y, s["ys"].at[c, step], s["yr"].at[c, step], p.dev_y(step))
            for way, (blocks, by_x) in enumerate(self.ways):
                if not by_x:
                    at = (c, way, step)
                    rows = from_y.at[blocks]
                    self.send(rows, rows, s["ds"].at[at], s["dr"].at[at], p.dev_x())
            self.send(from_y, from_y, s["cs"].at[c, 2 * step], s["cr"].at[c, 2 * step], p.dev_core())

    def corner(self):
        p, s, c = self.p, self.sems, self.c
        for step in range(1, p.geo.n_y):
            far = self.to(p.y_off(-step), 1 - p.x, p.core)
            for way, (blocks, _) in enumerate(self.ways):
                at = (c, way, step)
                self.arrived(far.at[blocks], s["ds"].at[at], s["dr"].at[at], p.dev_x())
            self.send(far, far, s["cs"].at[c, 2 * step + 1], s["cr"].at[c, 2 * step + 1], p.dev_core())

    def arrive(self):
        p, s, c = self.p, self.sems, self.c
        for step in range(p.geo.n_y):
            for flip in range(2):
                x = p.x if flip == 0 else 1 - p.x
                got = self.to(p.y_off(-step), x, 1 - p.core)
                at = 2 * step + flip
                self.arrived(got, s["cs"].at[c, at], s["cr"].at[c, at], p.dev_core())
        self.local.wait()

    def drain(self):
        for copy in self.pending:
            copy.wait_send()


def when(condition, act):
    pl.when(condition)(act)


def on_line(place, way, step):
    at = place.z - step if way == 0 else place.z + step
    return (at >= 0) & (at < place.geo.n_z), at


class GatherLine:
    def __init__(self, place, number, chunk, sources, wholes, sems):
        self.p, self.c = place, number
        _, at, lead, first = chunk
        _, sent, _, lanes = place.geo.kind["l"]
        self.source = sources["l"].at[at]
        self.half_a = number % 2 == 0
        whole = wholes["l"]

        def piece(y, x, core, z):
            device = (y * 4 + x * 2 + core) * place.geo.n_z + z
            rows = pl.ds(pl.multiple_of(device * sent, 16), sent)
            return whole.at[lead, rows, pl.ds(first, lanes)]

        self.piece = piece
        self.sems = sems
        self.pending, self.line_pending = [], []

    def send(self, src, dst, send, recv, device):
        copy = remote(src, dst, send, recv, device)
        copy.start()
        self.pending.append(copy)

    def arrived(self, dst, send, recv, device):
        remote(dst, dst, send, recv, device).wait_recv()

    def from_column(self, at, z, core):
        p = self.p
        return self.piece(p.y_off(-(at // 2)), p.x if at % 2 == 0 else 1 - p.x, core, z)

    def line_send(self, column, hop):
        p, s, c = self.p, self.sems, self.c
        for way in range(2):
            valid, z = on_line(p, way, hop - 1)
            further, target = on_line(p, 1 - way, 1)

            def copy(z=z, target=target, way=way):
                rows = self.from_column(column, z, p.core)
                at = (c, way, hop, column)
                return remote(rows, rows, s["gs"].at[at], s["gr"].at[at], (p.d, target))

            when(valid & further, lambda copy=copy: copy().start())
            self.line_pending.append((valid & further, copy))

    def to_core(self, column, z, at):
        s = self.sems
        rows = self.from_column(column, z, self.p.core)
        return remote(rows, rows, s["hs"].at[at], s["hr"].at[at], self.p.dev_core())

    def start(self):
        p, s, c = self.p, self.sems, self.c
        here = self.piece(p.y, p.x, p.core, p.z)
        self.local = pltpu.make_async_copy(self.source, here, s["gl"].at[c])
        self.send(self.source, here, s["gx"].at[c, 0], s["gx"].at[c, 1], p.dev_x())
        for step in range(1, p.geo.n_y):
            self.send(self.source, here, s["gy"].at[c, 0, step], s["gy"].at[c, 1, step], p.dev_y(step))
        self.local.start()
        at = (c, 0, 0, 0)
        self.send(self.source, here, s["hs"].at[at], s["hr"].at[at], p.dev_core())

    def forward(self):
        p, s, c = self.p, self.sems, self.c
        n_y = p.geo.n_y
        self.local.wait()
        rows = self.from_column(1, p.z, p.core)
        self.arrived(rows, s["gx"].at[c, 0], s["gx"].at[c, 1], p.dev_x())
        if self.half_a:
            for step in range(1, n_y):
                self.send(rows, rows, s["gd"].at[c, 0, step], s["gd"].at[c, 1, step], p.dev_y(step))
        self.keep_core(1)
        for step in range(1, n_y):
            rows = self.from_column(2 * step, p.z, p.core)
            self.arrived(rows, s["gy"].at[c, 0, step], s["gy"].at[c, 1, step], p.dev_y(step))
            if not self.half_a:
                self.send(rows, rows, s["gd"].at[c, 0, step], s["gd"].at[c, 1, step], p.dev_x())
            self.keep_core(2 * step)

    def keep_core(self, column):
        copy = self.to_core(column, self.p.z, (self.c, 0, 0, column))
        copy.start()
        self.pending.append(copy)

    def corner(self):
        p, s, c = self.p, self.sems, self.c
        for step in range(1, p.geo.n_y):
            rows = self.from_column(2 * step + 1, p.z, p.core)
            self.arrived(rows, s["gd"].at[c, 0, step], s["gd"].at[c, 1, step], p.dev_x())
            self.keep_core(2 * step + 1)

    def relay(self, hop, half):
        p, s, c = self.p, self.sems, self.c
        n_y = p.geo.n_y
        for column in range(half * n_y, (half + 1) * n_y):
            for way in range(2) if hop > 0 else ():
                valid, z = on_line(p, way, hop)
                at = (c, way, hop, column)

                def act(z=z, at=at):
                    rows = self.from_column(column, z, p.core)
                    remote(rows, rows, s["gs"].at[at], s["gr"].at[at], p.dev_x()).wait_recv()
                    self.to_core(column, z, at).start()

                when(valid, act)
                self.line_pending.append(
                    (valid, lambda column=column, z=z, at=at: self.to_core(column, z, at))
                )
            if hop < p.geo.n_z - 1:
                self.line_send(column, hop + 1)

    def arrive(self):
        p, s, c = self.p, self.sems, self.c
        for column in range(2 * p.geo.n_y):
            rows = self.from_column(column, p.z, 1 - p.core)
            at = (c, 0, 0, column)
            self.arrived(rows, s["hs"].at[at], s["hr"].at[at], p.dev_core())
            for hop in range(1, p.geo.n_z):
                for way in range(2):
                    valid, z = on_line(p, way, hop)
                    at = (c, way, hop, column)

                    def act(z=z, at=at):
                        rows = self.from_column(column, z, 1 - p.core)
                        self.arrived(rows, s["hs"].at[at], s["hr"].at[at], p.dev_core())

                    when(valid, act)

    def drain(self):
        for copy in self.pending:
            copy.wait_send()
        for valid, copy in self.line_pending:
            when(valid, lambda copy=copy: copy().wait_send())


def run_pipeline(stages, count, extra):
    last = max(lag for lag, _ in stages)
    first = min(lag for lag, _ in stages)
    for step in range(first, count + last):
        ahead = [stage for stage in stages if stage[0] < 0]
        ahead += stages[1:3]
        for lag, act in ahead + [(None, act) for act in extra.get(step, ())] + stages[len(ahead) :]:
            if lag is None:
                act()
            elif 0 <= step - lag < count:
                act(step - lag)


def dma(*shape):
    return pltpu.SemaphoreType.DMA(shape)


ANY = pl.BlockSpec(memory_space=pl.ANY)
IN_VMEM = pl.BlockSpec(memory_space=pltpu.VMEM)


def wide(values):
    return values.astype(F32)


class Scatter:
    def __init__(self, place, number, chunk, stage, sums, mids, ends, perms, z_send, z_recv, z_slot, before, put, sems):
        self.p, self.c = place, number
        name, at, _, _ = chunk
        self.k, self.sent, self.rows, self.lanes = place.geo.kind[name]
        self.ways = ways_of(number, self.k)
        self.part = slice(None)
        self.stage = stage
        self.sum = sums[name].at[at]
        shared, per_layer = name == "a", place.geo.pairs
        self.mid = mids[name].at[at % per_layer if shared else at]
        self.hands_on = shared and at >= per_layer
        self.takes_over = shared and at < place.geo.number[name] - per_layer
        self.heir = None
        self.end = ends[name].at[at]
        self.perm = perms.get(name)
        if name in z_send:
            self.z_send, self.z_recv = z_send[name].at[z_slot], z_recv[name].at[at]
        self.before, self.z_moves = before, []
        self.put = put
        self.sems = sems
        self.pending = []

    def send(self, src, dst, send, recv, device):
        copy = remote(src, dst, send, recv, device)
        copy.start()
        self.pending.append(copy)

    def arrived(self, dst, send, recv, device):
        remote(dst, dst, send, recv, device).wait_recv()

    def start(self):
        p, s, c = self.p, self.sems, self.c
        give = self.stage.at[:, :, :, 1 - p.core]
        self.given = remote(give, self.sum, s["cs"].at[c], s["cr"].at[c], p.dev_core())
        self.given.start()

    def pair(self):
        p, s, c = self.p, self.sems, self.c
        n_y = p.geo.n_y
        self.arrived(self.sum, s["cs"].at[c], s["cr"].at[c], p.dev_core())

        @pl.loop(0, self.k * n_y * 2)
        def _(at):
            where = (at // (2 * n_y), lax.rem(at // 2, n_y), lax.rem(at, 2))
            self.sum[where] = (wide(self.sum[where]) + wide(self.stage[where + (p.core,)])).astype(BF)

        self.given.wait_send()
        self.send_middle()

    def send_middle(self):
        p, s, c = self.p, self.sems, self.c
        n_y = p.geo.n_y
        for way, (blocks, by_x) in enumerate(self.ways):
            if self.takes_over:
                for step in range(1, n_y) if by_x else ():
                    pl.semaphore_wait(s["fy"].at[c, step], 1)
                if not by_x:
                    pl.semaphore_wait(s["fx"].at[c], 1)
            if by_x:
                for step in range(1, n_y):
                    at = (c, way, step)
                    self.send(
                        self.sum.at[blocks, p.y_off(step), :, self.part], self.mid.at[step - 1, blocks],
                        s["ms"].at[at], s["mr"].at[at], p.dev_y(step),
                    )
            else:
                for y in range(n_y):
                    at = (c, way, y)
                    self.send(
                        self.sum.at[blocks, y, 1 - p.x, self.part], self.mid.at[y // 2, blocks, y % 2],
                        s["ms"].at[at], s["mr"].at[at], p.dev_x(),
                    )

    def middle(self):
        for way, (blocks, by_x) in enumerate(self.ways):
            (self.middle_x if by_x else self.middle_y)(way, blocks)

    def middle_x(self, way, blocks):
        p, s, c = self.p, self.sems, self.c
        n_y, first = p.geo.n_y, blocks.start
        for step in range(1, n_y):
            at = (c, way, step)
            self.arrived(self.mid.at[step - 1, blocks], s["ms"].at[at], s["mr"].at[at], p.dev_y(step))

        @pl.loop(0, (blocks.stop - first) * 2)
        def _(at):
            where = (first + at // 2, p.y, lax.rem(at, 2), self.part)
            value = wide(self.sum[where])
            for step in range(1, n_y):
                value = value + wide(self.mid[step - 1, first + at // 2, lax.rem(at, 2)])
            self.sum[where] = value.astype(BF)

        if self.hands_on:
            for step in range(1, n_y):
                pl.semaphore_signal(
                    s["fy"].at[self.heir.c, step], inc=1, device_id=p.dev_y(-step), device_id_type=MESH
                )
        at = (c, way, 0)
        self.send(
            self.sum.at[blocks, p.y, 1 - p.x, self.part], self.end.at[0, blocks],
            s["es"].at[at], s["er"].at[at], p.dev_x(),
        )

    def middle_y(self, way, blocks):
        p, s, c = self.p, self.sems, self.c
        n_y, first = p.geo.n_y, blocks.start
        for y in range(n_y):
            at = (c, way, y)
            self.arrived(self.mid.at[y // 2, blocks, y % 2], s["ms"].at[at], s["mr"].at[at], p.dev_x())

        @pl.loop(0, (blocks.stop - first) * n_y)
        def _(at):
            y = lax.rem(at, n_y)
            where = (first + at // n_y, y, p.x, self.part)
            value = wide(self.sum[where]) + wide(self.mid[y // 2, first + at // n_y, lax.rem(y, 2)])
            self.sum[where] = value.astype(BF)

        if self.hands_on:
            pl.semaphore_signal(s["fx"].at[self.heir.c], inc=1, device_id=p.dev_x(), device_id_type=MESH)
        for step in range(1, n_y):
            at = (c, way, step)
            self.send(
                self.sum.at[blocks, p.y_off(step), p.x, self.part], self.end.at[step - 1, blocks],
                s["es"].at[at], s["er"].at[at], p.dev_y(step),
            )

    def column_sum(self):
        p, s, c = self.p, self.sems, self.c
        n_y = p.geo.n_y
        found = []
        for way, (blocks, by_x) in enumerate(self.ways):
            value = wide(self.sum[blocks, p.y, p.x, self.part])
            for step in (0,) if by_x else range(1, n_y):
                at = (c, way, step)
                got = self.end.at[0 if by_x else step - 1, blocks]
                self.arrived(got, s["es"].at[at], s["er"].at[at], p.dev_x())
                value = value + wide(got[...])
            found.append(value)
        return found[0] if len(found) == 1 else jnp.concatenate(found, 0)

    def last(self):
        p, s, c = self.p, self.sems, self.c
        n_z = p.geo.n_z
        value = self.column_sum().astype(BF).reshape(self.k * self.rows, self.lanes)
        if self.perm is not None:
            value = jnp.dot(self.perm[...], value, preferred_element_type=F32).astype(BF)
        if self.before is not None:
            self.before.left()
        self.z_send[...] = value.reshape(n_z, self.sent, self.lanes)
        for step in range(1, n_z):
            copy = remote(
                self.z_send.at[p.z_off(step)], self.z_recv.at[step],
                s["zs"].at[c, step], s["zr"].at[c, step], p.dev_z(step),
            )
            copy.start()
            self.z_moves.append(copy)

    def finish(self):
        p, s, c = self.p, self.sems, self.c
        value = wide(self.z_send[p.z])
        for step in range(1, p.geo.n_z):
            self.arrived(self.z_recv.at[step], s["zs"].at[c, step], s["zr"].at[c, step], p.dev_z(step))
            value = value + wide(self.z_recv[step])
        self.put(value)

    def left(self):
        while self.z_moves:
            self.z_moves.pop().wait_send()

    def drain(self):
        self.left()
        for copy in self.pending:
            copy.wait_send()


class ScatterLine(Scatter):
    def land(self, line):
        self.line = line
        p = self.p
        self.unit = self.rows // p.geo.n_z
        self.part = pl.ds(pl.multiple_of(p.z * self.unit, 16), self.unit)
        self.line_pending = []
        return self

    def slice_of(self, target):
        return pl.ds(target * self.unit, self.unit)

    def line_copy(self, src, way, target, further):
        s = self.sems
        at = (self.c_line, way, target)
        return remote(src, self.line.at[way, target], s["ls"].at[at], s["lr"].at[at], (self.p.d, further))

    def send_middle(self):
        p, last = self.p, self.p.geo.n_z - 1
        for way in range(2):
            ours = p.z == (0 if way == 0 else last)
            targets = range(last, 0, -1) if way == 0 else range(last)
            further = p.z + 1 if way == 0 else p.z - 1
            for target in targets:

                def copy(way=way, target=target, further=further):
                    return self.line_copy(self.sum.at[0, :, :, self.slice_of(target)], way, target, further)

                when(ours, lambda copy=copy: copy().start())
                self.line_pending.append((ours, copy))

    def relay(self, hop):
        p, s, last = self.p, self.sems, self.p.geo.n_z - 1
        for way in range(2):
            here = hop if way == 0 else last - hop
            targets = range(last, here, -1) if way == 0 else range(here)
            further = p.z + 1 if way == 0 else p.z - 1
            for target in targets:

                def copy(way=way, target=target, further=further):
                    return self.line_copy(self.line.at[way, target], way, target, further)

                def act(way=way, target=target, copy=copy):
                    self.add_line(way, target)
                    copy().start()

                when(p.z == here, act)
                self.line_pending.append((p.z == here, copy))

    def add_line(self, way, target):
        s, n_y = self.sems, self.p.geo.n_y
        at = (self.c_line, way, target)
        got = self.line.at[way, target]
        remote(got, got, s["ls"].at[at], s["lr"].at[at], self.p.dev_x()).wait_recv()

        @pl.loop(0, 2 * n_y)
        def _(index):
            where = (index // 2, lax.rem(index, 2))
            mine = wide(self.sum[(0,) + where + (self.slice_of(target),)])
            got[where] = (wide(got[where]) + mine).astype(BF)

    def collect(self):
        p, s, n_y, last = self.p, self.sems, self.p.geo.n_y, self.p.geo.n_z - 1
        for way in range(2):

            def act(way=way):
                at = (self.c_line, way, p.z)
                got = self.line.at[way, p.z]
                remote(got, got, s["ls"].at[at], s["lr"].at[at], p.dev_x()).wait_recv()

                @pl.loop(0, 2 * n_y)
                def _(index):
                    where = (index // 2, lax.rem(index, 2))
                    place = (0,) + where + (self.part,)
                    self.sum[place] = (wide(self.sum[place]) + wide(got[where])).astype(BF)

            when(p.z > 0 if way == 0 else p.z < last, act)
        Scatter.send_middle(self)

    def last(self):
        self.put(self.column_sum().reshape(self.unit, self.lanes))

    def finish(self):
        pass

    def drain(self):
        for valid, copy in self.line_pending:
            when(valid, lambda copy=copy: copy().wait_send())
        Scatter.drain(self)


def mm(left, right):
    return jnp.dot(left, right, preferred_element_type=F32)


def mm_nt(left, right):
    return lax.dot_general(left, right, (((1,), (1,)), ((), ())), preferred_element_type=F32)


def mm_tn(left, right):
    return lax.dot_general(left, right, (((0,), (0,)), ((), ())), preferred_element_type=F32)


def mean_of(values):
    return jnp.sum(values, -1, keepdims=True) * (1.0 / values.shape[-1])


def normal(values):
    centered = values - mean_of(values)
    scale = lax.rsqrt(mean_of(centered * centered) + epsilon)
    return centered * scale, scale


def norm_rows(source, gain, shift, target, block=32):
    @pl.loop(0, source.shape[0] // block)
    def _(at):
        rows = pl.ds(pl.multiple_of(at * block, block), block)
        unit, _ = normal(source[rows, :])
        target[rows, :] = (unit * gain + shift).astype(target.dtype)


def fold(values):
    total = values[0:8]
    for at in range(8, values.shape[0], 8):
        total = total + values[at : at + 8]
    return total


def norm_rows_back(source, gain, incoming, emit, sums, block=32):
    sums[...] = jnp.zeros_like(sums)

    @pl.loop(0, source.shape[0] // block)
    def _(at):
        rows = pl.ds(pl.multiple_of(at * block, block), block)
        unit, scale = normal(source[rows, :])
        back = incoming[rows, :]
        sums[0] += fold(back * unit)
        sums[1] += fold(back)
        inner = back * gain
        emit(rows, scale * (inner - mean_of(inner) - unit * mean_of(inner * unit)))


ROOT = 0.7978845608028654
CUBE = 0.044715


def gelu_parts(values):
    square = values * values
    curve = jnp.tanh(ROOT * (values + CUBE * (values * square)))
    return square, curve


class Layer:
    def __init__(self, refs, weight_a, weight_b, vec_d, vec_f, layer, heads):
        self.__dict__.update(refs)
        self.weight_a, self.weight_b = weight_a, weight_b
        self.vec_d, self.vec_f = vec_d, vec_f
        self.layer, self.heads = layer, heads

    def gain(self, at):
        return self.vec_d[self.layer * 10 + at : self.layer * 10 + at + 1, :]

    def shift(self, at):
        return self.gain(3 + at)

    def gain_f(self, at):
        return self.vec_f[self.layer * 3 + at : self.layer * 3 + at + 1, :]

    def lane_half(self, values, side):
        lane = lax.broadcasted_iota(jnp.int32, values.shape, 1)
        return (lane < HEAD_DIM) == (side == 0)

    def forward_norm(self):
        norm_rows(self.x, self.gain(0), self.shift(0), self.normed)

    def forward_qkv(self, part):
        value = mm(self.normed[...], self.weight_a(part))
        if part != 1:
            value = value + self.shift(3 if part == 0 else 4)
        self.qkv[part] = value.astype(BF)

    def forward_attention(self):
        valid = self.mask[...] > 0.5

        @pl.loop(0, self.heads // 2)
        def _(pair):
            lanes = pl.ds(pl.multiple_of(pair * 128, 128), 128)
            queries, keys, values = [self.qkv[part, :, lanes] for part in range(3)]
            context = None
            for side in range(2):
                half = self.lane_half(queries, side)
                scores = mm_nt(jnp.where(half, queries, jnp.zeros_like(queries)), keys)
                scores = jnp.where(valid, scores * HEAD_DIM**-0.5, -1e9)
                top = jnp.max(scores, -1, keepdims=True)
                grown = jnp.exp(scores - top)
                prob = grown / jnp.sum(grown, -1, keepdims=True)
                self.prob[2 * pair + side] = prob
                product = mm(prob.astype(BF), values)
                context = product if side == 0 else jnp.where(half, product, context)
            self.context[:, lanes] = context

    def forward_out(self):
        norm_rows(self.context, self.gain(1), self.shift(1), self.sub)
        self.after[...] = self.x[...] + (mm(self.sub[...], self.weight_a(3)) + self.shift(5))
        norm_rows(self.after, self.gain(2), self.shift(2), self.normed_ffn)

    def forward_up(self, part):
        width = self.x.shape[1]
        lanes = slice(part * width, (part + 1) * width)
        self.hidden[:, lanes] = mm(self.normed_ffn[...], self.weight_a(4 + part)) + self.gain_f(1)[:, lanes]

    def forward_gelu(self):
        @pl.loop(0, self.x.shape[0] // 16)
        def _(at):
            rows = pl.ds(pl.multiple_of(at * 16, 16), 16)
            values = self.hidden[rows, :]
            _, curve = gelu_parts(values)
            unit, _ = normal(0.5 * values * (1.0 + curve))
            self.sub_ffn[rows, :] = (unit * self.gain_f(0) + self.gain_f(2)).astype(BF)

    def forward_down(self, lanes):
        value = mm(self.sub_ffn[...], self.weight_b(slice(None), lanes))
        self.x_next[:, lanes] = self.after[:, lanes] + (value + self.shift(6)[:, lanes])


    def store_sums_d(self, at, sums):
        row = self.layer * 10 + at
        self.grad_d[row : row + 1, :] = jnp.sum(sums, 0, keepdims=True)

    def store_sums_f(self, at, sums):
        row = self.layer * 3 + at
        self.grad_f[row : row + 1, :] = jnp.sum(sums, 0, keepdims=True)

    def backward_start(self):
        self.low[...] = self.back[...].astype(BF)
        self.store_sums_d(9, wide(self.low[...]))

    def grad_up(self, part):
        width = self.x.shape[1]
        return mm_tn(self.normed_ffn[...], self.d_hidden[:, part * width : (part + 1) * width])

    def grad_out(self):
        return mm_tn(self.sub[...], self.low[...])

    def grad_qkv(self, part):
        return mm_tn(self.normed[...], self.d_qkv[part])

    def backward_down(self):
        width = self.x.shape[1]
        for part in range(self.hidden.shape[1] // width):
            lanes = slice(part * width, (part + 1) * width)
            self.wide_back[:, lanes] = mm_nt(self.low[...], self.weight_b(lanes, slice(None)))

    def backward_gelu(self):
        self.sums_f[...] = jnp.zeros_like(self.sums_f)

        @pl.loop(0, self.x.shape[0] // 16)
        def _(at):
            rows = pl.ds(pl.multiple_of(at * 16, 16), 16)
            values = self.hidden[rows, :]
            square, curve = gelu_parts(values)
            unit, scale = normal(0.5 * values * (1.0 + curve))
            back = self.wide_back[rows, :]
            self.sums_f[0] += fold(back * unit)
            self.sums_f[1] += fold(back)
            inner = back * self.gain_f(0)
            d_gelu = scale * (inner - mean_of(inner) - unit * mean_of(inner * unit))
            slope = 0.5 * (1.0 + curve) + 0.5 * values * (1.0 - curve * curve) * (
                ROOT * (1.0 + 3.0 * CUBE * square)
            )
            low = (d_gelu * slope).astype(BF)
            self.d_hidden[rows, :] = low
            self.sums_f[2] += fold(wide(low))

        self.store_sums_f(0, self.sums_f[0])
        self.store_sums_f(2, self.sums_f[1])
        self.store_sums_f(1, self.sums_f[2])

    def backward_up(self):
        width = self.x.shape[1]
        total = None
        for part in range(self.hidden.shape[1] // width):
            lanes = slice(part * width, (part + 1) * width)
            value = mm_nt(self.d_hidden[:, lanes], self.weight_a(4 + part))
            if part == 0:
                self.incoming[...] = value
            else:
                self.incoming[...] += value

        def emit(rows, value):
            value = self.back[rows, :] + value
            self.back[rows, :] = value
            self.low[rows, :] = value.astype(BF)

        norm_rows_back(self.after, self.gain(2), self.incoming, emit, self.sums_d)
        self.store_sums_d(2, self.sums_d[0])
        self.store_sums_d(5, self.sums_d[1])

    def backward_out(self):
        self.store_sums_d(8, wide(self.low[...]))
        self.incoming[...] = mm_nt(self.low[...], self.weight_a(3))

        def emit(rows, value):
            self.low[rows, :] = value.astype(BF)

        norm_rows_back(self.context, self.gain(1), self.incoming, emit, self.sums_d)
        self.store_sums_d(1, self.sums_d[0])
        self.store_sums_d(4, self.sums_d[1])

    def backward_attention(self):
        @pl.loop(0, self.heads // 2)
        def _(pair):
            lanes = pl.ds(pl.multiple_of(pair * 128, 128), 128)
            queries, keys, values = [self.qkv[part, :, lanes] for part in range(3)]
            d_context = self.low[:, lanes]
            found = [None] * 3
            for side in range(2):
                half = self.lane_half(d_context, side)
                prob = self.prob[2 * pair + side]
                d_prob = mm_nt(jnp.where(half, d_context, jnp.zeros_like(d_context)), values)
                dot = jnp.sum(prob * d_prob, -1, keepdims=True)
                d_scores = (prob * (d_prob - dot)).astype(BF)
                new = (
                    mm(d_scores, keys) * HEAD_DIM**-0.5,
                    mm_tn(d_scores, queries) * HEAD_DIM**-0.5,
                    mm_tn(prob.astype(BF), d_context),
                )
                found = [n if side == 0 else jnp.where(half, n, f) for n, f in zip(new, found)]
            for part in range(3):
                self.d_qkv[part, :, lanes] = found[part].astype(BF)

    def backward_qkv(self):
        self.store_sums_d(6, wide(self.d_qkv[0]))
        self.store_sums_d(7, wide(self.d_qkv[2]))
        for part in range(3):
            value = mm_nt(self.d_qkv[part], self.weight_a(part))
            if part == 0:
                self.incoming[...] = value
            else:
                self.incoming[...] += value

        def emit(rows, value):
            self.back[rows, :] = self.back[rows, :] + value

        norm_rows_back(self.x, self.gain(0), self.incoming, emit, self.sums_d)
        self.store_sums_d(0, self.sums_d[0])
        self.store_sums_d(3, self.sums_d[1])


def saved_shapes(rows, width, wide_width, heads):
    return {
        "normed": ((rows, width), BF),
        "qkv": ((3, rows, width), BF),
        "prob": ((heads, rows, rows), F32),
        "context": ((rows, width), F32),
        "sub": ((rows, width), BF),
        "after": ((rows, width), F32),
        "normed_ffn": ((rows, width), BF),
        "hidden": ((rows, wide_width), F32),
        "sub_ffn": ((rows, wide_width), BF),
    }


def work_shapes(rows, width, wide_width):
    return {
        "low": ((rows, width), BF),
        "incoming": ((rows, width), F32),
        "wide_back": ((rows, wide_width), F32),
        "d_qkv": ((3, rows, width), BF),
        "sums_d": ((2, 8, width), F32),
        "sums_f": ((3, 8, wide_width), F32),
    }


def spread_tables(geo):
    tables = []
    for width, real in ((geo.width, geo.rows_a), (geo.wide_width, geo.rows_b)):
        at = np.arange(width)
        owner = (at[None, :] // real == np.arange(geo.owners)[:, None]).astype(np.float32)
        tables += [jnp.asarray(owner, BF), jnp.asarray(at[None, :] % real, jnp.int32)]
    return tables


def unpack_vectors(geo, whole_v, wide_v, tables, vec_d, vec_f):
    owner_d, rest_d, owner_f, rest_f = tables
    lines = geo.kind["v"][1]
    wide_v[...] = wide(whole_v[0])
    line_of = lambda at: wide_v[pl.ds(at, geo.owners, stride=lines), :].astype(BF)
    pick_d = lax.broadcasted_iota(jnp.int32, (geo.slot, geo.width), 0) == rest_d[...]
    for line in range(geo.lines_d):
        spread = mm_tn(line_of(line), owner_d[...])
        for at in range(geo.per_row):
            part = spread[at * geo.slot : (at + 1) * geo.slot]
            row = line * geo.per_row + at
            if row < geo.layers * 10:
                vec_d[row : row + 1, :] = jnp.sum(jnp.where(pick_d, part, 0.0), 0, keepdims=True)
    pick_f = lax.broadcasted_iota(jnp.int32, (128, geo.width), 0)
    for row in range(geo.layers * 3):
        line = line_of(geo.lines_d + row)
        for first in range(0, geo.wide_width, geo.width):
            lanes = slice(first, first + geo.width)
            spread = jnp.where(pick_f == rest_f[:, lanes], mm_tn(line, owner_f[:, lanes]), 0.0)
            vec_f[row : row + 1, lanes] = jnp.sum(spread, 0, keepdims=True)


GATHER_SEMS = (
    "lz", "lo", "zs", "zr", "xs", "xr", "ys", "yr", "ds", "dr", "cs", "cr",
    "gl", "gx", "gy", "gd", "gs", "gr", "hs", "hr",
)
LINE_FIRST = (1, 6)


def forward_kernel(geo, names_perm, saved_names, *refs):
    refs = list(refs)
    take = lambda number: [refs.pop(0) for _ in range(number)]
    sources = dict(zip(geo.kinds, take(len(geo.kinds))))
    perms = dict(zip(names_perm, take(len(names_perm))))
    act_ref, mask_ref = take(2)
    tables = take(4)
    out_ref, vec_d, vec_f, kept_a, kept_b, kept_x = take(6)
    kept = [dict(zip(saved_names, take(len(saved_names)))) for _ in range(geo.layers)]
    wholes = dict(zip(("a", "v", "b"), take(3)))
    wholes.update({name: wholes["b"] for name in geo.down})
    bufs = dict(zip(geo.plain, take(len(geo.plain))))
    units = dict(zip(names_perm, take(len(names_perm))))
    saved = [dict(zip(saved_names, take(len(saved_names)))) for _ in range(geo.layers)]
    xs, wide_v, keep_sem = take(3)
    sems = dict(zip(GATHER_SEMS, take(len(GATHER_SEMS))))
    place = Place(geo)
    chunks, line_chunks = [("v", 0, 0, 0)], []
    for layer in range(geo.layers):
        chunks += [chunk_a(geo, layer, pair) for pair in range(geo.pairs)]
        for name in geo.down:
            (line_chunks if name == "l" else chunks).append(chunk_down(geo, layer, name))
    moves = [
        Gather(place, at, chunk, sources, bufs, units, perms, wholes, sems)
        for at, chunk in enumerate(chunks)
    ]
    lines = [
        GatherLine(place, at, chunk, sources, wholes, sems) for at, chunk in enumerate(line_chunks)
    ]
    keeps = []

    def keep(src, dst):
        copy = pltpu.make_async_copy(src, dst, keep_sem.at[len(keeps)])
        copy.start()
        keeps.append(copy)

    net = []
    for layer in range(geo.layers):
        fields = dict(saved[layer], x=xs.at[layer], x_next=xs.at[layer + 1], mask=mask_ref)
        read_a = lambda at, layer=layer: wholes["a"][layer * geo.blocks + at]
        read_b = lambda rows, lanes, layer=layer: wholes["b"][layer, rows, lanes]
        net.append(Layer(fields, read_a, read_b, vec_d, vec_f, layer, geo.width // HEAD_DIM))

    def compute(number):
        name, at, lead, first = chunks[number]
        if geo.lined and name == "c":
            lines[lead].arrive()
            down(lead, *geo.lanes_of["l"])
        moves[number].arrive()
        if name == "v":
            unpack_vectors(geo, wholes["v"], wide_v, tables, vec_d, vec_f)
            return
        k, _, _, lanes = geo.kind[name]
        layer = at // geo.pairs if name == "a" else at
        one = net[layer]
        save = lambda *found: [keep(saved[layer][field], kept[layer][field]) for field in found]
        if name == "a":
            keep(wholes["a"].at[pl.ds(lead, k)], kept_a.at[pl.ds(lead, k)])
            pair = at % geo.pairs
            if pair == 0:
                one.forward_norm()
                one.forward_qkv(0)
                one.forward_qkv(1)
            elif pair == 1:
                one.forward_qkv(2)
                save("normed", "qkv")
                one.forward_attention()
                one.forward_out()
                save("prob", "context", "sub", "after", "normed_ffn")
            else:
                one.forward_up(2 * pair - 4)
                one.forward_up(2 * pair - 3)
                if pair == geo.pairs - 1:
                    one.forward_gelu()
                    save("hidden", "sub_ffn")
        else:
            down(layer, first, lanes)
            if name == geo.down[-1] and layer < geo.layers - 1:
                keep(xs.at[layer + 1], kept_x.at[layer + 1])

    def down(layer, first, lanes):
        where = pl.ds(first, lanes)
        keep(wholes["b"].at[layer, :, where], kept_b.at[layer, :, where])
        net[layer].forward_down(slice(first, first + lanes))

    extra = {}
    for layer, line in enumerate(lines):
        plan = [line.start, line.forward, line.corner]
        plan += [
            lambda line=line, hop=hop, half=half: line.relay(hop, half)
            for hop in range(geo.n_z)
            for half in range(2)
        ]
        needed = chunks.index(chunk_down(geo, layer, "c")) + 2
        for at, act in enumerate(plan):
            step = at - 2 if at < 3 else LINE_FIRST[min(layer, 1)] + at - 3
            extra.setdefault(min(step, needed), []).append(act)

    place.greet()
    xs[0] = wide(act_ref[...])
    keep(xs.at[0], kept_x.at[0])
    place.meet()
    run_pipeline(
        [
            (-2, lambda c: moves[c].start_z()),
            (0, lambda c: moves[c].own()),
            (3, compute),
            (1, lambda c: moves[c].forward()),
            (2, lambda c: moves[c].corner()),
        ],
        len(moves),
        extra,
    )
    out_ref[...] = xs[geo.layers].astype(BF)
    for move in moves + lines:
        move.drain()
    for copy in keeps:
        copy.wait()


def run_forward(geo, sources, act, mask):
    names_perm = [name for name in geo.plain if geo.permuted(name)]
    perms = [jnp.asarray(geo.permutation(name), BF) for name in names_perm]
    rows, width = act.shape
    total = sum(geo.number.values())
    heads = width // HEAD_DIM
    saved = saved_shapes(rows, width, geo.wide_width, heads)
    bufs, units, wholes = [], [], []
    for name in geo.plain:
        k, sent, unit, lanes = geo.kind[name]
        bufs.append(pltpu.VMEM((geo.number[name], geo.n_z * sent, lanes), BF))
        if name in names_perm:
            units.append(pltpu.VMEM((geo.number[name], k, unit, lanes), BF))
    wholes = [(geo.whole_shape(name), BF) for name in ("a", "v", "c")]
    n_y, n_z = geo.n_y, geo.n_z
    n_keeps = geo.layers * (len(saved) + geo.pairs + len(geo.down) + 1)
    vec_rows = geo.layers * 10
    outs = [
        jax.ShapeDtypeStruct((rows, width), BF),
        jax.ShapeDtypeStruct((vec_rows, width), F32),
        jax.ShapeDtypeStruct((geo.layers * 3, geo.wide_width), F32),
        jax.ShapeDtypeStruct(*wholes[0]),
        jax.ShapeDtypeStruct(*wholes[2]),
        jax.ShapeDtypeStruct((geo.layers, rows, width), F32),
    ] + [jax.ShapeDtypeStruct(*saved[name]) for _ in range(geo.layers) for name in saved]
    found = pl.pallas_call(
        functools.partial(forward_kernel, geo, names_perm, list(saved)),
        out_shape=outs,
        in_specs=[IN_VMEM] * (len(sources) + len(perms) + 6),
        out_specs=[IN_VMEM] * 3 + [ANY] * (len(outs) - 3),
        scratch_shapes=[pltpu.VMEM(*whole) for whole in wholes]
        + bufs
        + units
        + [pltpu.VMEM(*saved[name]) for _ in range(geo.layers) for name in saved]
        + [
            pltpu.VMEM((geo.layers + 1, rows, width), F32),
            pltpu.VMEM(wholes[1][0][1:], F32),
            dma(n_keeps),
            dma(total),
            dma(total),
            dma(total, n_z),
            dma(total, n_z),
            dma(total),
            dma(total),
            dma(total, n_y),
            dma(total, n_y),
            dma(total, 2, n_y),
            dma(total, 2, n_y),
            dma(total, 2 * n_y),
            dma(total, 2 * n_y),
            dma(geo.layers),
            dma(geo.layers, 2),
            dma(geo.layers, 2, n_y),
            dma(geo.layers, 2, n_y),
        ]
        + [dma(geo.layers, 2, n_z, 2 * n_y)] * 4,
        compiler_params=pltpu.CompilerParams(
            collective_id=0, has_side_effects=True, vmem_limit_bytes=60 * 2**20
        ),
    )(*sources, *perms, act, mask, *spread_tables(geo))
    names = list(saved)
    kept = [dict(zip(names, found[6 + layer * len(names) :])) for layer in range(geo.layers)]
    return found[:6], kept


def pack_gradients(geo, grad_d, grad_f, tables, wide_v, stage_v):
    owner_d, rest_d, owner_f, rest_f = tables
    lines = geo.kind["v"][1]
    wide_v[...] = jnp.zeros_like(wide_v)
    pick_d = lax.broadcasted_iota(jnp.int32, (geo.slot, geo.width), 0) == rest_d[...]
    for line in range(geo.lines_d):
        parts = []
        for at in range(geo.per_row):
            row = line * geo.per_row + at
            if row < geo.layers * 10:
                parts.append(jnp.where(pick_d, grad_d[row : row + 1, :], 0.0))
            else:
                parts.append(jnp.zeros(pick_d.shape, F32))
        wide_v[pl.ds(line, geo.owners, stride=lines), :] = mm_nt(
            owner_d[...], jnp.concatenate(parts, 0).astype(BF)
        )
    pick_f = lax.broadcasted_iota(jnp.int32, (128, geo.width), 0)
    for row in range(geo.layers * 3):
        total = None
        for first in range(0, geo.wide_width, geo.width):
            lanes = slice(first, first + geo.width)
            part = jnp.where(pick_f == rest_f[:, lanes], grad_f[row : row + 1, lanes], 0.0).astype(BF)
            part = mm_nt(owner_f[:, lanes], part)
            total = part if total is None else total + part
        wide_v[pl.ds(geo.lines_d + row, geo.owners, stride=lines), :] = total
    stage_v[...] = wide_v[...].astype(BF).reshape(stage_v.shape)


class Ring:
    def __init__(self, sources, slots, sems):
        self.slots, self.size, self.used = slots, slots.shape[0], 0
        self.copies = [
            pltpu.make_async_copy(source, slots.at[at % self.size], sems.at[at % self.size])
            for at, source in enumerate(sources)
        ]
        for copy in self.copies[: self.size]:
            copy.start()

    def next(self):
        at = self.used
        self.used += 1
        if 0 < at and at - 1 + self.size < len(self.copies):
            self.copies[at - 1 + self.size].start()
        self.copies[at].wait()
        return self.slots[at % self.size]


SCATTER_SEMS = ("cs", "cr", "ms", "mr", "es", "er", "zs", "zr", "ls", "lr", "fx", "fy")
Z_SLOTS = 3
LINE_LAGS = (4, 3)
SCATTER_LAGS = (0, 1, 3, 5, 7)


def ring_slots(geo):
    return 3 if geo.roomy else 2


def backward_kernel(geo, names_perm, names, *refs):
    refs = list(refs)
    take = lambda number: [refs.pop(0) for _ in range(number)]
    by_kind = lambda kinds=geo.kinds: dict(zip(kinds, take(len(kinds))))
    saved_names, work_names = names
    layers, blocks, width = geo.layers, geo.blocks, geo.width
    perms = dict(zip(names_perm, take(len(names_perm))))
    cot_ref, vec_d, vec_f = take(3)
    tables = take(4)
    whole_a, whole_b, kept_x = take(3)
    kept = [dict(zip(saved_names, take(len(saved_names)))) for _ in range(layers)]
    for layer in range(layers):
        kept[layer]["x"] = kept_x.at[layer]
    back_ref, out_qkv, out_out, out_up, out_down, out_d, out_f = take(7)
    fields = dict(zip(saved_names, take(len(saved_names))))
    fields.update(zip(work_names, take(len(work_names))))
    stages, sums, mids, ends = [by_kind() for _ in range(4)]
    z_send, z_recv = [by_kind(geo.plain) for _ in range(2)]
    line_refs = take(1) if geo.lined else []
    x_ref, grad_d, grad_f, wide_v, slots = take(5)
    last_low, last_ffn = take(2) if geo.roomy else (None, None)
    sem_l, sem_w = take(2)
    sems = dict(zip(SCATTER_SEMS, take(len(SCATTER_SEMS))))
    fields.update(d_hidden=fields["sub_ffn"], x=x_ref, back=back_ref, grad_d=grad_d, grad_f=grad_f)
    place = Place(geo)

    def writer(chunk):
        name, at, lead, first = chunk
        rows_a, rows_b, lines = geo.rows_a, geo.rows_b, geo.lines_d

        def put_a(value):
            layer = at // geo.pairs
            for side in range(2):
                block = 2 * (at % geo.pairs) + side
                piece = value[side * rows_a : (side + 1) * rows_a]
                if block < 3:
                    out_qkv[layer, :, block * width : (block + 1) * width] = piece
                elif block == 3:
                    out_out[layer] = piece
                else:
                    out_up[layer, :, (block - 4) * width : (block - 3) * width] = piece

        def put_down(value):
            out_down[lead, :, first : first + value.shape[1]] = value[:rows_b]

        def put_v(value):
            out_d[...] = value[:lines]
            out_f[...] = value[lines : lines + layers * 3]

        return {"a": put_a, "v": put_v}.get(name, put_down)

    order, seen = [], {name: [] for name in geo.kinds}
    early = {layer: geo.down for layer in range(layers)}
    late = ("c", "d") if geo.roomy else ()
    early[0] = tuple(name for name in geo.down if name not in late)
    for layer in reversed(range(layers)):
        early[layer] = early[layer][::-1]
        order += [chunk_down(geo, layer, name) for name in early[layer]]
        order += [chunk_a(geo, layer, pair) for pair in list(range(2, geo.pairs)) + [1, 0]]
    order.append(("v", 0, 0, 0))
    order += [chunk_down(geo, 0, name) for name in late]
    moves, stage_of = [], []
    for number, chunk in enumerate(order):
        name = chunk[0]
        stage = stages[name].at[len(seen[name]) % stages[name].shape[0]]
        slots_z = z_send[name].shape[0] if name in z_send else 1
        z_slot = len(seen[name]) % slots_z
        before = seen[name][-slots_z] if len(seen[name]) >= slots_z else None
        move = (ScatterLine if name == "l" else Scatter)(
            place, number, chunk, stage, sums, mids, ends, perms, z_send, z_recv, z_slot, before,
            writer(chunk), sems,
        )
        if name == "l":
            move.c_line = len(seen[name])
            move.land(line_refs[0].at[move.c_line])
        seen[name].append(move)
        stage_of.append(stage)
        moves.append(move)
    for number, chunk in enumerate(order):
        if chunk[0] == "a" and chunk[1] >= geo.pairs:
            moves[number].heir = moves[[later[:2] for later in order].index(("a", chunk[1] - geo.pairs))]
    step, plan = [0], {}
    for number, chunk in enumerate(order):
        move = moves[number]
        acts = [move.start, move.pair, move.middle, move.last, move.finish]
        lags = list(SCATTER_LAGS)
        if chunk[0] == "l":
            hops = [lambda move=move, hop=hop: move.relay(hop) for hop in range(1, geo.n_z - 1)]
            acts[2:2] = hops + [move.collect]
            first, each = LINE_LAGS
            lags[2:] = [first + each * at for at in range(len(hops) + 1)]
            lags += [lags[-1] + 1, lags[-1] + 2, lags[-1] + 2]
        for lag, act in zip(lags, acts):
            plan.setdefault(number + lag, []).append((lag, act))

    def serve():
        for _, act in sorted(plan.get(step[0], []), key=lambda pair: pair[0]):
            act()
        step[0] += 1

    def stage_down(name, rows_ref, low_ref):
        unit = geo.kind[name][2]
        first, lanes = geo.lanes_of[name]
        for column in range(geo.n_dp // 2):
            rows = slice(column * 2 * unit, (column + 1) * 2 * unit)
            value = mm_tn(rows_ref[:, rows], low_ref[:, first : first + lanes])
            stage_of[step[0]][0, column // 2, column % 2] = value.astype(BF).reshape(2, unit, lanes)

    def stage_a(side, value):
        stage_of[step[0]][side] = value.astype(BF).reshape(geo.n_y, 2, 2, -1, width)

    loads = {}
    field_names = ["x"] + list(saved_names)

    def fetch(layer, *found):
        for name in found:
            loads[name] = pltpu.make_async_copy(
                kept[layer][name], fields[name], sem_l.at[field_names.index(name)]
            )
            loads[name].start()

    def ready(*found):
        for name in found:
            loads[name].wait()

    fetch(layers - 1, "sub_ffn")
    sources = []
    for layer in reversed(range(layers)):
        parts = geo.wide_width // width
        sources += [whole_b.at[layer, pl.ds(part * width, width)] for part in range(parts)]
        sources += [whole_a.at[layer * blocks + at] for at in list(range(4, blocks)) + [3, 0, 1, 2]]
    cot_copy = pltpu.make_async_copy(cot_ref, back_ref, sem_l.at[len(field_names)])
    cot_copy.start()
    place.greet()
    cot_copy.wait()
    loads["sub_ffn"].wait()
    ring = Ring(sources, slots, sem_w)
    fetch(
        layers - 1, "hidden", "normed_ffn", "after", "sub", "context", "prob", "qkv", "normed", "x"
    )
    for layer in reversed(range(layers)):
        one = Layer(
            fields, lambda at: ring.next(), lambda rows, lanes: ring.next(), vec_d, vec_f, layer,
            width // HEAD_DIM,
        )
        again = (lambda *found: fetch(layer - 1, *found)) if layer > 0 else (lambda *found: None)
        one.backward_start()
        if layer < layers - 1:
            ready("sub_ffn")
        for name in early[layer]:
            stage_down(name, one.sub_ffn, one.low)
            if step[0] == 0:
                place.meet()
            serve()
        if layer == 0 and late:
            last_low[...] = one.low[...]
            last_ffn[...] = one.sub_ffn[...]
        one.backward_down()
        ready("hidden")
        one.backward_gelu()
        again("hidden")
        ready("normed_ffn")
        for pair in range(2, geo.pairs):
            stage_a(0, one.grad_up(2 * pair - 4))
            stage_a(1, one.grad_up(2 * pair - 3))
            serve()
        again("normed_ffn")
        ready("after")
        one.backward_up()
        again("after", "sub_ffn")
        ready("sub", "context")
        stage_a(1, one.grad_out())
        one.backward_out()
        again("sub", "context")
        ready("prob", "qkv")
        one.backward_attention()
        again("prob", "qkv")
        ready("normed")
        stage_a(0, one.grad_qkv(2))
        serve()
        stage_a(0, one.grad_qkv(0))
        stage_a(1, one.grad_qkv(1))
        serve()
        again("normed")
        ready("x")
        one.backward_qkv()
        again("x")
    pack_gradients(geo, grad_d, grad_f, tables, wide_v, stage_of[step[0]])
    serve()
    for name in late:
        stage_down(name, last_ffn, last_low)
        serve()
    while step[0] <= max(plan):
        serve()
    for move in moves:
        move.drain()


def run_backward(geo, cot, vec_d, vec_f, whole_a, whole_b, kept_x, kept):
    rows, width = cot.shape
    layers, n_y, n_z = geo.layers, geo.n_y, geo.n_z
    heads = width // HEAD_DIM
    saved, work = saved_shapes(rows, width, geo.wide_width, heads), work_shapes(rows, width, geo.wide_width)
    names = (list(saved), list(work))
    names_perm = [name for name in geo.plain if geo.permuted(name)]
    perms = [jnp.asarray(geo.permutation(name).T, BF) for name in names_perm]
    total = sum(geo.number.values())
    groups = [[] for _ in range(6)]
    for name in geo.kinds:
        k, sent, unit, lanes = geo.kind[name]
        number = geo.number[name]
        mid_steps = max(n_y - 1, (n_y + 1) // 2)
        groups[0].append(pltpu.VMEM((2 if name == "a" else 1, k, n_y, 2, 2, unit, lanes), BF))
        groups[1].append(pltpu.VMEM((number, k, n_y, 2, unit, lanes), BF))
        landing = geo.pairs if name == "a" else number
        unit = sent if name == "l" else unit
        groups[2].append(pltpu.VMEM((landing, mid_steps, k, 2, unit, lanes), BF))
        groups[3].append(pltpu.VMEM((number, mid_steps, k, unit, lanes), BF))
        if name == "l":
            continue
        groups[4].append(pltpu.VMEM((min(number, Z_SLOTS), n_z, sent, lanes), BF))
        groups[5].append(pltpu.VMEM((number, n_z, sent, lanes), BF))
    scratch = [pltpu.VMEM(*saved[name]) for name in saved] + [pltpu.VMEM(*work[name]) for name in work]
    scratch += sum(groups, [])
    if geo.lined:
        _, sent, _, lanes = geo.kind["l"]
        scratch.append(pltpu.VMEM((layers, 2, n_z, n_y, 2, sent, lanes), BF))
    scratch += [
        pltpu.VMEM((rows, width), F32),
        pltpu.VMEM((layers * 10, width), F32),
        pltpu.VMEM((layers * 3, geo.wide_width), F32),
        pltpu.VMEM((geo.owners * geo.kind["v"][1], 128), F32),
        pltpu.VMEM((ring_slots(geo), width, width), BF),
    ]
    if geo.roomy:
        scratch += [pltpu.VMEM((rows, width), BF), pltpu.VMEM((rows, geo.wide_width), BF)]
    scratch += [
        dma(2 + len(saved)),
        dma(ring_slots(geo)),
        dma(total),
        dma(total),
        dma(total, 2, n_y),
        dma(total, 2, n_y),
        dma(total, 2, n_y),
        dma(total, 2, n_y),
        dma(total, n_z),
        dma(total, n_z),
        dma(layers, 2, n_z),
        dma(layers, 2, n_z),
        pltpu.SemaphoreType.REGULAR((total,)),
        pltpu.SemaphoreType.REGULAR((total, n_y)),
    ]
    return pl.pallas_call(
        functools.partial(backward_kernel, geo, names_perm, names),
        out_shape=[
            jax.ShapeDtypeStruct((rows, width), F32),
            jax.ShapeDtypeStruct((layers, geo.rows_a, 3 * width), F32),
            jax.ShapeDtypeStruct((layers, geo.rows_a, width), F32),
            jax.ShapeDtypeStruct((layers, geo.rows_a, geo.wide_width), F32),
            jax.ShapeDtypeStruct((layers, geo.rows_b, width), F32),
            jax.ShapeDtypeStruct((geo.lines_d, 128), F32),
            jax.ShapeDtypeStruct((layers * 3, 128), F32),
        ],
        in_specs=[IN_VMEM] * len(perms) + [ANY] + [IN_VMEM] * 6 + [ANY] * (3 + layers * len(saved)),
        out_specs=[IN_VMEM] * 7,
        scratch_shapes=scratch,
        compiler_params=pltpu.CompilerParams(
            collective_id=1, has_side_effects=True, vmem_limit_bytes=63 * 2**20
        ),
    )(
        *perms, cot, vec_d, vec_f, *spread_tables(geo), whole_a, whole_b, kept_x,
        *[kept[layer][name] for layer in range(layers) for name in saved],
    )


def pack_kernel(geo, *refs):
    act_short, act_long, len_short, len_long, w_qkv, w_out, w_up, w_down = refs[:8]
    norms_d, gains_ff, shifts_ff, cot_short, cot_long = refs[8:13]
    sources = dict(zip(geo.kinds, refs[13:]))
    act, mask, cot, lines = refs[13 + len(geo.kinds) :]
    width, rows_a, rows_b = geo.width, geo.rows_a, geo.rows_b

    def block(layer, at):
        if at == 3:
            return wide(w_out[layer])
        first = at if at < 3 else at - 4
        return wide((w_qkv if at < 3 else w_up)[layer, :, first * width : (first + 1) * width])

    def filled(pieces, rows):
        have = sum(piece.shape[0] for piece in pieces)
        if have < rows:
            pieces = pieces + [jnp.zeros((rows - have, pieces[0].shape[1]), F32)]
        return (jnp.concatenate(pieces, 0) if len(pieces) > 1 else pieces[0]).astype(BF)

    for layer in range(geo.layers):
        for pair in range(geo.pairs):
            pieces = [block(layer, 2 * pair), block(layer, 2 * pair + 1)]
            sources["a"][layer * geo.pairs + pair] = filled(pieces, geo.kind["a"][1])
        for name in geo.down:
            first, lanes = geo.lanes_of[name]
            piece = w_down[layer, :, first : first + lanes]
            if rows_b != geo.kind[name][1]:
                piece = filled([wide(piece)], geo.kind[name][1])
            sources[name][layer] = piece
    lines[...] = jnp.zeros_like(lines)
    gains_wide = wide(gains_ff[...])
    for layer in range(geo.layers):
        norms, shifts_wide = wide(norms_d[layer]), wide(shifts_ff[layer])
        for at in range(10):
            line, lane = divmod(layer * 10 + at, geo.per_row)
            lines[line : line + 1, lane * geo.slot : lane * geo.slot + rows_a] = norms[at : at + 1]
        for at in range(3):
            line = geo.lines_d + layer * 3 + at
            lines[line : line + 1, :rows_b] = gains_wide[layer : layer + 1] if at == 0 else shifts_wide[at - 1 : at]
    sources["v"][0] = lines[...].astype(BF)
    short = act_short.shape[0]
    act[:short] = act_short[...]
    act[short:] = act_long[...]
    rows = act.shape[0]

    def valid(shape, dim):
        at = lax.broadcasted_iota(jnp.int32, shape, dim)
        return jnp.where(jnp.where(at < short, at - len_short[0], at - short - len_long[0]) < 0, 1.0, 0.0)

    def bucket(dim):
        return jnp.where(lax.broadcasted_iota(jnp.int32, (rows, rows), dim) < short, 0, 1)

    mask[...] = jnp.where(bucket(0) == bucket(1), valid((rows, rows), 1), 0.0)
    keep = valid((rows, width), 0)
    cot[:short] = wide(cot_short[...]) * keep[:short]
    cot[short:] = wide(cot_long[...]) * keep[short:]


def run_pack(geo, args):
    rows = args[0].shape[0] + args[1].shape[0]
    shapes = []
    for name in geo.kinds:
        _, sent, _, lanes = geo.kind[name]
        shapes.append(jax.ShapeDtypeStruct((geo.number[name], sent, lanes), BF))
    shapes += [
        jax.ShapeDtypeStruct((rows, geo.width), BF),
        jax.ShapeDtypeStruct((rows, rows), F32),
        jax.ShapeDtypeStruct((rows, geo.width), F32),
    ]
    in_smem = pl.BlockSpec(memory_space=pltpu.SMEM)
    return pl.pallas_call(
        functools.partial(pack_kernel, geo),
        out_shape=shapes,
        in_specs=[IN_VMEM] * 2 + [in_smem] * 2 + [IN_VMEM] * 9,
        out_specs=[IN_VMEM] * len(shapes),
        scratch_shapes=[pltpu.VMEM((geo.kind["v"][1], 128), F32)],
        compiler_params=pltpu.CompilerParams(vmem_limit_bytes=63 * 2**20),
    )(*args[:8], jnp.concatenate(args[8:10], 1), *args[10:])


def unpack_kernel(geo, *refs):
    out, back, g_qkv, g_out, g_up, g_down, lines_d, lines_f = refs[:8]
    out_short, out_long, back_short, back_long, t_qkv, t_out, t_up, t_down = refs[8:16]
    t_gains_d, t_shifts_d, t_gains_ff, t_shifts_ff = refs[16:]
    short = out_short.shape[0]
    out_short[...] = out[:short]
    out_long[...] = out[short:]
    back_short[...] = back[:short]
    back_long[...] = back[short:]
    for source, target in ((g_qkv, t_qkv), (g_out, t_out), (g_up, t_up), (g_down, t_down)):
        target[...] = source[...]
    for layer in range(geo.layers):
        for at in range(10):
            line, lane = divmod(layer * 10 + at, geo.per_row)
            value = lines_d[line : line + 1, lane * geo.slot : lane * geo.slot + geo.rows_a]
            if at < 3:
                t_gains_d[layer, at : at + 1, :] = value
            else:
                t_shifts_d[layer, at - 3 : at - 2, :] = value
        for at in range(3):
            value = lines_f[layer * 3 + at : layer * 3 + at + 1, : geo.rows_b]
            if at == 0:
                t_gains_ff[layer : layer + 1, :] = value
            else:
                t_shifts_ff[layer, at - 1 : at, :] = value


def run_unpack(geo, found, args):
    like = lambda index, dtype: jax.ShapeDtypeStruct(args[index].shape, dtype)
    shapes = [like(0, BF), like(1, BF), like(0, F32), like(1, F32)]
    shapes += [like(index, F32) for index in range(4, 12)]
    return pl.pallas_call(
        functools.partial(unpack_kernel, geo),
        out_shape=shapes,
        in_specs=[IN_VMEM] * len(found),
        out_specs=[IN_VMEM] * len(shapes),
        compiler_params=pltpu.CompilerParams(vmem_limit_bytes=63 * 2**20),
    )(*found)


def on_device(*args):
    n_dp, n_z = lax.axis_size("dp"), lax.axis_size("fsdp")
    geo = Geometry(n_dp, n_z, args[4].shape, args[6].shape, args[7].shape)
    *sources, act, mask, cot = run_pack(geo, args)
    found, kept = run_forward(geo, sources, act, mask)
    out, vec_d, vec_f, whole_a, whole_b, kept_x = found
    grads = run_backward(geo, cot, vec_d, vec_f, whole_a, whole_b, kept_x, kept)
    return tuple(run_unpack(geo, (out,) + tuple(grads), args))


def solution(mesh):
    return jax.shard_map(
        on_device,
        mesh=mesh,
        in_specs=(
            P(("dp", "fsdp"), None),
            P(("dp", "fsdp"), None),
            P(("dp", "fsdp")),
            P(("dp", "fsdp")),
            P(None, ("dp", "fsdp"), None),
            P(None, ("dp", "fsdp"), None),
            P(None, ("dp", "fsdp"), None),
            P(None, ("dp", "fsdp"), None),
            P(None, None, ("dp", "fsdp")),
            P(None, None, ("dp", "fsdp")),
            P(None, ("dp", "fsdp")),
            P(None, None, ("dp", "fsdp")),
            P(("dp", "fsdp"), None),
            P(("dp", "fsdp"), None),
        ),
        out_specs=(
            P(("dp", "fsdp"), None),
            P(("dp", "fsdp"), None),
            P(("dp", "fsdp"), None),
            P(("dp", "fsdp"), None),
            P(None, ("dp", "fsdp"), None),
            P(None, ("dp", "fsdp"), None),
            P(None, ("dp", "fsdp"), None),
            P(None, ("dp", "fsdp"), None),
            P(None, None, ("dp", "fsdp")),
            P(None, None, ("dp", "fsdp")),
            P(None, ("dp", "fsdp")),
            P(None, None, ("dp", "fsdp")),
        ),
        check_vma=False,
    )
```

```python
import functools

import jax
import jax.numpy as jnp
import numpy as np
from jax import lax
from jax.experimental import pallas as pl
from jax.experimental.pallas import tpu as pltpu
from jax.sharding import PartitionSpec as P

HEAD_DIM = 64

epsilon = 1e-05


BF = jnp.bfloat16
F32 = jnp.float32
MESH = pl.DeviceIdType.MESH


def round16(count):
    return (count + 15) // 16 * 16


class Geometry:
    def __init__(self, n_dp, n_z, w_qkv, w_up, w_down):
        self.n_dp, self.n_z, self.n_y = n_dp, n_z, n_dp // 4
        self.layers = w_qkv[0]
        self.width = w_qkv[2] // 3
        self.rows_a, self.rows_b = w_qkv[1], w_down[1]
        self.blocks = 4 + w_up[2] // self.width
        self.pairs = self.blocks // 2
        half = self.width // 2
        self.lined = self.rows_b % 16 == 0
        self.roomy = self.n_y <= 2
        self.first_down = "l" if self.lined else "b"
        self.lanes_of = {self.first_down: (0, half), "c": (half, half - 128), "d": (2 * half - 128, 128)}
        self.down = tuple(self.lanes_of)
        self.kinds = ("a", "v") + self.down
        self.plain = tuple(name for name in self.kinds if name != "l")
        self.owners = n_dp * n_z
        self.wide_width = w_up[2]
        self.slot = 8
        while self.slot < self.rows_a:
            self.slot *= 2
        self.per_row = 128 // self.slot
        self.lines_d = -(-self.layers * 10 // self.per_row)
        lines = round16(self.lines_d + self.layers * 3)
        self.kind = {
            "a": (2, round16(2 * self.rows_a), self.rows_a * n_z, self.width),
            "v": (1, lines, lines * n_z, 128),
        }
        self.real = {"a": self.rows_a, "v": self.kind["v"][1]}
        self.number = {"a": self.layers * self.pairs, "v": 1}
        for name, (_, lanes) in self.lanes_of.items():
            self.kind[name] = (1, round16(self.rows_b), self.rows_b * n_z, lanes)
            self.real[name] = self.rows_b
            self.number[name] = self.layers

    def permuted(self, name):
        k, sent, unit, _ = self.kind[name]
        return k * unit != sent * self.n_z or k > 1

    def permutation(self, name):
        k, sent, unit, _ = self.kind[name]
        real = self.real[name]
        table = np.zeros((k * unit, self.n_z * sent), np.float32)
        for block in range(k):
            for z in range(self.n_z):
                for row in range(real):
                    table[block * unit + z * real + row, z * sent + block * real + row] = 1
        return table

    def whole_shape(self, name):
        _, _, unit, lanes = self.kind[name]
        lead = {"a": self.layers * self.blocks, "v": 1}.get(name, self.layers)
        return (lead, self.n_dp * unit, lanes if name == "v" else self.width)


class Place:
    def __init__(self, geo):
        self.geo = geo
        self.d, self.z = lax.axis_index("dp"), lax.axis_index("fsdp")
        self.core = lax.rem(self.d, 2)
        self.x = lax.rem(self.d // 2, 2)
        self.y = self.d // 4

    def y_off(self, step):
        return lax.rem(self.y + step + self.geo.n_y, self.geo.n_y)

    def z_off(self, step):
        return lax.rem(self.z + step + self.geo.n_z, self.geo.n_z)

    def dev_core(self):
        return (self.d + 1 - 2 * self.core, self.z)

    def dev_x(self):
        return (self.d + 2 - 4 * self.x, self.z)

    def dev_y(self, step):
        return (self.y_off(step) * 4 + self.x * 2 + self.core, self.z)

    def dev_z(self, step):
        return (self.d, self.z_off(step))

    def greet(self):
        barrier = pltpu.get_barrier_semaphore()
        partners = [self.dev_core(), self.dev_x()]
        partners += [self.dev_y(step) for step in range(1, self.geo.n_y)]
        partners += [self.dev_z(step) for step in range(1, self.geo.n_z)]
        for partner in partners:
            pl.semaphore_signal(barrier, inc=1, device_id=partner, device_id_type=MESH)
        self.awaited = len(partners)

    def meet(self):
        pl.semaphore_wait(pltpu.get_barrier_semaphore(), self.awaited)


def remote(src, dst, send, recv, device):
    return pltpu.make_async_remote_copy(
        src_ref=src, dst_ref=dst, send_sem=send, recv_sem=recv, device_id=device, device_id_type=MESH
    )


def chunk_a(geo, layer, pair):
    return ("a", layer * geo.pairs + pair, layer * geo.blocks + 2 * pair, 0)


def chunk_down(geo, layer, name):
    return (name, layer, layer, geo.lanes_of[name][0])


def rows_of(whole, name, lead, first, k, unit, lanes):
    def at(y, x, core):
        rows = pl.ds(pl.multiple_of((y * 4 + x * 2 + core) * unit, 16), unit)
        return whole.at[pl.ds(lead, k), rows, slice(None) if name in ("a", "v") else pl.ds(first, lanes)]

    return at


def ways_of(number, k):
    if k == 1:
        return [(slice(0, 1), number % 2 == 0)]
    return [(slice(0, 1), True), (slice(1, k), False)]


class Gather:
    def __init__(self, place, number, chunk, sources, bufs, units, perms, wholes, sems):
        self.p, self.c = place, number
        name, at, lead, first = chunk
        self.ways = ways_of(number, place.geo.kind[name][0])
        k, self.sent, unit, lanes = place.geo.kind[name]
        self.source = sources[name].at[at]
        self.buf = bufs[name].at[at]
        self.perm = perms.get(name)
        self.unit_buf = units[name].at[at] if self.perm is not None else None
        self.unit = self.unit_buf if self.perm is not None else bufs[name].at[pl.ds(at, 1)]
        self.to = rows_of(wholes[name], name, lead, first, k, unit, lanes)
        self.sems = sems
        self.pending = []

    def slot(self, z):
        return self.buf.at[pl.ds(pl.multiple_of(z * self.sent, 16), self.sent)]

    def send(self, src, dst, send, recv, device):
        copy = remote(src, dst, send, recv, device)
        copy.start()
        self.pending.append(copy)

    def arrived(self, dst, send, recv, device):
        remote(dst, dst, send, recv, device).wait_recv()

    def start_z(self):
        p, s, c = self.p, self.sems, self.c
        self.local_z = pltpu.make_async_copy(self.source, self.slot(p.z), s["lz"].at[c])
        self.local_z.start()
        for step in range(1, p.geo.n_z):
            self.send(self.source, self.slot(p.z), s["zs"].at[c, step], s["zr"].at[c, step], p.dev_z(step))

    def own(self):
        p, s, c = self.p, self.sems, self.c
        self.local_z.wait()
        for step in range(1, p.geo.n_z):
            self.arrived(self.slot(p.z_off(-step)), s["zs"].at[c, step], s["zr"].at[c, step], p.dev_z(step))
        if self.perm is not None:
            k, unit, lanes = self.unit_buf.shape
            mixed = jnp.dot(self.perm[...], self.buf[...], preferred_element_type=F32)
            self.unit_buf[...] = mixed.astype(BF).reshape(k, unit, lanes)
        here = self.to(p.y, p.x, p.core)
        self.local = pltpu.make_async_copy(self.unit, here, s["lo"].at[c])
        self.send(self.unit, here, s["xs"].at[c], s["xr"].at[c], p.dev_x())
        for step in range(1, p.geo.n_y):
            self.send(self.unit, here, s["ys"].at[c, step], s["yr"].at[c, step], p.dev_y(step))
        self.send(self.unit, here, s["cs"].at[c, 0], s["cr"].at[c, 0], p.dev_core())
        self.local.start()

    def forward(self):
        p, s, c = self.p, self.sems, self.c
        n_y = p.geo.n_y
        from_x = self.to(p.y, 1 - p.x, p.core)
        self.arrived(from_x, s["xs"].at[c], s["xr"].at[c], p.dev_x())
        for way, (blocks, by_x) in enumerate(self.ways):
            for step in range(1, n_y) if by_x else ():
                at = (c, way, step)
                rows = from_x.at[blocks]
                self.send(rows, rows, s["ds"].at[at], s["dr"].at[at], p.dev_y(step))
        self.send(from_x, from_x, s["cs"].at[c, 1], s["cr"].at[c, 1], p.dev_core())
        for step in range(1, n_y):
            from_y = self.to(p.y_off(-step), p.x, p.core)
            self.arrived(from_y, s["ys"].at[c, step], s["yr"].at[c, step], p.dev_y(step))
            for way, (blocks, by_x) in enumerate(self.ways):
                if not by_x:
                    at = (c, way, step)
                    rows = from_y.at[blocks]
                    self.send(rows, rows, s["ds"].at[at], s["dr"].at[at], p.dev_x())
            self.send(from_y, from_y, s["cs"].at[c, 2 * step], s["cr"].at[c, 2 * step], p.dev_core())

    def corner(self):
        p, s, c = self.p, self.sems, self.c
        for step in range(1, p.geo.n_y):
            far = self.to(p.y_off(-step), 1 - p.x, p.core)
            for way, (blocks, _) in enumerate(self.ways):
                at = (c, way, step)
                self.arrived(far.at[blocks], s["ds"].at[at], s["dr"].at[at], p.dev_x())
            self.send(far, far, s["cs"].at[c, 2 * step + 1], s["cr"].at[c, 2 * step + 1], p.dev_core())

    def arrive(self):
        p, s, c = self.p, self.sems, self.c
        for step in range(p.geo.n_y):
            for flip in range(2):
                x = p.x if flip == 0 else 1 - p.x
                got = self.to(p.y_off(-step), x, 1 - p.core)
                at = 2 * step + flip
                self.arrived(got, s["cs"].at[c, at], s["cr"].at[c, at], p.dev_core())
        self.local.wait()

    def drain(self):
        for copy in self.pending:
            copy.wait_send()


def when(condition, act):
    pl.when(condition)(act)


def on_line(place, way, step):
    at = place.z - step if way == 0 else place.z + step
    return (at >= 0) & (at < place.geo.n_z), at


class GatherLine:
    def __init__(self, place, number, chunk, sources, wholes, sems):
        self.p, self.c = place, number
        _, at, lead, first = chunk
        _, sent, _, lanes = place.geo.kind["l"]
        self.source = sources["l"].at[at]
        self.half_a = number % 2 == 0
        whole = wholes["l"]

        def piece(y, x, core, z):
            device = (y * 4 + x * 2 + core) * place.geo.n_z + z
            rows = pl.ds(pl.multiple_of(device * sent, 16), sent)
            return whole.at[lead, rows, pl.ds(first, lanes)]

        self.piece = piece
        self.sems = sems
        self.pending, self.line_pending = [], []

    def send(self, src, dst, send, recv, device):
        copy = remote(src, dst, send, recv, device)
        copy.start()
        self.pending.append(copy)

    def arrived(self, dst, send, recv, device):
        remote(dst, dst, send, recv, device).wait_recv()

    def from_column(self, at, z, core):
        p = self.p
        return self.piece(p.y_off(-(at // 2)), p.x if at % 2 == 0 else 1 - p.x, core, z)

    def line_send(self, column, hop):
        p, s, c = self.p, self.sems, self.c
        for way in range(2):
            valid, z = on_line(p, way, hop - 1)
            further, target = on_line(p, 1 - way, 1)

            def copy(z=z, target=target, way=way):
                rows = self.from_column(column, z, p.core)
                at = (c, way, hop, column)
                return remote(rows, rows, s["gs"].at[at], s["gr"].at[at], (p.d, target))

            when(valid & further, lambda copy=copy: copy().start())
            self.line_pending.append((valid & further, copy))

    def to_core(self, column, z, at):
        s = self.sems
        rows = self.from_column(column, z, self.p.core)
        return remote(rows, rows, s["hs"].at[at], s["hr"].at[at], self.p.dev_core())

    def start(self):
        p, s, c = self.p, self.sems, self.c
        here = self.piece(p.y, p.x, p.core, p.z)
        self.local = pltpu.make_async_copy(self.source, here, s["gl"].at[c])
        self.send(self.source, here, s["gx"].at[c, 0], s["gx"].at[c, 1], p.dev_x())
        for step in range(1, p.geo.n_y):
            self.send(self.source, here, s["gy"].at[c, 0, step], s["gy"].at[c, 1, step], p.dev_y(step))
        self.local.start()
        at = (c, 0, 0, 0)
        self.send(self.source, here, s["hs"].at[at], s["hr"].at[at], p.dev_core())

    def forward(self):
        p, s, c = self.p, self.sems, self.c
        n_y = p.geo.n_y
        self.local.wait()
        rows = self.from_column(1, p.z, p.core)
        self.arrived(rows, s["gx"].at[c, 0], s["gx"].at[c, 1], p.dev_x())
        if self.half_a:
            for step in range(1, n_y):
                self.send(rows, rows, s["gd"].at[c, 0, step], s["gd"].at[c, 1, step], p.dev_y(step))
        self.keep_core(1)
        for step in range(1, n_y):
            rows = self.from_column(2 * step, p.z, p.core)
            self.arrived(rows, s["gy"].at[c, 0, step], s["gy"].at[c, 1, step], p.dev_y(step))
            if not self.half_a:
                self.send(rows, rows, s["gd"].at[c, 0, step], s["gd"].at[c, 1, step], p.dev_x())
            self.keep_core(2 * step)

    def keep_core(self, column):
        copy = self.to_core(column, self.p.z, (self.c, 0, 0, column))
        copy.start()
        self.pending.append(copy)

    def corner(self):
        p, s, c = self.p, self.sems, self.c
        for step in range(1, p.geo.n_y):
            rows = self.from_column(2 * step + 1, p.z, p.core)
            self.arrived(rows, s["gd"].at[c, 0, step], s["gd"].at[c, 1, step], p.dev_x())
            self.keep_core(2 * step + 1)

    def relay(self, hop, half):
        p, s, c = self.p, self.sems, self.c
        n_y = p.geo.n_y
        for column in range(half * n_y, (half + 1) * n_y):
            for way in range(2) if hop > 0 else ():
                valid, z = on_line(p, way, hop)
                at = (c, way, hop, column)

                def act(z=z, at=at):
                    rows = self.from_column(column, z, p.core)
                    remote(rows, rows, s["gs"].at[at], s["gr"].at[at], p.dev_x()).wait_recv()
                    self.to_core(column, z, at).start()

                when(valid, act)
                self.line_pending.append(
                    (valid, lambda column=column, z=z, at=at: self.to_core(column, z, at))
                )
            if hop < p.geo.n_z - 1:
                self.line_send(column, hop + 1)

    def arrive(self):
        p, s, c = self.p, self.sems, self.c
        for column in range(2 * p.geo.n_y):
            rows = self.from_column(column, p.z, 1 - p.core)
            at = (c, 0, 0, column)
            self.arrived(rows, s["hs"].at[at], s["hr"].at[at], p.dev_core())
            for hop in range(1, p.geo.n_z):
                for way in range(2):
                    valid, z = on_line(p, way, hop)
                    at = (c, way, hop, column)

                    def act(z=z, at=at):
                        rows = self.from_column(column, z, 1 - p.core)
                        self.arrived(rows, s["hs"].at[at], s["hr"].at[at], p.dev_core())

                    when(valid, act)

    def drain(self):
        for copy in self.pending:
            copy.wait_send()
        for valid, copy in self.line_pending:
            when(valid, lambda copy=copy: copy().wait_send())


def run_pipeline(stages, count, extra):
    last = max(lag for lag, _ in stages)
    first = min(lag for lag, _ in stages)
    for step in range(first, count + last):
        ahead = [stage for stage in stages if stage[0] < 0]
        ahead += stages[1:4]
        for lag, act in ahead + [(None, act) for act in extra.get(step, ())] + stages[len(ahead) :]:
            if lag is None:
                act()
            elif 0 <= step - lag < count:
                act(step - lag)


def dma(*shape):
    return pltpu.SemaphoreType.DMA(shape)


ANY = pl.BlockSpec(memory_space=pl.ANY)
IN_VMEM = pl.BlockSpec(memory_space=pltpu.VMEM)


def wide(values):
    return values.astype(F32)


class Scatter:
    def __init__(self, place, number, chunk, stage, sums, mids, ends, perms, z_send, z_recv, z_slot, before, put, sems):
        self.p, self.c = place, number
        name, at, _, _ = chunk
        self.k, self.sent, self.rows, self.lanes = place.geo.kind[name]
        self.ways = ways_of(number, self.k)
        self.part = slice(None)
        self.stage = stage
        self.sum = sums[name].at[at]
        shared, per_layer = name == "a", place.geo.pairs
        self.mid = mids[name].at[at % per_layer if shared else at]
        self.hands_on = shared and at >= per_layer
        self.takes_over = shared and at < place.geo.number[name] - per_layer
        self.heir = None
        self.end = ends[name].at[at]
        self.perm = perms.get(name)
        if name in z_send:
            self.z_send, self.z_recv = z_send[name].at[z_slot], z_recv[name].at[at]
        self.before, self.z_moves = before, []
        self.put = put
        self.sems = sems
        self.pending = []

    def send(self, src, dst, send, recv, device):
        copy = remote(src, dst, send, recv, device)
        copy.start()
        self.pending.append(copy)

    def arrived(self, dst, send, recv, device):
        remote(dst, dst, send, recv, device).wait_recv()

    def start(self):
        p, s, c = self.p, self.sems, self.c
        give = self.stage.at[:, :, :, 1 - p.core]
        self.given = remote(give, self.sum, s["cs"].at[c], s["cr"].at[c], p.dev_core())
        self.given.start()

    def pair(self):
        p, s, c = self.p, self.sems, self.c
        n_y = p.geo.n_y
        self.arrived(self.sum, s["cs"].at[c], s["cr"].at[c], p.dev_core())

        @pl.loop(0, self.k * n_y * 2)
        def _(at):
            where = (at // (2 * n_y), lax.rem(at // 2, n_y), lax.rem(at, 2))
            self.sum[where] = (wide(self.sum[where]) + wide(self.stage[where + (p.core,)])).astype(BF)

        self.given.wait_send()
        self.send_middle()

    def send_middle(self):
        p, s, c = self.p, self.sems, self.c
        n_y = p.geo.n_y
        for way, (blocks, by_x) in enumerate(self.ways):
            if self.takes_over:
                for step in range(1, n_y) if by_x else ():
                    pl.semaphore_wait(s["fy"].at[c, step], 1)
                if not by_x:
                    pl.semaphore_wait(s["fx"].at[c], 1)
            if by_x:
                for step in range(1, n_y):
                    at = (c, way, step)
                    self.send(
                        self.sum.at[blocks, p.y_off(step), :, self.part], self.mid.at[step - 1, blocks],
                        s["ms"].at[at], s["mr"].at[at], p.dev_y(step),
                    )
            else:
                for y in range(n_y):
                    at = (c, way, y)
                    self.send(
                        self.sum.at[blocks, y, 1 - p.x, self.part], self.mid.at[y // 2, blocks, y % 2],
                        s["ms"].at[at], s["mr"].at[at], p.dev_x(),
                    )

    def middle(self):
        for way, (blocks, by_x) in enumerate(self.ways):
            (self.middle_x if by_x else self.middle_y)(way, blocks)

    def middle_x(self, way, blocks):
        p, s, c = self.p, self.sems, self.c
        n_y, first = p.geo.n_y, blocks.start
        for step in range(1, n_y):
            at = (c, way, step)
            self.arrived(self.mid.at[step - 1, blocks], s["ms"].at[at], s["mr"].at[at], p.dev_y(step))

        @pl.loop(0, (blocks.stop - first) * 2)
        def _(at):
            where = (first + at // 2, p.y, lax.rem(at, 2), self.part)
            value = wide(self.sum[where])
            for step in range(1, n_y):
                value = value + wide(self.mid[step - 1, first + at // 2, lax.rem(at, 2)])
            self.sum[where] = value.astype(BF)

        if self.hands_on:
            for step in range(1, n_y):
                pl.semaphore_signal(
                    s["fy"].at[self.heir.c, step], inc=1, device_id=p.dev_y(-step), device_id_type=MESH
                )
        at = (c, way, 0)
        self.send(
            self.sum.at[blocks, p.y, 1 - p.x, self.part], self.end.at[0, blocks],
            s["es"].at[at], s["er"].at[at], p.dev_x(),
        )

    def middle_y(self, way, blocks):
        p, s, c = self.p, self.sems, self.c
        n_y, first = p.geo.n_y, blocks.start
        for y in range(n_y):
            at = (c, way, y)
            self.arrived(self.mid.at[y // 2, blocks, y % 2], s["ms"].at[at], s["mr"].at[at], p.dev_x())

        @pl.loop(0, (blocks.stop - first) * n_y)
        def _(at):
            y = lax.rem(at, n_y)
            where = (first + at // n_y, y, p.x, self.part)
            value = wide(self.sum[where]) + wide(self.mid[y // 2, first + at // n_y, lax.rem(y, 2)])
            self.sum[where] = value.astype(BF)

        if self.hands_on:
            pl.semaphore_signal(s["fx"].at[self.heir.c], inc=1, device_id=p.dev_x(), device_id_type=MESH)
        for step in range(1, n_y):
            at = (c, way, step)
            self.send(
                self.sum.at[blocks, p.y_off(step), p.x, self.part], self.end.at[step - 1, blocks],
                s["es"].at[at], s["er"].at[at], p.dev_y(step),
            )

    def column_sum(self):
        p, s, c = self.p, self.sems, self.c
        n_y = p.geo.n_y
        found = []
        for way, (blocks, by_x) in enumerate(self.ways):
            value = wide(self.sum[blocks, p.y, p.x, self.part])
            for step in (0,) if by_x else range(1, n_y):
                at = (c, way, step)
                got = self.end.at[0 if by_x else step - 1, blocks]
                self.arrived(got, s["es"].at[at], s["er"].at[at], p.dev_x())
                value = value + wide(got[...])
            found.append(value)
        return found[0] if len(found) == 1 else jnp.concatenate(found, 0)

    def last(self):
        p, s, c = self.p, self.sems, self.c
        n_z = p.geo.n_z
        value = self.column_sum().astype(BF).reshape(self.k * self.rows, self.lanes)
        if self.perm is not None:
            value = jnp.dot(self.perm[...], value, preferred_element_type=F32).astype(BF)
        if self.before is not None:
            self.before.left()
        self.z_send[...] = value.reshape(n_z, self.sent, self.lanes)
        for step in range(1, n_z):
            copy = remote(
                self.z_send.at[p.z_off(step)], self.z_recv.at[step],
                s["zs"].at[c, step], s["zr"].at[c, step], p.dev_z(step),
            )
            copy.start()
            self.z_moves.append(copy)

    def finish(self):
        p, s, c = self.p, self.sems, self.c
        value = wide(self.z_send[p.z])
        for step in range(1, p.geo.n_z):
            self.arrived(self.z_recv.at[step], s["zs"].at[c, step], s["zr"].at[c, step], p.dev_z(step))
            value = value + wide(self.z_recv[step])
        self.put(value)

    def left(self):
        while self.z_moves:
            self.z_moves.pop().wait_send()

    def drain(self):
        self.left()
        for copy in self.pending:
            copy.wait_send()


class ScatterLine(Scatter):
    def land(self, line):
        self.line = line
        p = self.p
        self.unit = self.rows // p.geo.n_z
        self.part = pl.ds(pl.multiple_of(p.z * self.unit, 16), self.unit)
        self.line_pending = []
        return self

    def slice_of(self, target):
        return pl.ds(target * self.unit, self.unit)

    def line_copy(self, src, way, target, further):
        s = self.sems
        at = (self.c_line, way, target)
        return remote(src, self.line.at[way, target], s["ls"].at[at], s["lr"].at[at], (self.p.d, further))

    def send_middle(self):
        p, last = self.p, self.p.geo.n_z - 1
        for way in range(2):
            ours = p.z == (0 if way == 0 else last)
            targets = range(last, 0, -1) if way == 0 else range(last)
            further = p.z + 1 if way == 0 else p.z - 1
            for target in targets:

                def copy(way=way, target=target, further=further):
                    return self.line_copy(self.sum.at[0, :, :, self.slice_of(target)], way, target, further)

                when(ours, lambda copy=copy: copy().start())
                self.line_pending.append((ours, copy))

    def relay(self, hop):
        p, s, last = self.p, self.sems, self.p.geo.n_z - 1
        for way in range(2):
            here = hop if way == 0 else last - hop
            targets = range(last, here, -1) if way == 0 else range(here)
            further = p.z + 1 if way == 0 else p.z - 1
            for target in targets:

                def copy(way=way, target=target, further=further):
                    return self.line_copy(self.line.at[way, target], way, target, further)

                def act(way=way, target=target, copy=copy):
                    self.add_line(way, target)
                    copy().start()

                when(p.z == here, act)
                self.line_pending.append((p.z == here, copy))

    def add_line(self, way, target):
        s, n_y = self.sems, self.p.geo.n_y
        at = (self.c_line, way, target)
        got = self.line.at[way, target]
        remote(got, got, s["ls"].at[at], s["lr"].at[at], self.p.dev_x()).wait_recv()

        @pl.loop(0, 2 * n_y)
        def _(index):
            where = (index // 2, lax.rem(index, 2))
            mine = wide(self.sum[(0,) + where + (self.slice_of(target),)])
            got[where] = (wide(got[where]) + mine).astype(BF)

    def collect(self):
        p, s, n_y, last = self.p, self.sems, self.p.geo.n_y, self.p.geo.n_z - 1
        for way in range(2):

            def act(way=way):
                at = (self.c_line, way, p.z)
                got = self.line.at[way, p.z]
                remote(got, got, s["ls"].at[at], s["lr"].at[at], p.dev_x()).wait_recv()

                @pl.loop(0, 2 * n_y)
                def _(index):
                    where = (index // 2, lax.rem(index, 2))
                    place = (0,) + where + (self.part,)
                    self.sum[place] = (wide(self.sum[place]) + wide(got[where])).astype(BF)

            when(p.z > 0 if way == 0 else p.z < last, act)
        Scatter.send_middle(self)

    def last(self):
        self.put(self.column_sum().reshape(self.unit, self.lanes))

    def finish(self):
        pass

    def drain(self):
        for valid, copy in self.line_pending:
            when(valid, lambda copy=copy: copy().wait_send())
        Scatter.drain(self)


def mm(left, right):
    return jnp.dot(left, right, preferred_element_type=F32)


def mm_nt(left, right):
    return lax.dot_general(left, right, (((1,), (1,)), ((), ())), preferred_element_type=F32)


def mm_tn(left, right):
    return lax.dot_general(left, right, (((0,), (0,)), ((), ())), preferred_element_type=F32)


def mean_of(values):
    return jnp.sum(values, -1, keepdims=True) * (1.0 / values.shape[-1])


def normal(values):
    centered = values - mean_of(values)
    scale = lax.rsqrt(mean_of(centered * centered) + epsilon)
    return centered * scale, scale


def norm_rows(source, gain, shift, target, block=32):
    @pl.loop(0, source.shape[0] // block)
    def _(at):
        rows = pl.ds(pl.multiple_of(at * block, block), block)
        unit, _ = normal(source[rows, :])
        target[rows, :] = (unit * gain + shift).astype(target.dtype)


def fold(values):
    total = values[0:8]
    for at in range(8, values.shape[0], 8):
        total = total + values[at : at + 8]
    return total


def norm_rows_back(source, gain, incoming, emit, sums, block=32):
    sums[...] = jnp.zeros_like(sums)

    @pl.loop(0, source.shape[0] // block)
    def _(at):
        rows = pl.ds(pl.multiple_of(at * block, block), block)
        unit, scale = normal(source[rows, :])
        back = incoming[rows, :]
        sums[0] += fold(back * unit)
        sums[1] += fold(back)
        inner = back * gain
        emit(rows, scale * (inner - mean_of(inner) - unit * mean_of(inner * unit)))


ROOT = 0.7978845608028654
CUBE = 0.044715


def gelu_parts(values):
    square = values * values
    curve = jnp.tanh(ROOT * (values + CUBE * (values * square)))
    return square, curve


class Layer:
    def __init__(self, refs, weight_a, weight_b, vec_d, vec_f, layer, heads):
        self.__dict__.update(refs)
        self.weight_a, self.weight_b = weight_a, weight_b
        self.vec_d, self.vec_f = vec_d, vec_f
        self.layer, self.heads = layer, heads

    def gain(self, at):
        return self.vec_d[self.layer * 10 + at : self.layer * 10 + at + 1, :]

    def shift(self, at):
        return self.gain(3 + at)

    def gain_f(self, at):
        return self.vec_f[self.layer * 3 + at : self.layer * 3 + at + 1, :]

    def lane_half(self, values, side):
        lane = lax.broadcasted_iota(jnp.int32, values.shape, 1)
        return (lane < HEAD_DIM) == (side == 0)

    def forward_norm(self):
        norm_rows(self.x, self.gain(0), self.shift(0), self.normed)

    def forward_qkv(self, part):
        value = mm(self.normed[...], self.weight_a(part))
        if part != 1:
            value = value + self.shift(3 if part == 0 else 4)
        self.qkv[part] = value.astype(BF)

    def forward_attention(self):
        valid = self.mask[...] > 0.5

        @pl.loop(0, self.heads // 2)
        def _(pair):
            lanes = pl.ds(pl.multiple_of(pair * 128, 128), 128)
            queries, keys, values = [self.qkv[part, :, lanes] for part in range(3)]
            context = None
            for side in range(2):
                half = self.lane_half(queries, side)
                scores = mm_nt(jnp.where(half, queries, jnp.zeros_like(queries)), keys)
                scores = jnp.where(valid, scores * HEAD_DIM**-0.5, -1e9)
                top = jnp.max(scores, -1, keepdims=True)
                grown = jnp.exp(scores - top)
                prob = grown / jnp.sum(grown, -1, keepdims=True)
                self.prob[2 * pair + side] = prob
                product = mm(prob.astype(BF), values)
                context = product if side == 0 else jnp.where(half, product, context)
            self.context[:, lanes] = context

    def forward_out(self):
        norm_rows(self.context, self.gain(1), self.shift(1), self.sub)
        self.after[...] = self.x[...] + (mm(self.sub[...], self.weight_a(3)) + self.shift(5))
        norm_rows(self.after, self.gain(2), self.shift(2), self.normed_ffn)

    def forward_up(self, part):
        width = self.x.shape[1]
        lanes = slice(part * width, (part + 1) * width)
        self.hidden[:, lanes] = mm(self.normed_ffn[...], self.weight_a(4 + part)) + self.gain_f(1)[:, lanes]

    def forward_gelu(self):
        @pl.loop(0, self.x.shape[0] // 16)
        def _(at):
            rows = pl.ds(pl.multiple_of(at * 16, 16), 16)
            values = self.hidden[rows, :]
            _, curve = gelu_parts(values)
            unit, _ = normal(0.5 * values * (1.0 + curve))
            self.sub_ffn[rows, :] = (unit * self.gain_f(0) + self.gain_f(2)).astype(BF)

    def forward_down(self, lanes):
        value = mm(self.sub_ffn[...], self.weight_b(slice(None), lanes))
        self.x_next[:, lanes] = self.after[:, lanes] + (value + self.shift(6)[:, lanes])


    def store_sums_d(self, at, sums):
        row = self.layer * 10 + at
        self.grad_d[row : row + 1, :] = jnp.sum(sums, 0, keepdims=True)

    def store_sums_f(self, at, sums):
        row = self.layer * 3 + at
        self.grad_f[row : row + 1, :] = jnp.sum(sums, 0, keepdims=True)

    def backward_start(self):
        self.low[...] = self.back[...].astype(BF)
        self.store_sums_d(9, wide(self.low[...]))

    def grad_up(self, part):
        width = self.x.shape[1]
        return mm_tn(self.normed_ffn[...], self.d_hidden[:, part * width : (part + 1) * width])

    def grad_out(self):
        return mm_tn(self.sub[...], self.low[...])

    def grad_qkv(self, part):
        return mm_tn(self.normed[...], self.d_qkv[part])

    def backward_down(self):
        width = self.x.shape[1]
        for part in range(self.hidden.shape[1] // width):
            lanes = slice(part * width, (part + 1) * width)
            self.wide_back[:, lanes] = mm_nt(self.low[...], self.weight_b(lanes, slice(None)))

    def backward_gelu(self):
        self.sums_f[...] = jnp.zeros_like(self.sums_f)

        @pl.loop(0, self.x.shape[0] // 16)
        def _(at):
            rows = pl.ds(pl.multiple_of(at * 16, 16), 16)
            values = self.hidden[rows, :]
            square, curve = gelu_parts(values)
            unit, scale = normal(0.5 * values * (1.0 + curve))
            back = self.wide_back[rows, :]
            self.sums_f[0] += fold(back * unit)
            self.sums_f[1] += fold(back)
            inner = back * self.gain_f(0)
            d_gelu = scale * (inner - mean_of(inner) - unit * mean_of(inner * unit))
            slope = 0.5 * (1.0 + curve) + 0.5 * values * (1.0 - curve * curve) * (
                ROOT * (1.0 + 3.0 * CUBE * square)
            )
            low = (d_gelu * slope).astype(BF)
            self.d_hidden[rows, :] = low
            self.sums_f[2] += fold(wide(low))

        self.store_sums_f(0, self.sums_f[0])
        self.store_sums_f(2, self.sums_f[1])
        self.store_sums_f(1, self.sums_f[2])

    def backward_up(self):
        width = self.x.shape[1]
        total = None
        for part in range(self.hidden.shape[1] // width):
            lanes = slice(part * width, (part + 1) * width)
            value = mm_nt(self.d_hidden[:, lanes], self.weight_a(4 + part))
            if part == 0:
                self.incoming[...] = value
            else:
                self.incoming[...] += value

        def emit(rows, value):
            value = self.back[rows, :] + value
            self.back[rows, :] = value
            self.low[rows, :] = value.astype(BF)

        norm_rows_back(self.after, self.gain(2), self.incoming, emit, self.sums_d)
        self.store_sums_d(2, self.sums_d[0])
        self.store_sums_d(5, self.sums_d[1])

    def backward_out(self):
        self.store_sums_d(8, wide(self.low[...]))
        self.incoming[...] = mm_nt(self.low[...], self.weight_a(3))

        def emit(rows, value):
            self.low[rows, :] = value.astype(BF)

        norm_rows_back(self.context, self.gain(1), self.incoming, emit, self.sums_d)
        self.store_sums_d(1, self.sums_d[0])
        self.store_sums_d(4, self.sums_d[1])

    def backward_attention(self):
        @pl.loop(0, self.heads // 2)
        def _(pair):
            lanes = pl.ds(pl.multiple_of(pair * 128, 128), 128)
            queries, keys, values = [self.qkv[part, :, lanes] for part in range(3)]
            d_context = self.low[:, lanes]
            found = [None] * 3
            for side in range(2):
                half = self.lane_half(d_context, side)
                prob = self.prob[2 * pair + side]
                d_prob = mm_nt(jnp.where(half, d_context, jnp.zeros_like(d_context)), values)
                dot = jnp.sum(prob * d_prob, -1, keepdims=True)
                d_scores = (prob * (d_prob - dot)).astype(BF)
                new = (
                    mm(d_scores, keys) * HEAD_DIM**-0.5,
                    mm_tn(d_scores, queries) * HEAD_DIM**-0.5,
                    mm_tn(prob.astype(BF), d_context),
                )
                found = [n if side == 0 else jnp.where(half, n, f) for n, f in zip(new, found)]
            for part in range(3):
                self.d_qkv[part, :, lanes] = found[part].astype(BF)

    def backward_qkv(self):
        self.store_sums_d(6, wide(self.d_qkv[0]))
        self.store_sums_d(7, wide(self.d_qkv[2]))
        for part in range(3):
            value = mm_nt(self.d_qkv[part], self.weight_a(part))
            if part == 0:
                self.incoming[...] = value
            else:
                self.incoming[...] += value

        def emit(rows, value):
            self.back[rows, :] = self.back[rows, :] + value

        norm_rows_back(self.x, self.gain(0), self.incoming, emit, self.sums_d)
        self.store_sums_d(0, self.sums_d[0])
        self.store_sums_d(3, self.sums_d[1])


def saved_shapes(rows, width, wide_width, heads):
    return {
        "normed": ((rows, width), BF),
        "qkv": ((3, rows, width), BF),
        "prob": ((heads, rows, rows), F32),
        "context": ((rows, width), F32),
        "sub": ((rows, width), BF),
        "after": ((rows, width), F32),
        "normed_ffn": ((rows, width), BF),
        "hidden": ((rows, wide_width), F32),
        "sub_ffn": ((rows, wide_width), BF),
    }


def work_shapes(rows, width, wide_width):
    return {
        "low": ((rows, width), BF),
        "incoming": ((rows, width), F32),
        "wide_back": ((rows, wide_width), F32),
        "d_qkv": ((3, rows, width), BF),
        "sums_d": ((2, 8, width), F32),
        "sums_f": ((3, 8, wide_width), F32),
    }


def spread_tables(geo):
    tables = []
    for width, real in ((geo.width, geo.rows_a), (geo.wide_width, geo.rows_b)):
        at = np.arange(width)
        owner = (at[None, :] // real == np.arange(geo.owners)[:, None]).astype(np.float32)
        tables += [jnp.asarray(owner, BF), jnp.asarray(at[None, :] % real, jnp.int32)]
    return tables


def unpack_vectors(geo, whole_v, wide_v, tables, vec_d, vec_f):
    owner_d, rest_d, owner_f, rest_f = tables
    lines = geo.kind["v"][1]
    wide_v[...] = wide(whole_v[0])
    line_of = lambda at: wide_v[pl.ds(at, geo.owners, stride=lines), :].astype(BF)
    pick_d = lax.broadcasted_iota(jnp.int32, (geo.slot, geo.width), 0) == rest_d[...]
    for line in range(geo.lines_d):
        spread = mm_tn(line_of(line), owner_d[...])
        for at in range(geo.per_row):
            part = spread[at * geo.slot : (at + 1) * geo.slot]
            row = line * geo.per_row + at
            if row < geo.layers * 10:
                vec_d[row : row + 1, :] = jnp.sum(jnp.where(pick_d, part, 0.0), 0, keepdims=True)
    pick_f = lax.broadcasted_iota(jnp.int32, (128, geo.width), 0)
    for row in range(geo.layers * 3):
        line = line_of(geo.lines_d + row)
        for first in range(0, geo.wide_width, geo.width):
            lanes = slice(first, first + geo.width)
            spread = jnp.where(pick_f == rest_f[:, lanes], mm_tn(line, owner_f[:, lanes]), 0.0)
            vec_f[row : row + 1, lanes] = jnp.sum(spread, 0, keepdims=True)


GATHER_SEMS = (
    "lz", "lo", "zs", "zr", "xs", "xr", "ys", "yr", "ds", "dr", "cs", "cr",
    "gl", "gx", "gy", "gd", "gs", "gr", "hs", "hr",
)
LINE_FIRST = (1, 6)


def forward_kernel(geo, names_perm, saved_names, *refs):
    refs = list(refs)
    take = lambda number: [refs.pop(0) for _ in range(number)]
    sources = dict(zip(geo.kinds, take(len(geo.kinds))))
    perms = dict(zip(names_perm, take(len(names_perm))))
    act_ref, mask_ref = take(2)
    tables = take(4)
    out_ref, vec_d, vec_f, kept_a, kept_b, kept_x = take(6)
    kept = [dict(zip(saved_names, take(len(saved_names)))) for _ in range(geo.layers)]
    wholes = dict(zip(("a", "v", "b"), take(3)))
    wholes.update({name: wholes["b"] for name in geo.down})
    bufs = dict(zip(geo.plain, take(len(geo.plain))))
    units = dict(zip(names_perm, take(len(names_perm))))
    saved = [dict(zip(saved_names, take(len(saved_names)))) for _ in range(geo.layers)]
    xs, wide_v, keep_sem = take(3)
    sems = dict(zip(GATHER_SEMS, take(len(GATHER_SEMS))))
    place = Place(geo)
    chunks, line_chunks = [("v", 0, 0, 0)], []
    for layer in range(geo.layers):
        chunks += [chunk_a(geo, layer, pair) for pair in range(geo.pairs)]
        for name in geo.down:
            (line_chunks if name == "l" else chunks).append(chunk_down(geo, layer, name))
    moves = [
        Gather(place, at, chunk, sources, bufs, units, perms, wholes, sems)
        for at, chunk in enumerate(chunks)
    ]
    lines = [
        GatherLine(place, at, chunk, sources, wholes, sems) for at, chunk in enumerate(line_chunks)
    ]
    keeps = []

    def keep(src, dst):
        copy = pltpu.make_async_copy(src, dst, keep_sem.at[len(keeps)])
        copy.start()
        keeps.append(copy)

    net = []
    for layer in range(geo.layers):
        fields = dict(saved[layer], x=xs.at[layer], x_next=xs.at[layer + 1], mask=mask_ref)
        read_a = lambda at, layer=layer: wholes["a"][layer * geo.blocks + at]
        read_b = lambda rows, lanes, layer=layer: wholes["b"][layer, rows, lanes]
        net.append(Layer(fields, read_a, read_b, vec_d, vec_f, layer, geo.width // HEAD_DIM))

    def compute(number):
        name, at, lead, first = chunks[number]
        if geo.lined and name == "c":
            lines[lead].arrive()
            down(lead, *geo.lanes_of["l"])
        moves[number].arrive()
        if name == "v":
            unpack_vectors(geo, wholes["v"], wide_v, tables, vec_d, vec_f)
            return
        k, _, _, lanes = geo.kind[name]
        layer = at // geo.pairs if name == "a" else at
        one = net[layer]
        save = lambda *found: [keep(saved[layer][field], kept[layer][field]) for field in found]
        if name == "a":
            keep(wholes["a"].at[pl.ds(lead, k)], kept_a.at[pl.ds(lead, k)])
            pair = at % geo.pairs
            if pair == 0:
                one.forward_norm()
                one.forward_qkv(0)
                one.forward_qkv(1)
            elif pair == 1:
                one.forward_qkv(2)
                save("normed", "qkv")
                one.forward_attention()
                one.forward_out()
                save("prob", "context", "sub", "after", "normed_ffn")
            else:
                one.forward_up(2 * pair - 4)
                one.forward_up(2 * pair - 3)
                if pair == geo.pairs - 1:
                    one.forward_gelu()
                    save("hidden", "sub_ffn")
        else:
            down(layer, first, lanes)
            if name == geo.down[-1] and layer < geo.layers - 1:
                keep(xs.at[layer + 1], kept_x.at[layer + 1])

    def down(layer, first, lanes):
        where = pl.ds(first, lanes)
        keep(wholes["b"].at[layer, :, where], kept_b.at[layer, :, where])
        net[layer].forward_down(slice(first, first + lanes))

    extra = {}
    for layer, line in enumerate(lines):
        plan = [line.start, line.forward, line.corner]
        plan += [
            lambda line=line, hop=hop, half=half: line.relay(hop, half)
            for hop in range(geo.n_z)
            for half in range(2)
        ]
        needed = chunks.index(chunk_down(geo, layer, "c")) + 2
        for at, act in enumerate(plan):
            step = at - 2 if at < 3 else LINE_FIRST[min(layer, 1)] + at - 3
            extra.setdefault(min(step, needed), []).append(act)

    place.greet()
    xs[0] = wide(act_ref[...])
    keep(xs.at[0], kept_x.at[0])
    place.meet()
    run_pipeline(
        [
            (-2, lambda c: moves[c].start_z()),
            (0, lambda c: moves[c].own()),
            (1, lambda c: moves[c].forward()),
            (3, compute),
            (2, lambda c: moves[c].corner()),
        ],
        len(moves),
        extra,
    )
    out_ref[...] = xs[geo.layers].astype(BF)
    for move in moves + lines:
        move.drain()
    for copy in keeps:
        copy.wait()


def run_forward(geo, sources, act, mask):
    names_perm = [name for name in geo.plain if geo.permuted(name)]
    perms = [jnp.asarray(geo.permutation(name), BF) for name in names_perm]
    rows, width = act.shape
    total = sum(geo.number.values())
    heads = width // HEAD_DIM
    saved = saved_shapes(rows, width, geo.wide_width, heads)
    bufs, units, wholes = [], [], []
    for name in geo.plain:
        k, sent, unit, lanes = geo.kind[name]
        bufs.append(pltpu.VMEM((geo.number[name], geo.n_z * sent, lanes), BF))
        if name in names_perm:
            units.append(pltpu.VMEM((geo.number[name], k, unit, lanes), BF))
    wholes = [(geo.whole_shape(name), BF) for name in ("a", "v", "c")]
    n_y, n_z = geo.n_y, geo.n_z
    n_keeps = geo.layers * (len(saved) + geo.pairs + len(geo.down) + 1)
    vec_rows = geo.layers * 10
    outs = [
        jax.ShapeDtypeStruct((rows, width), BF),
        jax.ShapeDtypeStruct((vec_rows, width), F32),
        jax.ShapeDtypeStruct((geo.layers * 3, geo.wide_width), F32),
        jax.ShapeDtypeStruct(*wholes[0]),
        jax.ShapeDtypeStruct(*wholes[2]),
        jax.ShapeDtypeStruct((geo.layers, rows, width), F32),
    ] + [jax.ShapeDtypeStruct(*saved[name]) for _ in range(geo.layers) for name in saved]
    found = pl.pallas_call(
        functools.partial(forward_kernel, geo, names_perm, list(saved)),
        out_shape=outs,
        in_specs=[IN_VMEM] * (len(sources) + len(perms) + 6),
        out_specs=[IN_VMEM] * 3 + [ANY] * (len(outs) - 3),
        scratch_shapes=[pltpu.VMEM(*whole) for whole in wholes]
        + bufs
        + units
        + [pltpu.VMEM(*saved[name]) for _ in range(geo.layers) for name in saved]
        + [
            pltpu.VMEM((geo.layers + 1, rows, width), F32),
            pltpu.VMEM(wholes[1][0][1:], F32),
            dma(n_keeps),
            dma(total),
            dma(total),
            dma(total, n_z),
            dma(total, n_z),
            dma(total),
            dma(total),
            dma(total, n_y),
            dma(total, n_y),
            dma(total, 2, n_y),
            dma(total, 2, n_y),
            dma(total, 2 * n_y),
            dma(total, 2 * n_y),
            dma(geo.layers),
            dma(geo.layers, 2),
            dma(geo.layers, 2, n_y),
            dma(geo.layers, 2, n_y),
        ]
        + [dma(geo.layers, 2, n_z, 2 * n_y)] * 4,
        compiler_params=pltpu.CompilerParams(
            collective_id=0, has_side_effects=True, vmem_limit_bytes=60 * 2**20
        ),
    )(*sources, *perms, act, mask, *spread_tables(geo))
    names = list(saved)
    kept = [dict(zip(names, found[6 + layer * len(names) :])) for layer in range(geo.layers)]
    return found[:6], kept


def pack_gradients(geo, grad_d, grad_f, tables, wide_v, stage_v):
    owner_d, rest_d, owner_f, rest_f = tables
    lines = geo.kind["v"][1]
    wide_v[...] = jnp.zeros_like(wide_v)
    pick_d = lax.broadcasted_iota(jnp.int32, (geo.slot, geo.width), 0) == rest_d[...]
    for line in range(geo.lines_d):
        parts = []
        for at in range(geo.per_row):
            row = line * geo.per_row + at
            if row < geo.layers * 10:
                parts.append(jnp.where(pick_d, grad_d[row : row + 1, :], 0.0))
            else:
                parts.append(jnp.zeros(pick_d.shape, F32))
        wide_v[pl.ds(line, geo.owners, stride=lines), :] = mm_nt(
            owner_d[...], jnp.concatenate(parts, 0).astype(BF)
        )
    pick_f = lax.broadcasted_iota(jnp.int32, (128, geo.width), 0)
    for row in range(geo.layers * 3):
        total = None
        for first in range(0, geo.wide_width, geo.width):
            lanes = slice(first, first + geo.width)
            part = jnp.where(pick_f == rest_f[:, lanes], grad_f[row : row + 1, lanes], 0.0).astype(BF)
            part = mm_nt(owner_f[:, lanes], part)
            total = part if total is None else total + part
        wide_v[pl.ds(geo.lines_d + row, geo.owners, stride=lines), :] = total
    stage_v[...] = wide_v[...].astype(BF).reshape(stage_v.shape)


class Ring:
    def __init__(self, sources, slots, sems):
        self.slots, self.size, self.used = slots, slots.shape[0], 0
        self.copies = [
            pltpu.make_async_copy(source, slots.at[at % self.size], sems.at[at % self.size])
            for at, source in enumerate(sources)
        ]
        for copy in self.copies[: self.size]:
            copy.start()

    def next(self):
        at = self.used
        self.used += 1
        if 0 < at and at - 1 + self.size < len(self.copies):
            self.copies[at - 1 + self.size].start()
        self.copies[at].wait()
        return self.slots[at % self.size]


SCATTER_SEMS = ("cs", "cr", "ms", "mr", "es", "er", "zs", "zr", "ls", "lr", "fx", "fy")
Z_SLOTS = 3
LINE_LAGS = (4, 3)
SCATTER_LAGS = (0, 1, 3, 5, 7)


def ring_slots(geo):
    return 3 if geo.roomy else 2


def backward_kernel(geo, names_perm, names, *refs):
    refs = list(refs)
    take = lambda number: [refs.pop(0) for _ in range(number)]
    by_kind = lambda kinds=geo.kinds: dict(zip(kinds, take(len(kinds))))
    saved_names, work_names = names
    layers, blocks, width = geo.layers, geo.blocks, geo.width
    perms = dict(zip(names_perm, take(len(names_perm))))
    cot_ref, vec_d, vec_f = take(3)
    tables = take(4)
    whole_a, whole_b, kept_x = take(3)
    kept = [dict(zip(saved_names, take(len(saved_names)))) for _ in range(layers)]
    for layer in range(layers):
        kept[layer]["x"] = kept_x.at[layer]
    back_ref, out_qkv, out_out, out_up, out_down, out_d, out_f = take(7)
    fields = dict(zip(saved_names, take(len(saved_names))))
    fields.update(zip(work_names, take(len(work_names))))
    stages, sums, mids, ends = [by_kind() for _ in range(4)]
    z_send, z_recv = [by_kind(geo.plain) for _ in range(2)]
    line_refs = take(1) if geo.lined else []
    x_ref, grad_d, grad_f, wide_v, slots = take(5)
    last_low, last_ffn = take(2) if geo.roomy else (None, None)
    sem_l, sem_w = take(2)
    sems = dict(zip(SCATTER_SEMS, take(len(SCATTER_SEMS))))
    fields.update(d_hidden=fields["sub_ffn"], x=x_ref, back=back_ref, grad_d=grad_d, grad_f=grad_f)
    place = Place(geo)

    def writer(chunk):
        name, at, lead, first = chunk
        rows_a, rows_b, lines = geo.rows_a, geo.rows_b, geo.lines_d

        def put_a(value):
            layer = at // geo.pairs
            for side in range(2):
                block = 2 * (at % geo.pairs) + side
                piece = value[side * rows_a : (side + 1) * rows_a]
                if block < 3:
                    out_qkv[layer, :, block * width : (block + 1) * width] = piece
                elif block == 3:
                    out_out[layer] = piece
                else:
                    out_up[layer, :, (block - 4) * width : (block - 3) * width] = piece

        def put_down(value):
            out_down[lead, :, first : first + value.shape[1]] = value[:rows_b]

        def put_v(value):
            out_d[...] = value[:lines]
            out_f[...] = value[lines : lines + layers * 3]

        return {"a": put_a, "v": put_v}.get(name, put_down)

    order, seen = [], {name: [] for name in geo.kinds}
    early = {layer: geo.down for layer in range(layers)}
    late = ("c", "d") if geo.roomy else ()
    early[0] = tuple(name for name in geo.down if name not in late)
    for layer in reversed(range(layers)):
        early[layer] = early[layer][::-1]
        order += [chunk_down(geo, layer, name) for name in early[layer]]
        order += [chunk_a(geo, layer, pair) for pair in list(range(2, geo.pairs)) + [1, 0]]
    order.append(("v", 0, 0, 0))
    order += [chunk_down(geo, 0, name) for name in late]
    moves, stage_of = [], []
    for number, chunk in enumerate(order):
        name = chunk[0]
        stage = stages[name].at[len(seen[name]) % stages[name].shape[0]]
        slots_z = z_send[name].shape[0] if name in z_send else 1
        z_slot = len(seen[name]) % slots_z
        before = seen[name][-slots_z] if len(seen[name]) >= slots_z else None
        move = (ScatterLine if name == "l" else Scatter)(
            place, number, chunk, stage, sums, mids, ends, perms, z_send, z_recv, z_slot, before,
            writer(chunk), sems,
        )
        if name == "l":
            move.c_line = len(seen[name])
            move.land(line_refs[0].at[move.c_line])
        seen[name].append(move)
        stage_of.append(stage)
        moves.append(move)
    for number, chunk in enumerate(order):
        if chunk[0] == "a" and chunk[1] >= geo.pairs:
            moves[number].heir = moves[[later[:2] for later in order].index(("a", chunk[1] - geo.pairs))]
    step, plan = [0], {}
    for number, chunk in enumerate(order):
        move = moves[number]
        acts = [move.start, move.pair, move.middle, move.last, move.finish]
        lags = list(SCATTER_LAGS)
        if chunk[0] == "l":
            hops = [lambda move=move, hop=hop: move.relay(hop) for hop in range(1, geo.n_z - 1)]
            acts[2:2] = hops + [move.collect]
            first, each = LINE_LAGS
            lags[2:] = [first + each * at for at in range(len(hops) + 1)]
            lags += [lags[-1] + 1, lags[-1] + 2, lags[-1] + 2]
        for lag, act in zip(lags, acts):
            plan.setdefault(number + lag, []).append((lag, act))

    def serve():
        for _, act in sorted(plan.get(step[0], []), key=lambda pair: pair[0]):
            act()
        step[0] += 1

    def stage_down(name, rows_ref, low_ref):
        unit = geo.kind[name][2]
        first, lanes = geo.lanes_of[name]
        for column in range(geo.n_dp // 2):
            rows = slice(column * 2 * unit, (column + 1) * 2 * unit)
            value = mm_tn(rows_ref[:, rows], low_ref[:, first : first + lanes])
            stage_of[step[0]][0, column // 2, column % 2] = value.astype(BF).reshape(2, unit, lanes)

    def stage_a(side, value):
        stage_of[step[0]][side] = value.astype(BF).reshape(geo.n_y, 2, 2, -1, width)

    loads = {}
    field_names = ["x"] + list(saved_names)

    def fetch(layer, *found):
        for name in found:
            loads[name] = pltpu.make_async_copy(
                kept[layer][name], fields[name], sem_l.at[field_names.index(name)]
            )
            loads[name].start()

    def ready(*found):
        for name in found:
            loads[name].wait()

    fetch(layers - 1, "sub_ffn")
    sources = []
    for layer in reversed(range(layers)):
        parts = geo.wide_width // width
        sources += [whole_b.at[layer, pl.ds(part * width, width)] for part in range(parts)]
        sources += [whole_a.at[layer * blocks + at] for at in list(range(4, blocks)) + [3, 0, 1, 2]]
    cot_copy = pltpu.make_async_copy(cot_ref, back_ref, sem_l.at[len(field_names)])
    cot_copy.start()
    place.greet()
    cot_copy.wait()
    loads["sub_ffn"].wait()
    ring = Ring(sources, slots, sem_w)
    fetch(
        layers - 1, "hidden", "normed_ffn", "after", "sub", "context", "prob", "qkv", "normed", "x"
    )
    for layer in reversed(range(layers)):
        one = Layer(
            fields, lambda at: ring.next(), lambda rows, lanes: ring.next(), vec_d, vec_f, layer,
            width // HEAD_DIM,
        )
        again = (lambda *found: fetch(layer - 1, *found)) if layer > 0 else (lambda *found: None)
        one.backward_start()
        if layer < layers - 1:
            ready("sub_ffn")
        for name in early[layer]:
            stage_down(name, one.sub_ffn, one.low)
            if step[0] == 0:
                place.meet()
            serve()
        if layer == 0 and late:
            last_low[...] = one.low[...]
            last_ffn[...] = one.sub_ffn[...]
        one.backward_down()
        ready("hidden")
        one.backward_gelu()
        again("hidden")
        ready("normed_ffn")
        for pair in range(2, geo.pairs):
            stage_a(0, one.grad_up(2 * pair - 4))
            stage_a(1, one.grad_up(2 * pair - 3))
            serve()
        again("normed_ffn")
        ready("after")
        one.backward_up()
        again("after", "sub_ffn")
        ready("sub", "context")
        stage_a(1, one.grad_out())
        one.backward_out()
        again("sub", "context")
        ready("prob", "qkv")
        one.backward_attention()
        again("prob", "qkv")
        ready("normed")
        stage_a(0, one.grad_qkv(2))
        serve()
        stage_a(0, one.grad_qkv(0))
        stage_a(1, one.grad_qkv(1))
        serve()
        again("normed")
        ready("x")
        one.backward_qkv()
        again("x")
    pack_gradients(geo, grad_d, grad_f, tables, wide_v, stage_of[step[0]])
    serve()
    for name in late:
        stage_down(name, last_ffn, last_low)
        serve()
    while step[0] <= max(plan):
        serve()
    for move in moves:
        move.drain()


def run_backward(geo, cot, vec_d, vec_f, whole_a, whole_b, kept_x, kept):
    rows, width = cot.shape
    layers, n_y, n_z = geo.layers, geo.n_y, geo.n_z
    heads = width // HEAD_DIM
    saved, work = saved_shapes(rows, width, geo.wide_width, heads), work_shapes(rows, width, geo.wide_width)
    names = (list(saved), list(work))
    names_perm = [name for name in geo.plain if geo.permuted(name)]
    perms = [jnp.asarray(geo.permutation(name).T, BF) for name in names_perm]
    total = sum(geo.number.values())
    groups = [[] for _ in range(6)]
    for name in geo.kinds:
        k, sent, unit, lanes = geo.kind[name]
        number = geo.number[name]
        mid_steps = max(n_y - 1, (n_y + 1) // 2)
        groups[0].append(pltpu.VMEM((2 if name == "a" else 1, k, n_y, 2, 2, unit, lanes), BF))
        groups[1].append(pltpu.VMEM((number, k, n_y, 2, unit, lanes), BF))
        landing = geo.pairs if name == "a" else number
        unit = sent if name == "l" else unit
        groups[2].append(pltpu.VMEM((landing, mid_steps, k, 2, unit, lanes), BF))
        groups[3].append(pltpu.VMEM((number, mid_steps, k, unit, lanes), BF))
        if name == "l":
            continue
        groups[4].append(pltpu.VMEM((min(number, Z_SLOTS), n_z, sent, lanes), BF))
        groups[5].append(pltpu.VMEM((number, n_z, sent, lanes), BF))
    scratch = [pltpu.VMEM(*saved[name]) for name in saved] + [pltpu.VMEM(*work[name]) for name in work]
    scratch += sum(groups, [])
    if geo.lined:
        _, sent, _, lanes = geo.kind["l"]
        scratch.append(pltpu.VMEM((layers, 2, n_z, n_y, 2, sent, lanes), BF))
    scratch += [
        pltpu.VMEM((rows, width), F32),
        pltpu.VMEM((layers * 10, width), F32),
        pltpu.VMEM((layers * 3, geo.wide_width), F32),
        pltpu.VMEM((geo.owners * geo.kind["v"][1], 128), F32),
        pltpu.VMEM((ring_slots(geo), width, width), BF),
    ]
    if geo.roomy:
        scratch += [pltpu.VMEM((rows, width), BF), pltpu.VMEM((rows, geo.wide_width), BF)]
    scratch += [
        dma(2 + len(saved)),
        dma(ring_slots(geo)),
        dma(total),
        dma(total),
        dma(total, 2, n_y),
        dma(total, 2, n_y),
        dma(total, 2, n_y),
        dma(total, 2, n_y),
        dma(total, n_z),
        dma(total, n_z),
        dma(layers, 2, n_z),
        dma(layers, 2, n_z),
        pltpu.SemaphoreType.REGULAR((total,)),
        pltpu.SemaphoreType.REGULAR((total, n_y)),
    ]
    return pl.pallas_call(
        functools.partial(backward_kernel, geo, names_perm, names),
        out_shape=[
            jax.ShapeDtypeStruct((rows, width), F32),
            jax.ShapeDtypeStruct((layers, geo.rows_a, 3 * width), F32),
            jax.ShapeDtypeStruct((layers, geo.rows_a, width), F32),
            jax.ShapeDtypeStruct((layers, geo.rows_a, geo.wide_width), F32),
            jax.ShapeDtypeStruct((layers, geo.rows_b, width), F32),
            jax.ShapeDtypeStruct((geo.lines_d, 128), F32),
            jax.ShapeDtypeStruct((layers * 3, 128), F32),
        ],
        in_specs=[IN_VMEM] * len(perms) + [ANY] + [IN_VMEM] * 6 + [ANY] * (3 + layers * len(saved)),
        out_specs=[IN_VMEM] * 7,
        scratch_shapes=scratch,
        compiler_params=pltpu.CompilerParams(
            collective_id=1, has_side_effects=True, vmem_limit_bytes=63 * 2**20
        ),
    )(
        *perms, cot, vec_d, vec_f, *spread_tables(geo), whole_a, whole_b, kept_x,
        *[kept[layer][name] for layer in range(layers) for name in saved],
    )


def pack_kernel(geo, *refs):
    act_short, act_long, len_short, len_long, w_qkv, w_out, w_up, w_down = refs[:8]
    norms_d, gains_ff, shifts_ff, cot_short, cot_long = refs[8:13]
    sources = dict(zip(geo.kinds, refs[13:]))
    act, mask, cot, lines = refs[13 + len(geo.kinds) :]
    width, rows_a, rows_b = geo.width, geo.rows_a, geo.rows_b

    def block(layer, at):
        if at == 3:
            return wide(w_out[layer])
        first = at if at < 3 else at - 4
        return wide((w_qkv if at < 3 else w_up)[layer, :, first * width : (first + 1) * width])

    def filled(pieces, rows):
        have = sum(piece.shape[0] for piece in pieces)
        if have < rows:
            pieces = pieces + [jnp.zeros((rows - have, pieces[0].shape[1]), F32)]
        return (jnp.concatenate(pieces, 0) if len(pieces) > 1 else pieces[0]).astype(BF)

    for layer in range(geo.layers):
        for pair in range(geo.pairs):
            pieces = [block(layer, 2 * pair), block(layer, 2 * pair + 1)]
            sources["a"][layer * geo.pairs + pair] = filled(pieces, geo.kind["a"][1])
        for name in geo.down:
            first, lanes = geo.lanes_of[name]
            piece = w_down[layer, :, first : first + lanes]
            if rows_b != geo.kind[name][1]:
                piece = filled([wide(piece)], geo.kind[name][1])
            sources[name][layer] = piece
    lines[...] = jnp.zeros_like(lines)
    gains_wide = wide(gains_ff[...])
    for layer in range(geo.layers):
        norms, shifts_wide = wide(norms_d[layer]), wide(shifts_ff[layer])
        for at in range(10):
            line, lane = divmod(layer * 10 + at, geo.per_row)
            lines[line : line + 1, lane * geo.slot : lane * geo.slot + rows_a] = norms[at : at + 1]
        for at in range(3):
            line = geo.lines_d + layer * 3 + at
            lines[line : line + 1, :rows_b] = gains_wide[layer : layer + 1] if at == 0 else shifts_wide[at - 1 : at]
    sources["v"][0] = lines[...].astype(BF)
    short = act_short.shape[0]
    act[:short] = act_short[...]
    act[short:] = act_long[...]
    rows = act.shape[0]

    def valid(shape, dim):
        at = lax.broadcasted_iota(jnp.int32, shape, dim)
        return jnp.where(jnp.where(at < short, at - len_short[0], at - short - len_long[0]) < 0, 1.0, 0.0)

    def bucket(dim):
        return jnp.where(lax.broadcasted_iota(jnp.int32, (rows, rows), dim) < short, 0, 1)

    mask[...] = jnp.where(bucket(0) == bucket(1), valid((rows, rows), 1), 0.0)
    keep = valid((rows, width), 0)
    cot[:short] = wide(cot_short[...]) * keep[:short]
    cot[short:] = wide(cot_long[...]) * keep[short:]


def run_pack(geo, args):
    rows = args[0].shape[0] + args[1].shape[0]
    shapes = []
    for name in geo.kinds:
        _, sent, _, lanes = geo.kind[name]
        shapes.append(jax.ShapeDtypeStruct((geo.number[name], sent, lanes), BF))
    shapes += [
        jax.ShapeDtypeStruct((rows, geo.width), BF),
        jax.ShapeDtypeStruct((rows, rows), F32),
        jax.ShapeDtypeStruct((rows, geo.width), F32),
    ]
    in_smem = pl.BlockSpec(memory_space=pltpu.SMEM)
    return pl.pallas_call(
        functools.partial(pack_kernel, geo),
        out_shape=shapes,
        in_specs=[IN_VMEM] * 2 + [in_smem] * 2 + [IN_VMEM] * 9,
        out_specs=[IN_VMEM] * len(shapes),
        scratch_shapes=[pltpu.VMEM((geo.kind["v"][1], 128), F32)],
        compiler_params=pltpu.CompilerParams(vmem_limit_bytes=63 * 2**20),
    )(*args[:8], jnp.concatenate(args[8:10], 1), *args[10:])


def unpack_kernel(geo, *refs):
    out, back, g_qkv, g_out, g_up, g_down, lines_d, lines_f = refs[:8]
    out_short, out_long, back_short, back_long, t_qkv, t_out, t_up, t_down = refs[8:16]
    t_gains_d, t_shifts_d, t_gains_ff, t_shifts_ff = refs[16:]
    short = out_short.shape[0]
    out_short[...] = out[:short]
    out_long[...] = out[short:]
    back_short[...] = back[:short]
    back_long[...] = back[short:]
    for source, target in ((g_qkv, t_qkv), (g_out, t_out), (g_up, t_up), (g_down, t_down)):
        target[...] = source[...]
    for layer in range(geo.layers):
        for at in range(10):
            line, lane = divmod(layer * 10 + at, geo.per_row)
            value = lines_d[line : line + 1, lane * geo.slot : lane * geo.slot + geo.rows_a]
            if at < 3:
                t_gains_d[layer, at : at + 1, :] = value
            else:
                t_shifts_d[layer, at - 3 : at - 2, :] = value
        for at in range(3):
            value = lines_f[layer * 3 + at : layer * 3 + at + 1, : geo.rows_b]
            if at == 0:
                t_gains_ff[layer : layer + 1, :] = value
            else:
                t_shifts_ff[layer, at - 1 : at, :] = value


def run_unpack(geo, found, args):
    like = lambda index, dtype: jax.ShapeDtypeStruct(args[index].shape, dtype)
    shapes = [like(0, BF), like(1, BF), like(0, F32), like(1, F32)]
    shapes += [like(index, F32) for index in range(4, 12)]
    return pl.pallas_call(
        functools.partial(unpack_kernel, geo),
        out_shape=shapes,
        in_specs=[IN_VMEM] * len(found),
        out_specs=[IN_VMEM] * len(shapes),
        compiler_params=pltpu.CompilerParams(vmem_limit_bytes=63 * 2**20),
    )(*found)


def on_device(*args):
    n_dp, n_z = lax.axis_size("dp"), lax.axis_size("fsdp")
    geo = Geometry(n_dp, n_z, args[4].shape, args[6].shape, args[7].shape)
    *sources, act, mask, cot = run_pack(geo, args)
    found, kept = run_forward(geo, sources, act, mask)
    out, vec_d, vec_f, whole_a, whole_b, kept_x = found
    grads = run_backward(geo, cot, vec_d, vec_f, whole_a, whole_b, kept_x, kept)
    return tuple(run_unpack(geo, (out,) + tuple(grads), args))


def solution(mesh):
    return jax.shard_map(
        on_device,
        mesh=mesh,
        in_specs=(
            P(("dp", "fsdp"), None),
            P(("dp", "fsdp"), None),
            P(("dp", "fsdp")),
            P(("dp", "fsdp")),
            P(None, ("dp", "fsdp"), None),
            P(None, ("dp", "fsdp"), None),
            P(None, ("dp", "fsdp"), None),
            P(None, ("dp", "fsdp"), None),
            P(None, None, ("dp", "fsdp")),
            P(None, None, ("dp", "fsdp")),
            P(None, ("dp", "fsdp")),
            P(None, None, ("dp", "fsdp")),
            P(("dp", "fsdp"), None),
            P(("dp", "fsdp"), None),
        ),
        out_specs=(
            P(("dp", "fsdp"), None),
            P(("dp", "fsdp"), None),
            P(("dp", "fsdp"), None),
            P(("dp", "fsdp"), None),
            P(None, ("dp", "fsdp"), None),
            P(None, ("dp", "fsdp"), None),
            P(None, ("dp", "fsdp"), None),
            P(None, ("dp", "fsdp"), None),
            P(None, None, ("dp", "fsdp")),
            P(None, None, ("dp", "fsdp")),
            P(None, ("dp", "fsdp")),
            P(None, None, ("dp", "fsdp")),
        ),
        check_vma=False,
    )
```
